32 devices in a mesh: dir: 2 (over x), dp: 16 (over z, y, core).
Axes of the slice: x: 2, y: 2, z: 4, core: 2. Of those that a mesh axis runs over, the one named last changes fastest.
Arguments:
- hidden_in: bfloat16 [2, 16384, 768], P('dir', 'dp'), may hold values from -6 to 6
- lengths: int32 [16, 8], P('dp'), may hold values from 1 to 1024, 2048 in all within a row
- gain_in: float32 [768], replicated, may hold values from 0.5 to 1.5
- w_x: bfloat16 [768, 1536], replicated, may hold values from -0.21875 to 0.21875
- w_z: bfloat16 [768, 1536], replicated, may hold values from -0.21875 to 0.21875
- w_bcdt: bfloat16 [768, 304], replicated, may hold values from -0.21875 to 0.21875
- conv_w: float32 [4, 1792], replicated, may hold values from -3 to 3
- dt_bias: float32 [2, 24], replicated, may hold values from -6 to -2
- a_log: float32 [2, 24], replicated, may hold values from -4 to 0.5
- d_skip: float32 [24], replicated, may hold values from 0.5 to 2
- gain_mix: float32 [1536], replicated, may hold values from 0.5 to 1.5
- w_out: bfloat16 [1536, 768], replicated, may hold values from -0.15625 to 0.15625
- cotangent: bfloat16 [2, 16384, 768], P('dir', 'dp'), may hold values from -6 to 6
Outputs:
- hidden_out: bfloat16 [2, 16384, 768], P('dir', 'dp')
- grad_in: bfloat16 [2, 16384, 768], P('dir', 'dp')
- grad_w_x: float32 [768, 1536], P('dp')
- grad_w_z: float32 [768, 1536], P('dp')
- grad_w_bcdt: float32 [768, 304], P('dp')
- grad_w_out: float32 [1536, 768], P('dp')
- grad_gain_in: float32 [768], replicated
- grad_conv_w: float32 [4, 1792], replicated
- grad_dt_bias: float32 [2, 24], replicated
- grad_a_log: float32 [2, 24], replicated
- grad_d_skip: float32 [24], replicated
- grad_gain_mix: float32 [1536], replicated
The draws below stay inside these ranges and needn't reach their ends.
Inputs may be any that keep to these rules, and one draw needn't show every extreme that they name: In each row the first 7 entries are sequence lengths and the last is padding; the row sums to 2048 and its largest entry is exactly 1024.
All inputs are finite; a program needn't handle non-finite values.
Results may differ from the reference program's by a relative error of at most 0.013.
Values may be sent and summed in bfloat16 or wider, within the bound.
No kernel may reach another device: no remote copies, remote signals or barrier semaphores. Data moves between devices by JAX's collectives and lax.ppermute only.
A program may use at most 320 MiB of HBM per device.

```python
import math
import jax
import jax.numpy as jnp
import numpy as np
from jax import lax

D = 768
INNER = 1536
HEADDIM = 64
STATE = 64
CONV = 4
SPAN = 128
TOK_DEV = 1024
SEQS = 8
HEADS = 24
GROUP = 2048
LONGEST = 1024
BCW = 304
CH = 1792
N_DP = 16


def block_scale(own_key, shape, cuts, least, largest):
    def one(position, parts):
        heights = jax.random.uniform(jax.random.fold_in(jax.random.fold_in(own_key, 6), position), (parts,), jnp.float32, least / len(cuts), largest / len(cuts))
        return jnp.repeat(jnp.exp(heights), shape[position] // parts).reshape((-1,) + (1,) * (len(shape) - position - 1))

    level = one(*cuts[0])
    for cut in cuts[1:]:
        level = level * one(*cut)
    return level


def split_up(count, total, limit, slope):
    portions = [(1 << 20) // math.isqrt(grade ** slope) + 1 for grade in range(2, count + 1)]
    spare, counts = total - limit - (count - 1), [1] * (count - 1)
    while spare > 0:
        movable = [i for i in range(count - 1) if counts[i] < limit]
        whole, left = sum([portions[i] for i in movable]), spare
        for i in movable:
            more = min(limit - counts[i], max(1, left * portions[i] // whole), spare)
            counts[i] = counts[i] + more
            spare = spare - more
    return np.array([limit] + counts)


def uneven(stream_key, amount, total, most, slope):
    if amount == 2:
        one = jax.random.randint(stream_key, (), max(1, total - most), min(most, total - 1) + 1)
        return jnp.stack([one, total - one])
    sizes = jnp.asarray(split_up(amount, total, most, slope), jnp.int32)
    pairs = (amount - 1) // 2
    giver, receiver = sizes[1:1 + 2 * pairs:2], sizes[2:2 + 2 * pairs:2]
    margin = jnp.minimum(giver - 1, most - receiver)
    passed = jax.random.randint(jax.random.fold_in(stream_key, 1), (pairs,), 0, 1 << 20) % (margin + 1)
    sizes = sizes.at[1:1 + 2 * pairs:2].set(giver - passed).at[2:2 + 2 * pairs:2].set(receiver + passed)
    return sizes[jax.random.permutation(jax.random.fold_in(stream_key, 2), amount)]


def normal_values(stream_key, extent, scale, limit, split=(), held_as=jnp.bfloat16):
    entries = scale * jax.random.normal(stream_key, extent, jnp.float32)
    if split:
        entries = entries * block_scale(stream_key, extent, split, -0.22, 0.18)
    return jnp.clip(entries, -limit, limit).astype(held_as)


def setup_inputs(seed: int = 0) -> dict:
    arg_keys = jax.random.split(jax.random.key(seed), 14)
    hidden_in = normal_values(arg_keys[0], (2, N_DP * TOK_DEV, D), 1.0, 6.0, ((0, 2), (1, 16)))
    lengths = jax.vmap(lambda own: uneven(own, SEQS, GROUP, LONGEST, 2))(jax.random.split(arg_keys[1], N_DP)).reshape((N_DP, SEQS)).astype(jnp.int32)
    gain_in = jnp.clip(1.0 + 0.1 * jax.random.normal(arg_keys[2], (D,), jnp.float32), 0.5, 1.5)
    w_x = normal_values(arg_keys[3], (D, INNER), D ** -0.5, 0.21875)
    w_z = normal_values(arg_keys[4], (D, INNER), D ** -0.5, 0.21875)
    w_bcdt = normal_values(arg_keys[5], (D, BCW), D ** -0.5, 0.21875)
    conv_w = normal_values(arg_keys[6], (CONV, CH), CONV ** -0.5, 3.0, (), jnp.float32)
    dt_bias = jnp.clip(jax.random.uniform(arg_keys[7], (2, HEADS), jnp.float32, -6.0, -2.0), -6.0, -2.0)
    a_log = jnp.clip(jax.random.uniform(arg_keys[8], (2, HEADS), jnp.float32, -4.0, 0.5), -4.0, 0.5)
    d_skip = jnp.clip(jax.random.uniform(arg_keys[9], (HEADS,), jnp.float32, 0.5, 2.0), 0.5, 2.0)
    gain_mix = jnp.clip(1.0 + 0.1 * jax.random.normal(arg_keys[10], (INNER,), jnp.float32), 0.5, 1.5)
    w_out = normal_values(arg_keys[11], (INNER, D), INNER ** -0.5, 0.15625)
    cotangent = normal_values(arg_keys[12], (2, N_DP * TOK_DEV, D), 1.0, 6.0, ((0, 2), (1, 16)))
    return dict(hidden_in=hidden_in, lengths=lengths, gain_in=gain_in, w_x=w_x, w_z=w_z, w_bcdt=w_bcdt, conv_w=conv_w, dt_bias=dt_bias, a_log=a_log, d_skip=d_skip, gain_mix=gain_mix, w_out=w_out, cotangent=cotangent)


epsilon = 1e-05
highest = lax.Precision.HIGHEST

@jax.custom_vjp
def low(v):
    return lax.optimization_barrier(v.astype(jnp.bfloat16)).astype(jnp.float32)

@jax.custom_vjp
def low_back(v):
    return v

def low_keep(v):
    return (low(v), None)

def low_pass(kept, grad):
    return (grad,)

def back_keep(v):
    return (v, None)

def back_low(kept, grad):
    return (low(grad),)
low.defvjp(low_keep, low_pass)
low_back.defvjp(back_keep, back_low)

def matmul(left_side, right_side):
    return jnp.dot(left_side, right_side, precision=highest, preferred_element_type=jnp.float32)

def segment_ids(lengths_row, row_count):
    bounds = jnp.cumsum(lengths_row.astype(jnp.int32))
    positions = jnp.arange(row_count, dtype=jnp.int32)
    return lax.optimization_barrier(jnp.sum((positions[:, None] >= bounds[None, :]).astype(jnp.int32), axis=1)).astype(jnp.int32)

def causal_conv(values, weights, segment):
    row_count = values.shape[0]
    running = jnp.zeros_like(values)
    for offset in range(CONV):
        lag_rows = CONV - 1 - offset
        shifted = jnp.pad(values, ((lag_rows, 0), (0, 0)))[:row_count]
        seg_back = jnp.pad(segment, (lag_rows, 0), constant_values=-1)[:row_count]
        kept_mask = (seg_back == segment).astype(jnp.float32)
        running = running + weights[offset][None, :] * shifted * kept_mask[:, None]
    return running

def span_scan(inputs_x, inputs_b, inputs_c, step_sizes, decay_rates, segment):
    row_count, inner_width = inputs_x.shape
    head_count = step_sizes.shape[1]
    head_width = inner_width // head_count
    state_size = inputs_b.shape[1]
    blocks = row_count // SPAN
    earlier = jnp.concatenate([jnp.full((1,), -1, jnp.int32), segment[:-1]])
    before = earlier.reshape(blocks, SPAN)[:, 0]
    positions = jnp.arange(SPAN)
    below_mask = positions[:, None] > positions[None, :]

    def block_step(carried, pieces):
        block_x, block_b, block_c, block_dt, block_seg, seg_before = pieces
        cumulative = jnp.cumsum(-block_dt * decay_rates[None, :], axis=0)
        scaled = block_x * block_dt[:, :, None]
        within = jnp.logical_and(below_mask, block_seg[:, None] == block_seg[None, :]).astype(jnp.float32)
        spread = cumulative[:, None, :] - cumulative[None, :, :]
        weights = jnp.exp(jnp.minimum(spread, 0.0)) * within[:, :, None]
        scores = jnp.dot(block_c, block_b.T, precision=highest)
        inside = jnp.einsum('tsh,shp->thp', scores[:, :, None] * weights, scaled, precision=highest)
        entering = (block_seg == seg_before).astype(jnp.float32)[:, None] * jnp.exp(cumulative)
        carried_in = jnp.einsum('tn,hnp->thp', block_c, carried, precision=highest) * entering[:, :, None]
        last_seg = block_seg[SPAN - 1]
        to_end = jnp.exp(cumulative[SPAN - 1][None, :] - cumulative) * (block_seg == last_seg).astype(jnp.float32)[:, None]
        fresh_state = jnp.einsum('sn,shp->hnp', block_b, scaled * to_end[:, :, None], precision=highest)
        kept_part = jnp.exp(cumulative[SPAN - 1]) * (seg_before == last_seg).astype(jnp.float32)
        updated = fresh_state + kept_part[:, None, None] * carried
        return (updated, inside + carried_in)
    pieces = (inputs_x.reshape(blocks, SPAN, head_count, head_width), inputs_b.reshape(blocks, SPAN, state_size), inputs_c.reshape(blocks, SPAN, state_size), step_sizes.reshape(blocks, SPAN, head_count), segment.reshape(blocks, SPAN), before)
    initial = jnp.zeros((head_count, state_size, head_width), jnp.float32)
    final_state, outputs = lax.scan(jax.checkpoint(block_step), initial, pieces)
    return outputs.reshape(row_count, inner_width)

def group_forward(rows_in, gain_in, w_x, w_z, w_bcdt, conv_w, dt_bias, a_log, d_skip, gain_mix, w_out, segment):
    inv_scale = lax.rsqrt(lax.optimization_barrier(jnp.mean(rows_in * rows_in, axis=1, keepdims=True)) + epsilon)
    normed = low(rows_in * inv_scale * gain_in[None, :])
    pre_x = low(matmul(normed, w_x))
    pre_bc = low(matmul(normed, w_bcdt))
    gate_z = low_back(matmul(normed, w_z))
    live_rows = (segment < SEQS - 1).astype(jnp.float32)
    upper_half = (jnp.arange(GROUP, dtype=jnp.int32) >= TOK_DEV).astype(jnp.float32)
    skip_row = jnp.repeat(d_skip, HEADDIM)
    mixer_rows = jnp.zeros((GROUP, INNER), jnp.float32)
    for direction in range(2):
        proj_x = low_back(pre_x)
        proj_bc = low_back(pre_bc)
        conv_x = jax.nn.silu(causal_conv(proj_x, conv_w[:, :INNER], segment))
        if direction == 0:
            own_half = 1.0 - upper_half
        else:
            own_half = upper_half
        mixer_rows = mixer_rows + skip_row[None, :] * conv_x * own_half[:, None]
        first_col = 2 * STATE * direction
        conv_bc = jax.nn.silu(causal_conv(proj_bc[:, first_col:first_col + 2 * STATE], conv_w[:, INNER + first_col:INNER + first_col + 2 * STATE], segment))
        step_col = 4 * STATE + HEADS * direction
        step_sizes = jax.nn.softplus(proj_bc[:, step_col:step_col + HEADS] + dt_bias[direction][None, :])
        decay_rates = jnp.exp(a_log[direction])
        if direction == 0:
            mixer_rows = mixer_rows + span_scan(conv_x, conv_bc[:, :STATE], conv_bc[:, STATE:], step_sizes, decay_rates, segment)
        else:
            reversed_out = span_scan(jnp.flip(conv_x, 0), jnp.flip(conv_bc[:, :STATE], 0), jnp.flip(conv_bc[:, STATE:], 0), jnp.flip(step_sizes, 0), decay_rates, jnp.flip(segment, 0))
            mixer_rows = mixer_rows + jnp.flip(reversed_out, 0)
    mixer_rows = mixer_rows * live_rows[:, None]
    gated_rows = mixer_rows * jax.nn.silu(gate_z)
    norm_scale = lax.rsqrt(lax.optimization_barrier(jnp.mean(gated_rows * gated_rows, axis=1, keepdims=True)) + epsilon)
    mixed_norm = low(gated_rows * norm_scale * gain_mix[None, :])
    return rows_in + matmul(mixed_norm, w_out)

def reference(hidden_in, lengths, gain_in, w_x, w_z, w_bcdt, conv_w, dt_bias, a_log, d_skip, gain_mix, w_out, cotangent):

    def to_groups(values):
        return values.astype(jnp.float32).reshape(2, N_DP, TOK_DEV, D).transpose(1, 0, 2, 3).reshape(N_DP, GROUP, D)

    def from_groups(values):
        return values.reshape(N_DP, 2, TOK_DEV, D).transpose(1, 0, 2, 3).reshape(2, N_DP * TOK_DEV, D).astype(jnp.bfloat16)
    params = tuple((member.astype(jnp.float32) for member in (gain_in, w_x, w_z, w_bcdt, conv_w, dt_bias, a_log, d_skip, gain_mix, w_out)))

    def per_group(totals, pieces):
        rows_in, cot_rows, lengths_row = pieces
        segment = segment_ids(lengths_row, GROUP)

        def forward(rows_value, *weights):
            return group_forward(rows_value, *weights, segment)
        result, pullback = jax.vjp(forward, rows_in, *params)
        grads = pullback(cot_rows)
        totals = tuple((total_grad + new_grad for total_grad, new_grad in zip(totals, grads[1:])))
        return (totals, (result, grads[0]))
    initial = tuple((jnp.zeros_like(member) for member in params))
    totals, (outputs, input_grads) = lax.scan(per_group, initial, (to_groups(hidden_in), to_groups(cotangent), lengths))
    return (from_groups(outputs), from_groups(input_grads), totals[1], totals[2], totals[3], totals[9], totals[0], totals[4], totals[5], totals[6], totals[7], totals[8])
```

```python
import functools

import jax
import jax.numpy as jnp
import numpy as np
from jax import lax
from jax.experimental import pallas as pl
from jax.experimental.pallas import tpu as pltpu
from jax.sharding import PartitionSpec as P

F32 = jnp.float32
BF16 = jnp.bfloat16
CHUNK = 128
ROWS = 256
EPS = 1e-05
VMEM_BYTES = 56 * 1024 * 1024
NT = (((1,), (1,)), ((), ()))
TN = (((0,), (0,)), ((), ()))
EXACT = lax.Precision.HIGHEST


def mm(left, right):
    return jnp.dot(left, right, preferred_element_type=F32)


def mm_nt(left, right):
    return lax.dot_general(left, right, NT, preferred_element_type=F32)


def mm_tn(left, right):
    return lax.dot_general(left, right, TN, preferred_element_type=F32)


def exact_mm(left, right):
    return jnp.dot(left, right, precision=EXACT, preferred_element_type=F32)


def sequence_bounds(info_ref):
    count = info_ref.shape[0] - 1
    bounds, total = [], 0
    for position in range(count):
        total = total + info_ref[position]
        bounds.append(total)
    return bounds, info_ref[count]


def start_of(row, bounds):
    start = jnp.where(row < 0, -1, 0)
    for bound in bounds:
        start = jnp.where(row >= bound, bound, start)
    return start


def row_iota(count):
    return lax.broadcasted_iota(jnp.int32, (count, 1), 0)


def lane_iota(count):
    return lax.broadcasted_iota(jnp.int32, (1, count), 1)


def split_columns(rows):
    high = rows.astype(BF16).astype(F32)
    return jnp.concatenate([high, rows - high], axis=0).T.astype(BF16)


def head_sums(values, heads_ref, head_count):
    return mm_nt(heads_ref[0:head_count, :], values.astype(BF16))


def chunk_factors(dt, inc, rate, bounds, first):
    heads = dt.shape[0] // 2
    starts = start_of(first + lane_iota(CHUNK), bounds)
    before = start_of(first - 1, bounds)
    left = start_of(first, bounds)
    right = start_of(first + CHUNK - 1, bounds)
    after = start_of(first + CHUNK, bounds)
    inc0, inc1 = inc[:heads], inc[heads:]
    exc1 = inc1 - dt[heads:] * rate[heads:]
    total0, total1 = inc0[:, CHUNK - 1 : CHUNK], inc1[:, CHUNK - 1 : CHUNK]
    enter0 = jnp.where(starts == before, jnp.exp(-inc0), 0.0)
    enter1 = jnp.where(starts == after, jnp.exp(exc1 - total1), 0.0)
    leave0 = jnp.where(starts == right, dt[:heads] * jnp.exp(inc0 - total0), 0.0)
    leave1 = jnp.where(starts == left, dt[heads:] * jnp.exp(-exc1), 0.0)
    keep0 = jnp.where(before == right, jnp.exp(-total0), 0.0)
    keep1 = jnp.where(after == left, jnp.exp(-total1), 0.0)
    enter = jnp.concatenate([enter0, enter1], axis=0)
    leave = jnp.concatenate([leave0, leave1], axis=0)
    keep = jnp.concatenate([keep0, keep1], axis=0)
    return enter, leave, keep


def gates_kernel(x_ref, c_ref, gain_ref, wz_ref, wo_ref, normed_ref, z_ref, dnorm_ref):
    x = x_ref[...].astype(F32)
    inv = lax.rsqrt(jnp.mean(x * x, axis=1, keepdims=True) + EPS)
    normed = (x * inv * gain_ref[...]).astype(BF16)
    normed_ref[...] = normed
    z_ref[...] = mm(normed, wz_ref[...]).astype(BF16)
    dnorm_ref[...] = mm_nt(c_ref[...], wo_ref[...]).astype(BF16)


def proj_kernel(
    info_ref,
    normed_ref,
    halo_ref,
    gain_ref,
    wx_ref,
    wbc_ref,
    wdt_ref,
    taps_ref,
    bias_ref,
    alog_ref,
    e0_ref,
    e1_ref,
    pre_ref,
    act_ref,
    slope_ref,
    raw_ref,
    dt_ref,
    inc_ref,
    sf0_ref,
    sf1_ref,
    keep_ref,
    send_ref,
    buf,
    acc0,
    acc1,
    run1,
):
    step = pl.program_id(0)
    bounds, base = sequence_bounds(info_ref)
    inner = wx_ref.shape[1]
    channels = taps_ref.shape[1]
    heads = bias_ref.shape[0] // 2
    state = (channels - inner) // 4

    @pl.when(step == 0)
    def _():
        x = halo_ref[...].astype(F32)
        inv = lax.rsqrt(jnp.mean(x * x, axis=1, keepdims=True) + EPS)
        normed = (x * inv * gain_ref[...]).astype(BF16)
        px = mm(normed, wx_ref[...]).astype(BF16).astype(F32)
        pb = mm(normed, wbc_ref[...]).astype(BF16).astype(F32)
        buf[0:8, 0:inner] = px[8:16]
        buf[0:8, inner:channels] = pb[8:16]
        acc0[...] = jnp.zeros_like(acc0)
        acc1[...] = jnp.zeros_like(acc1)
        run1[...] = jnp.ones_like(run1)

    @pl.when(step > 0)
    def _():
        buf[0:8, :] = buf[ROWS : ROWS + 8, :]

    normed = normed_ref[...]
    px = mm(normed, wx_ref[...]).astype(BF16)
    pre_ref[:, 0:inner] = px
    buf[8 : ROWS + 8, 0:inner] = px.astype(F32)
    pb = mm(normed, wbc_ref[...]).astype(BF16)
    pre_ref[:, inner:channels] = pb
    buf[8 : ROWS + 8, inner:channels] = pb.astype(F32)

    first = base + step * ROWS
    rows = first + row_iota(ROWS)
    place = rows - start_of(rows, bounds)
    masks = [jnp.where(place >= lag, 1.0, 0.0) for lag in (1, 2, 3)]
    for tile in range(channels // 256):
        cols = slice(tile * 256, tile * 256 + 256)
        conv = buf[8 : ROWS + 8, cols] * taps_ref[3:4, cols]
        for lag in (1, 2, 3):
            conv = conv + buf[8 - lag : ROWS + 8 - lag, cols] * taps_ref[3 - lag : 4 - lag, cols] * (
                masks[lag - 1]
            )
        sig = jax.nn.sigmoid(conv)
        act_ref[:, cols] = (conv * sig).astype(BF16)
        slope_ref[:, cols] = (sig * (1.0 + conv * (1.0 - sig))).astype(BF16)

    raw = mm_nt(wdt_ref[...], normed).astype(BF16).astype(F32) + bias_ref[...]
    raw_ref[...] = raw
    dt = jnp.maximum(raw, 0.0) + jnp.log1p(jnp.exp(-jnp.abs(raw)))
    dt_ref[...] = dt
    rate = jnp.exp(alog_ref[...])
    upto = jnp.where(row_iota(CHUNK) <= lane_iota(CHUNK), 1.0, 0.0)
    for part in range(ROWS // CHUNK):
        span = slice(part * CHUNK, part * CHUNK + CHUNK)
        dt_c = dt[:, span]
        inc = exact_mm(dt_c * rate, upto)
        inc_ref[:, span] = inc
        _, leave, keep = chunk_factors(dt_c, inc, rate, bounds, first + part * CHUNK)
        leave_cols = split_columns(leave)
        keep_cols = split_columns(jnp.broadcast_to(keep, (2 * heads, CHUNK)))[0:16]
        keep0 = mm(keep_cols, e0_ref[...])[0:1]
        keep1 = mm(keep_cols, e1_ref[...])[0:1]
        keep_ref[part, 0:1, :] = keep0
        keep_ref[part, 1:2, :] = keep1
        x = act_ref[span, 0:inner].astype(F32)
        b0 = act_ref[span, inner : inner + state]
        b1 = act_ref[span, inner + 2 * state : inner + 3 * state]
        fresh0 = mm_tn(b0, (x * mm(leave_cols, e0_ref[...])).astype(BF16))
        sf0_ref[part] = fresh0.astype(BF16)
        acc0[...] = keep0 * acc0[...] + fresh0
        fresh1 = mm_tn(b1, (x * mm(leave_cols, e1_ref[...])).astype(BF16))
        sf1_ref[part] = fresh1.astype(BF16)
        acc1[...] = acc1[...] + run1[...] * fresh1
        run1[...] = run1[...] * keep1

    @pl.when(step == pl.num_programs(0) - 1)
    def _():
        send_ref[...] = jnp.where(base > 0, acc1[...], acc0[...]).astype(BF16)


def intra_kernel(info_ref, act_ref, dt_ref, inc_ref, alog_ref, y_ref, *, inner, state):
    bounds, base = sequence_bounds(info_ref)
    first = base + pl.program_id(0) * CHUNK
    heads = alog_ref.shape[0] // 2
    width = inner // heads
    t, s = row_iota(CHUNK), lane_iota(CHUNK)
    same = start_of(first + t, bounds) == start_of(first + s, bounds)
    lower = t > s
    b0 = act_ref[:, inner : inner + state]
    c0 = act_ref[:, inner + state : inner + 2 * state]
    b1 = act_ref[:, inner + 2 * state : inner + 3 * state]
    c1 = act_ref[:, inner + 3 * state : inner + 4 * state]
    scores = jnp.where(lower, mm_nt(c0, b0), mm_nt(c1, b1))
    scores = jnp.where(same & (t != s), scores, 0.0)
    dt = dt_ref[...]
    inc = inc_ref[...]
    log_dt = jnp.log(jnp.maximum(dt, 1e-37))
    exc1 = inc[heads:] - dt[heads:] * jnp.exp(alog_ref[heads:, :])
    out_cols = jnp.concatenate([-inc[:heads], exc1], axis=0).T
    in_rows = jnp.concatenate([inc[:heads] + log_dt[:heads], log_dt[heads:] - exc1], axis=0)
    lanes = lane_iota(2 * width)
    for pair in range(heads // 2):
        cols = slice(pair * 2 * width, (pair + 1) * 2 * width)
        weights = []
        for head in (2 * pair, 2 * pair + 1):
            spread = jnp.where(
                lower,
                out_cols[:, head : head + 1] + in_rows[head : head + 1, :],
                out_cols[:, heads + head : heads + head + 1]
                + in_rows[heads + head : heads + head + 1, :],
            )
            weights.append((jnp.exp(spread) * scores).astype(BF16))
        x = act_ref[:, cols]
        zero = jnp.zeros_like(x)
        x_cut = jnp.concatenate(
            [jnp.where(lanes < width, x, zero), jnp.where(lanes < width, zero, x)], axis=0
        )
        y_ref[:, cols] = mm(jnp.concatenate(weights, axis=1), x_cut).astype(BF16)


def mix_kernel(
    info_ref,
    x_ref,
    act_ref,
    dt_ref,
    inc_ref,
    alog_ref,
    sf0_ref,
    sf1_ref,
    keep_ref,
    recv_ref,
    yin_ref,
    z_ref,
    dnorm_ref,
    wo_ref,
    gain_ref,
    skip_ref,
    e0_ref,
    e1_ref,
    out_ref,
    mixed_ref,
    dz_ref,
    dy_ref,
    r_ref,
    df0_ref,
    df1_ref,
    s0_ref,
    s1_ref,
    send_ref,
    ggain_ref,
    gskip_ref,
    all0,
    all1,
    acc0,
    acc1,
    run0,
):
    step = pl.program_id(0)
    bounds, base = sequence_bounds(info_ref)
    first = base + step * CHUNK
    inner = gain_ref.shape[1]
    heads = alog_ref.shape[0] // 2
    state = recv_ref.shape[0]
    chunks = sf0_ref.shape[0]

    @pl.when(step == 0)
    def _():
        recv = recv_ref[...].astype(F32)
        zero = jnp.zeros_like(recv)
        carried = jnp.where(base > 0, recv, zero)
        for chunk in range(chunks):
            all0[chunk] = carried.astype(BF16)
            carried = keep_ref[chunk, 0:1, :] * carried + sf0_ref[chunk].astype(F32)
        carried = jnp.where(base > 0, zero, recv)
        for chunk in range(chunks - 1, -1, -1):
            all1[chunk] = carried.astype(BF16)
            carried = keep_ref[chunk, 1:2, :] * carried + sf1_ref[chunk].astype(F32)
        acc0[...] = jnp.zeros_like(acc0)
        acc1[...] = jnp.zeros_like(acc1)
        run0[...] = jnp.ones_like(run0)
        ggain_ref[...] = jnp.zeros_like(ggain_ref)
        gskip_ref[...] = jnp.zeros_like(gskip_ref)

    s0 = all0[step]
    s1 = all1[step]
    s0_ref[0] = s0
    s1_ref[0] = s1
    enter, _, _ = chunk_factors(dt_ref[...], inc_ref[...], jnp.exp(alog_ref[...]), bounds, first)
    enter_cols = split_columns(enter)
    enter0 = mm(enter_cols, e0_ref[...])
    enter1 = mm(enter_cols, e1_ref[...])
    c0 = act_ref[:, inner + state : inner + 2 * state]
    c1 = act_ref[:, inner + 3 * state : inner + 4 * state]
    y0 = enter0 * mm(c0, s0)
    y1 = enter1 * mm(c1, s1)
    conv = act_ref[:, 0:inner].astype(F32)
    live = jnp.where(first + row_iota(CHUNK) < bounds[len(bounds) - 2], 1.0, 0.0)
    mixer = live * (yin_ref[...].astype(F32) + y0 + y1 + skip_ref[...] * conv)
    z = z_ref[...].astype(F32)
    sig = jax.nn.sigmoid(z)
    gate = z * sig
    gated = mixer * gate
    scale = lax.rsqrt(jnp.mean(gated * gated, axis=1, keepdims=True) + EPS)
    unit = gated * scale
    mixed = (unit * gain_ref[...]).astype(BF16)
    mixed_ref[...] = mixed
    out_ref[...] = (x_ref[...].astype(F32) + mm(mixed, wo_ref[...])).astype(BF16)
    dnorm = dnorm_ref[...].astype(F32)
    ggain_ref[...] += jnp.sum(dnorm * unit, axis=0, keepdims=True)
    scaled = dnorm * gain_ref[...]
    dgated = scale * (scaled - unit * jnp.mean(scaled * unit, axis=1, keepdims=True))
    dz_ref[...] = (dgated * mixer * sig * (1.0 + z * (1.0 - sig))).astype(BF16)
    dmixer = live * dgated * gate
    dy = dmixer.astype(BF16)
    dy_ref[...] = dy
    gskip_ref[...] += jnp.sum(dmixer * conv, axis=0, keepdims=True)
    dy = dy.astype(F32)
    r_ref[0:heads, :] = head_sums(dy * y0, e0_ref, heads)
    r_ref[heads : 2 * heads, :] = head_sums(dy * y1, e0_ref, heads)
    df0 = mm_tn(c0, (dy * enter0).astype(BF16))
    df0_ref[0] = df0.astype(BF16)
    acc0[...] = acc0[...] + run0[...] * df0
    run0[...] = run0[...] * keep_ref[step, 0:1, :]
    df1 = mm_tn(c1, (dy * enter1).astype(BF16))
    df1_ref[0] = df1.astype(BF16)
    acc1[...] = keep_ref[step, 1:2, :] * acc1[...] + df1

    @pl.when(step == pl.num_programs(0) - 1)
    def _():
        send_ref[...] = jnp.where(base > 0, acc0[...], acc1[...]).astype(BF16)


def back_kernel(
    info_ref,
    act_ref,
    slope_ref,
    raw_ref,
    dt_ref,
    inc_ref,
    r_ref,
    alog_ref,
    dy_ref,
    s0_ref,
    s1_ref,
    df0_ref,
    df1_ref,
    keep_ref,
    recv_ref,
    skip_ref,
    e0_ref,
    e1_ref,
    dpre_ref,
    draw_ref,
    gbias_ref,
    galog_ref,
    all0,
    all1,
    cut0,
    cut1,
    own0,
    own1,
    dscore,
    dx,
):
    step = pl.program_id(0)
    bounds, base = sequence_bounds(info_ref)
    first = base + step * CHUNK
    inner = skip_ref.shape[1]
    heads = alog_ref.shape[0] // 2
    width = inner // heads
    state = recv_ref.shape[0]
    chunks = df0_ref.shape[0]

    @pl.when(step == 0)
    def _():
        recv = recv_ref[...].astype(F32)
        zero = jnp.zeros_like(recv)
        carried = jnp.where(base > 0, zero, recv)
        for chunk in range(chunks - 1, -1, -1):
            all0[chunk] = carried.astype(BF16)
            carried = keep_ref[chunk, 0:1, :] * carried + df0_ref[chunk].astype(F32)
        carried = jnp.where(base > 0, recv, zero)
        for chunk in range(chunks):
            all1[chunk] = carried.astype(BF16)
            carried = keep_ref[chunk, 1:2, :] * carried + df1_ref[chunk].astype(F32)
        gbias_ref[...] = jnp.zeros_like(gbias_ref)
        galog_ref[...] = jnp.zeros_like(galog_ref)

    s, t = row_iota(CHUNK), lane_iota(CHUNK)
    same = (start_of(first + s, bounds) == start_of(first + t, bounds)) & (s != t)
    early = s < t
    b0 = act_ref[:, inner : inner + state]
    c0 = act_ref[:, inner + state : inner + 2 * state]
    b1 = act_ref[:, inner + 2 * state : inner + 3 * state]
    c1 = act_ref[:, inner + 3 * state : inner + 4 * state]
    scores = jnp.where(early, mm_nt(b0, c0), mm_nt(b1, c1))
    scores = jnp.where(same, scores, 0.0)
    dt = dt_ref[...]
    inc = inc_ref[...]
    rate = jnp.exp(alog_ref[...])
    log_dt = jnp.log(jnp.maximum(dt, 1e-37))
    exc1 = inc[heads:] - dt[heads:] * rate[heads:]
    out_rows = jnp.concatenate([-inc[:heads], exc1], axis=0)
    in_cols = jnp.concatenate([inc[:heads] + log_dt[:heads], log_dt[heads:] - exc1], axis=0).T
    lanes = lane_iota(2 * width)
    beyond = jnp.where(s > t, 1.0, 0.0).astype(BF16)
    within = jnp.where(s < t, 1.0, 0.0).astype(BF16)
    tails = jnp.concatenate([beyond, within], axis=1)
    dscore[...] = jnp.zeros_like(dscore)
    for pair in range(heads // 2):
        cols = slice(pair * 2 * width, (pair + 1) * 2 * width)
        x = act_ref[:, cols]
        dy = dy_ref[:, cols]
        zero = jnp.zeros_like(x)
        x_cut = jnp.concatenate(
            [jnp.where(lanes < width, x, zero), jnp.where(lanes < width, zero, x)], axis=0
        )
        dweights = mm_nt(x_cut, dy)
        weights = []
        for part in (0, 1):
            head = 2 * pair + part
            spread = jnp.where(
                early,
                in_cols[:, head : head + 1] + out_rows[head : head + 1, :],
                in_cols[:, heads + head : heads + head + 1]
                + out_rows[heads + head : heads + head + 1, :],
            )
            decay = jnp.exp(spread)
            dweight = dweights[part * CHUNK : (part + 1) * CHUNK]
            weight = decay * scores
            weights.append(weight.astype(BF16))
            dscore[...] += dweight * decay
            sums = mm((dweight * weight).astype(BF16), tails)
            sums0, sums1 = sums[:, 0:CHUNK], sums[:, CHUNK : 2 * CHUNK]
            row = slice(head, head + 1)
            cut0[row, :] = jnp.sum(jnp.where(s <= t, sums0, 0.0), axis=0, keepdims=True)
            own0[row, :] = jnp.sum(jnp.where(s == t, sums0, 0.0), axis=0, keepdims=True)
            cut1[row, :] = jnp.sum(jnp.where(s >= t, sums1, 0.0), axis=0, keepdims=True)
            own1[row, :] = jnp.sum(jnp.where(s == t, sums1, 0.0), axis=0, keepdims=True)
        dy_cut = jnp.concatenate(
            [jnp.where(lanes < width, dy, zero), jnp.where(lanes < width, zero, dy)], axis=0
        )
        dx[:, cols] = mm(jnp.concatenate(weights, axis=1), dy_cut)
    dscores = jnp.where(same, dscore[...], 0.0)
    dscore0 = jnp.where(early, dscores, 0.0).astype(BF16)
    dscore1 = jnp.where(early, 0.0, dscores).astype(BF16)

    s0, s1 = s0_ref[0], s1_ref[0]
    ds0, ds1 = all0[step], all1[step]
    enter, leave, _ = chunk_factors(dt, inc, rate, bounds, first)
    enter_cols = split_columns(enter)
    leave_cols = split_columns(leave)
    xf = act_ref[:, 0:inner].astype(F32)
    dyf = dy_ref[...].astype(F32)
    from0 = mm(b0, ds0)
    leave0 = mm(leave_cols, e0_ref[...])
    out0 = xf * leave0
    k0 = head_sums(out0 * from0, e0_ref, heads)
    from1 = mm(b1, ds1)
    leave1 = mm(leave_cols, e1_ref[...])
    out1 = xf * leave1
    k1 = head_sums(out1 * from1, e0_ref, heads)
    dconv = dx[...] + leave0 * from0 + leave1 * from1 + skip_ref[...] * dyf
    dpre_ref[:, 0:inner] = (dconv * slope_ref[:, 0:inner].astype(F32)).astype(BF16)
    db0 = mm(dscore0, c0) + mm_nt(out0.astype(BF16), ds0)
    db1 = mm(dscore1, c1) + mm_nt(out1.astype(BF16), ds1)
    in0 = (dyf * mm(enter_cols, e0_ref[...])).astype(BF16)
    in1 = (dyf * mm(enter_cols, e1_ref[...])).astype(BF16)
    dc0 = mm_tn(dscore0, b0) + mm_nt(in0, s0)
    dc1 = mm_tn(dscore1, b1) + mm_nt(in1, s1)
    dbc = jnp.concatenate([db0, dc0, db1, dc1], axis=1)
    dpre_ref[:, inner:] = (dbc * slope_ref[:, inner:].astype(F32)).astype(BF16)

    kept0 = jnp.sum(ds0.astype(F32) * s0.astype(F32), axis=0, keepdims=True) * keep_ref[step, 0:1, :]
    kept1 = jnp.sum(ds1.astype(F32) * s1.astype(F32), axis=0, keepdims=True) * keep_ref[step, 1:2, :]
    kept = jnp.concatenate([kept0, kept1, jnp.zeros((6, inner), F32)], axis=0)
    kept_high = kept.astype(BF16)
    kept_low = (kept - kept_high.astype(F32)).astype(BF16)
    ones = e0_ref[0:heads, :]
    kept_sum = mm_nt(ones, kept_high) + mm_nt(ones, kept_low)
    r0, r1 = r_ref[0:heads, :], r_ref[heads : 2 * heads, :]
    after = jnp.where(s >= t, 1.0, 0.0)
    ahead = jnp.where(s < t, 1.0, 0.0)
    da0 = -(
        pltpu.roll(cut0[...], 1, 1)
        + exact_mm(r0, after)
        + exact_mm(k0, ahead)
        + kept_sum[:, 0:1]
    )
    da1 = -(
        pltpu.roll(cut1[...], CHUNK - 1, 1)
        + exact_mm(r1, 1.0 - ahead.T)
        + exact_mm(k1, 1.0 - after.T)
        + kept_sum[:, 1:2]
    )
    da = jnp.concatenate([da0, da1], axis=0)
    dlog = jnp.concatenate([own0[...] + k0, own1[...] + k1], axis=0)
    raw = raw_ref[...]
    sig = jax.nn.sigmoid(raw)
    ratio = jnp.where(raw < -20.0, 1.0, sig / jnp.maximum(dt, 1e-37))
    draw = dlog * ratio + da * rate * sig
    draw_ref[...] = draw.astype(BF16)
    gbias_ref[...] += jnp.sum(draw, axis=1, keepdims=True)
    galog_ref[...] += jnp.sum(da * dt * rate, axis=1, keepdims=True)


def weights_kernel(normed_ref, dz_ref, mixed_ref, c_ref, gz_ref, go_ref):
    gz_ref[...] = mm_tn(normed_ref[...], dz_ref[...]).astype(BF16)
    go_ref[...] = mm_tn(mixed_ref[...], c_ref[...]).astype(BF16)


def conv_back_kernel(
    info_ref, normed_ref, dpre_ref, halo_ref, pre_ref, taps_ref, dproj_ref, gw_ref, gtaps_ref, buf
):
    bounds, base = sequence_bounds(info_ref)
    count = dpre_ref.shape[0]
    buf[0:count, :] = dpre_ref[...].astype(F32)
    buf[count : count + 8, :] = halo_ref[0:8, :].astype(F32)
    rows = base + row_iota(count + 8)
    place = rows - start_of(rows, bounds)
    pre = pre_ref[...].astype(F32)
    shifted = buf[0:count, :]
    dproj = shifted * taps_ref[3:4, :]
    gtaps_ref[3:4, :] = jnp.sum(pre * shifted, axis=0, keepdims=True)
    for lag in (1, 2, 3):
        mask = jnp.where(place[lag : count + lag] >= lag, 1.0, 0.0)
        shifted = buf[lag : count + lag, :] * mask
        dproj = dproj + shifted * taps_ref[3 - lag : 4 - lag, :]
        gtaps_ref[3 - lag : 4 - lag, :] = jnp.sum(pre * shifted, axis=0, keepdims=True)
    dproj = dproj.astype(BF16)
    dproj_ref[...] = dproj
    gw_ref[...] = mm_tn(normed_ref[...], dproj).astype(BF16)


def inputs_kernel(
    x_ref,
    c_ref,
    gain_ref,
    dproj_ref,
    draw_ref,
    dz_ref,
    wx_ref,
    wbc_ref,
    wdt_ref,
    wz_ref,
    gin_ref,
    ggain_ref,
):
    inner = wx_ref.shape[1]

    @pl.when(pl.program_id(0) == 0)
    def _():
        ggain_ref[...] = jnp.zeros_like(ggain_ref)

    dn = mm_nt(dproj_ref[:, 0:inner], wx_ref[...])
    dn = dn + mm_nt(dproj_ref[:, inner:], wbc_ref[...])
    dn = dn + mm_nt(dz_ref[...], wz_ref[...])
    dn = dn + mm_tn(draw_ref[...], wdt_ref[...])
    x = x_ref[...].astype(F32)
    inv = lax.rsqrt(jnp.mean(x * x, axis=1, keepdims=True) + EPS)
    unit = x * inv
    ggain_ref[...] += jnp.sum(dn * unit, axis=0, keepdims=True)
    f = dn * gain_ref[...]
    back = inv * (f - unit * jnp.mean(f * unit, axis=1, keepdims=True))
    gin_ref[...] = (c_ref[...].astype(F32) + back).astype(BF16)


def smem():
    return pl.BlockSpec(memory_space=pltpu.SMEM)


def whole(shape):
    return pl.BlockSpec(shape, lambda i: (0,) * len(shape))


def rows_of(count, width):
    return pl.BlockSpec((count, width), lambda i: (i, 0))


def lanes_of(height, count):
    return pl.BlockSpec((height, count), lambda i: (0, i))


def parts_of(count, *rest):
    return pl.BlockSpec((count,) + rest, lambda i: (i,) + (0,) * len(rest))


def call(kernel, name, grid, in_specs, outs, scratch, flops, moved, args):
    return pl.pallas_call(
        kernel,
        name=name,
        grid=(grid,),
        in_specs=in_specs,
        out_specs=[spec for spec, _, _ in outs],
        out_shape=[jax.ShapeDtypeStruct(shape, dtype) for _, shape, dtype in outs],
        scratch_shapes=scratch,
        compiler_params=pltpu.CompilerParams(
            vmem_limit_bytes=VMEM_BYTES, dimension_semantics=("arbitrary",)
        ),
        cost_estimate=pl.CostEstimate(flops=flops, bytes_accessed=moved, transcendentals=0),
    )(*args)


def sum_shards(grad, dp_count):
    rows, width = grad.shape
    index = lax.axis_index("dp")
    held = grad.reshape(dp_count, rows // dp_count, width)
    bit = 1
    while bit < dp_count:
        paired = held.reshape(held.shape[0] // 2, 2, held.shape[1], width)
        mine = (index // bit) % 2
        kept = lax.dynamic_index_in_dim(paired, mine, 1, keepdims=False)
        sent = lax.dynamic_index_in_dim(paired, 1 - mine, 1, keepdims=False).astype(BF16)
        got = lax.ppermute(sent, "dp", [(i, i ^ bit) for i in range(dp_count)])
        held = kept.astype(F32) + got.astype(F32)
        bit *= 2
    held = held[0].astype(BF16)
    got = lax.ppermute(held, "dir", [(0, 1), (1, 0)])
    return held.astype(F32) + got.astype(F32)


def sum_all(values, dp_count):
    bit = 1
    while bit < dp_count:
        values = values + lax.ppermute(values, "dp", [(i, i ^ bit) for i in range(dp_count)])
        bit *= 2
    return values + lax.ppermute(values, "dir", [(0, 1), (1, 0)])


def local(
    dp_count,
    hidden_in,
    lengths,
    gain_in,
    w_x,
    w_z,
    w_bcdt,
    conv_w,
    dt_bias,
    a_log,
    d_skip,
    gain_mix,
    w_out,
    cotangent,
):
    x = hidden_in[0]
    cot = cotangent[0]
    count, model = x.shape
    inner = w_x.shape[1]
    channels = conv_w.shape[1]
    heads = d_skip.shape[0]
    width = inner // heads
    state = (channels - inner) // 4
    chunks = count // CHUNK
    steps = 2 * heads
    direction = lax.axis_index("dir")
    info = jnp.concatenate([lengths[0], (direction * count).astype(jnp.int32)[None]])
    swap = [(0, 1), (1, 0)]

    halo = lax.ppermute(x[count - 16 :], "dir", [(0, 1)])

    gain_row = gain_in[None, :]
    mix_row = gain_mix[None, :]
    skip_row = jnp.repeat(d_skip, width)[None, :]
    w_bc = w_bcdt[:, : 4 * state]
    w_dt = w_bcdt[:, 4 * state :].T
    bias = dt_bias.reshape(steps, 1)
    alog = a_log.reshape(steps, 1)
    spread = np.repeat(np.eye(heads, dtype=np.float32), width, axis=1)
    zeros = np.zeros_like(spread)
    e0 = jnp.asarray(np.concatenate([spread, zeros, spread, zeros]), BF16)
    e1 = jnp.asarray(np.concatenate([zeros, spread, zeros, spread]), BF16)

    def rows_out(size, columns, dtype):
        return (rows_of(size, columns), (count, columns), dtype)

    normed, gate_z, d_norm = call(
        gates_kernel,
        "gates",
        count // ROWS,
        [
            rows_of(ROWS, model),
            rows_of(ROWS, model),
            whole((1, model)),
            whole((model, inner)),
            whole((inner, model)),
        ],
        [
            rows_out(ROWS, model, BF16),
            rows_out(ROWS, inner, BF16),
            rows_out(ROWS, inner, BF16),
        ],
        [],
        4 * count * model * inner,
        4 * count * (model + inner) + 4 * model * inner,
        (x, cot, gain_row, w_z, w_out),
    )

    per = ROWS // CHUNK
    pre, act, slope, raw, dt, inc, sf0, sf1, keep, send = call(
        proj_kernel,
        "proj",
        count // ROWS,
        [
            smem(),
            rows_of(ROWS, model),
            whole((16, model)),
            whole((1, model)),
            whole((model, inner)),
            whole((model, 4 * state)),
            whole((steps, model)),
            whole(conv_w.shape),
            whole((steps, 1)),
            whole((steps, 1)),
            whole(e0.shape),
            whole(e1.shape),
        ],
        [
            rows_out(ROWS, channels, BF16),
            rows_out(ROWS, channels, BF16),
            rows_out(ROWS, channels, BF16),
            (lanes_of(steps, ROWS), (steps, count), F32),
            (lanes_of(steps, ROWS), (steps, count), F32),
            (lanes_of(steps, ROWS), (steps, count), F32),
            (parts_of(per, state, inner), (chunks, state, inner), BF16),
            (parts_of(per, state, inner), (chunks, state, inner), BF16),
            (parts_of(per, 2, inner), (chunks, 2, inner), F32),
            (whole((state, inner)), (state, inner), BF16),
        ],
        [
            pltpu.VMEM((ROWS + 8, channels), F32),
            pltpu.VMEM((state, inner), F32),
            pltpu.VMEM((state, inner), F32),
            pltpu.VMEM((1, inner), F32),
        ],
        3 * count * model * inner,
        8 * count * inner,
        (info, normed, halo, gain_row, w_x, w_bc, w_dt, conv_w, bias, alog, e0, e1),
    )
    received = lax.ppermute(send, "dir", swap)

    (y_in,) = call(
        functools.partial(intra_kernel, inner=inner, state=state),
        "intra",
        chunks,
        [
            smem(),
            rows_of(CHUNK, channels),
            lanes_of(steps, CHUNK),
            lanes_of(steps, CHUNK),
            whole((steps, 1)),
        ],
        [rows_out(CHUNK, inner, BF16)],
        [],
        8 * count * CHUNK * inner,
        6 * count * inner,
        (info, act, dt, inc, alog),
    )

    states = (parts_of(1, state, inner), (chunks, state, inner), BF16)
    all_states = whole((chunks, state, inner))
    out, mixed, dz, dy, r, df0, df1, s0, s1, d_send, g_gain_mix, g_skip = call(
        mix_kernel,
        "mix",
        chunks,
        [
            smem(),
            rows_of(CHUNK, model),
            rows_of(CHUNK, channels),
            lanes_of(steps, CHUNK),
            lanes_of(steps, CHUNK),
            whole((steps, 1)),
            all_states,
            all_states,
            whole((chunks, 2, inner)),
            whole((state, inner)),
            rows_of(CHUNK, inner),
            rows_of(CHUNK, inner),
            rows_of(CHUNK, inner),
            whole((inner, model)),
            whole((1, inner)),
            whole((1, inner)),
            whole(e0.shape),
            whole(e1.shape),
        ],
        [
            rows_out(CHUNK, model, BF16),
            rows_out(CHUNK, inner, BF16),
            rows_out(CHUNK, inner, BF16),
            rows_out(CHUNK, inner, BF16),
            (lanes_of(steps, CHUNK), (steps, count), F32),
            states,
            states,
            states,
            states,
            (whole((state, inner)), (state, inner), BF16),
            (whole((1, inner)), (1, inner), F32),
            (whole((1, inner)), (1, inner), F32),
        ],
        [
            pltpu.VMEM((chunks, state, inner), BF16),
            pltpu.VMEM((chunks, state, inner), BF16),
            pltpu.VMEM((state, inner), F32),
            pltpu.VMEM((state, inner), F32),
            pltpu.VMEM((1, inner), F32),
        ],
        3 * count * model * inner,
        16 * count * inner,
        (
            info,
            x,
            act,
            dt,
            inc,
            alog,
            sf0,
            sf1,
            keep,
            received,
            y_in,
            gate_z,
            d_norm,
            w_out,
            mix_row,
            skip_row,
            e0,
            e1,
        ),
    )
    d_received = lax.ppermute(d_send, "dir", swap)

    blocks = 4
    g_z, g_out = call(
        weights_kernel,
        "weights",
        blocks,
        [
            whole((count, model)),
            lanes_of(count, inner // blocks),
            lanes_of(count, inner // blocks),
            whole((count, model)),
        ],
        [
            (lanes_of(model, inner // blocks), (model, inner), BF16),
            (rows_of(inner // blocks, model), (inner, model), BF16),
        ],
        [],
        4 * count * model * inner,
        6 * count * inner,
        (normed, dz, mixed, cot),
    )

    dpre, draw, g_bias, g_alog = call(
        back_kernel,
        "back",
        chunks,
        [
            smem(),
            rows_of(CHUNK, channels),
            rows_of(CHUNK, channels),
            lanes_of(steps, CHUNK),
            lanes_of(steps, CHUNK),
            lanes_of(steps, CHUNK),
            lanes_of(steps, CHUNK),
            whole((steps, 1)),
            rows_of(CHUNK, inner),
            states[0],
            states[0],
            all_states,
            all_states,
            whole((chunks, 2, inner)),
            whole((state, inner)),
            whole((1, inner)),
            whole(e0.shape),
            whole(e1.shape),
        ],
        [
            rows_out(CHUNK, channels, BF16),
            (lanes_of(steps, CHUNK), (steps, count), BF16),
            (whole((steps, 1)), (steps, 1), F32),
            (whole((steps, 1)), (steps, 1), F32),
        ],
        [
            pltpu.VMEM((chunks, state, inner), BF16),
            pltpu.VMEM((chunks, state, inner), BF16),
            pltpu.VMEM((heads, CHUNK), F32),
            pltpu.VMEM((heads, CHUNK), F32),
            pltpu.VMEM((heads, CHUNK), F32),
            pltpu.VMEM((heads, CHUNK), F32),
            pltpu.VMEM((CHUNK, CHUNK), F32),
            pltpu.VMEM((CHUNK, inner), F32),
        ],
        24 * count * CHUNK * inner,
        16 * count * inner,
        (
            info,
            act,
            slope,
            raw,
            dt,
            inc,
            r,
            alog,
            dy,
            s0,
            s1,
            df0,
            df1,
            keep,
            d_received,
            skip_row,
            e0,
            e1,
        ),
    )
    d_halo = lax.ppermute(dpre[:16], "dir", [(1, 0)])

    tile = 256
    dproj, g_proj, g_taps = call(
        conv_back_kernel,
        "conv_back",
        channels // tile,
        [
            smem(),
            whole((count, model)),
            lanes_of(count, tile),
            lanes_of(16, tile),
            lanes_of(count, tile),
            lanes_of(conv_w.shape[0], tile),
        ],
        [
            (lanes_of(count, tile), (count, channels), BF16),
            (lanes_of(model, tile), (model, channels), BF16),
            (lanes_of(conv_w.shape[0], tile), conv_w.shape, F32),
        ],
        [pltpu.VMEM((count + 8, tile), F32)],
        2 * count * model * channels,
        6 * count * channels,
        (info, normed, dpre, d_halo, pre, conv_w),
    )
    g_dt = lax.dot_general(normed, draw, (((0,), (1,)), ((), ())), preferred_element_type=F32)
    g_bcdt = jnp.concatenate([g_proj[:, inner:], g_dt.astype(BF16)], axis=1)

    grad_in, g_gain_in = call(
        inputs_kernel,
        "inputs",
        count // ROWS,
        [
            rows_of(ROWS, model),
            rows_of(ROWS, model),
            whole((1, model)),
            rows_of(ROWS, channels),
            lanes_of(steps, ROWS),
            rows_of(ROWS, inner),
            whole((model, inner)),
            whole((model, 4 * state)),
            whole((steps, model)),
            whole((model, inner)),
        ],
        [
            rows_out(ROWS, model, BF16),
            (whole((1, model)), (1, model), F32),
        ],
        [],
        5 * count * model * inner,
        8 * count * inner,
        (x, cot, gain_row, dproj, draw, dz, w_x, w_bc, w_dt, w_z),
    )

    parts = [
        g_gain_in.reshape(-1),
        g_taps.reshape(-1),
        g_bias.reshape(-1),
        g_alog.reshape(-1),
        jnp.sum(g_skip.reshape(heads, width), axis=1),
        g_gain_mix.reshape(-1),
    ]
    sizes = [part.shape[0] for part in parts]
    small = sum_all(jnp.concatenate(parts), dp_count)
    ends = list(np.cumsum(sizes))
    small = [small[end - size : end] for end, size in zip(ends, sizes)]
    return (
        out[None],
        grad_in[None],
        sum_shards(g_proj[:, :inner], dp_count),
        sum_shards(g_z, dp_count),
        sum_shards(g_bcdt, dp_count),
        sum_shards(g_out, dp_count),
        small[0],
        small[1].reshape(conv_w.shape),
        small[2].reshape(dt_bias.shape),
        small[3].reshape(a_log.shape),
        small[4],
        small[5],
    )


def solution(mesh):
    return jax.shard_map(
        functools.partial(local, mesh.shape["dp"]),
        mesh=mesh,
        in_specs=(
            P("dir", "dp", None),
            P("dp", None),
            P(),
            P(),
            P(),
            P(),
            P(),
            P(),
            P(),
            P(),
            P(),
            P(),
            P("dir", "dp", None),
        ),
        out_specs=(
            P("dir", "dp", None),
            P("dir", "dp", None),
            P("dp", None),
            P("dp", None),
            P("dp", None),
            P("dp", None),
            P(),
            P(),
            P(),
            P(),
            P(),
            P(),
        ),
        check_vma=False,
    )
```

```python
import functools

import jax
import jax.numpy as jnp
import numpy as np
from jax import lax
from jax.experimental import pallas as pl
from jax.experimental.pallas import tpu as pltpu
from jax.sharding import PartitionSpec as P

F32 = jnp.float32
BF16 = jnp.bfloat16
CHUNK = 128
ROWS = 256
SUB = 64
EPS = 1e-05
LOG2E = 1.4426950408889634
SWAP = [(0, 1), (1, 0)]
MIB = 1024 * 1024
VMEM_GATES = 18
VMEM_PROJ = 20
VMEM_INTRA = 12
VMEM_MIX = 28
VMEM_WEIGHTS = 16
VMEM_BACK = 20
VMEM_CONV = 20
VMEM_INPUTS = 20
VMEM_SUMS = 8
NT = (((1,), (1,)), ((), ()))
TN = (((0,), (0,)), ((), ()))
EXACT = lax.Precision.HIGHEST


def mm(left, right):
    return jnp.dot(left, right, preferred_element_type=F32)


def mm_nt(left, right):
    return lax.dot_general(left, right, NT, preferred_element_type=F32)


def mm_tn(left, right):
    return lax.dot_general(left, right, TN, preferred_element_type=F32)


def exact_mm(left, right):
    return jnp.dot(left, right, precision=EXACT, preferred_element_type=F32)


def sequence_bounds(lengths_ref, half_rows):
    bounds, total = [], 0
    for position in range(lengths_ref.shape[1]):
        total = total + lengths_ref[0, position]
        bounds.append(total)
    return bounds, lax.axis_index("dir") * half_rows


def start_of(row, bounds):
    start = jnp.where(row < 0, -1, 0)
    for bound in bounds:
        start = jnp.where(row >= bound, bound, start)
    return start


def row_iota(count):
    return lax.broadcasted_iota(jnp.int32, (count, 1), 0)


def lane_iota(count):
    return lax.broadcasted_iota(jnp.int32, (1, count), 1)


def flag(condition):
    return jnp.where(condition, 1.0, 0.0)


def in_parts(values, parts):
    out = []
    for _ in range(parts):
        part = values.astype(BF16).astype(F32)
        out.append(part)
        values = values - part
    return jnp.concatenate(out, axis=0)


def fold(values):
    return jnp.sum(values.reshape(values.shape[0] // 8, 8, values.shape[1]), axis=0)


def row_of(ref):
    return ref[...].reshape(1, ref.shape[0])


def column_of(ref, steps):
    heads = steps // 2
    place = row_iota(steps)
    column = jnp.zeros((steps, 1), F32)
    for step in range(steps):
        column = jnp.where(place == step, ref[step // heads, step % heads], column)
    return column


def gates_kernel(
    lengths_ref,
    bias_ref,
    alog_ref,
    x_ref,
    c_ref,
    gain_ref,
    wz_ref,
    wo_ref,
    wbc_ref,
    e0_ref,
    e1_ref,
    normed_ref,
    turned_ref,
    z_ref,
    dnorm_ref,
    raw_ref,
    dt_ref,
    rate_ref,
    target_ref,
    source_ref,
    factors_ref,
    keeps_ref,
):
    step = pl.program_id(0)
    model = x_ref.shape[1]
    steps = raw_ref.shape[0]
    heads = steps // 2
    count = raw_ref.shape[1]
    x = x_ref[...].astype(F32)
    inv = lax.rsqrt(jnp.mean(x * x, axis=1, keepdims=True) + EPS)
    normed = (x * inv * row_of(gain_ref)).astype(BF16)
    normed_ref[...] = normed
    turned_ref[...] = normed.T
    z_ref[...] = mm(normed, wz_ref[...]).astype(BF16)
    dnorm_ref[...] = mm_nt(c_ref[...], wo_ref[...]).astype(BF16)
    raw = mm(normed, wbc_ref[:, wbc_ref.shape[1] - steps :]).astype(BF16).astype(F32).T
    raw_ref[:, pl.ds(pl.multiple_of(step * ROWS, ROWS), ROWS)] = raw

    @pl.when(step == pl.num_programs(0) - 1)
    def _():
        bounds, base = sequence_bounds(lengths_ref, count)
        rate = jnp.exp(column_of(alog_ref, steps))
        rate_ref[...] = jnp.broadcast_to(rate, (steps, 128))
        raw = raw_ref[...] + column_of(bias_ref, steps)
        raw_ref[...] = raw
        dt = jnp.maximum(raw, 0.0) + jnp.log1p(jnp.exp(-jnp.abs(raw)))
        dt_ref[...] = dt
        log_dt = jnp.log(jnp.maximum(dt, 1e-37))
        chunks = count // CHUNK
        upto = flag(row_iota(CHUNK) <= lane_iota(CHUNK))
        fall = dt * rate
        stacked = [fall[:, chunk * CHUNK : (chunk + 1) * CHUNK] for chunk in range(chunks)]
        summed = exact_mm(jnp.concatenate(stacked, axis=0), upto)
        lane = lane_iota(CHUNK)
        keeps = jnp.zeros((steps, CHUNK), F32)
        for chunk in range(chunks):
            span = slice(chunk * CHUNK, (chunk + 1) * CHUNK)
            first = base + chunk * CHUNK
            inc = summed[chunk * steps : (chunk + 1) * steps]
            dt_c, log_c = dt[:, span], log_dt[:, span]
            inc0 = inc[:heads]
            exc1 = inc[heads:] - fall[heads:, span]
            total0 = inc0[:, CHUNK - 1 :]
            total1 = inc[heads:, CHUNK - 1 :]
            target = jnp.concatenate([-inc0, exc1], axis=0) * LOG2E
            source = jnp.concatenate([inc0 + log_c[:heads], log_c[heads:] - exc1], axis=0) * LOG2E
            target_ref[:, span] = target
            source_ref[:, span] = source
            starts = start_of(first + lane, bounds)
            before = start_of(first - 1, bounds)
            left = start_of(first, bounds)
            right = start_of(first + CHUNK - 1, bounds)
            after = start_of(first + CHUNK, bounds)
            enter0 = jnp.where(starts == before, jnp.exp(-inc0), 0.0)
            enter1 = jnp.where(starts == after, jnp.exp(exc1 - total1), 0.0)
            leave0 = jnp.where(starts == right, dt_c[:heads] * jnp.exp(inc0 - total0), 0.0)
            leave1 = jnp.where(starts == left, dt_c[heads:] * jnp.exp(-exc1), 0.0)
            enter = jnp.concatenate([enter0, enter1], axis=0)
            leave = jnp.concatenate([leave0, leave1], axis=0)
            factors_ref[0, span, :] = in_parts(enter, 2).T.astype(BF16)
            factors_ref[1, span, :] = in_parts(leave, 2).T.astype(BF16)
            keep0 = jnp.where(before == right, jnp.exp(-total0), 0.0)
            keep1 = jnp.where(after == left, jnp.exp(-total1), 0.0)
            keeps = jnp.where(lane == chunk, jnp.concatenate([keep0, keep1], axis=0), keeps)
        ahead = jnp.zeros_like(keeps)
        behind = jnp.zeros_like(keeps)
        run_a = jnp.ones((steps, 1), F32)
        run_b = jnp.ones((steps, 1), F32)
        for chunk in range(chunks):
            ahead = jnp.where(lane == chunk, run_a, ahead)
            run_a = run_a * keeps[:, chunk : chunk + 1]
            last = chunks - 1 - chunk
            behind = jnp.where(lane == last, run_b, behind)
            run_b = run_b * keeps[:, last : last + 1]
        for place, values in enumerate((keeps, ahead, behind)):
            columns = in_parts(values, 2).T.astype(BF16)[0:16]
            keeps_ref[2 * place] = mm(columns, e0_ref[...])[0:chunks]
            keeps_ref[2 * place + 1] = mm(columns, e1_ref[...])[0:chunks]


def shifts(places, sign, height):
    row = lax.broadcasted_iota(jnp.int32, (height, 2 * CHUNK), 0)
    col = lax.broadcasted_iota(jnp.int32, (height, 2 * CHUNK), 1)
    parts = []
    for lag in (1, 2, 3):
        wanted = {-1: row + CHUNK - lag, 1: row + lag, 0: row - height + lag}[sign]
        parts.append(flag((col == wanted) & (places[lag - 1] >= lag)))
    return jnp.concatenate(parts, axis=0).astype(BF16)


def proj_kernel(
    lengths_ref,
    normed_ref,
    halo_ref,
    gain_ref,
    wx_ref,
    wbc_ref,
    taps_ref,
    factors_ref,
    keeps_ref,
    e0_ref,
    e1_ref,
    pre_ref,
    act_ref,
    slope_ref,
    s0_ref,
    sf1_ref,
    send_ref,
    prehalo_ref,
    turnhalo_ref,
    buf,
    acc0,
    acc1,
    left0,
    left1,
):
    step = pl.program_id(0)
    per = ROWS // CHUNK
    bounds, base = sequence_bounds(lengths_ref, pl.num_programs(0) * ROWS)
    inner = wx_ref.shape[1]
    channels = taps_ref.shape[1]
    state = (channels - inner) // 4

    @pl.when(step == 0)
    def _():
        x = halo_ref[...].astype(F32)
        inv = lax.rsqrt(jnp.mean(x * x, axis=1, keepdims=True) + EPS)
        normed = x * inv * row_of(gain_ref)
        turnhalo_ref[...] = normed.T.astype(BF16)
        normed = normed.astype(BF16)
        buf[0 : CHUNK - 16, :] = jnp.zeros((CHUNK - 16, channels), BF16)
        prehalo_ref[:, 0:inner] = mm(normed, wx_ref[...]).astype(BF16)
        prehalo_ref[:, inner:channels] = mm(normed, wbc_ref[:, 0 : channels - inner]).astype(BF16)
        buf[CHUNK - 16 : CHUNK, :] = prehalo_ref[...]
        acc0[...] = jnp.zeros_like(acc0)
        acc1[...] = jnp.zeros_like(acc1)

    @pl.when(step > 0)
    def _():
        buf[CHUNK - 16 : CHUNK, :] = buf[ROWS + CHUNK - 16 : ROWS + CHUNK, :]

    normed = normed_ref[...]
    for tile in range(inner // 256):
        cols = slice(tile * 256, tile * 256 + 256)
        px = mm(normed, wx_ref[:, cols]).astype(BF16)
        pre_ref[:, cols] = px
        buf[CHUNK : CHUNK + ROWS, cols] = px
    pb = mm(normed, wbc_ref[:, 0 : channels - inner]).astype(BF16)
    pre_ref[:, inner:channels] = pb
    buf[CHUNK : CHUNK + ROWS, inner:channels] = pb

    first = base + step * ROWS
    for part in range(per):
        offset = part * CHUNK
        rows = first + offset + row_iota(CHUNK)
        place = rows - start_of(rows, bounds)
        shift = shifts([place] * 3, -1, CHUNK)
        leave_cols = factors_ref[0, offset : offset + CHUNK, :]
        for tile in range(channels // 256):
            wide = slice(tile * 256, tile * 256 + 256)
            moved = mm(shift, buf[offset : offset + 2 * CHUNK, wide])
            if tile * 256 < inner:
                leave0 = mm(leave_cols, e0_ref[:, wide])
                leave1 = mm(leave_cols, e1_ref[:, wide])
            for column in (0, 128):
                cols = slice(tile * 256 + column, tile * 256 + column + 128)
                cut = slice(column, column + 128)
                for row in range(0, CHUNK, SUB):
                    here = buf[offset + CHUNK + row : offset + CHUNK + row + SUB, cols]
                    conv = here.astype(F32) * taps_ref[3:4, cols]
                    for lag in (1, 2, 3):
                        at = (lag - 1) * CHUNK + row
                        conv = conv + moved[at : at + SUB, cut] * taps_ref[3 - lag : 4 - lag, cols]
                    sig = jax.nn.sigmoid(conv)
                    act = conv * sig
                    span = slice(offset + row, offset + row + SUB)
                    act_ref[span, cols] = act.astype(BF16)
                    slope_ref[span, cols] = (sig + act - act * sig).astype(BF16)
                    if tile * 256 < inner:
                        held = slice(row, row + SUB)
                        left0[held, cols] = (act * leave0[held, cut]).astype(BF16)
                        left1[held, cols] = (act * leave1[held, cut]).astype(BF16)
        turned = act_ref[offset : offset + CHUNK, inner:channels].astype(F32).T.astype(BF16)
        s0_ref[part] = acc0[...].astype(BF16)
        chunk = pl.ds(step * per + part, 1)
        acc0[...] = keeps_ref[0, chunk, :] * acc0[...] + mm(turned[0:state], left0[...])
        fresh1 = mm(turned[2 * state : 3 * state], left1[...])
        sf1_ref[part] = fresh1.astype(BF16)
        acc1[...] = acc1[...] + keeps_ref[3, chunk, :] * fresh1

    @pl.when(step == pl.num_programs(0) - 1)
    def _():
        send_ref[...] = jnp.where(base > 0, acc1[...], acc0[...]).astype(BF16)


def bc_columns(act_ref, inner, state):
    return [act_ref[:, inner + part * state : inner + (part + 1) * state] for part in range(4)]


def cut_pair(values, width):
    zero = jnp.zeros_like(values)
    first = lane_iota(2 * width) < width
    return jnp.concatenate([jnp.where(first, values, zero), jnp.where(first, zero, values)], axis=0)


def intra_kernel(lengths_ref, act_ref, target_ref, source_ref, y_ref, *, heads, state):
    bounds, base = sequence_bounds(lengths_ref, pl.num_programs(0) * CHUNK)
    first = base + pl.program_id(0) * CHUNK
    inner = y_ref.shape[1]
    width = inner // heads
    t, s = row_iota(CHUNK), lane_iota(CHUNK)
    lower = t > s
    same = (start_of(first + t, bounds) == start_of(first + s, bounds)) & (t != s)
    b0, c0, b1, c1 = bc_columns(act_ref, inner, state)
    scores = jnp.where(lower, mm_nt(c0, b0), mm_nt(c1, b1))
    scores = jnp.where(same, scores, 0.0)
    columns = target_ref[...].T
    for pair in range(heads // 2):
        cols = slice(pair * 2 * width, (pair + 1) * 2 * width)
        weights = []
        for head in (2 * pair, 2 * pair + 1):
            power = jnp.where(
                lower,
                columns[:, head : head + 1] + source_ref[head : head + 1, :],
                columns[:, heads + head : heads + head + 1]
                + source_ref[heads + head : heads + head + 1, :],
            )
            weights.append((jnp.exp2(power) * scores).astype(BF16))
        x_cut = cut_pair(act_ref[:, cols], width)
        y_ref[:, cols] = mm(jnp.concatenate(weights, axis=1), x_cut).astype(BF16)


def mix_kernel(
    lengths_ref,
    skip_ref,
    x_ref,
    act_ref,
    factors_ref,
    sl0_ref,
    sf1_ref,
    keeps_ref,
    recv_ref,
    yin_ref,
    z_ref,
    dnorm_ref,
    wo_ref,
    gain_ref,
    e0_ref,
    e1_ref,
    out_ref,
    mixed_ref,
    dz_ref,
    dy_ref,
    r_ref,
    dcc_ref,
    dl0_ref,
    df1_ref,
    s0_ref,
    s1_ref,
    send_ref,
    sums_ref,
    carry1,
    acc0,
    acc1,
    enter0,
    enter1,
    from0,
    from1,
    gated_s,
    slope_s,
    gate_s,
    in0,
    in1,
    prod0,
    prod1,
    skip_s,
    gain_s,
):
    step = pl.program_id(0)
    chunk = pl.num_programs(0) - 1 - step
    bounds, base = sequence_bounds(lengths_ref, pl.num_programs(0) * CHUNK)
    first = base + chunk * CHUNK
    inner = gain_ref.shape[0]
    heads = r_ref.shape[0] // 2
    width = inner // heads
    state = recv_ref.shape[0]
    small = 32

    @pl.when(step == 0)
    def _():
        recv = recv_ref[...].astype(F32)
        carry1[...] = jnp.where(base > 0, jnp.zeros_like(recv), recv)
        acc0[...] = jnp.zeros_like(acc0)
        acc1[...] = jnp.zeros_like(acc1)
        sums_ref[...] = jnp.zeros_like(sums_ref)
        gain_s[...] = row_of(gain_ref)
        left = lane_iota(2 * width) < width
        for pair in range(heads // 2):
            skip_s[:, pair * 2 * width : (pair + 1) * 2 * width] = jnp.where(
                left, skip_ref[2 * pair], skip_ref[2 * pair + 1]
            )

    keep0 = keeps_ref[0, pl.ds(chunk, 1), :]
    keep1 = keeps_ref[1, pl.ds(chunk, 1), :]
    ahead0 = keeps_ref[2, pl.ds(chunk, 1), :] * jnp.where(base > 0, 1.0, 0.0)
    s0 = (sl0_ref[0].astype(F32) + ahead0 * recv_ref[...].astype(F32)).astype(BF16)
    s1 = carry1[...].astype(BF16)
    carry1[...] = keep1 * carry1[...] + sf1_ref[0].astype(F32)
    s0_ref[0] = s0
    s1_ref[0] = s1
    enter_cols = factors_ref[0]
    turned = act_ref[:, inner:].astype(F32).T.astype(BF16)
    _, c0, _, c1 = bc_columns(act_ref, inner, state)
    enter0[...] = mm(enter_cols, e0_ref[...])
    from0[...] = mm(c0, s0)
    enter1[...] = mm(enter_cols, e1_ref[...])
    from1[...] = mm(c1, s1)
    tiles = [slice(tile * 128, tile * 128 + 128) for tile in range(inner // 128)]
    for row in range(0, CHUNK, small):
        rows = slice(row, row + small)
        square = jnp.zeros((small, 128), F32)
        cross = jnp.zeros((small, 128), F32)
        for cols in tiles:
            mixer = yin_ref[rows, cols].astype(F32) + skip_s[:, cols] * act_ref[rows, cols].astype(F32)
            mixer = mixer + enter0[rows, cols] * from0[rows, cols]
            mixer = mixer + enter1[rows, cols] * from1[rows, cols]
            z = z_ref[rows, cols].astype(F32)
            sig = jax.nn.sigmoid(z)
            gate = z * sig
            gated = mixer * gate
            square = square + gated * gated
            cross = cross + dnorm_ref[rows, cols].astype(F32) * gain_s[:, cols] * gated
            gated_s[rows, cols] = gated
            gate_s[rows, cols] = gate
            slope_s[rows, cols] = mixer * (sig + gate - gate * sig)
        live = flag(first + row + row_iota(small) < bounds[len(bounds) - 2])
        scale = lax.rsqrt(jnp.sum(square, axis=1, keepdims=True) * (1.0 / inner) + EPS)
        back = scale * scale * (jnp.sum(cross, axis=1, keepdims=True) * (1.0 / inner))
        scale = jnp.broadcast_to(scale * live, (small, 128))
        back = jnp.broadcast_to(back, (small, 128))
        for cols in tiles:
            gated = gated_s[rows, cols]
            unit = gated * scale
            gain = gain_s[:, cols]
            mixed_ref[rows, cols] = (unit * gain).astype(BF16)
            dnorm = dnorm_ref[rows, cols].astype(F32)
            sums_ref[0:8, cols] += fold(dnorm * unit)
            dgated = scale * (dnorm * gain - gated * back)
            dz_ref[rows, cols] = (dgated * slope_s[rows, cols]).astype(BF16)
            dy = dgated * gate_s[rows, cols]
            dy_ref[rows, cols] = dy.astype(BF16)
            sums_ref[8:16, cols] += fold(dy * act_ref[rows, cols].astype(F32))
            entered0 = dy * enter0[rows, cols]
            entered1 = dy * enter1[rows, cols]
            in0[rows, cols] = entered0.astype(BF16)
            in1[rows, cols] = entered1.astype(BF16)
            prod0[rows, cols] = (entered0 * from0[rows, cols]).astype(BF16)
            prod1[rows, cols] = (entered1 * from1[rows, cols]).astype(BF16)
    out_ref[...] = (x_ref[...].astype(F32) + mm(mixed_ref[...], wo_ref[...])).astype(BF16)
    ones = e0_ref[0:heads, :]
    r_ref[0:heads, :] = mm_nt(ones, prod0[...])
    r_ref[heads : 2 * heads, :] = mm_nt(ones, prod1[...])
    dcc_ref[:, 0:state] = mm_nt(in0[...], s0)
    dcc_ref[:, state : 2 * state] = mm_nt(in1[...], s1)
    dl0_ref[0] = acc0[...].astype(BF16)
    acc0[...] = keep0 * acc0[...] + mm(turned[state : 2 * state], in0[...])
    df1 = mm(turned[3 * state : 4 * state], in1[...])
    df1_ref[0] = df1.astype(BF16)
    acc1[...] = acc1[...] + keeps_ref[5, pl.ds(chunk, 1), :] * df1

    @pl.when(step == pl.num_programs(0) - 1)
    def _():
        send_ref[...] = jnp.where(base > 0, acc0[...], acc1[...]).astype(BF16)


def back_kernel(
    lengths_ref,
    skip_ref,
    act_ref,
    slope_ref,
    target_ref,
    source_ref,
    factors_ref,
    dcc_ref,
    dy_ref,
    s0_ref,
    s1_ref,
    dl0_ref,
    df1_ref,
    keeps_ref,
    recv_ref,
    start_ref,
    e0_ref,
    e1_ref,
    spans_ref,
    dpre_ref,
    moves_ref,
    last_ref,
    carry1,
    dscore,
    low_s,
    all_s,
    out0,
    out1,
    prod0,
    prod1,
    ds0,
    ds1,
    *,
    skipped,
    chunks,
):
    step = pl.program_id(0)
    chunk = step + skipped
    bounds, base = sequence_bounds(lengths_ref, chunks * CHUNK)
    first = base + chunk * CHUNK
    heads = skip_ref.shape[0]
    inner = keeps_ref.shape[2]
    width = inner // heads
    state = recv_ref.shape[0]

    @pl.when(step == 0)
    def _():
        if skipped:
            carry1[...] = start_ref[...]
        else:
            recv = recv_ref[...].astype(F32)
            carry1[...] = jnp.where(base > 0, recv, jnp.zeros_like(recv))

    keep0 = keeps_ref[0, pl.ds(chunk, 1), :]
    keep1 = keeps_ref[1, pl.ds(chunk, 1), :]
    behind0 = keeps_ref[4, pl.ds(chunk, 1), :] * jnp.where(base > 0, 0.0, 1.0)
    d0 = dl0_ref[0].astype(F32) + behind0 * recv_ref[...].astype(F32)
    d1 = carry1[...]
    ds0[...] = d0.astype(BF16)
    ds1[...] = d1.astype(BF16)
    kept0 = jnp.sum(d0 * s0_ref[0].astype(F32), axis=0, keepdims=True) * keep0
    kept1 = jnp.sum(d1 * s1_ref[0].astype(F32), axis=0, keepdims=True) * keep1
    carry1[...] = keep1 * d1 + df1_ref[0].astype(F32)
    ones = e0_ref[0:heads, :]
    kept = jnp.concatenate([kept0, kept1, jnp.zeros((6, inner), F32)], axis=0)
    kept_high = kept.astype(BF16)
    kept_low = (kept - kept_high.astype(F32)).astype(BF16)
    kept_sum = mm_nt(ones, kept_high) + mm_nt(ones, kept_low)

    t = lane_iota(CHUNK)
    starts = start_of(first + t, bounds)
    b0, c0, b1, c1 = bc_columns(act_ref, inner, state)
    forward = mm_nt(b0, c0)
    backward = mm_nt(b1, c1)
    halves = []
    for row in range(0, CHUNK, SUB):
        s = row + row_iota(SUB)
        early = s < t
        same = (start_of(first + s, bounds) == starts) & (s != t)
        both = jnp.where(early, forward[row : row + SUB], backward[row : row + SUB])
        halves.append((slice(row, row + SUB), early, flag(early), jnp.where(same, both, 0.0)))
    in_cols = source_ref[...].T
    leave_cols = factors_ref[0]
    dscore[...] = jnp.zeros_like(dscore)
    left = lane_iota(2 * width) < width
    for pair in range(heads // 2):
        cols = slice(pair * 2 * width, (pair + 1) * 2 * width)
        dweights = mm_nt(cut_pair(act_ref[:, cols], width), dy_ref[:, cols])
        weights = []
        for part in (0, 1):
            head = 2 * pair + part
            held = slice(head * CHUNK, (head + 1) * CHUNK)
            parts = []
            sum0 = jnp.zeros((8, CHUNK), F32)
            sum1 = jnp.zeros((8, CHUNK), F32)
            for rows, early, early_f, scores in halves:
                power = jnp.where(
                    early,
                    in_cols[rows, head : head + 1] + target_ref[head : head + 1, :],
                    in_cols[rows, heads + head : heads + head + 1]
                    + target_ref[heads + head : heads + head + 1, :],
                )
                decay = jnp.exp2(power)
                parts.append((decay * scores).astype(BF16))
                at = part * CHUNK + rows.start
                dweight = dweights[at : at + SUB] * decay
                dscore[rows, :] += dweight
                change = dweight * scores
                low = change * early_f
                low_s[rows, held] = low.astype(BF16)
                all_s[rows, held] = change.astype(BF16)
                sum0 = sum0 + fold(low)
                sum1 = sum1 + fold(change)
            weights.append(jnp.concatenate(parts, axis=0))
            moves_ref[head : head + 1, :] = jnp.sum(sum0, axis=0, keepdims=True)
            moves_ref[heads + head : heads + head + 1, :] = jnp.sum(sum1, axis=0, keepdims=True)
        dx = mm(jnp.concatenate(weights, axis=1), cut_pair(dy_ref[:, cols], width))
        leave0 = mm(leave_cols, e0_ref[:, cols])
        leave1 = mm(leave_cols, e1_ref[:, cols])
        from0 = mm(b0, ds0[:, cols])
        from1 = mm(b1, ds1[:, cols])
        skip = jnp.where(left, skip_ref[2 * pair], skip_ref[2 * pair + 1])
        for rows, _, _, _ in halves:
            xf = act_ref[rows, cols].astype(F32)
            came0 = leave0[rows] * from0[rows]
            came1 = leave1[rows] * from1[rows]
            dconv = dx[rows] + skip * dy_ref[rows, cols].astype(F32) + came0 + came1
            dpre_ref[rows, cols] = (dconv * slope_ref[rows, cols].astype(F32)).astype(BF16)
            out0[rows, cols] = (xf * leave0[rows]).astype(BF16)
            out1[rows, cols] = (xf * leave1[rows]).astype(BF16)
            prod0[rows, cols] = (xf * came0).astype(BF16)
            prod1[rows, cols] = (xf * came1).astype(BF16)
    dscore0, dscore1 = [], []
    for rows, early, _, _ in halves:
        s = rows.start + row_iota(SUB)
        same = (start_of(first + s, bounds) == starts) & (s != t)
        both = jnp.where(same, dscore[rows, :], 0.0)
        dscore0.append(jnp.where(early, both, 0.0).astype(BF16))
        dscore1.append(jnp.where(early, 0.0, both).astype(BF16))
    dscore0 = jnp.concatenate(dscore0, axis=0)
    dscore1 = jnp.concatenate(dscore1, axis=0)
    moves_ref[2 * heads : 3 * heads, :] = mm_nt(spans_ref[...], low_s[...])
    moves_ref[3 * heads : 4 * heads, :] = mm_nt(spans_ref[...], all_s[...])
    moves_ref[4 * heads : 5 * heads, :] = mm_nt(ones, prod0[...])
    moves_ref[5 * heads : 6 * heads, :] = mm_nt(ones, prod1[...])
    moves_ref[6 * heads : 7 * heads, :] = jnp.broadcast_to(kept_sum[:, 0:1], (heads, CHUNK))
    moves_ref[7 * heads : 8 * heads, :] = jnp.broadcast_to(kept_sum[:, 1:2], (heads, CHUNK))
    db0 = mm(dscore0, c0) + mm_nt(out0[...], ds0[...])
    db1 = mm(dscore1, c1) + mm_nt(out1[...], ds1[...])
    dc0 = mm_tn(dscore0, b0) + dcc_ref[:, 0:state]
    dc1 = mm_tn(dscore1, b1) + dcc_ref[:, state : 2 * state]
    dbc = jnp.concatenate([db0, dc0, db1, dc1], axis=1)
    dpre_ref[:, inner:] = (dbc * slope_ref[:, inner:].astype(F32)).astype(BF16)

    @pl.when(step == pl.num_programs(0) - 1)
    def _():
        last_ref[...] = carry1[...]


def steps_back(raw, dt, rate, moves, r):
    steps = raw.shape[0]
    heads = steps // 2
    chunks = raw.shape[1] // CHUNK
    s, t = row_iota(CHUNK), lane_iota(CHUNK)

    def stack(values):
        parts = [values[:, chunk * CHUNK : (chunk + 1) * CHUNK] for chunk in range(chunks)]
        return jnp.concatenate(parts, axis=0)

    def unstack(values):
        parts = [values[chunk * heads : (chunk + 1) * heads] for chunk in range(chunks)]
        return jnp.concatenate(parts, axis=1)

    got0, got, own0, own, k0, k1, kept0, kept1 = [
        moves[part * heads : (part + 1) * heads] for part in range(8)
    ]
    own1, got1 = own - own0, got - got0
    da0 = exact_mm(stack(got0 + r[:heads] - own0), flag(s >= t)) + exact_mm(stack(k0), flag(s < t))
    da1 = exact_mm(stack(got1 + r[heads:] - own1), flag(s <= t)) + exact_mm(stack(k1), flag(s > t))
    da = -jnp.concatenate([unstack(da0) + kept0, unstack(da1) + kept1], axis=0)
    dlog = jnp.concatenate([own0 + k0, own1 + k1], axis=0)
    sig = jax.nn.sigmoid(raw)
    ratio = jnp.where(raw < -20.0, 1.0, sig / jnp.maximum(dt, 1e-37))
    return dlog * ratio + da * rate * sig, jnp.sum(da * dt, axis=1, keepdims=True) * rate


def weights_kernel(turned_ref, dz_ref, mixed_ref, c_ref, go_ref, gz_ref, *, half):
    gz_ref[...] = mm(turned_ref[...], dz_ref[...]).astype(BF16)
    product = mm_tn(mixed_ref[...], c_ref[...]).astype(BF16)
    if not half:
        go_ref[...] = product
        return
    model = c_ref.shape[1]
    for shard in range(product.shape[0] // (2 * half)):
        span = slice(shard * half, (shard + 1) * half)
        go_ref[span, 0:model] = product[2 * shard * half : (2 * shard + 1) * half]
        go_ref[span, model : 2 * model] = product[(2 * shard + 1) * half : (2 * shard + 2) * half]


def conv_back_kernel(
    lengths_ref,
    turned_ref,
    turnhalo_ref,
    dpre_ref,
    pre_ref,
    prehalo_ref,
    taps_ref,
    raw_ref,
    dt_ref,
    rate_ref,
    moves_ref,
    r_ref,
    dproj_ref,
    dhalo_ref,
    mine_ref,
    theirs_ref,
    draw_ref,
    sums_ref,
    shift,
    buf,
    *,
    shard,
):
    step = pl.program_id(0)
    count, wide = dpre_ref.shape
    chunks = count // CHUNK
    steps = raw_ref.shape[0]
    bounds, base = sequence_bounds(lengths_ref, count)

    @pl.when(step == 0)
    def _():
        for chunk in range(chunks):
            places = []
            for lag in (1, 2, 3):
                rows = base + chunk * CHUNK + lag + row_iota(CHUNK)
                places.append(rows - start_of(rows, bounds))
            shift[chunk * 3 * CHUNK : (chunk + 1) * 3 * CHUNK, :] = shifts(places, 1, CHUNK)
        places = []
        for lag in (1, 2, 3):
            rows = base + lag - 16 + row_iota(16)
            places.append(rows - start_of(rows, bounds))
        shift[chunks * 3 * CHUNK :, :] = shifts(places, 0, 16)
        buf[...] = jnp.zeros_like(buf)

    def hand_over(product):
        if not shard:
            mine_ref[...] = product
            return
        pieces = [product[place : place + shard] for place in range(0, product.shape[0], shard)]
        even = jnp.concatenate(pieces[0::2], axis=0)
        odd = jnp.concatenate(pieces[1::2], axis=0)
        core = lax.rem(lax.axis_index("dp"), 2)

        @pl.when(core == 0)
        def _():
            mine_ref[...] = even
            theirs_ref[...] = odd

        @pl.when(core == 1)
        def _():
            mine_ref[...] = odd
            theirs_ref[...] = even

    @pl.when(step < pl.num_programs(0) - 1)
    def _():
        buf[0:CHUNK, :] = dpre_ref[count - CHUNK :, :]
        moved = mm(shift[chunks * 3 * CHUNK :, :], dpre_ref[0 : 2 * CHUNK, :])
        halo_sums = [None] * 4
        dproj = jnp.zeros((16, wide), F32)
        pre = prehalo_ref[...].astype(F32)
        for lag in (1, 2, 3):
            part = moved[(lag - 1) * 16 : lag * 16]
            dproj = dproj + part * taps_ref[3 - lag : 4 - lag, :]
            halo_sums[3 - lag] = jnp.sum(pre * part, axis=0, keepdims=True)
        halo_sums[3] = jnp.zeros((1, wide), F32)
        dhalo_ref[...] = dproj.astype(BF16)
        sums = [[jnp.zeros((8, 128), F32) for _ in range(4)] for _ in range(wide // 128)]
        for chunk in range(chunks):
            if chunk < chunks - 1:
                pair = dpre_ref[chunk * CHUNK : chunk * CHUNK + 2 * CHUNK, :]
            else:
                pair = buf[...]
            moved = mm(shift[chunk * 3 * CHUNK : (chunk + 1) * 3 * CHUNK, :], pair)
            for place in range(wide // 128):
                cols = slice(place * 128, place * 128 + 128)
                for row in range(0, CHUNK, SUB):
                    span = slice(chunk * CHUNK + row, chunk * CHUNK + row + SUB)
                    pre = pre_ref[span, cols].astype(F32)
                    here = dpre_ref[span, cols].astype(F32)
                    dproj = here * taps_ref[3:4, cols]
                    sums[place][3] = sums[place][3] + fold(pre * here)
                    for lag in (1, 2, 3):
                        at = (lag - 1) * CHUNK + row
                        part = moved[at : at + SUB, cols]
                        dproj = dproj + part * taps_ref[3 - lag : 4 - lag, cols]
                        sums[place][3 - lag] = sums[place][3 - lag] + fold(pre * part)
                    dproj_ref[span, cols] = dproj.astype(BF16)
        sums_ref[...] = jnp.zeros_like(sums_ref)
        for place in range(wide // 128):
            cols = slice(place * 128, place * 128 + 128)
            for tap in range(4):
                sums_ref[tap : tap + 1, cols] = (
                    jnp.sum(sums[place][tap], axis=0, keepdims=True) + halo_sums[tap][:, cols]
                )
        product = mm(turned_ref[...], dproj_ref[...]) + mm(turnhalo_ref[...], dhalo_ref[...])
        hand_over(product.astype(BF16))

    @pl.when(step == pl.num_programs(0) - 1)
    def _():
        rate = rate_ref[:, 0:1]
        draw, drate = steps_back(raw_ref[...], dt_ref[...], rate, moves_ref[...], r_ref[...])
        low = draw.astype(BF16)
        draw_ref[...] = low
        product = mm_nt(turned_ref[...], low).astype(BF16)
        hand_over(
            jnp.concatenate([product, jnp.zeros((product.shape[0], wide - steps), BF16)], axis=1)
        )
        columns = [jnp.sum(draw, axis=1, keepdims=True), drate, jnp.zeros((steps, 6), F32)]
        sums_ref[...] = jnp.zeros_like(sums_ref)
        sums_ref[:, 0:steps] = jnp.concatenate(columns, axis=1).T


def quarters_kernel(mine_ref, got_ref, keep_ref, across_ref, along_ref, both_ref, *, shard):
    half = mine_ref.shape[1] // 2
    row_bit = lax.rem(lax.axis_index("dp") // 2, 2)
    side = lax.axis_index("dir")
    for place in range(keep_ref.shape[0] // shard):
        rows = slice(place * shard, (place + 1) * shard)
        for out_ref, row, column in (
            (keep_ref, row_bit, side),
            (across_ref, row_bit, 1 - side),
            (along_ref, 1 - row_bit, side),
            (both_ref, 1 - row_bit, 1 - side),
        ):
            here = pl.ds(pl.multiple_of((2 * place + row) * shard, shard), shard)
            cols = pl.ds(pl.multiple_of(column * half, half), half)
            total = mine_ref[here, cols].astype(F32) + got_ref[here, cols].astype(F32)
            out_ref[rows, :] = total.astype(out_ref.dtype)


def levels_kernel(keep_ref, a_ref, b_ref, c_ref, own_ref, s1_ref, s2_ref, s3_ref, *, shard):
    level = lax.axis_index("dp") // 4
    for bits, out_ref in enumerate((own_ref, s1_ref, s2_ref, s3_ref)):
        wanted = jnp.bitwise_xor(level, bits)
        rows = pl.ds(pl.multiple_of(wanted * shard, shard), shard)
        total = keep_ref[rows, :] + a_ref[rows, :].astype(F32)
        total = total + (b_ref[rows, :].astype(F32) + c_ref[rows, :].astype(F32))
        out_ref[...] = total.astype(out_ref.dtype)


def last_kernel(own_ref, a_ref, b_ref, c_ref, out_ref):
    total = own_ref[...] + a_ref[...].astype(F32)
    total = total + (b_ref[...].astype(F32) + c_ref[...].astype(F32))
    out_ref[...] = total.astype(BF16)


def finish_kernel(
    late_ref, lategot_ref, early_ref, earlygot_ref, small_ref, gx_ref, gz_ref, gbc_ref, go_ref,
    gtaps_ref, gmix_ref, gin_ref, gskip_ref, gbias_ref, galog_ref
):
    side = lax.axis_index("dir")
    half = late_ref.shape[1]
    inner = gx_ref.shape[1]
    model = go_ref.shape[1]
    shard = gx_ref.shape[0]
    first = jnp.where(side == 0, late_ref[...].astype(F32), lategot_ref[...].astype(F32))
    second = jnp.where(side == 0, lategot_ref[...].astype(F32), late_ref[...].astype(F32))
    gx_ref[:, 0:half] = first
    gx_ref[:, half:inner] = second[:, 0 : inner - half]
    gbc_ref[...] = second[:, inner - half : inner - half + gbc_ref.shape[1]]
    early = early_ref[...].astype(F32) + earlygot_ref[...].astype(F32)
    go_ref[0:shard, :] = early[:, 0:model]
    go_ref[shard : 2 * shard, :] = early[:, model : 2 * model]
    gz_ref[...] = early[:, 2 * model :]
    gtaps_ref[...] = small_ref[0:4, 0 : gtaps_ref.shape[1]]
    gmix_ref[...] = small_ref[4:5, 0:inner].reshape(inner)
    gin_ref[...] = small_ref[5:6, 0:model].reshape(model)
    heads = gskip_ref.shape[0]
    gskip_ref[...] = small_ref[6:7, 0:128].reshape(128)[0:heads]
    gbias_ref[0:1, :] = small_ref[6:7, 128 : 128 + heads]
    gbias_ref[1:2, :] = small_ref[6:7, 128 + heads : 128 + 2 * heads]
    galog_ref[0:1, :] = small_ref[6:7, 256 : 256 + heads]
    galog_ref[1:2, :] = small_ref[6:7, 256 + heads : 256 + 2 * heads]


def inputs_kernel(
    x_ref,
    c_ref,
    gain_ref,
    dproj_ref,
    dhalo_ref,
    draw_ref,
    dz_ref,
    wx_ref,
    wbc_ref,
    wz_ref,
    mix_sums_ref,
    tap_sums_ref,
    e0_ref,
    gin_ref,
    small_ref,
    total,
    dproj,
):
    step = pl.program_id(0)
    model, inner = wx_ref.shape
    steps = draw_ref.shape[0]
    heads = steps // 2
    narrow = wbc_ref.shape[1] - steps
    channels = inner + narrow

    @pl.when(step == 0)
    def _():
        total[...] = jnp.zeros_like(total)

    @pl.when(step == pl.num_programs(0) - 1)
    def _():
        tail = slice(dproj_ref.shape[0] - 16, dproj_ref.shape[0])
        both = dproj_ref[tail, :].astype(F32) + dhalo_ref[...].astype(F32)
        dproj[...] = dproj_ref[...]
        dproj[tail, :] = both.astype(BF16)

    @pl.when(step < pl.num_programs(0) - 1)
    def _():
        dproj[...] = dproj_ref[...]

    dn = mm_nt(dproj[:, 0:inner], wx_ref[...])
    dn = dn + mm_nt(dz_ref[...], wz_ref[...])
    dn = dn + mm_nt(dproj[:, inner:], wbc_ref[:, 0:narrow])
    dn = dn + mm_nt(draw_ref[...].astype(F32).T.astype(BF16), wbc_ref[:, narrow:])
    x = x_ref[...].astype(F32)
    inv = lax.rsqrt(jnp.mean(x * x, axis=1, keepdims=True) + EPS)
    unit = x * inv
    total[...] += fold(dn * unit)
    f = dn * row_of(gain_ref)
    back = inv * (f - unit * jnp.mean(f * unit, axis=1, keepdims=True))
    gin_ref[...] = (c_ref[...].astype(F32) + back).astype(BF16)

    @pl.when(step == pl.num_programs(0) - 1)
    def _():
        small_ref[...] = jnp.zeros_like(small_ref)
        small_ref[0:4, 0:channels] = tap_sums_ref[0:4, 0:channels]
        small_ref[4:5, 0:inner] = jnp.sum(mix_sums_ref[0:8, :], axis=0, keepdims=True)
        small_ref[5:6, 0:model] = jnp.sum(total[...], axis=0, keepdims=True)
        skips = in_parts(mix_sums_ref[8:16, :], 2).astype(BF16)
        skips = jnp.sum(mm_nt(e0_ref[0:heads, :], skips), axis=1, keepdims=True)
        skips = jnp.broadcast_to(skips, (heads, 128)).T
        small_ref[6:7, 0:heads] = skips[0:1]
        small_ref[6:7, 128:256] = tap_sums_ref[0:1, channels : channels + 128]
        small_ref[6:7, 256:384] = tap_sums_ref[1:2, channels : channels + 128]


def smem():
    return pl.BlockSpec(memory_space=pltpu.SMEM)


def resident():
    return pl.BlockSpec(memory_space=pltpu.VMEM)


def whole(shape):
    return pl.BlockSpec(shape, lambda i: (0,) * len(shape), pipeline_mode=pl.Buffered(1))


def rows_of(count, width):
    return pl.BlockSpec((count, width), lambda i: (i, 0))


def lanes_of(height, count):
    return pl.BlockSpec((height, count), lambda i: (0, i))


def parts_of(count, *rest):
    return pl.BlockSpec((count,) + rest, lambda i: (i,) + (0,) * len(rest))


def call(kernel, name, grid, in_specs, outs, scratch, flops, moved, args, vmem):
    return pl.pallas_call(
        kernel,
        name=name,
        grid=(grid,),
        in_specs=in_specs,
        out_specs=[spec for spec, _, _ in outs],
        out_shape=[jax.ShapeDtypeStruct(shape, dtype) for _, shape, dtype in outs],
        scratch_shapes=scratch,
        compiler_params=pltpu.CompilerParams(
            vmem_limit_bytes=vmem * MIB, dimension_semantics=("arbitrary",)
        ),
        cost_estimate=pl.CostEstimate(flops=flops, bytes_accessed=moved, transcendentals=0),
    )(*args)


def traded(values, axis, bit, size):
    return lax.ppermute(values, axis, [(i, i ^ bit) for i in range(size)])


def sum_shards(grad, dp_count):
    index = lax.axis_index("dp")
    held = grad.reshape(dp_count, grad.shape[0] // dp_count, grad.shape[1])
    bit = 1
    while bit < dp_count:
        paired = held.reshape(held.shape[0] // 2, 2, held.shape[1], held.shape[2])
        mine = (index // bit) % 2
        kept = lax.dynamic_index_in_dim(paired, mine, 1, keepdims=False)
        sent = lax.dynamic_index_in_dim(paired, 1 - mine, 1, keepdims=False).astype(BF16)
        held = kept.astype(F32) + traded(sent, "dp", bit, dp_count).astype(F32)
        bit *= 2
    held = held[0].astype(BF16)
    return held.astype(F32) + traded(held, "dir", 1, 2).astype(F32)


def sum_all(values, dp_count):
    bit = 1
    while bit < dp_count:
        values = values + traded(values, "dp", bit, dp_count)
        bit *= 2
    return values + traded(values, "dir", 1, 2)


def local(
    dp_count,
    hidden_in,
    lengths,
    gain_in,
    w_x,
    w_z,
    w_bcdt,
    conv_w,
    dt_bias,
    a_log,
    d_skip,
    gain_mix,
    w_out,
    cotangent,
):
    x = hidden_in[0]
    cot = cotangent[0]
    count, model = x.shape
    inner = w_x.shape[1]
    channels = conv_w.shape[1]
    heads = d_skip.shape[0]
    width = inner // heads
    state = (channels - inner) // 4
    chunks = count // CHUNK
    steps = 2 * heads

    halo = lax.ppermute(x[count - 16 :], "dir", [(0, 1)])

    spread = np.repeat(np.eye(heads, dtype=np.float32), width, axis=1)
    zeros = np.zeros_like(spread)
    e0 = jnp.asarray(np.concatenate([spread, zeros, spread, zeros]), BF16)
    e1 = jnp.asarray(np.concatenate([zeros, spread, zeros, spread]), BF16)
    spans = jnp.asarray(np.repeat(np.eye(heads, dtype=np.float32), CHUNK, axis=1), BF16)
    def rows_out(size, columns, dtype):
        return (rows_of(size, columns), (count, columns), dtype)

    def full(shape, dtype):
        return (pl.BlockSpec(shape, lambda i: (0,) * len(shape)), shape, dtype)

    normed, turned, gate_z, d_norm, raw, dt, rate, target, source, factors, keeps = call(
        gates_kernel,
        "gates",
        count // ROWS,
        [
            smem(),
            smem(),
            smem(),
            rows_of(ROWS, model),
            rows_of(ROWS, model),
            whole((model,)),
            whole((model, inner)),
            whole((inner, model)),
            whole(w_bcdt.shape),
            whole(e0.shape),
            whole(e1.shape),
        ],
        [
            rows_out(ROWS, model, BF16),
            (lanes_of(model, ROWS), (model, count), BF16),
            rows_out(ROWS, inner, BF16),
            rows_out(ROWS, inner, BF16),
            full((steps, count), F32),
            full((steps, count), F32),
            full((steps, 128), F32),
            full((steps, count), F32),
            full((steps, count), F32),
            full((2, count, 2 * steps), BF16),
            full((6, chunks, inner), F32),
        ],
        [],
        4 * count * model * inner,
        4 * count * (model + inner) + 4 * model * inner,
        (lengths, dt_bias, a_log, x, cot, gain_in, w_z, w_out, w_bcdt, e0, e1),
        VMEM_GATES,
    )

    per = ROWS // CHUNK
    state_f32 = pltpu.VMEM((state, inner), F32)
    state_bf16 = pltpu.VMEM((state, inner), BF16)
    row_f32 = pltpu.VMEM((1, inner), F32)
    chunk_f32 = pltpu.VMEM((CHUNK, inner), F32)
    chunk_bf16 = pltpu.VMEM((CHUNK, inner), BF16)
    pre, act, slope, sl0, sf1, send, pre_halo, turn_halo = call(
        proj_kernel,
        "proj",
        count // ROWS,
        [
            smem(),
            rows_of(ROWS, model),
            whole((16, model)),
            whole((model,)),
            whole((model, inner)),
            whole(w_bcdt.shape),
            whole(conv_w.shape),
            pl.BlockSpec((1, ROWS, 2 * steps), lambda i: (1, i, 0)),
            whole((6, chunks, inner)),
            whole(e0.shape),
            whole(e1.shape),
        ],
        [
            rows_out(ROWS, channels, BF16),
            rows_out(ROWS, channels, BF16),
            rows_out(ROWS, channels, BF16),
            (parts_of(per, state, inner), (chunks, state, inner), BF16),
            (parts_of(per, state, inner), (chunks, state, inner), BF16),
            full((state, inner), BF16),
            full((16, channels), BF16),
            full((model, 16), BF16),
        ],
        [
            pltpu.VMEM((CHUNK + ROWS, channels), BF16),
            state_f32,
            state_f32,
            chunk_bf16,
            chunk_bf16,
        ],
        3 * count * model * inner,
        8 * count * inner,
        (lengths, normed, halo, gain_in, w_x, w_bcdt, conv_w, factors, keeps, e0, e1),
        VMEM_PROJ,
    )
    received = lax.ppermute(send, "dir", SWAP)

    (y_in,) = call(
        functools.partial(intra_kernel, heads=heads, state=state),
        "intra",
        chunks,
        [
            smem(),
            rows_of(CHUNK, channels),
            lanes_of(steps, CHUNK),
            lanes_of(steps, CHUNK),
        ],
        [rows_out(CHUNK, inner, BF16)],
        [],
        8 * count * CHUNK * inner,
        6 * count * inner,
        (lengths, act, target, source),
        VMEM_INTRA,
    )

    def down_rows(width):
        return pl.BlockSpec((CHUNK, width), lambda i: (chunks - 1 - i, 0))

    def down_lanes(height):
        return pl.BlockSpec((height, CHUNK), lambda i: (0, chunks - 1 - i))

    def down_parts(*rest):
        return pl.BlockSpec((1,) + rest, lambda i: (chunks - 1 - i,) + (0,) * len(rest))

    states = (down_parts(state, inner), (chunks, state, inner), BF16)
    out, mixed, dz, dy, r, dcc, dl0, df1, s0, s1, d_send, mix_sums = call(
        mix_kernel,
        "mix",
        chunks,
        [
            smem(),
            smem(),
            down_rows(model),
            down_rows(channels),
            pl.BlockSpec((1, CHUNK, 2 * steps), lambda i: (0, chunks - 1 - i, 0)),
            down_parts(state, inner),
            down_parts(state, inner),
            whole((6, chunks, inner)),
            whole((state, inner)),
            down_rows(inner),
            down_rows(inner),
            down_rows(inner),
            whole((inner, model)),
            whole((inner,)),
            whole(e0.shape),
            whole(e1.shape),
        ],
        [
            (down_rows(model), (count, model), BF16),
            (down_rows(inner), (count, inner), BF16),
            (down_rows(inner), (count, inner), BF16),
            (down_rows(inner), (count, inner), BF16),
            (down_lanes(steps), (steps, count), F32),
            (down_rows(2 * state), (count, 2 * state), F32),
            states,
            states,
            states,
            states,
            full((state, inner), BF16),
            full((16, inner), F32),
        ],
        [state_f32] * 3 + [chunk_f32] * 7 + [chunk_bf16] * 4 + [row_f32] * 2,
        3 * count * model * inner,
        16 * count * inner,
        (
            lengths,
            d_skip,
            x,
            act,
            factors,
            sl0,
            sf1,
            keeps,
            received,
            y_in,
            gate_z,
            d_norm,
            w_out,
            gain_mix,
            e0,
            e1,
        ),
        VMEM_MIX,
    )
    d_received = lax.ppermute(d_send, "dir", SWAP)

    blocks = 4
    shard = model // dp_count
    half = shard if shard % 16 == 0 else 0
    out_spec = (
        (rows_of(model // blocks, inner), (model, inner), BF16)
        if half
        else (rows_of(inner // blocks, model), (inner, model), BF16)
    )
    g_out, g_z = call(
        functools.partial(weights_kernel, half=half),
        "weights",
        blocks,
        [
            whole((model, count)),
            lanes_of(count, inner // blocks),
            lanes_of(count, inner // blocks),
            whole((count, model)),
        ],
        [out_spec, (lanes_of(model, inner // blocks), (model, inner), BF16)],
        [],
        4 * count * model * inner,
        6 * count * inner,
        (turned, dz, mixed, cot),
        VMEM_WEIGHTS,
    )
    if not half:
        g_out = g_out.reshape(dp_count, 2, shard, model)
        g_out = g_out.transpose(0, 2, 1, 3).reshape(model, inner)
    g_early = jnp.concatenate([g_out, g_z], axis=1)
    early = lax.psum_scatter(g_early, "dp", scatter_dimension=0, tiled=True)

    def back(skipped, taken, start):
        def rows_from(width):
            return pl.BlockSpec((CHUNK, width), lambda i: (i + skipped, 0))

        def lanes_from(height):
            return pl.BlockSpec((height, CHUNK), lambda i: (0, i + skipped))

        def parts_from(*rest):
            return pl.BlockSpec((1,) + rest, lambda i: (i + skipped,) + (0,) * len(rest))

        return call(
            functools.partial(back_kernel, skipped=skipped, chunks=chunks),
            "back" + str(skipped),
            taken,
            [
                smem(),
                smem(),
                rows_from(channels),
                rows_from(channels),
                lanes_from(steps),
                lanes_from(steps),
                pl.BlockSpec((1, CHUNK, 2 * steps), lambda i: (1, i + skipped, 0)),
                rows_from(2 * state),
                rows_from(inner),
                parts_from(state, inner),
                parts_from(state, inner),
                parts_from(state, inner),
                parts_from(state, inner),
                whole((6, chunks, inner)),
                whole((state, inner)),
                whole(start.shape),
                whole(e0.shape),
                whole(e1.shape),
                whole(spans.shape),
            ],
            [
                (rows_of(CHUNK, channels), (taken * CHUNK, channels), BF16),
                (lanes_of(8 * heads, CHUNK), (8 * heads, taken * CHUNK), F32),
                full((state, inner), F32),
            ],
            [
                state_f32,
                pltpu.VMEM((CHUNK, CHUNK), F32),
                pltpu.VMEM((CHUNK, heads * CHUNK), BF16),
                pltpu.VMEM((CHUNK, heads * CHUNK), BF16),
            ]
            + [chunk_bf16] * 4
            + [state_bf16] * 2,
            24 * taken * CHUNK * CHUNK * inner,
            16 * taken * CHUNK * inner,
            (
                lengths,
                d_skip,
                act,
                slope,
                target,
                source,
                factors,
                dcc,
                dy,
                s0,
                s1,
                dl0,
                df1,
                keeps,
                d_received,
                start,
                e0,
                e1,
                spans,
            ),
            VMEM_BACK,
        )

    dpre, moves, _ = back(0, chunks, d_received)

    tile = 256
    tiles = channels // tile
    def tile_of(height):
        return pl.BlockSpec((height, tile), lambda i: (0, jnp.minimum(i, tiles - 1)))

    wide = (tiles + 1) * tile
    kept_rows = model // 2 if half else model
    dproj, dhalo, mine, theirs, draw, tap_sums = call(
        functools.partial(conv_back_kernel, shard=half),
        "conv_back",
        tiles + 1,
        [
            smem(),
            whole((model, count)),
            whole((model, 16)),
            tile_of(count),
            tile_of(count),
            tile_of(16),
            tile_of(conv_w.shape[0]),
            whole((steps, count)),
            whole((steps, count)),
            whole((steps, 128)),
            whole((8 * heads, count)),
            whole((steps, count)),
        ],
        [
            (tile_of(count), (count, channels), BF16),
            (tile_of(16), (16, channels), BF16),
            (lanes_of(kept_rows, tile), (kept_rows, wide), BF16),
            (lanes_of(kept_rows, tile), (kept_rows, wide), BF16),
            full((steps, count), BF16),
            (lanes_of(8, tile), (8, wide), F32),
        ],
        [
            pltpu.VMEM((3 * count + 48, 2 * CHUNK), BF16),
            pltpu.VMEM((2 * CHUNK, tile), BF16),
        ],
        2 * count * model * channels,
        6 * count * channels,
        (lengths, turned, turn_halo, dpre, pre, pre_halo, conv_w, raw, dt, rate, moves, r),
        VMEM_CONV,
    )
    d_halo = lax.ppermute(dhalo, "dir", [(1, 0)])

    grad_in, small = call(
        inputs_kernel,
        "inputs",
        count // ROWS,
        [
            rows_of(ROWS, model),
            rows_of(ROWS, model),
            whole((model,)),
            rows_of(ROWS, channels),
            whole((16, channels)),
            lanes_of(steps, ROWS),
            rows_of(ROWS, inner),
            whole((model, inner)),
            whole(w_bcdt.shape),
            whole((model, inner)),
            whole(mix_sums.shape),
            whole(tap_sums.shape),
            whole(e0.shape),
        ],
        [
            rows_out(ROWS, model, BF16),
            full((8, tap_sums.shape[1]), F32),
        ],
        [pltpu.VMEM((8, model), F32), pltpu.VMEM((ROWS, channels), BF16)],
        5 * count * model * inner,
        8 * count * inner,
        (x, cot, gain_in, dproj, d_halo, draw, dz, w_x, w_bcdt, w_z, mix_sums, tap_sums, e0),
        VMEM_INPUTS,
    )
    early_got = traded(early, "dir", 1, 2)
    small = sum_all(small, dp_count)
    if not half or dp_count != 16:
        late = sum_shards(mine, dp_count)
        early = early.astype(F32) + early_got.astype(F32)
        grad_out = jnp.concatenate([early[:, :model], early[:, model:inner]], axis=0)
        return (
            out[None],
            grad_in[None],
            late[:, :inner],
            early[:, inner:],
            late[:, inner : inner + 4 * state + steps],
            grad_out,
            small[5, :model],
            small[0:4, :channels],
            small[6, 128 : 128 + steps].reshape(dt_bias.shape),
            small[6, 256 : 256 + steps].reshape(a_log.shape),
            small[6, :heads],
            small[4, :inner],
        )

    def plain(kernel, name, args, outs):
        return pl.pallas_call(
            kernel,
            name=name,
            in_specs=[pl.BlockSpec(memory_space=pltpu.VMEM)] * len(args),
            out_specs=[pl.BlockSpec(memory_space=pltpu.VMEM)] * len(outs),
            out_shape=[jax.ShapeDtypeStruct(shape, dtype) for shape, dtype in outs],
            compiler_params=pltpu.CompilerParams(vmem_limit_bytes=VMEM_SUMS * MIB),
        )(*args)

    got = traded(theirs, "dp", 1, dp_count)
    quarter = (model // 4, wide // 2)
    kept, across, along, both = plain(
        functools.partial(quarters_kernel, shard=shard),
        "quarters",
        (mine, got),
        [(quarter, F32), (quarter, BF16), (quarter, BF16), (quarter, BF16)],
    )
    corners = [(a, b) for a in range(2) for b in range(dp_count)]
    across = traded(across, "dir", 1, 2)
    along = traded(along, "dp", 2, dp_count)
    both = lax.ppermute(
        both,
        ("dir", "dp"),
        [(a * dp_count + b, (1 - a) * dp_count + (b ^ 2)) for a, b in corners],
    )
    piece = (shard, wide // 2)
    own, *sends = plain(
        functools.partial(levels_kernel, shard=shard),
        "levels",
        (kept, across, along, both),
        [(piece, F32)] + [(piece, BF16)] * 3,
    )
    gots = [traded(sent, "dp", 4 * bits, dp_count) for bits, sent in zip((1, 2, 3), sends)]
    (late,) = plain(last_kernel, "last", (own, *gots), [(piece, BF16)])
    late_got = traded(late, "dir", 1, 2)
    g_x, g_zz, g_bc, g_o, g_taps, g_mix, g_in, g_skip, g_bias, g_alog = plain(
        finish_kernel,
        "finish",
        (late, late_got, early, early_got, small),
        [
            ((shard, inner), F32),
            ((shard, inner), F32),
            ((shard, w_bcdt.shape[1]), F32),
            ((2 * shard, model), F32),
            (conv_w.shape, F32),
            ((inner,), F32),
            ((model,), F32),
            ((heads,), F32),
            (dt_bias.shape, F32),
            (a_log.shape, F32),
        ],
    )
    return (
        out[None],
        grad_in[None],
        g_x,
        g_zz,
        g_bc,
        g_o,
        g_in,
        g_taps,
        g_bias,
        g_alog,
        g_skip,
        g_mix,
    )


def solution(mesh):
    return jax.shard_map(
        functools.partial(local, mesh.shape["dp"]),
        mesh=mesh,
        in_specs=(
            P("dir", "dp", None),
            P("dp", None),
            P(),
            P(),
            P(),
            P(),
            P(),
            P(),
            P(),
            P(),
            P(),
            P(),
            P("dir", "dp", None),
        ),
        out_specs=(
            P("dir", "dp", None),
            P("dir", "dp", None),
            P("dp", None),
            P("dp", None),
            P("dp", None),
            P("dp", None),
            P(),
            P(),
            P(),
            P(),
            P(),
            P(),
        ),
        check_vma=False,
    )
```

```python
import functools

import jax
import jax.numpy as jnp
import numpy as np
from jax import lax
from jax.experimental import pallas as pl
from jax.experimental.pallas import tpu as pltpu
from jax.sharding import PartitionSpec as P

F32 = jnp.float32
BF16 = jnp.bfloat16
CHUNK = 128
ROWS = 256
SUB = 64
EPS = 1e-05
LOG2E = 1.4426950408889634
SWAP = [(0, 1), (1, 0)]
MIB = 1024 * 1024
VMEM_GATES = 56
VMEM_PROJ = 56
VMEM_INTRA = 12
VMEM_MIX = 56
VMEM_WEIGHTS = 56
VMEM_BACK = 56
VMEM_CONV = 56
VMEM_INPUTS = 56
VMEM_SUMS = 8
US_GATES = 10
US_PROJ = 20
US_INTRA = 12
US_MIX = 35
US_WEIGHTS = 10
US_BACK = 30
US_CONV = 17
US_INPUTS = 12
US_SUMS = 2
NT = (((1,), (1,)), ((), ()))
TN = (((0,), (0,)), ((), ()))
EXACT = lax.Precision.HIGHEST


def mm(left, right):
    return jnp.dot(left, right, preferred_element_type=F32)


def mm_nt(left, right):
    return lax.dot_general(left, right, NT, preferred_element_type=F32)


def mm_tn(left, right):
    return lax.dot_general(left, right, TN, preferred_element_type=F32)


def exact_mm(left, right):
    return jnp.dot(left, right, precision=EXACT, preferred_element_type=F32)


def sequence_bounds(lengths_ref, half_rows):
    bounds, total = [], 0
    for position in range(lengths_ref.shape[1]):
        total = total + lengths_ref[0, position]
        bounds.append(total)
    return bounds, lax.axis_index("dir") * half_rows


def start_of(row, bounds):
    start = jnp.where(row < 0, -1, 0)
    for bound in bounds:
        start = jnp.where(row >= bound, bound, start)
    return start


def same_sequence(first, bounds):
    starts = start_of(first + lane_iota(CHUNK), bounds)
    turned = jnp.broadcast_to(starts.astype(F32), (8, CHUNK)).T[:, 0:1]
    return (turned == starts.astype(F32)) & (row_iota(CHUNK) != lane_iota(CHUNK))


def row_iota(count):
    return lax.broadcasted_iota(jnp.int32, (count, 1), 0)


def lane_iota(count):
    return lax.broadcasted_iota(jnp.int32, (1, count), 1)


def flag(condition):
    return jnp.where(condition, 1.0, 0.0)


def in_parts(values, parts):
    out = []
    for _ in range(parts):
        part = values.astype(BF16).astype(F32)
        out.append(part)
        values = values - part
    return jnp.concatenate(out, axis=0)


def fold(values):
    return jnp.sum(values.reshape(values.shape[0] // 8, 8, values.shape[1]), axis=0)


def row_of(ref):
    return ref[...].reshape(1, ref.shape[0])


def column_of(ref, steps):
    heads = steps // 2
    place = row_iota(steps)
    column = jnp.zeros((steps, 1), F32)
    for step in range(steps):
        column = jnp.where(place == step, ref[step // heads, step % heads], column)
    return column


def gates_kernel(normed_ref, c_ref, wz_ref, wo_ref, z_ref, dnorm_ref, turned_ref):
    turned_ref[...] = normed_ref[...].T
    z_ref[...] = mm(normed_ref[...], wz_ref[...]).astype(BF16)
    dnorm_ref[...] = mm_nt(c_ref[...], wo_ref[...]).astype(BF16)


def step_factors(
    lengths_ref,
    bias_ref,
    alog_ref,
    e0_ref,
    e1_ref,
    raw_ref,
    dt_ref,
    rate_ref,
    target_ref,
    source_ref,
    factors_ref,
    keeps_ref,
):
    steps, count = raw_ref.shape
    heads = steps // 2
    bounds, base = sequence_bounds(lengths_ref, count)
    rate = jnp.exp(column_of(alog_ref, steps))
    rate_ref[...] = jnp.broadcast_to(rate, (steps, 128))
    raw = raw_ref[...] + column_of(bias_ref, steps)
    raw_ref[...] = raw
    dt = jnp.maximum(raw, 0.0) + jnp.log1p(jnp.exp(-jnp.abs(raw)))
    dt_ref[...] = dt
    log_dt = jnp.log(jnp.maximum(dt, 1e-37))
    chunks = count // CHUNK
    upto = flag(row_iota(CHUNK) <= lane_iota(CHUNK))
    fall = dt * rate
    stacked = [fall[:, chunk * CHUNK : (chunk + 1) * CHUNK] for chunk in range(chunks)]
    summed = exact_mm(jnp.concatenate(stacked, axis=0), upto)
    lane = lane_iota(CHUNK)
    keeps = jnp.zeros((steps, CHUNK), F32)
    for chunk in range(chunks):
        span = slice(chunk * CHUNK, (chunk + 1) * CHUNK)
        first = base + chunk * CHUNK
        inc = summed[chunk * steps : (chunk + 1) * steps]
        dt_c, log_c = dt[:, span], log_dt[:, span]
        inc0 = inc[:heads]
        exc1 = inc[heads:] - fall[heads:, span]
        total0 = inc0[:, CHUNK - 1 :]
        total1 = inc[heads:, CHUNK - 1 :]
        target = jnp.concatenate([-inc0, exc1], axis=0) * LOG2E
        source = jnp.concatenate([inc0 + log_c[:heads], log_c[heads:] - exc1], axis=0) * LOG2E
        target_ref[:, span] = target
        source_ref[:, span] = source
        starts = start_of(first + lane, bounds)
        before = start_of(first - 1, bounds)
        left = start_of(first, bounds)
        right = start_of(first + CHUNK - 1, bounds)
        after = start_of(first + CHUNK, bounds)
        enter0 = jnp.where(starts == before, jnp.exp(-inc0), 0.0)
        enter1 = jnp.where(starts == after, jnp.exp(exc1 - total1), 0.0)
        leave0 = jnp.where(starts == right, dt_c[:heads] * jnp.exp(inc0 - total0), 0.0)
        leave1 = jnp.where(starts == left, dt_c[heads:] * jnp.exp(-exc1), 0.0)
        enter = jnp.concatenate([enter0, enter1], axis=0)
        leave = jnp.concatenate([leave0, leave1], axis=0)
        factors_ref[0, span, :] = in_parts(enter, 2).T.astype(BF16)
        factors_ref[1, span, :] = in_parts(leave, 2).T.astype(BF16)
        keep0 = jnp.where(before == right, jnp.exp(-total0), 0.0)
        keep1 = jnp.where(after == left, jnp.exp(-total1), 0.0)
        keeps = jnp.where(lane == chunk, jnp.concatenate([keep0, keep1], axis=0), keeps)
    ahead = jnp.zeros_like(keeps)
    behind = jnp.zeros_like(keeps)
    run_a = jnp.ones((steps, 1), F32)
    run_b = jnp.ones((steps, 1), F32)
    for chunk in range(chunks):
        ahead = jnp.where(lane == chunk, run_a, ahead)
        run_a = run_a * keeps[:, chunk : chunk + 1]
        last = chunks - 1 - chunk
        behind = jnp.where(lane == last, run_b, behind)
        run_b = run_b * keeps[:, last : last + 1]
    for place, values in enumerate((keeps, ahead, behind)):
        columns = in_parts(values, 2).T.astype(BF16)[0:16]
        keeps_ref[2 * place] = mm(columns, e0_ref[...])[0:chunks]
        keeps_ref[2 * place + 1] = mm(columns, e1_ref[...])[0:chunks]


def shifts(first, bounds, sign, height):
    row = lax.broadcasted_iota(jnp.int32, (height, CHUNK + 16), 0)
    col = lane_iota(CHUNK + 16)
    parts = []
    for lag in (1, 2, 3):
        later = first + col + (lag - 16 if sign < 0 else 0)
        near = later - start_of(later, bounds) < lag
        place = jnp.where(near, -CHUNK, col)
        offset = {-1: 16 - lag, 1: lag, 0: lag - height}[sign]
        parts.append(flag(place == row + offset))
    return jnp.concatenate(parts, axis=0).astype(BF16)


def proj_kernel(
    lengths_ref,
    bias_ref,
    alog_ref,
    x_ref,
    halo_ref,
    gain_ref,
    wx_ref,
    wbc_ref,
    taps_ref,
    e0_ref,
    e1_ref,
    normed_ref,
    raw_ref,
    dt_ref,
    rate_ref,
    target_ref,
    source_ref,
    factors_ref,
    keeps_ref,
    pre_ref,
    act_ref,
    slope_ref,
    s0_ref,
    sf1_ref,
    send_ref,
    prehalo_ref,
    turnhalo_ref,
    buf,
    acc0,
    acc1,
    left0,
    left1,
):
    step = pl.program_id(0)
    per = ROWS // CHUNK
    bounds, base = sequence_bounds(lengths_ref, pl.num_programs(0) * ROWS)
    inner = wx_ref.shape[1]
    channels = taps_ref.shape[1]
    state = (channels - inner) // 4

    @pl.when(step == 0)
    def _():
        count = x_ref.shape[0]
        gain = row_of(gain_ref)

        @pl.loop(0, count // CHUNK, unroll=4)
        def _(chunk):
            rows = pl.ds(pl.multiple_of(chunk * CHUNK, CHUNK), CHUNK)
            x = x_ref[rows, :].astype(F32)
            inv = lax.rsqrt(jnp.mean(x * x, axis=1, keepdims=True) + EPS)
            normed = (x * inv * gain).astype(BF16)
            normed_ref[rows, :] = normed
            raw = mm_nt(wbc_ref[channels - inner :, :], normed)
            raw_ref[:, rows] = raw.astype(BF16).astype(F32)

        step_factors(
            lengths_ref,
            bias_ref,
            alog_ref,
            e0_ref,
            e1_ref,
            raw_ref,
            dt_ref,
            rate_ref,
            target_ref,
            source_ref,
            factors_ref,
            keeps_ref,
        )
        x = halo_ref[...].astype(F32)
        inv = lax.rsqrt(jnp.mean(x * x, axis=1, keepdims=True) + EPS)
        normed = x * inv * gain
        turnhalo_ref[...] = normed.T.astype(BF16)
        normed = normed.astype(BF16)
        prehalo_ref[:, 0:inner] = mm(normed, wx_ref[...]).astype(BF16)
        prehalo_ref[:, inner:channels] = mm_nt(normed, wbc_ref[0 : channels - inner, :]).astype(BF16)
        buf[0:16, :] = prehalo_ref[...]
        acc0[...] = jnp.zeros_like(acc0)
        acc1[...] = jnp.zeros_like(acc1)

    @pl.when(step > 0)
    def _():
        buf[0:16, :] = buf[ROWS : ROWS + 16, :]

    normed = normed_ref[pl.ds(pl.multiple_of(step * ROWS, ROWS), ROWS), :]
    for tile in range(inner // 256):
        cols = slice(tile * 256, tile * 256 + 256)
        px = mm(normed, wx_ref[:, cols]).astype(BF16)
        pre_ref[:, cols] = px
        buf[16 : 16 + ROWS, cols] = px
    pb = mm_nt(normed, wbc_ref[0 : channels - inner, :]).astype(BF16)
    pre_ref[:, inner:channels] = pb
    buf[16 : 16 + ROWS, inner:channels] = pb

    first = base + step * ROWS
    for part in range(per):
        offset = part * CHUNK
        shift = shifts(first + offset, bounds, -1, CHUNK)
        here = pl.ds(pl.multiple_of(step * ROWS + offset, CHUNK), CHUNK)
        leave_cols = factors_ref[1, here, :]
        for tile in range(channels // 256):
            wide = slice(tile * 256, tile * 256 + 256)
            moved = mm(shift, buf[offset : offset + CHUNK + 16, wide])
            if tile * 256 < inner:
                leave0 = mm(leave_cols, e0_ref[:, wide])
                leave1 = mm(leave_cols, e1_ref[:, wide])
            for column in (0, 128):
                cols = slice(tile * 256 + column, tile * 256 + column + 128)
                cut = slice(column, column + 128)
                for row in range(0, CHUNK, SUB):
                    here = buf[offset + 16 + row : offset + 16 + row + SUB, cols]
                    conv = here.astype(F32) * taps_ref[3:4, cols]
                    for lag in (1, 2, 3):
                        at = (lag - 1) * CHUNK + row
                        conv = conv + moved[at : at + SUB, cut] * taps_ref[3 - lag : 4 - lag, cols]
                    sig = jax.nn.sigmoid(conv)
                    act = conv * sig
                    span = slice(offset + row, offset + row + SUB)
                    act_ref[span, cols] = act.astype(BF16)
                    slope_ref[span, cols] = (sig + act - act * sig).astype(BF16)
                    if tile * 256 < inner:
                        held = slice(row, row + SUB)
                        left0[held, cols] = (act * leave0[held, cut]).astype(BF16)
                        left1[held, cols] = (act * leave1[held, cut]).astype(BF16)
        turned = act_ref[offset : offset + CHUNK, inner:channels].astype(F32).T.astype(BF16)
        s0_ref[part] = acc0[...].astype(BF16)
        chunk = pl.ds(step * per + part, 1)
        acc0[...] = keeps_ref[0, chunk, :] * acc0[...] + mm(turned[0:state], left0[...])
        fresh1 = mm(turned[2 * state : 3 * state], left1[...])
        sf1_ref[part] = fresh1.astype(BF16)
        acc1[...] = acc1[...] + keeps_ref[3, chunk, :] * fresh1

    @pl.when(step == pl.num_programs(0) - 1)
    def _():
        send_ref[...] = jnp.where(base > 0, acc1[...], acc0[...]).astype(BF16)


def bc_columns(act_ref, inner, state):
    return [act_ref[:, inner + part * state : inner + (part + 1) * state] for part in range(4)]


def cut_pair(values, width):
    zero = jnp.zeros_like(values)
    first = lane_iota(2 * width) < width
    return jnp.concatenate([jnp.where(first, values, zero), jnp.where(first, zero, values)], axis=0)


def mix_kernel(
    lengths_ref,
    skip_ref,
    x_ref,
    act_ref,
    target_ref,
    source_ref,
    factors_ref,
    sl0_ref,
    sf1_ref,
    keeps_ref,
    recv_ref,
    z_ref,
    dnorm_ref,
    wo_ref,
    gain_ref,
    e0_ref,
    e1_ref,
    out_ref,
    mixed_ref,
    dz_ref,
    dy_ref,
    r_ref,
    dcc_ref,
    dl0_ref,
    df1_ref,
    s0_ref,
    s1_ref,
    send_ref,
    sums_ref,
    carry1,
    acc0,
    acc1,
    enter0,
    enter1,
    from0,
    from1,
    within,
    gated_s,
    slope_s,
    gate_s,
    in0,
    in1,
    prod0,
    prod1,
    skip_s,
    gain_s,
):
    step = pl.program_id(0)
    chunk = pl.num_programs(0) - 1 - step
    bounds, base = sequence_bounds(lengths_ref, pl.num_programs(0) * CHUNK)
    first = base + chunk * CHUNK
    inner = gain_ref.shape[0]
    heads = r_ref.shape[0] // 2
    width = inner // heads
    state = recv_ref.shape[0]
    small = 32

    @pl.when(step == 0)
    def _():
        recv = recv_ref[...].astype(F32)
        carry1[...] = jnp.where(base > 0, jnp.zeros_like(recv), recv)
        acc0[...] = jnp.zeros_like(acc0)
        acc1[...] = jnp.zeros_like(acc1)
        sums_ref[...] = jnp.zeros_like(sums_ref)
        gain_s[...] = row_of(gain_ref)
        left = lane_iota(2 * width) < width
        for pair in range(heads // 2):
            skip_s[:, pair * 2 * width : (pair + 1) * 2 * width] = jnp.where(
                left, skip_ref[2 * pair], skip_ref[2 * pair + 1]
            )

    keep0 = keeps_ref[0, pl.ds(chunk, 1), :]
    keep1 = keeps_ref[1, pl.ds(chunk, 1), :]
    ahead0 = keeps_ref[2, pl.ds(chunk, 1), :] * jnp.where(base > 0, 1.0, 0.0)
    s0 = (sl0_ref[0].astype(F32) + ahead0 * recv_ref[...].astype(F32)).astype(BF16)
    s1 = carry1[...].astype(BF16)
    carry1[...] = keep1 * carry1[...] + sf1_ref[0].astype(F32)
    s0_ref[0] = s0
    s1_ref[0] = s1
    enter_cols = factors_ref[0]
    turned = act_ref[:, inner:].astype(F32).T.astype(BF16)
    b0, c0, b1, c1 = bc_columns(act_ref, inner, state)
    enter0[...] = mm(enter_cols, e0_ref[...])
    from0[...] = mm(c0, s0)
    enter1[...] = mm(enter_cols, e1_ref[...])
    from1[...] = mm(c1, s1)
    t, s = row_iota(CHUNK), lane_iota(CHUNK)
    lower = t > s
    scores = jnp.where(lower, mm_nt(c0, b0), mm_nt(c1, b1))
    scores = jnp.where(same_sequence(first, bounds), scores, 0.0)
    columns = target_ref[...].T
    for pair in range(heads // 2):
        cols = slice(pair * 2 * width, (pair + 1) * 2 * width)
        weights = []
        for head in (2 * pair, 2 * pair + 1):
            power = jnp.where(
                lower,
                columns[:, head : head + 1] + source_ref[head : head + 1, :],
                columns[:, heads + head : heads + head + 1]
                + source_ref[heads + head : heads + head + 1, :],
            )
            weights.append((jnp.exp2(power) * scores).astype(BF16))
        x_cut = cut_pair(act_ref[:, cols], width)
        within[:, cols] = mm(jnp.concatenate(weights, axis=1), x_cut)
    tiles = [slice(tile * 128, tile * 128 + 128) for tile in range(inner // 128)]
    for row in range(0, CHUNK, small):
        rows = slice(row, row + small)
        square = jnp.zeros((small, 128), F32)
        cross = jnp.zeros((small, 128), F32)
        for cols in tiles:
            mixer = within[rows, cols] + skip_s[:, cols] * act_ref[rows, cols].astype(F32)
            mixer = mixer + enter0[rows, cols] * from0[rows, cols]
            mixer = mixer + enter1[rows, cols] * from1[rows, cols]
            z = z_ref[rows, cols].astype(F32)
            sig = jax.nn.sigmoid(z)
            gate = z * sig
            gated = mixer * gate
            square = square + gated * gated
            cross = cross + dnorm_ref[rows, cols].astype(F32) * gain_s[:, cols] * gated
            gated_s[rows, cols] = gated
            gate_s[rows, cols] = gate
            slope_s[rows, cols] = mixer * (sig + gate - gate * sig)
        live = flag(first + row + row_iota(small) < bounds[len(bounds) - 2])
        scale = lax.rsqrt(jnp.sum(square, axis=1, keepdims=True) * (1.0 / inner) + EPS)
        back = scale * scale * (jnp.sum(cross, axis=1, keepdims=True) * (1.0 / inner))
        scale = jnp.broadcast_to(scale * live, (small, 128))
        back = jnp.broadcast_to(back, (small, 128))
        for cols in tiles:
            gated = gated_s[rows, cols]
            unit = gated * scale
            gain = gain_s[:, cols]
            mixed_ref[rows, cols] = (unit * gain).astype(BF16)
            dnorm = dnorm_ref[rows, cols].astype(F32)
            sums_ref[0:8, cols] += fold(dnorm * unit)
            dgated = scale * (dnorm * gain - gated * back)
            dz_ref[rows, cols] = (dgated * slope_s[rows, cols]).astype(BF16)
            dy = dgated * gate_s[rows, cols]
            dy_ref[rows, cols] = dy.astype(BF16)
            sums_ref[8:16, cols] += fold(dy * act_ref[rows, cols].astype(F32))
            entered0 = dy * enter0[rows, cols]
            entered1 = dy * enter1[rows, cols]
            in0[rows, cols] = entered0.astype(BF16)
            in1[rows, cols] = entered1.astype(BF16)
            prod0[rows, cols] = (entered0 * from0[rows, cols]).astype(BF16)
            prod1[rows, cols] = (entered1 * from1[rows, cols]).astype(BF16)
    out_ref[...] = (x_ref[...].astype(F32) + mm(mixed_ref[...], wo_ref[...])).astype(BF16)
    ones = e0_ref[0:heads, :]
    r_ref[0:heads, :] = mm_nt(ones, prod0[...])
    r_ref[heads : 2 * heads, :] = mm_nt(ones, prod1[...])
    dcc_ref[:, 0:state] = mm_nt(in0[...], s0)
    dcc_ref[:, state : 2 * state] = mm_nt(in1[...], s1)
    dl0_ref[0] = acc0[...].astype(BF16)
    acc0[...] = keep0 * acc0[...] + mm(turned[state : 2 * state], in0[...])
    df1 = mm(turned[3 * state : 4 * state], in1[...])
    df1_ref[0] = df1.astype(BF16)
    acc1[...] = acc1[...] + keeps_ref[5, pl.ds(chunk, 1), :] * df1

    @pl.when(step == pl.num_programs(0) - 1)
    def _():
        send_ref[...] = jnp.where(base > 0, acc0[...], acc1[...]).astype(BF16)


def back_kernel(
    lengths_ref,
    skip_ref,
    act_ref,
    slope_ref,
    target_ref,
    source_ref,
    factors_ref,
    dcc_ref,
    dy_ref,
    s0_ref,
    s1_ref,
    dl0_ref,
    df1_ref,
    keeps_ref,
    recv_ref,
    start_ref,
    e0_ref,
    e1_ref,
    spans_ref,
    dpre_ref,
    moves_ref,
    last_ref,
    carry1,
    dscore,
    low_s,
    all_s,
    out0,
    out1,
    prod0,
    prod1,
    ds0,
    ds1,
    *,
    skipped,
    chunks,
):
    step = pl.program_id(0)
    chunk = step + skipped
    bounds, base = sequence_bounds(lengths_ref, chunks * CHUNK)
    first = base + chunk * CHUNK
    heads = skip_ref.shape[0]
    inner = keeps_ref.shape[2]
    width = inner // heads
    state = recv_ref.shape[0]

    @pl.when(step == 0)
    def _():
        if skipped:
            carry1[...] = start_ref[...]
        else:
            recv = recv_ref[...].astype(F32)
            carry1[...] = jnp.where(base > 0, recv, jnp.zeros_like(recv))

    keep0 = keeps_ref[0, pl.ds(chunk, 1), :]
    keep1 = keeps_ref[1, pl.ds(chunk, 1), :]
    behind0 = keeps_ref[4, pl.ds(chunk, 1), :] * jnp.where(base > 0, 0.0, 1.0)
    d0 = dl0_ref[0].astype(F32) + behind0 * recv_ref[...].astype(F32)
    d1 = carry1[...]
    ds0[...] = d0.astype(BF16)
    ds1[...] = d1.astype(BF16)
    kept0 = jnp.sum(d0 * s0_ref[0].astype(F32), axis=0, keepdims=True) * keep0
    kept1 = jnp.sum(d1 * s1_ref[0].astype(F32), axis=0, keepdims=True) * keep1
    carry1[...] = keep1 * d1 + df1_ref[0].astype(F32)
    ones = e0_ref[0:heads, :]
    kept = jnp.concatenate([kept0, kept1, jnp.zeros((6, inner), F32)], axis=0)
    kept_high = kept.astype(BF16)
    kept_low = (kept - kept_high.astype(F32)).astype(BF16)
    kept_sum = mm_nt(ones, kept_high) + mm_nt(ones, kept_low)

    t = lane_iota(CHUNK)
    b0, c0, b1, c1 = bc_columns(act_ref, inner, state)
    same = same_sequence(first, bounds)
    both = jnp.where(row_iota(CHUNK) < t, mm_nt(b0, c0), mm_nt(b1, c1))
    both = jnp.where(same, both, 0.0)
    halves = []
    for row in range(0, CHUNK, SUB):
        early = row + row_iota(SUB) < t
        halves.append((slice(row, row + SUB), early, flag(early), both[row : row + SUB]))
    in_cols = source_ref[...].T
    leave_cols = factors_ref[0]
    dscore[...] = jnp.zeros_like(dscore)
    left = lane_iota(2 * width) < width
    for pair in range(heads // 2):
        cols = slice(pair * 2 * width, (pair + 1) * 2 * width)
        dweights = mm_nt(cut_pair(act_ref[:, cols], width), dy_ref[:, cols])
        weights = []
        for part in (0, 1):
            head = 2 * pair + part
            held = slice(head * CHUNK, (head + 1) * CHUNK)
            parts = []
            sum0 = jnp.zeros((8, CHUNK), F32)
            sum1 = jnp.zeros((8, CHUNK), F32)
            for rows, early, early_f, scores in halves:
                power = jnp.where(
                    early,
                    in_cols[rows, head : head + 1] + target_ref[head : head + 1, :],
                    in_cols[rows, heads + head : heads + head + 1]
                    + target_ref[heads + head : heads + head + 1, :],
                )
                decay = jnp.exp2(power)
                parts.append((decay * scores).astype(BF16))
                at = part * CHUNK + rows.start
                dweight = dweights[at : at + SUB] * decay
                dscore[rows, :] += dweight
                change = dweight * scores
                low = change * early_f
                low_s[rows, held] = low.astype(BF16)
                all_s[rows, held] = change.astype(BF16)
                sum0 = sum0 + fold(low)
                sum1 = sum1 + fold(change)
            weights.append(jnp.concatenate(parts, axis=0))
            moves_ref[head : head + 1, :] = jnp.sum(sum0, axis=0, keepdims=True)
            moves_ref[heads + head : heads + head + 1, :] = jnp.sum(sum1, axis=0, keepdims=True)
        dx = mm(jnp.concatenate(weights, axis=1), cut_pair(dy_ref[:, cols], width))
        leave0 = mm(leave_cols, e0_ref[:, cols])
        leave1 = mm(leave_cols, e1_ref[:, cols])
        from0 = mm(b0, ds0[:, cols])
        from1 = mm(b1, ds1[:, cols])
        skip = jnp.where(left, skip_ref[2 * pair], skip_ref[2 * pair + 1])
        for rows, _, _, _ in halves:
            xf = act_ref[rows, cols].astype(F32)
            came0 = leave0[rows] * from0[rows]
            came1 = leave1[rows] * from1[rows]
            dconv = dx[rows] + skip * dy_ref[rows, cols].astype(F32) + came0 + came1
            dpre_ref[rows, cols] = (dconv * slope_ref[rows, cols].astype(F32)).astype(BF16)
            out0[rows, cols] = (xf * leave0[rows]).astype(BF16)
            out1[rows, cols] = (xf * leave1[rows]).astype(BF16)
            prod0[rows, cols] = (xf * came0).astype(BF16)
            prod1[rows, cols] = (xf * came1).astype(BF16)
    dscores = jnp.where(same, dscore[...], 0.0)
    dscore0 = jnp.where(row_iota(CHUNK) < t, dscores, 0.0).astype(BF16)
    dscore1 = jnp.where(row_iota(CHUNK) < t, 0.0, dscores).astype(BF16)
    moves_ref[2 * heads : 3 * heads, :] = mm_nt(spans_ref[...], low_s[...])
    moves_ref[3 * heads : 4 * heads, :] = mm_nt(spans_ref[...], all_s[...])
    moves_ref[4 * heads : 5 * heads, :] = mm_nt(ones, prod0[...])
    moves_ref[5 * heads : 6 * heads, :] = mm_nt(ones, prod1[...])
    moves_ref[6 * heads : 7 * heads, :] = jnp.broadcast_to(kept_sum[:, 0:1], (heads, CHUNK))
    moves_ref[7 * heads : 8 * heads, :] = jnp.broadcast_to(kept_sum[:, 1:2], (heads, CHUNK))
    db0 = mm(dscore0, c0) + mm_nt(out0[...], ds0[...])
    db1 = mm(dscore1, c1) + mm_nt(out1[...], ds1[...])
    dc0 = mm_tn(dscore0, b0) + dcc_ref[:, 0:state]
    dc1 = mm_tn(dscore1, b1) + dcc_ref[:, state : 2 * state]
    dbc = jnp.concatenate([db0, dc0, db1, dc1], axis=1)
    dpre_ref[:, inner:] = (dbc * slope_ref[:, inner:].astype(F32)).astype(BF16)

    @pl.when(step == pl.num_programs(0) - 1)
    def _():
        last_ref[...] = carry1[...]


def steps_back(raw, dt, rate, moves, r):
    steps = raw.shape[0]
    heads = steps // 2
    chunks = raw.shape[1] // CHUNK
    s, t = row_iota(CHUNK), lane_iota(CHUNK)

    def stack(values):
        parts = [values[:, chunk * CHUNK : (chunk + 1) * CHUNK] for chunk in range(chunks)]
        return jnp.concatenate(parts, axis=0)

    def unstack(values):
        parts = [values[chunk * heads : (chunk + 1) * heads] for chunk in range(chunks)]
        return jnp.concatenate(parts, axis=1)

    got0, got, own0, own, k0, k1, kept0, kept1 = [
        moves[part * heads : (part + 1) * heads] for part in range(8)
    ]
    own1, got1 = own - own0, got - got0
    da0 = exact_mm(stack(got0 + r[:heads] - own0), flag(s >= t)) + exact_mm(stack(k0), flag(s < t))
    da1 = exact_mm(stack(got1 + r[heads:] - own1), flag(s <= t)) + exact_mm(stack(k1), flag(s > t))
    da = -jnp.concatenate([unstack(da0) + kept0, unstack(da1) + kept1], axis=0)
    dlog = jnp.concatenate([own0 + k0, own1 + k1], axis=0)
    sig = jax.nn.sigmoid(raw)
    ratio = jnp.where(raw < -20.0, 1.0, sig / jnp.maximum(dt, 1e-37))
    return dlog * ratio + da * rate * sig, jnp.sum(da * dt, axis=1, keepdims=True) * rate


def weights_kernel(turned_ref, dz_ref, mixed_ref, c_ref, both_ref, *, half):
    model = c_ref.shape[1]
    product = mm_tn(mixed_ref[...], c_ref[...]).astype(BF16)
    for shard in range(product.shape[0] // (2 * half)):
        span = slice(shard * half, (shard + 1) * half)
        both_ref[span, 0:model] = product[2 * shard * half : (2 * shard + 1) * half]
        both_ref[span, model : 2 * model] = product[(2 * shard + 1) * half : (2 * shard + 2) * half]
    both_ref[:, 2 * model :] = mm(turned_ref[...], dz_ref[...]).astype(BF16)


def conv_back_kernel(
    lengths_ref,
    turned_ref,
    turnhalo_ref,
    dpre_ref,
    pre_ref,
    prehalo_ref,
    taps_ref,
    raw_ref,
    dt_ref,
    rate_ref,
    moves_ref,
    r_ref,
    dproj_ref,
    dhalo_ref,
    mine_ref,
    theirs_ref,
    draw_ref,
    sums_ref,
    shift,
    buf,
    *,
    shard,
):
    step = pl.program_id(0)
    count, wide = dpre_ref.shape
    chunks = count // CHUNK
    steps = raw_ref.shape[0]
    bounds, base = sequence_bounds(lengths_ref, count)

    @pl.when(step == 0)
    def _():
        for chunk in range(chunks):
            shift[chunk * 3 * CHUNK : (chunk + 1) * 3 * CHUNK, :] = shifts(
                base + chunk * CHUNK, bounds, 1, CHUNK
            )
        shift[chunks * 3 * CHUNK :, :] = shifts(base, bounds, 0, 16)
        buf[...] = jnp.zeros_like(buf)

    def hand_over(product):
        if not shard:
            mine_ref[...] = product
            return
        pieces = [product[place : place + shard] for place in range(0, product.shape[0], shard)]
        even = jnp.concatenate(pieces[0::2], axis=0)
        odd = jnp.concatenate(pieces[1::2], axis=0)
        core = lax.rem(lax.axis_index("dp"), 2)

        @pl.when(core == 0)
        def _():
            mine_ref[...] = even
            theirs_ref[...] = odd

        @pl.when(core == 1)
        def _():
            mine_ref[...] = odd
            theirs_ref[...] = even

    @pl.when(step < pl.num_programs(0) - 1)
    def _():
        buf[0:CHUNK, :] = dpre_ref[count - CHUNK :, :]
        moved = mm(shift[chunks * 3 * CHUNK :, :], dpre_ref[0 : CHUNK + 16, :])
        halo_sums = [None] * 4
        dproj = jnp.zeros((16, wide), F32)
        pre = prehalo_ref[...].astype(F32)
        for lag in (1, 2, 3):
            part = moved[(lag - 1) * 16 : lag * 16]
            dproj = dproj + part * taps_ref[3 - lag : 4 - lag, :]
            halo_sums[3 - lag] = jnp.sum(pre * part, axis=0, keepdims=True)
        halo_sums[3] = jnp.zeros((1, wide), F32)
        dhalo_ref[...] = dproj.astype(BF16)
        sums = [[jnp.zeros((8, 128), F32) for _ in range(4)] for _ in range(wide // 128)]
        for chunk in range(chunks):
            if chunk < chunks - 1:
                pair = dpre_ref[chunk * CHUNK : chunk * CHUNK + CHUNK + 16, :]
            else:
                pair = buf[...]
            moved = mm(shift[chunk * 3 * CHUNK : (chunk + 1) * 3 * CHUNK, :], pair)
            for place in range(wide // 128):
                cols = slice(place * 128, place * 128 + 128)
                for row in range(0, CHUNK, SUB):
                    span = slice(chunk * CHUNK + row, chunk * CHUNK + row + SUB)
                    pre = pre_ref[span, cols].astype(F32)
                    here = dpre_ref[span, cols].astype(F32)
                    dproj = here * taps_ref[3:4, cols]
                    sums[place][3] = sums[place][3] + fold(pre * here)
                    for lag in (1, 2, 3):
                        at = (lag - 1) * CHUNK + row
                        part = moved[at : at + SUB, cols]
                        dproj = dproj + part * taps_ref[3 - lag : 4 - lag, cols]
                        sums[place][3 - lag] = sums[place][3 - lag] + fold(pre * part)
                    dproj_ref[span, cols] = dproj.astype(BF16)
        sums_ref[...] = jnp.zeros_like(sums_ref)
        for place in range(wide // 128):
            cols = slice(place * 128, place * 128 + 128)
            for tap in range(4):
                sums_ref[tap : tap + 1, cols] = (
                    jnp.sum(sums[place][tap], axis=0, keepdims=True) + halo_sums[tap][:, cols]
                )
        product = mm(turned_ref[...], dproj_ref[...]) + mm(turnhalo_ref[...], dhalo_ref[...])
        hand_over(product.astype(BF16))

    @pl.when(step == pl.num_programs(0) - 1)
    def _():
        rate = rate_ref[:, 0:1]
        draw, drate = steps_back(raw_ref[...], dt_ref[...], rate, moves_ref[...], r_ref[...])
        low = draw.astype(BF16)
        draw_ref[...] = low
        product = mm_nt(turned_ref[...], low).astype(BF16)
        hand_over(
            jnp.concatenate([product, jnp.zeros((product.shape[0], wide - steps), BF16)], axis=1)
        )
        columns = [jnp.sum(draw, axis=1, keepdims=True), drate, jnp.zeros((steps, 6), F32)]
        sums_ref[...] = jnp.zeros_like(sums_ref)
        sums_ref[:, 0:steps] = jnp.concatenate(columns, axis=1).T


def quarters_kernel(mine_ref, got_ref, keep_ref, across_ref, along_ref, both_ref, *, shard):
    half = mine_ref.shape[1] // 2
    row_bit = lax.rem(lax.axis_index("dp") // 2, 2)
    side = lax.axis_index("dir")
    for place in range(keep_ref.shape[0] // shard):
        rows = slice(place * shard, (place + 1) * shard)
        for out_ref, row, column in (
            (keep_ref, row_bit, side),
            (across_ref, row_bit, 1 - side),
            (along_ref, 1 - row_bit, side),
            (both_ref, 1 - row_bit, 1 - side),
        ):
            here = pl.ds(pl.multiple_of((2 * place + row) * shard, shard), shard)
            cols = pl.ds(pl.multiple_of(column * half, half), half)
            total = mine_ref[here, cols].astype(F32) + got_ref[here, cols].astype(F32)
            out_ref[rows, :] = total.astype(out_ref.dtype)


def two_halves(small):
    half = small.shape[1] // 2
    return jnp.concatenate([small[:, 0:half], small[:, half:]], axis=0)


def levels_kernel(
    keep_ref, a_ref, b_ref, c_ref, small_ref, own_ref, s1_ref, s2_ref, s3_ref, *, shard
):
    level = lax.axis_index("dp") // 4
    parts = in_parts(two_halves(small_ref[...]), 2)
    few = parts.shape[0] // 2
    own_ref[shard : shard + few, :] = parts[0:few] + parts[few:]
    for bits, out_ref in enumerate((own_ref, s1_ref, s2_ref, s3_ref)):
        wanted = jnp.bitwise_xor(level, bits)
        rows = pl.ds(pl.multiple_of(wanted * shard, shard), shard)
        total = keep_ref[rows, :] + a_ref[rows, :].astype(F32)
        total = total + (b_ref[rows, :].astype(F32) + c_ref[rows, :].astype(F32))
        out_ref[0:shard, :] = total.astype(out_ref.dtype)
        if bits:
            out_ref[shard : shard + 2 * few, :] = parts.astype(BF16)


def joined(ref, shard):
    few = (ref.shape[0] - shard) // 2
    small = ref[shard : shard + few, :].astype(F32) + ref[shard + few :, :].astype(F32)
    return ref[0:shard, :].astype(F32), small


def last_kernel(own_ref, a_ref, b_ref, c_ref, out_ref, *, shard):
    a, b, c = (joined(ref, shard) for ref in (a_ref, b_ref, c_ref))
    out_ref[0:shard, :] = (own_ref[0:shard, :] + a[0] + (b[0] + c[0])).astype(BF16)
    small = in_parts(own_ref[shard:, :] + a[1] + (b[1] + c[1]), 2)
    out_ref[shard:, :] = small.astype(BF16)


def finish_kernel(
    late_ref,
    lategot_ref,
    early_ref,
    earlygot_ref,
    gx_ref,
    gz_ref,
    gbc_ref,
    go_ref,
    gtaps_ref,
    gmix_ref,
    gin_ref,
    gskip_ref,
    gbias_ref,
    galog_ref,
):
    side = lax.axis_index("dir")
    half = late_ref.shape[1]
    inner = gx_ref.shape[1]
    model = go_ref.shape[1]
    shard = gx_ref.shape[0]
    mine, small = joined(late_ref, shard)
    other, small_other = joined(lategot_ref, shard)
    first = jnp.where(side == 0, mine, other)
    second = jnp.where(side == 0, other, mine)
    gx_ref[:, 0:half] = first
    gx_ref[:, half:inner] = second[:, 0 : inner - half]
    gbc_ref[...] = second[:, inner - half : inner - half + gbc_ref.shape[1]]
    early = early_ref[...].astype(F32) + earlygot_ref[...].astype(F32)
    go_ref[0:shard, :] = early[:, 0:model]
    go_ref[shard : 2 * shard, :] = early[:, model : 2 * model]
    gz_ref[...] = early[:, 2 * model :]
    small = small + small_other
    small = jnp.concatenate([small[0:8], small[8:16]], axis=1)
    gtaps_ref[...] = small[0:4, 0 : gtaps_ref.shape[1]]
    gmix_ref[...] = small[4:5, 0:inner].reshape(inner)
    gin_ref[...] = small[5:6, 0:model].reshape(model)
    heads = gskip_ref.shape[0]
    gskip_ref[...] = small[6:7, 0:128].reshape(128)[0:heads]
    gbias_ref[0:1, :] = small[6:7, 128 : 128 + heads]
    gbias_ref[1:2, :] = small[6:7, 128 + heads : 128 + 2 * heads]
    galog_ref[0:1, :] = small[6:7, 256 : 256 + heads]
    galog_ref[1:2, :] = small[6:7, 256 + heads : 256 + 2 * heads]


def inputs_kernel(
    x_ref,
    c_ref,
    gain_ref,
    dproj_ref,
    dhalo_ref,
    draw_ref,
    dz_ref,
    wx_ref,
    wbc_ref,
    wz_ref,
    mix_sums_ref,
    tap_sums_ref,
    e0_ref,
    gin_ref,
    small_ref,
    total,
    dproj,
):
    step = pl.program_id(0)
    model, inner = wx_ref.shape
    steps = draw_ref.shape[0]
    heads = steps // 2
    narrow = wbc_ref.shape[0] - steps
    channels = inner + narrow

    @pl.when(step == 0)
    def _():
        total[...] = jnp.zeros_like(total)

    @pl.when(step == pl.num_programs(0) - 1)
    def _():
        tail = slice(dproj_ref.shape[0] - 16, dproj_ref.shape[0])
        both = dproj_ref[tail, :].astype(F32) + dhalo_ref[...].astype(F32)
        dproj[...] = dproj_ref[...]
        dproj[tail, :] = both.astype(BF16)

    @pl.when(step < pl.num_programs(0) - 1)
    def _():
        dproj[...] = dproj_ref[...]

    dn = mm_nt(dproj[:, 0:inner], wx_ref[...])
    dn = dn + mm_nt(dz_ref[...], wz_ref[...])
    dn = dn + mm(dproj[:, inner:], wbc_ref[0:narrow, :])
    dn = dn + mm_tn(draw_ref[...], wbc_ref[narrow:, :])
    x = x_ref[...].astype(F32)
    inv = lax.rsqrt(jnp.mean(x * x, axis=1, keepdims=True) + EPS)
    unit = x * inv
    total[...] += fold(dn * unit)
    f = dn * row_of(gain_ref)
    back = inv * (f - unit * jnp.mean(f * unit, axis=1, keepdims=True))
    gin_ref[...] = (c_ref[...].astype(F32) + back).astype(BF16)

    @pl.when(step == pl.num_programs(0) - 1)
    def _():
        small_ref[...] = jnp.zeros_like(small_ref)
        small_ref[0:4, 0:channels] = tap_sums_ref[0:4, 0:channels]
        small_ref[4:5, 0:inner] = jnp.sum(mix_sums_ref[0:8, :], axis=0, keepdims=True)
        small_ref[5:6, 0:model] = jnp.sum(total[...], axis=0, keepdims=True)
        skips = in_parts(mix_sums_ref[8:16, :], 2).astype(BF16)
        skips = jnp.sum(mm_nt(e0_ref[0:heads, :], skips), axis=1, keepdims=True)
        skips = jnp.broadcast_to(skips, (heads, 128)).T
        small_ref[6:7, 0:heads] = skips[0:1]
        small_ref[6:7, 128:256] = tap_sums_ref[0:1, channels : channels + 128]
        small_ref[6:7, 256:384] = tap_sums_ref[1:2, channels : channels + 128]


def smem():
    return pl.BlockSpec(memory_space=pltpu.SMEM)


def resident():
    return pl.BlockSpec(memory_space=pltpu.VMEM)


def whole(shape):
    return pl.BlockSpec(shape, lambda i: (0,) * len(shape), pipeline_mode=pl.Buffered(1))


def rows_of(count, width):
    return pl.BlockSpec((count, width), lambda i: (i, 0))


def lanes_of(height, count):
    return pl.BlockSpec((height, count), lambda i: (0, i))


def parts_of(count, *rest):
    return pl.BlockSpec((count,) + rest, lambda i: (i,) + (0,) * len(rest))


def cost(microseconds):
    flops = int(microseconds * 1.15e9)
    return pl.CostEstimate(flops=flops, bytes_accessed=0, transcendentals=0)


def call(kernel, name, grid, in_specs, outs, scratch, cost_us, args, vmem):
    return pl.pallas_call(
        kernel,
        name=name,
        grid=(grid,),
        in_specs=in_specs,
        out_specs=[spec for spec, _, _ in outs],
        out_shape=[jax.ShapeDtypeStruct(shape, dtype) for _, shape, dtype in outs],
        scratch_shapes=scratch,
        compiler_params=pltpu.CompilerParams(
            vmem_limit_bytes=vmem * MIB, dimension_semantics=("arbitrary",)
        ),
        cost_estimate=cost(cost_us),
    )(*args)


def traded(values, axis, bit, size):
    return lax.ppermute(values, axis, [(i, i ^ bit) for i in range(size)])


def ordered(first, second):
    return lax.optimization_barrier((first, second))


def sum_shards(grad, dp_count):
    index = lax.axis_index("dp")
    held = grad.reshape(dp_count, grad.shape[0] // dp_count, grad.shape[1])
    bit = 1
    while bit < dp_count:
        paired = held.reshape(held.shape[0] // 2, 2, held.shape[1], held.shape[2])
        mine = (index // bit) % 2
        kept = lax.dynamic_index_in_dim(paired, mine, 1, keepdims=False)
        sent = lax.dynamic_index_in_dim(paired, 1 - mine, 1, keepdims=False).astype(BF16)
        held = kept.astype(F32) + traded(sent, "dp", bit, dp_count).astype(F32)
        bit *= 2
    held = held[0].astype(BF16)
    return held.astype(F32) + traded(held, "dir", 1, 2).astype(F32)


def sum_all(values, dp_count):
    bit = 1
    while bit < dp_count:
        values = values + traded(values, "dp", bit, dp_count)
        bit *= 2
    return values + traded(values, "dir", 1, 2)


def local(
    dp_count,
    hidden_in,
    lengths,
    gain_in,
    w_x,
    w_z,
    w_bcdt,
    conv_w,
    dt_bias,
    a_log,
    d_skip,
    gain_mix,
    w_out,
    cotangent,
):
    x = hidden_in[0]
    cot = cotangent[0]
    count, model = x.shape
    inner = w_x.shape[1]
    channels = conv_w.shape[1]
    heads = d_skip.shape[0]
    width = inner // heads
    state = (channels - inner) // 4
    chunks = count // CHUNK
    steps = 2 * heads

    w_narrow = w_bcdt.T
    halo = lax.ppermute(x[count - 16 :], "dir", [(0, 1)])

    spread = np.repeat(np.eye(heads, dtype=np.float32), width, axis=1)
    zeros = np.zeros_like(spread)
    e0 = jnp.asarray(np.concatenate([spread, zeros, spread, zeros]), BF16)
    e1 = jnp.asarray(np.concatenate([zeros, spread, zeros, spread]), BF16)
    spans = jnp.asarray(np.repeat(np.eye(heads, dtype=np.float32), CHUNK, axis=1), BF16)
    def rows_out(size, columns, dtype):
        return (rows_of(size, columns), (count, columns), dtype)

    def full(shape, dtype):
        return (pl.BlockSpec(shape, lambda i: (0,) * len(shape)), shape, dtype)

    per = ROWS // CHUNK
    state_f32 = pltpu.VMEM((state, inner), F32)
    state_bf16 = pltpu.VMEM((state, inner), BF16)
    row_f32 = pltpu.VMEM((1, inner), F32)
    chunk_f32 = pltpu.VMEM((CHUNK, inner), F32)
    chunk_bf16 = pltpu.VMEM((CHUNK, inner), BF16)
    (
        normed,
        raw,
        dt,
        rate,
        target,
        source,
        factors,
        keeps,
        pre,
        act,
        slope,
        sl0,
        sf1,
        send,
        pre_halo,
        turn_halo,
    ) = call(
        proj_kernel,
        "proj",
        count // ROWS,
        [
            smem(),
            smem(),
            smem(),
            whole((count, model)),
            whole((16, model)),
            whole((model,)),
            whole((model, inner)),
            whole(w_narrow.shape),
            whole(conv_w.shape),
            whole(e0.shape),
            whole(e1.shape),
        ],
        [
            full((count, model), BF16),
            full((steps, count), F32),
            full((steps, count), F32),
            full((steps, 128), F32),
            full((steps, count), F32),
            full((steps, count), F32),
            full((2, count, 2 * steps), BF16),
            full((6, chunks, inner), F32),
            rows_out(ROWS, channels, BF16),
            rows_out(ROWS, channels, BF16),
            rows_out(ROWS, channels, BF16),
            (parts_of(per, state, inner), (chunks, state, inner), BF16),
            (parts_of(per, state, inner), (chunks, state, inner), BF16),
            full((state, inner), BF16),
            full((16, channels), BF16),
            full((model, 16), BF16),
        ],
        [
            pltpu.VMEM((16 + ROWS, channels), BF16),
            state_f32,
            state_f32,
            chunk_bf16,
            chunk_bf16,
        ],
        US_PROJ,
        (lengths, dt_bias, a_log, x, halo, gain_in, w_x, w_narrow, conv_w, e0, e1),
        VMEM_PROJ,
    )
    received = lax.ppermute(send, "dir", SWAP)

    gate_z, d_norm, turned = call(
        gates_kernel,
        "gates",
        count // ROWS,
        [
            rows_of(ROWS, model),
            rows_of(ROWS, model),
            whole((model, inner)),
            whole((inner, model)),
        ],
        [
            rows_out(ROWS, inner, BF16),
            rows_out(ROWS, inner, BF16),
            (lanes_of(model, ROWS), (model, count), BF16),
        ],
        [],
        US_GATES,
        (normed, cot, w_z, w_out),
        VMEM_GATES,
    )

    def down_rows(width):
        return pl.BlockSpec((CHUNK, width), lambda i: (chunks - 1 - i, 0))

    def down_lanes(height):
        return pl.BlockSpec((height, CHUNK), lambda i: (0, chunks - 1 - i))

    def down_parts(*rest):
        return pl.BlockSpec((1,) + rest, lambda i: (chunks - 1 - i,) + (0,) * len(rest))

    states = (down_parts(state, inner), (chunks, state, inner), BF16)
    out, mixed, dz, dy, r, dcc, dl0, df1, s0, s1, d_send, mix_sums = call(
        mix_kernel,
        "mix",
        chunks,
        [
            smem(),
            smem(),
            down_rows(model),
            down_rows(channels),
            down_lanes(steps),
            down_lanes(steps),
            pl.BlockSpec((1, CHUNK, 2 * steps), lambda i: (0, chunks - 1 - i, 0)),
            down_parts(state, inner),
            down_parts(state, inner),
            whole((6, chunks, inner)),
            whole((state, inner)),
            down_rows(inner),
            down_rows(inner),
            whole((inner, model)),
            whole((inner,)),
            whole(e0.shape),
            whole(e1.shape),
        ],
        [
            (down_rows(model), (count, model), BF16),
            (down_rows(inner), (count, inner), BF16),
            (down_rows(inner), (count, inner), BF16),
            (down_rows(inner), (count, inner), BF16),
            (down_lanes(steps), (steps, count), F32),
            (down_rows(2 * state), (count, 2 * state), F32),
            states,
            states,
            states,
            states,
            full((state, inner), BF16),
            full((16, inner), F32),
        ],
        [state_f32] * 3 + [chunk_f32] * 8 + [chunk_bf16] * 4 + [row_f32] * 2,
        US_MIX,
        (
            lengths,
            d_skip,
            x,
            act,
            target,
            source,
            factors,
            sl0,
            sf1,
            keeps,
            received,
            gate_z,
            d_norm,
            w_out,
            gain_mix,
            e0,
            e1,
        ),
        VMEM_MIX,
    )
    d_received = lax.ppermute(d_send, "dir", SWAP)

    blocks = 4
    shard = model // dp_count
    half = shard if shard % 16 == 0 else 0
    (g_early,) = call(
        functools.partial(weights_kernel, half=half or model // 16),
        "weights",
        blocks,
        [
            rows_of(model // blocks, count),
            whole((count, inner)),
            lanes_of(count, inner // blocks),
            whole((count, model)),
        ],
        [(rows_of(model // blocks, 2 * inner), (model, 2 * inner), BF16)],
        [],
        US_WEIGHTS,
        (turned, dz, mixed, cot),
        VMEM_WEIGHTS,
    )
    if not half:
        g_out = g_early[:, :inner].reshape(16, model // 16, 2, model).transpose(0, 2, 1, 3)
        g_out = g_out.reshape(dp_count, 2, shard, model).transpose(0, 2, 1, 3)
        g_early = jnp.concatenate([g_out.reshape(model, inner), g_early[:, inner:]], axis=1)
    g_early, d_received = ordered(g_early, d_received)
    early = lax.psum_scatter(g_early, "dp", scatter_dimension=0, tiled=True)

    def back(skipped, taken, start):
        def rows_from(width):
            return pl.BlockSpec((CHUNK, width), lambda i: (i + skipped, 0))

        def lanes_from(height):
            return pl.BlockSpec((height, CHUNK), lambda i: (0, i + skipped))

        def parts_from(*rest):
            return pl.BlockSpec((1,) + rest, lambda i: (i + skipped,) + (0,) * len(rest))

        return call(
            functools.partial(back_kernel, skipped=skipped, chunks=chunks),
            "back" + str(skipped),
            taken,
            [
                smem(),
                smem(),
                rows_from(channels),
                rows_from(channels),
                lanes_from(steps),
                lanes_from(steps),
                pl.BlockSpec((1, CHUNK, 2 * steps), lambda i: (1, i + skipped, 0)),
                rows_from(2 * state),
                rows_from(inner),
                parts_from(state, inner),
                parts_from(state, inner),
                parts_from(state, inner),
                parts_from(state, inner),
                whole((6, chunks, inner)),
                whole((state, inner)),
                whole(start.shape),
                whole(e0.shape),
                whole(e1.shape),
                whole(spans.shape),
            ],
            [
                (rows_of(CHUNK, channels), (taken * CHUNK, channels), BF16),
                (lanes_of(8 * heads, CHUNK), (8 * heads, taken * CHUNK), F32),
                full((state, inner), F32),
            ],
            [
                state_f32,
                pltpu.VMEM((CHUNK, CHUNK), F32),
                pltpu.VMEM((CHUNK, heads * CHUNK), BF16),
                pltpu.VMEM((CHUNK, heads * CHUNK), BF16),
            ]
            + [chunk_bf16] * 4
            + [state_bf16] * 2,
            US_BACK,
            (
                lengths,
                d_skip,
                act,
                slope,
                target,
                source,
                factors,
                dcc,
                dy,
                s0,
                s1,
                dl0,
                df1,
                keeps,
                d_received,
                start,
                e0,
                e1,
                spans,
            ),
            VMEM_BACK,
        )

    dpre, moves, _ = back(0, chunks, d_received)

    tile = 256
    tiles = channels // tile
    def tile_of(height):
        return pl.BlockSpec((height, tile), lambda i: (0, jnp.minimum(i, tiles - 1)))

    wide = (tiles + 1) * tile
    kept_rows = model // 2 if half else model
    dproj, dhalo, mine, theirs, draw, tap_sums = call(
        functools.partial(conv_back_kernel, shard=half),
        "conv_back",
        tiles + 1,
        [
            smem(),
            whole((model, count)),
            whole((model, 16)),
            tile_of(count),
            tile_of(count),
            tile_of(16),
            tile_of(conv_w.shape[0]),
            whole((steps, count)),
            whole((steps, count)),
            whole((steps, 128)),
            whole((8 * heads, count)),
            whole((steps, count)),
        ],
        [
            (tile_of(count), (count, channels), BF16),
            (tile_of(16), (16, channels), BF16),
            (lanes_of(kept_rows, tile), (kept_rows, wide), BF16),
            (lanes_of(kept_rows, tile), (kept_rows, wide), BF16),
            full((steps, count), BF16),
            (lanes_of(8, tile), (8, wide), F32),
        ],
        [
            pltpu.VMEM((3 * count + 48, CHUNK + 16), BF16),
            pltpu.VMEM((CHUNK + 16, tile), BF16),
        ],
        US_CONV,
        (lengths, turned, turn_halo, dpre, pre, pre_halo, conv_w, raw, dt, rate, moves, r),
        VMEM_CONV,
    )
    d_halo = lax.ppermute(dhalo, "dir", [(1, 0)])

    grad_in, small = call(
        inputs_kernel,
        "inputs",
        count // ROWS,
        [
            rows_of(ROWS, model),
            rows_of(ROWS, model),
            whole((model,)),
            rows_of(ROWS, channels),
            whole((16, channels)),
            lanes_of(steps, ROWS),
            rows_of(ROWS, inner),
            whole((model, inner)),
            whole(w_narrow.shape),
            whole((model, inner)),
            whole(mix_sums.shape),
            whole(tap_sums.shape),
            whole(e0.shape),
        ],
        [
            rows_out(ROWS, model, BF16),
            full((8, tap_sums.shape[1]), F32),
        ],
        [pltpu.VMEM((8, model), F32), pltpu.VMEM((ROWS, channels), BF16)],
        US_INPUTS,
        (x, cot, gain_in, dproj, d_halo, draw, dz, w_x, w_narrow, w_z, mix_sums, tap_sums, e0),
        VMEM_INPUTS,
    )
    if not half or dp_count != 16:
        small = sum_all(small, dp_count)
        late = sum_shards(mine, dp_count)
        early_got = traded(early, "dir", 1, 2)
        early = early.astype(F32) + early_got.astype(F32)
        grad_out = jnp.concatenate([early[:, :model], early[:, model:inner]], axis=0)
        return (
            out[None],
            grad_in[None],
            late[:, :inner],
            early[:, inner:],
            late[:, inner : inner + 4 * state + steps],
            grad_out,
            small[5, :model],
            small[0:4, :channels],
            small[6, 128 : 128 + steps].reshape(dt_bias.shape),
            small[6, 256 : 256 + steps].reshape(a_log.shape),
            small[6, :heads],
            small[4, :inner],
        )

    def plain(kernel, name, args, outs):
        return pl.pallas_call(
            kernel,
            name=name,
            in_specs=[pl.BlockSpec(memory_space=pltpu.VMEM)] * len(args),
            out_specs=[pl.BlockSpec(memory_space=pltpu.VMEM)] * len(outs),
            out_shape=[jax.ShapeDtypeStruct(shape, dtype) for shape, dtype in outs],
            compiler_params=pltpu.CompilerParams(vmem_limit_bytes=VMEM_SUMS * MIB),
            cost_estimate=cost(US_SUMS),
        )(*args)

    got = traded(theirs, "dp", 1, dp_count)
    quarter = (model // 4, wide // 2)
    kept, across, along, both = plain(
        functools.partial(quarters_kernel, shard=shard),
        "quarters",
        (mine, got),
        [(quarter, F32), (quarter, BF16), (quarter, BF16), (quarter, BF16)],
    )
    corners = [(a, b) for a in range(2) for b in range(dp_count)]
    across = traded(across, "dir", 1, 2)
    along = traded(along, "dp", 2, dp_count)
    both = lax.ppermute(
        both,
        ("dir", "dp"),
        [(a * dp_count + b, (1 - a) * dp_count + (b ^ 2)) for a, b in corners],
    )
    _, both = ordered(small, both)
    for bit in (1, 2):
        small = small + traded(small, "dp", bit, dp_count)
    piece = (shard + 4 * small.shape[0], wide // 2)
    own, *sends = plain(
        functools.partial(levels_kernel, shard=shard),
        "levels",
        (kept, across, along, both, small),
        [((shard + 2 * small.shape[0], wide // 2), F32)] + [(piece, BF16)] * 3,
    )
    gots = [traded(sent, "dp", 4 * bits, dp_count) for bits, sent in zip((1, 2, 3), sends)]
    (late,) = plain(
        functools.partial(last_kernel, shard=shard), "last", (own, *gots), [(piece, BF16)]
    )
    early, _ = ordered(early, late)
    early_got = traded(early, "dir", 1, 2)
    late_got = traded(late, "dir", 1, 2)
    g_x, g_zz, g_bc, g_o, g_taps, g_mix, g_in, g_skip, g_bias, g_alog = plain(
        finish_kernel,
        "finish",
        (late, late_got, early, early_got),
        [
            ((shard, inner), F32),
            ((shard, inner), F32),
            ((shard, w_bcdt.shape[1]), F32),
            ((2 * shard, model), F32),
            (conv_w.shape, F32),
            ((inner,), F32),
            ((model,), F32),
            ((heads,), F32),
            (dt_bias.shape, F32),
            (a_log.shape, F32),
        ],
    )
    return (
        out[None],
        grad_in[None],
        g_x,
        g_zz,
        g_bc,
        g_o,
        g_in,
        g_taps,
        g_bias,
        g_alog,
        g_skip,
        g_mix,
    )


def solution(mesh):
    return jax.shard_map(
        functools.partial(local, mesh.shape["dp"]),
        mesh=mesh,
        in_specs=(
            P("dir", "dp", None),
            P("dp", None),
            P(),
            P(),
            P(),
            P(),
            P(),
            P(),
            P(),
            P(),
            P(),
            P(),
            P("dir", "dp", None),
        ),
        out_specs=(
            P("dir", "dp", None),
            P("dir", "dp", None),
            P("dp", None),
            P("dp", None),
            P("dp", None),
            P("dp", None),
            P(),
            P(),
            P(),
            P(),
            P(),
            P(),
        ),
        check_vma=False,
    )
```

```python
import functools

import jax
import jax.numpy as jnp
import numpy as np
from jax import lax
from jax.experimental import pallas as pl
from jax.experimental.pallas import tpu as pltpu
from jax.sharding import PartitionSpec as P

F32 = jnp.float32
BF16 = jnp.bfloat16
CHUNK = 128
ROWS = 256
SUB = 64
EPS = 1e-05
LOG2E = 1.4426950408889634
SWAP = [(0, 1), (1, 0)]
MIB = 1024 * 1024
VMEM_GATES = 56
VMEM_PROJ = 56
VMEM_INTRA = 12
VMEM_MIX = 56
VMEM_WEIGHTS = 56
VMEM_BACK = 56
VMEM_CONV = 56
VMEM_INPUTS = 56
VMEM_SUMS = 8
US_GATES = 10
US_PROJ = 20
US_INTRA = 12
US_MIX = 35
US_WEIGHTS = 10
US_BACK = 30
US_CONV = 17
US_INPUTS = 12
US_SUMS = 2
NT = (((1,), (1,)), ((), ()))
TN = (((0,), (0,)), ((), ()))
EXACT = lax.Precision.HIGHEST


def mm(left, right):
    return jnp.dot(left, right, preferred_element_type=F32)


def mm_nt(left, right):
    return lax.dot_general(left, right, NT, preferred_element_type=F32)


def mm_tn(left, right):
    return lax.dot_general(left, right, TN, preferred_element_type=F32)


def exact_mm(left, right):
    return jnp.dot(left, right, precision=EXACT, preferred_element_type=F32)


def sequence_bounds(lengths_ref, half_rows):
    bounds, total = [], 0
    for position in range(lengths_ref.shape[1]):
        total = total + lengths_ref[0, position]
        bounds.append(total)
    return bounds, lax.axis_index("dir") * half_rows


def start_of(row, bounds):
    start = jnp.where(row < 0, -1, 0)
    for bound in bounds:
        start = jnp.where(row >= bound, bound, start)
    return start


def same_sequence(first, bounds):
    starts = start_of(first + lane_iota(CHUNK), bounds)
    turned = jnp.broadcast_to(starts.astype(F32), (8, CHUNK)).T[:, 0:1]
    return (turned == starts.astype(F32)) & (row_iota(CHUNK) != lane_iota(CHUNK))


def row_iota(count):
    return lax.broadcasted_iota(jnp.int32, (count, 1), 0)


def lane_iota(count):
    return lax.broadcasted_iota(jnp.int32, (1, count), 1)


def flag(condition):
    return jnp.where(condition, 1.0, 0.0)


def in_parts(values, parts):
    out = []
    for _ in range(parts):
        part = values.astype(BF16).astype(F32)
        out.append(part)
        values = values - part
    return jnp.concatenate(out, axis=0)


def fold(values):
    return jnp.sum(values.reshape(values.shape[0] // 8, 8, values.shape[1]), axis=0)


def row_of(ref):
    return ref[...].reshape(1, ref.shape[0])


def column_of(ref, steps):
    heads = steps // 2
    place = row_iota(steps)
    column = jnp.zeros((steps, 1), F32)
    for step in range(steps):
        column = jnp.where(place == step, ref[step // heads, step % heads], column)
    return column


def gates_kernel(normed_ref, c_ref, wz_ref, wo_ref, z_ref, dnorm_ref, turned_ref):
    turned_ref[...] = normed_ref[...].T
    z_ref[...] = mm(normed_ref[...], wz_ref[...]).astype(BF16)
    dnorm_ref[...] = mm_nt(c_ref[...], wo_ref[...]).astype(BF16)


def step_factors(
    lengths_ref,
    bias_ref,
    alog_ref,
    e0_ref,
    e1_ref,
    raw_ref,
    dt_ref,
    rate_ref,
    target_ref,
    source_ref,
    factors_ref,
    keeps_ref,
):
    steps, count = raw_ref.shape
    heads = steps // 2
    bounds, base = sequence_bounds(lengths_ref, count)
    rate = jnp.exp(column_of(alog_ref, steps))
    rate_ref[...] = jnp.broadcast_to(rate, (steps, 128))
    raw = raw_ref[...] + column_of(bias_ref, steps)
    raw_ref[...] = raw
    dt = jnp.maximum(raw, 0.0) + jnp.log1p(jnp.exp(-jnp.abs(raw)))
    dt_ref[...] = dt
    log_dt = jnp.log(jnp.maximum(dt, 1e-37))
    chunks = count // CHUNK
    upto = flag(row_iota(CHUNK) <= lane_iota(CHUNK))
    fall = dt * rate
    stacked = [fall[:, chunk * CHUNK : (chunk + 1) * CHUNK] for chunk in range(chunks)]
    summed = exact_mm(jnp.concatenate(stacked, axis=0), upto)
    lane = lane_iota(CHUNK)
    keeps = jnp.zeros((steps, CHUNK), F32)
    for chunk in range(chunks):
        span = slice(chunk * CHUNK, (chunk + 1) * CHUNK)
        first = base + chunk * CHUNK
        inc = summed[chunk * steps : (chunk + 1) * steps]
        dt_c, log_c = dt[:, span], log_dt[:, span]
        inc0 = inc[:heads]
        exc1 = inc[heads:] - fall[heads:, span]
        total0 = inc0[:, CHUNK - 1 :]
        total1 = inc[heads:, CHUNK - 1 :]
        target = jnp.concatenate([-inc0, exc1], axis=0) * LOG2E
        source = jnp.concatenate([inc0 + log_c[:heads], log_c[heads:] - exc1], axis=0) * LOG2E
        target_ref[:, span] = target
        source_ref[:, span] = source
        starts = start_of(first + lane, bounds)
        before = start_of(first - 1, bounds)
        left = start_of(first, bounds)
        right = start_of(first + CHUNK - 1, bounds)
        after = start_of(first + CHUNK, bounds)
        enter0 = jnp.where(starts == before, jnp.exp(-inc0), 0.0)
        enter1 = jnp.where(starts == after, jnp.exp(exc1 - total1), 0.0)
        leave0 = jnp.where(starts == right, dt_c[:heads] * jnp.exp(inc0 - total0), 0.0)
        leave1 = jnp.where(starts == left, dt_c[heads:] * jnp.exp(-exc1), 0.0)
        enter = jnp.concatenate([enter0, enter1], axis=0)
        leave = jnp.concatenate([leave0, leave1], axis=0)
        factors_ref[0, span, :] = in_parts(enter, 2).T.astype(BF16)
        factors_ref[1, span, :] = in_parts(leave, 2).T.astype(BF16)
        keep0 = jnp.where(before == right, jnp.exp(-total0), 0.0)
        keep1 = jnp.where(after == left, jnp.exp(-total1), 0.0)
        keeps = jnp.where(lane == chunk, jnp.concatenate([keep0, keep1], axis=0), keeps)
    ahead = jnp.zeros_like(keeps)
    behind = jnp.zeros_like(keeps)
    run_a = jnp.ones((steps, 1), F32)
    run_b = jnp.ones((steps, 1), F32)
    for chunk in range(chunks):
        ahead = jnp.where(lane == chunk, run_a, ahead)
        run_a = run_a * keeps[:, chunk : chunk + 1]
        last = chunks - 1 - chunk
        behind = jnp.where(lane == last, run_b, behind)
        run_b = run_b * keeps[:, last : last + 1]
    for place, values in enumerate((keeps, ahead, behind)):
        columns = in_parts(values, 2).T.astype(BF16)[0:16]
        keeps_ref[2 * place] = mm(columns, e0_ref[...])[0:chunks]
        keeps_ref[2 * place + 1] = mm(columns, e1_ref[...])[0:chunks]


def shifts(first, bounds, sign, height):
    row = lax.broadcasted_iota(jnp.int32, (height, CHUNK + 16), 0)
    col = lane_iota(CHUNK + 16)
    parts = []
    for lag in (1, 2, 3):
        later = first + col + (lag - 16 if sign < 0 else 0)
        near = later - start_of(later, bounds) < lag
        place = jnp.where(near, -CHUNK, col)
        offset = {-1: 16 - lag, 1: lag, 0: lag - height}[sign]
        parts.append(flag(place == row + offset))
    return jnp.concatenate(parts, axis=0).astype(BF16)


def proj_kernel(
    lengths_ref,
    bias_ref,
    alog_ref,
    x_ref,
    halo_ref,
    gain_ref,
    wx_ref,
    wbc_ref,
    taps_ref,
    e0_ref,
    e1_ref,
    normed_ref,
    raw_ref,
    dt_ref,
    rate_ref,
    target_ref,
    source_ref,
    factors_ref,
    keeps_ref,
    pre_ref,
    act_ref,
    slope_ref,
    s0_ref,
    sf1_ref,
    send_ref,
    prehalo_ref,
    turnhalo_ref,
    buf,
    acc0,
    acc1,
    left0,
    left1,
):
    step = pl.program_id(0)
    per = ROWS // CHUNK
    bounds, base = sequence_bounds(lengths_ref, pl.num_programs(0) * ROWS)
    inner = wx_ref.shape[1]
    channels = taps_ref.shape[1]
    state = (channels - inner) // 4

    @pl.when(step == 0)
    def _():
        count = x_ref.shape[0]
        gain = row_of(gain_ref)

        @pl.loop(0, count // CHUNK, unroll=4)
        def _(chunk):
            rows = pl.ds(pl.multiple_of(chunk * CHUNK, CHUNK), CHUNK)
            x = x_ref[rows, :].astype(F32)
            inv = lax.rsqrt(jnp.mean(x * x, axis=1, keepdims=True) + EPS)
            normed = (x * inv * gain).astype(BF16)
            normed_ref[rows, :] = normed
            raw = mm_nt(wbc_ref[channels - inner :, :], normed)
            raw_ref[:, rows] = raw.astype(BF16).astype(F32)

        step_factors(
            lengths_ref,
            bias_ref,
            alog_ref,
            e0_ref,
            e1_ref,
            raw_ref,
            dt_ref,
            rate_ref,
            target_ref,
            source_ref,
            factors_ref,
            keeps_ref,
        )
        x = halo_ref[...].astype(F32)
        inv = lax.rsqrt(jnp.mean(x * x, axis=1, keepdims=True) + EPS)
        normed = x * inv * gain
        turnhalo_ref[...] = normed.T.astype(BF16)
        normed = normed.astype(BF16)
        prehalo_ref[:, 0:inner] = mm(normed, wx_ref[...]).astype(BF16)
        prehalo_ref[:, inner:channels] = mm_nt(normed, wbc_ref[0 : channels - inner, :]).astype(BF16)
        buf[0:16, :] = prehalo_ref[...]
        acc0[...] = jnp.zeros_like(acc0)
        acc1[...] = jnp.zeros_like(acc1)

    @pl.when(step > 0)
    def _():
        buf[0:16, :] = buf[ROWS : ROWS + 16, :]

    normed = normed_ref[pl.ds(pl.multiple_of(step * ROWS, ROWS), ROWS), :]
    for tile in range(inner // 256):
        cols = slice(tile * 256, tile * 256 + 256)
        px = mm(normed, wx_ref[:, cols]).astype(BF16)
        pre_ref[:, cols] = px
        buf[16 : 16 + ROWS, cols] = px
    pb = mm_nt(normed, wbc_ref[0 : channels - inner, :]).astype(BF16)
    pre_ref[:, inner:channels] = pb
    buf[16 : 16 + ROWS, inner:channels] = pb

    first = base + step * ROWS
    for part in range(per):
        offset = part * CHUNK
        shift = shifts(first + offset, bounds, -1, CHUNK)
        here = pl.ds(pl.multiple_of(step * ROWS + offset, CHUNK), CHUNK)
        leave_cols = factors_ref[1, here, :]
        for tile in range(channels // 256):
            wide = slice(tile * 256, tile * 256 + 256)
            moved = mm(shift, buf[offset : offset + CHUNK + 16, wide])
            if tile * 256 < inner:
                leave0 = mm(leave_cols, e0_ref[:, wide])
                leave1 = mm(leave_cols, e1_ref[:, wide])
            for column in (0, 128):
                cols = slice(tile * 256 + column, tile * 256 + column + 128)
                cut = slice(column, column + 128)
                for row in range(0, CHUNK, SUB):
                    here = buf[offset + 16 + row : offset + 16 + row + SUB, cols]
                    conv = here.astype(F32) * taps_ref[3:4, cols]
                    for lag in (1, 2, 3):
                        at = (lag - 1) * CHUNK + row
                        conv = conv + moved[at : at + SUB, cut] * taps_ref[3 - lag : 4 - lag, cols]
                    sig = jax.nn.sigmoid(conv)
                    act = conv * sig
                    span = slice(offset + row, offset + row + SUB)
                    act_ref[span, cols] = act.astype(BF16)
                    slope_ref[span, cols] = (sig + act - act * sig).astype(BF16)
                    if tile * 256 < inner:
                        held = slice(row, row + SUB)
                        left0[held, cols] = (act * leave0[held, cut]).astype(BF16)
                        left1[held, cols] = (act * leave1[held, cut]).astype(BF16)
        turned = act_ref[offset : offset + CHUNK, inner:channels].astype(F32).T.astype(BF16)
        s0_ref[part] = acc0[...].astype(BF16)
        chunk = pl.ds(step * per + part, 1)
        acc0[...] = keeps_ref[0, chunk, :] * acc0[...] + mm(turned[0:state], left0[...])
        fresh1 = mm(turned[2 * state : 3 * state], left1[...])
        sf1_ref[part] = fresh1.astype(BF16)
        acc1[...] = acc1[...] + keeps_ref[3, chunk, :] * fresh1

    @pl.when(step == pl.num_programs(0) - 1)
    def _():
        send_ref[...] = jnp.where(base > 0, acc1[...], acc0[...]).astype(BF16)


def bc_columns(act_ref, inner, state):
    return [act_ref[:, inner + part * state : inner + (part + 1) * state] for part in range(4)]


def cut_pair(values, width):
    zero = jnp.zeros_like(values)
    first = lane_iota(2 * width) < width
    return jnp.concatenate([jnp.where(first, values, zero), jnp.where(first, zero, values)], axis=0)


def mix_kernel(
    lengths_ref,
    skip_ref,
    x_ref,
    act_ref,
    target_ref,
    source_ref,
    factors_ref,
    sl0_ref,
    sf1_ref,
    keeps_ref,
    recv_ref,
    z_ref,
    dnorm_ref,
    wo_ref,
    gain_ref,
    e0_ref,
    e1_ref,
    out_ref,
    mixed_ref,
    dz_ref,
    dy_ref,
    r_ref,
    dcc_ref,
    dl0_ref,
    df1_ref,
    s0_ref,
    s1_ref,
    send_ref,
    sums_ref,
    carry1,
    acc0,
    acc1,
    enter0,
    enter1,
    from0,
    from1,
    within,
    gated_s,
    slope_s,
    gate_s,
    in0,
    in1,
    prod0,
    prod1,
    skip_s,
    gain_s,
):
    step = pl.program_id(0)
    chunk = pl.num_programs(0) - 1 - step
    bounds, base = sequence_bounds(lengths_ref, pl.num_programs(0) * CHUNK)
    first = base + chunk * CHUNK
    inner = gain_ref.shape[0]
    heads = r_ref.shape[0] // 2
    width = inner // heads
    state = recv_ref.shape[0]
    small = 32

    @pl.when(step == 0)
    def _():
        recv = recv_ref[...].astype(F32)
        carry1[...] = jnp.where(base > 0, jnp.zeros_like(recv), recv)
        acc0[...] = jnp.zeros_like(acc0)
        acc1[...] = jnp.zeros_like(acc1)
        sums_ref[...] = jnp.zeros_like(sums_ref)
        gain_s[...] = row_of(gain_ref)
        left = lane_iota(2 * width) < width
        for pair in range(heads // 2):
            skip_s[:, pair * 2 * width : (pair + 1) * 2 * width] = jnp.where(
                left, skip_ref[2 * pair], skip_ref[2 * pair + 1]
            )

    keep0 = keeps_ref[0, pl.ds(chunk, 1), :]
    keep1 = keeps_ref[1, pl.ds(chunk, 1), :]
    ahead0 = keeps_ref[2, pl.ds(chunk, 1), :] * jnp.where(base > 0, 1.0, 0.0)
    s0 = (sl0_ref[0].astype(F32) + ahead0 * recv_ref[...].astype(F32)).astype(BF16)
    s1 = carry1[...].astype(BF16)
    carry1[...] = keep1 * carry1[...] + sf1_ref[0].astype(F32)
    s0_ref[0] = s0
    s1_ref[0] = s1
    enter_cols = factors_ref[0]
    turned = act_ref[:, inner:].astype(F32).T.astype(BF16)
    b0, c0, b1, c1 = bc_columns(act_ref, inner, state)
    enter0[...] = mm(enter_cols, e0_ref[...])
    from0[...] = mm(c0, s0)
    enter1[...] = mm(enter_cols, e1_ref[...])
    from1[...] = mm(c1, s1)
    t, s = row_iota(CHUNK), lane_iota(CHUNK)
    lower = t > s
    scores = jnp.where(lower, mm_nt(c0, b0), mm_nt(c1, b1))
    scores = jnp.where(same_sequence(first, bounds), scores, 0.0)
    columns = target_ref[...].T
    for pair in range(heads // 2):
        cols = slice(pair * 2 * width, (pair + 1) * 2 * width)
        weights = []
        for head in (2 * pair, 2 * pair + 1):
            power = jnp.where(
                lower,
                columns[:, head : head + 1] + source_ref[head : head + 1, :],
                columns[:, heads + head : heads + head + 1]
                + source_ref[heads + head : heads + head + 1, :],
            )
            weights.append((jnp.exp2(power) * scores).astype(BF16))
        x_cut = cut_pair(act_ref[:, cols], width)
        within[:, cols] = mm(jnp.concatenate(weights, axis=1), x_cut)
    tiles = [slice(tile * 128, tile * 128 + 128) for tile in range(inner // 128)]
    for row in range(0, CHUNK, small):
        rows = slice(row, row + small)
        square = jnp.zeros((small, 128), F32)
        cross = jnp.zeros((small, 128), F32)
        for cols in tiles:
            mixer = within[rows, cols] + skip_s[:, cols] * act_ref[rows, cols].astype(F32)
            mixer = mixer + enter0[rows, cols] * from0[rows, cols]
            mixer = mixer + enter1[rows, cols] * from1[rows, cols]
            z = z_ref[rows, cols].astype(F32)
            sig = jax.nn.sigmoid(z)
            gate = z * sig
            gated = mixer * gate
            square = square + gated * gated
            cross = cross + dnorm_ref[rows, cols].astype(F32) * gain_s[:, cols] * gated
            gated_s[rows, cols] = gated
            gate_s[rows, cols] = gate
            slope_s[rows, cols] = mixer * (sig + gate - gate * sig)
        live = flag(first + row + row_iota(small) < bounds[len(bounds) - 2])
        scale = lax.rsqrt(jnp.sum(square, axis=1, keepdims=True) * (1.0 / inner) + EPS)
        back = scale * scale * (jnp.sum(cross, axis=1, keepdims=True) * (1.0 / inner))
        scale = jnp.broadcast_to(scale * live, (small, 128))
        back = jnp.broadcast_to(back, (small, 128))
        for cols in tiles:
            gated = gated_s[rows, cols]
            unit = gated * scale
            gain = gain_s[:, cols]
            mixed_ref[rows, cols] = (unit * gain).astype(BF16)
            dnorm = dnorm_ref[rows, cols].astype(F32)
            sums_ref[0:8, cols] += fold(dnorm * unit)
            dgated = scale * (dnorm * gain - gated * back)
            dz_ref[rows, cols] = (dgated * slope_s[rows, cols]).astype(BF16)
            dy = dgated * gate_s[rows, cols]
            dy_ref[rows, cols] = dy.astype(BF16)
            sums_ref[8:16, cols] += fold(dy * act_ref[rows, cols].astype(F32))
            entered0 = dy * enter0[rows, cols]
            entered1 = dy * enter1[rows, cols]
            in0[rows, cols] = entered0.astype(BF16)
            in1[rows, cols] = entered1.astype(BF16)
            prod0[rows, cols] = (entered0 * from0[rows, cols]).astype(BF16)
            prod1[rows, cols] = (entered1 * from1[rows, cols]).astype(BF16)
    out_ref[...] = (x_ref[...].astype(F32) + mm(mixed_ref[...], wo_ref[...])).astype(BF16)
    ones = e0_ref[0:heads, :]
    r_ref[0:heads, :] = mm_nt(ones, prod0[...])
    r_ref[heads : 2 * heads, :] = mm_nt(ones, prod1[...])
    dcc_ref[:, 0:state] = mm_nt(in0[...], s0)
    dcc_ref[:, state : 2 * state] = mm_nt(in1[...], s1)
    dl0_ref[0] = acc0[...].astype(BF16)
    acc0[...] = keep0 * acc0[...] + mm(turned[state : 2 * state], in0[...])
    df1 = mm(turned[3 * state : 4 * state], in1[...])
    df1_ref[0] = df1.astype(BF16)
    acc1[...] = acc1[...] + keeps_ref[5, pl.ds(chunk, 1), :] * df1

    @pl.when(step == pl.num_programs(0) - 1)
    def _():
        send_ref[...] = jnp.where(base > 0, acc0[...], acc1[...]).astype(BF16)


def back_kernel(
    lengths_ref,
    skip_ref,
    act_ref,
    slope_ref,
    target_ref,
    source_ref,
    factors_ref,
    dcc_ref,
    dy_ref,
    s0_ref,
    s1_ref,
    dl0_ref,
    df1_ref,
    keeps_ref,
    recv_ref,
    start_ref,
    e0_ref,
    e1_ref,
    spans_ref,
    _dpre_ref,
    _moves_ref,
    dpre_ref,
    moves_ref,
    last_ref,
    carry1,
    dscore,
    low_s,
    all_s,
    out0,
    out1,
    prod0,
    prod1,
    ds0,
    ds1,
    *,
    skipped,
    chunks,
):
    step = pl.program_id(0)
    chunk = step + skipped
    bounds, base = sequence_bounds(lengths_ref, chunks * CHUNK)
    first = base + chunk * CHUNK
    heads = skip_ref.shape[0]
    inner = keeps_ref.shape[2]
    width = inner // heads
    state = recv_ref.shape[0]

    @pl.when(step == 0)
    def _():
        if skipped:
            carry1[...] = start_ref[...]
        else:
            recv = recv_ref[...].astype(F32)
            carry1[...] = jnp.where(base > 0, recv, jnp.zeros_like(recv))

    keep0 = keeps_ref[0, pl.ds(chunk, 1), :]
    keep1 = keeps_ref[1, pl.ds(chunk, 1), :]
    behind0 = keeps_ref[4, pl.ds(chunk, 1), :] * jnp.where(base > 0, 0.0, 1.0)
    d0 = dl0_ref[0].astype(F32) + behind0 * recv_ref[...].astype(F32)
    d1 = carry1[...]
    ds0[...] = d0.astype(BF16)
    ds1[...] = d1.astype(BF16)
    kept0 = jnp.sum(d0 * s0_ref[0].astype(F32), axis=0, keepdims=True) * keep0
    kept1 = jnp.sum(d1 * s1_ref[0].astype(F32), axis=0, keepdims=True) * keep1
    carry1[...] = keep1 * d1 + df1_ref[0].astype(F32)
    ones = e0_ref[0:heads, :]
    kept = jnp.concatenate([kept0, kept1, jnp.zeros((6, inner), F32)], axis=0)
    kept_high = kept.astype(BF16)
    kept_low = (kept - kept_high.astype(F32)).astype(BF16)
    kept_sum = mm_nt(ones, kept_high) + mm_nt(ones, kept_low)

    t = lane_iota(CHUNK)
    b0, c0, b1, c1 = bc_columns(act_ref, inner, state)
    same = same_sequence(first, bounds)
    both = jnp.where(row_iota(CHUNK) < t, mm_nt(b0, c0), mm_nt(b1, c1))
    both = jnp.where(same, both, 0.0)
    halves = []
    for row in range(0, CHUNK, SUB):
        early = row + row_iota(SUB) < t
        halves.append((slice(row, row + SUB), early, flag(early), both[row : row + SUB]))
    in_cols = source_ref[...].T
    leave_cols = factors_ref[0]
    dscore[...] = jnp.zeros_like(dscore)
    left = lane_iota(2 * width) < width
    for pair in range(heads // 2):
        cols = slice(pair * 2 * width, (pair + 1) * 2 * width)
        dweights = mm_nt(cut_pair(act_ref[:, cols], width), dy_ref[:, cols])
        weights = []
        for part in (0, 1):
            head = 2 * pair + part
            held = slice(head * CHUNK, (head + 1) * CHUNK)
            parts = []
            sum0 = jnp.zeros((8, CHUNK), F32)
            sum1 = jnp.zeros((8, CHUNK), F32)
            for rows, early, early_f, scores in halves:
                power = jnp.where(
                    early,
                    in_cols[rows, head : head + 1] + target_ref[head : head + 1, :],
                    in_cols[rows, heads + head : heads + head + 1]
                    + target_ref[heads + head : heads + head + 1, :],
                )
                decay = jnp.exp2(power)
                parts.append((decay * scores).astype(BF16))
                at = part * CHUNK + rows.start
                dweight = dweights[at : at + SUB] * decay
                dscore[rows, :] += dweight
                change = dweight * scores
                low = change * early_f
                low_s[rows, held] = low.astype(BF16)
                all_s[rows, held] = change.astype(BF16)
                sum0 = sum0 + fold(low)
                sum1 = sum1 + fold(change)
            weights.append(jnp.concatenate(parts, axis=0))
            moves_ref[head : head + 1, :] = jnp.sum(sum0, axis=0, keepdims=True)
            moves_ref[heads + head : heads + head + 1, :] = jnp.sum(sum1, axis=0, keepdims=True)
        dx = mm(jnp.concatenate(weights, axis=1), cut_pair(dy_ref[:, cols], width))
        leave0 = mm(leave_cols, e0_ref[:, cols])
        leave1 = mm(leave_cols, e1_ref[:, cols])
        from0 = mm(b0, ds0[:, cols])
        from1 = mm(b1, ds1[:, cols])
        skip = jnp.where(left, skip_ref[2 * pair], skip_ref[2 * pair + 1])
        for rows, _, _, _ in halves:
            xf = act_ref[rows, cols].astype(F32)
            came0 = leave0[rows] * from0[rows]
            came1 = leave1[rows] * from1[rows]
            dconv = dx[rows] + skip * dy_ref[rows, cols].astype(F32) + came0 + came1
            dpre_ref[rows, cols] = (dconv * slope_ref[rows, cols].astype(F32)).astype(BF16)
            out0[rows, cols] = (xf * leave0[rows]).astype(BF16)
            out1[rows, cols] = (xf * leave1[rows]).astype(BF16)
            prod0[rows, cols] = (xf * came0).astype(BF16)
            prod1[rows, cols] = (xf * came1).astype(BF16)
    dscores = jnp.where(same, dscore[...], 0.0)
    dscore0 = jnp.where(row_iota(CHUNK) < t, dscores, 0.0).astype(BF16)
    dscore1 = jnp.where(row_iota(CHUNK) < t, 0.0, dscores).astype(BF16)
    moves_ref[2 * heads : 3 * heads, :] = mm_nt(spans_ref[...], low_s[...])
    moves_ref[3 * heads : 4 * heads, :] = mm_nt(spans_ref[...], all_s[...])
    moves_ref[4 * heads : 5 * heads, :] = mm_nt(ones, prod0[...])
    moves_ref[5 * heads : 6 * heads, :] = mm_nt(ones, prod1[...])
    moves_ref[6 * heads : 7 * heads, :] = jnp.broadcast_to(kept_sum[:, 0:1], (heads, CHUNK))
    moves_ref[7 * heads : 8 * heads, :] = jnp.broadcast_to(kept_sum[:, 1:2], (heads, CHUNK))
    db0 = mm(dscore0, c0) + mm_nt(out0[...], ds0[...])
    db1 = mm(dscore1, c1) + mm_nt(out1[...], ds1[...])
    dc0 = mm_tn(dscore0, b0) + dcc_ref[:, 0:state]
    dc1 = mm_tn(dscore1, b1) + dcc_ref[:, state : 2 * state]
    dbc = jnp.concatenate([db0, dc0, db1, dc1], axis=1)
    dpre_ref[:, inner:] = (dbc * slope_ref[:, inner:].astype(F32)).astype(BF16)

    @pl.when(step == pl.num_programs(0) - 1)
    def _():
        last_ref[...] = carry1[...]


def steps_back(raw, dt, rate, moves, r):
    steps = raw.shape[0]
    heads = steps // 2
    chunks = raw.shape[1] // CHUNK
    s, t = row_iota(CHUNK), lane_iota(CHUNK)

    def stack(values):
        parts = [values[:, chunk * CHUNK : (chunk + 1) * CHUNK] for chunk in range(chunks)]
        return jnp.concatenate(parts, axis=0)

    def unstack(values):
        parts = [values[chunk * heads : (chunk + 1) * heads] for chunk in range(chunks)]
        return jnp.concatenate(parts, axis=1)

    got0, got, own0, own, k0, k1, kept0, kept1 = [
        moves[part * heads : (part + 1) * heads] for part in range(8)
    ]
    own1, got1 = own - own0, got - got0
    da0 = exact_mm(stack(got0 + r[:heads] - own0), flag(s >= t)) + exact_mm(stack(k0), flag(s < t))
    da1 = exact_mm(stack(got1 + r[heads:] - own1), flag(s <= t)) + exact_mm(stack(k1), flag(s > t))
    da = -jnp.concatenate([unstack(da0) + kept0, unstack(da1) + kept1], axis=0)
    dlog = jnp.concatenate([own0 + k0, own1 + k1], axis=0)
    sig = jax.nn.sigmoid(raw)
    ratio = jnp.where(raw < -20.0, 1.0, sig / jnp.maximum(dt, 1e-37))
    return dlog * ratio + da * rate * sig, jnp.sum(da * dt, axis=1, keepdims=True) * rate


def by_core(product, shard, mine_ref, theirs_ref):
    pieces = [product[place : place + shard] for place in range(0, product.shape[0], shard)]
    even = jnp.concatenate(pieces[0::2], axis=0)
    odd = jnp.concatenate(pieces[1::2], axis=0)
    core = lax.rem(lax.axis_index("dp"), 2)

    @pl.when(core == 0)
    def _():
        mine_ref[...] = even
        theirs_ref[...] = odd

    @pl.when(core == 1)
    def _():
        mine_ref[...] = odd
        theirs_ref[...] = even


def weights_kernel(
    turned_ref, dz_ref, mixed_ref, c_ref, wz_ref, mine_ref, theirs_ref, gain_ref, *, shard
):
    product = mm_tn(mixed_ref[...], c_ref[...]).astype(BF16)
    pieces = []
    for place in range(0, product.shape[0], 2 * shard):
        pieces.append(
            jnp.concatenate(
                [product[place : place + shard], product[place + shard : place + 2 * shard]], axis=1
            )
        )
    gate = mm(turned_ref[...], dz_ref[...])
    both = jnp.concatenate([jnp.concatenate(pieces, axis=0), gate.astype(BF16)], axis=1)
    by_core(both, shard, mine_ref, theirs_ref)
    share = (gate * wz_ref[...].astype(F32)).astype(BF16)
    gain_ref[0] = mm_nt(jnp.ones((8, share.shape[1]), BF16), share)[0:1]


def conv_back_kernel(
    lengths_ref,
    turned_ref,
    turnhalo_ref,
    dpre_ref,
    pre_ref,
    prehalo_ref,
    taps_ref,
    raw_ref,
    dt_ref,
    rate_ref,
    moves_ref,
    r_ref,
    w_ref,
    narrow_ref,
    gain_ref,
    share_ref,
    mix_sums_ref,
    e0_ref,
    dproj_ref,
    dhalo_ref,
    mine_ref,
    theirs_ref,
    draw_ref,
    small_ref,
    shift,
    buf,
    gains,
    sums_ref,
    *,
    shard,
):
    step = pl.program_id(0)
    count, wide = dpre_ref.shape
    chunks = count // CHUNK
    steps = raw_ref.shape[0]
    bounds, base = sequence_bounds(lengths_ref, count)

    @pl.when(step == 0)
    def _():
        for chunk in range(chunks):
            shift[chunk * 3 * CHUNK : (chunk + 1) * 3 * CHUNK, :] = shifts(
                base + chunk * CHUNK, bounds, 1, CHUNK
            )
        shift[chunks * 3 * CHUNK :, :] = shifts(base, bounds, 0, 16)
        buf[...] = jnp.zeros_like(buf)
        gains[...] = jnp.zeros_like(gains)
        sums_ref[...] = jnp.zeros_like(sums_ref)

    last = pl.num_programs(0) - 1
    inner = w_ref.shape[1]
    tile_here = pl.ds(pl.multiple_of(step * wide, wide), wide)

    def hand_over(product, weights):
        share = (product * weights.astype(F32)).astype(BF16)
        gains[...] += mm_nt(jnp.ones((8, share.shape[1]), BF16), share)
        by_core(product.astype(BF16), shard, mine_ref, theirs_ref)

    @pl.when(step < pl.num_programs(0) - 1)
    def _():
        buf[0:CHUNK, :] = dpre_ref[count - CHUNK :, :]
        moved = mm(shift[chunks * 3 * CHUNK :, :], dpre_ref[0 : CHUNK + 16, :])
        halo_sums = [None] * 4
        dproj = jnp.zeros((16, wide), F32)
        pre = prehalo_ref[...].astype(F32)
        for lag in (1, 2, 3):
            part = moved[(lag - 1) * 16 : lag * 16]
            dproj = dproj + part * taps_ref[3 - lag : 4 - lag, :]
            halo_sums[3 - lag] = jnp.sum(pre * part, axis=0, keepdims=True)
        halo_sums[3] = jnp.zeros((1, wide), F32)
        dhalo_ref[...] = dproj.astype(BF16)
        sums = [[jnp.zeros((8, 128), F32) for _ in range(4)] for _ in range(wide // 128)]
        for chunk in range(chunks):
            if chunk < chunks - 1:
                pair = dpre_ref[chunk * CHUNK : chunk * CHUNK + CHUNK + 16, :]
            else:
                pair = buf[...]
            moved = mm(shift[chunk * 3 * CHUNK : (chunk + 1) * 3 * CHUNK, :], pair)
            for place in range(wide // 128):
                cols = slice(place * 128, place * 128 + 128)
                for row in range(0, CHUNK, SUB):
                    span = slice(chunk * CHUNK + row, chunk * CHUNK + row + SUB)
                    pre = pre_ref[span, cols].astype(F32)
                    here = dpre_ref[span, cols].astype(F32)
                    dproj = here * taps_ref[3:4, cols]
                    sums[place][3] = sums[place][3] + fold(pre * here)
                    for lag in (1, 2, 3):
                        at = (lag - 1) * CHUNK + row
                        part = moved[at : at + SUB, cols]
                        dproj = dproj + part * taps_ref[3 - lag : 4 - lag, cols]
                        sums[place][3 - lag] = sums[place][3 - lag] + fold(pre * part)
                    dproj_ref[span, cols] = dproj.astype(BF16)
        for place in range(wide // 128):
            cols = slice(place * 128, place * 128 + 128)
            at = pl.ds(pl.multiple_of(step * wide + place * 128, 128), 128)
            for tap in range(4):
                sums_ref[tap : tap + 1, at] = (
                    jnp.sum(sums[place][tap], axis=0, keepdims=True) + halo_sums[tap][:, cols]
                )
        product = mm(turned_ref[...], dproj_ref[...]) + mm(turnhalo_ref[...], dhalo_ref[...])

        @pl.when(step < last - 1)
        def _():
            hand_over(product, w_ref[:, tile_here])

        @pl.when(step == last - 1)
        def _():
            hand_over(product, narrow_ref[0:wide, :].astype(F32).T)

    @pl.when(step == pl.num_programs(0) - 1)
    def _():
        rate = rate_ref[:, 0:1]
        draw, drate = steps_back(raw_ref[...], dt_ref[...], rate, moves_ref[...], r_ref[...])
        low = draw.astype(BF16)
        draw_ref[...] = low
        product = mm_nt(turned_ref[...], low)
        fill = jnp.zeros((product.shape[0], wide - steps), F32)
        steps_weights = narrow_ref[narrow_ref.shape[0] - steps :, :].astype(F32).T
        hand_over(
            jnp.concatenate([product, fill], axis=1),
            jnp.concatenate([steps_weights, fill], axis=1),
        )
        heads = steps // 2
        model = w_ref.shape[0]
        sums_ref[4:5, 0:inner] = jnp.sum(mix_sums_ref[0:8, :], axis=0, keepdims=True)
        share = jnp.concatenate([share_ref[part] for part in range(share_ref.shape[0])], axis=1)
        sums_ref[5:6, 0:model] = (gains[0:1, :] + share) / row_of(gain_ref)
        skips = in_parts(mix_sums_ref[8:16, :], 2).astype(BF16)
        skips = jnp.sum(mm_nt(e0_ref[0:heads, :], skips), axis=1, keepdims=True)
        columns = [jnp.concatenate([skips, skips], axis=0), jnp.sum(draw, axis=1, keepdims=True)]
        columns = jnp.concatenate(columns + [drate, jnp.zeros((steps, 5), F32)], axis=1).T
        for place in range(3):
            sums_ref[6:7, 128 * place : 128 * place + steps] = columns[place : place + 1]
        small_ref[...] = in_parts(sums_ref[...], 2).astype(BF16)


def halve_kernel(kept_ref, got_ref, keep_ref, send_ref, *, bit):
    shard = keep_ref.shape[0]
    mine = lax.rem(lax.axis_index("dp") // bit, 2)
    for place, out_ref in ((mine, keep_ref), (1 - mine, send_ref)):
        rows = pl.ds(pl.multiple_of(place * shard, shard), shard)
        total = kept_ref[rows, :].astype(F32) + got_ref[rows, :].astype(F32)
        out_ref[...] = total.astype(out_ref.dtype)


def sum_kernel(kept_ref, got_ref, out_ref):
    out_ref[...] = (kept_ref[...].astype(F32) + got_ref[...].astype(F32)).astype(BF16)


def two_halves(small):
    half = small.shape[1] // 2
    return jnp.concatenate([small[:, 0:half], small[:, half:]], axis=0)


def parts_sum(parts):
    half = parts.shape[0] // 2
    return parts[0:half].astype(F32) + parts[half:].astype(F32)


def quarters_kernel(
    mine_ref,
    got_ref,
    small_ref,
    smallgot_ref,
    keep_ref,
    across_ref,
    along_ref,
    both_ref,
    *,
    shard,
):
    half = mine_ref.shape[1] // 2
    row_bit = lax.rem(lax.axis_index("dp") // 2, 2)
    side = lax.axis_index("dir")
    count = mine_ref.shape[0] // 2
    small = two_halves(parts_sum(small_ref[...]) + parts_sum(smallgot_ref[...]))
    few = small.shape[0]
    parts = in_parts(small, 2)
    keep_ref[count:, :] = parts[0:few] + parts[few:]
    for out_ref, row, column in (
        (keep_ref, row_bit, side),
        (across_ref, row_bit, 1 - side),
        (along_ref, 1 - row_bit, side),
        (both_ref, 1 - row_bit, 1 - side),
    ):
        if out_ref is not keep_ref:
            out_ref[count:, :] = parts.astype(BF16)
        for place in range(count // shard):
            rows = slice(place * shard, (place + 1) * shard)
            here = pl.ds(pl.multiple_of((2 * place + row) * shard, shard), shard)
            cols = pl.ds(pl.multiple_of(column * half, half), half)
            total = mine_ref[here, cols].astype(F32) + got_ref[here, cols].astype(F32)
            out_ref[rows, :] = total.astype(out_ref.dtype)


def levels_kernel(keep_ref, a_ref, b_ref, c_ref, own_ref, s1_ref, s2_ref, s3_ref, *, shard):
    level = lax.axis_index("dp") // 4
    count = 4 * shard
    small = [parts_sum(ref[count:, :]) for ref in (a_ref, b_ref, c_ref)]
    parts = in_parts(keep_ref[count:, :] + small[0] + (small[1] + small[2]), 2)
    few = parts.shape[0] // 2
    own_ref[shard : shard + few, :] = parts[0:few] + parts[few:]
    for bits, out_ref in enumerate((own_ref, s1_ref, s2_ref, s3_ref)):
        wanted = jnp.bitwise_xor(level, bits)
        rows = pl.ds(pl.multiple_of(wanted * shard, shard), shard)
        total = keep_ref[rows, :] + a_ref[rows, :].astype(F32)
        total = total + (b_ref[rows, :].astype(F32) + c_ref[rows, :].astype(F32))
        out_ref[0:shard, :] = total.astype(out_ref.dtype)
        if bits:
            out_ref[shard : shard + 2 * few, :] = parts.astype(BF16)


def joined(ref, shard):
    return ref[0:shard, :].astype(F32), parts_sum(ref[shard:, :])


def last_kernel(own_ref, a_ref, b_ref, c_ref, out_ref, small_ref, *, shard):
    a, b, c = (joined(ref, shard) for ref in (a_ref, b_ref, c_ref))
    out_ref[...] = (own_ref[0:shard, :] + a[0] + (b[0] + c[0])).astype(BF16)
    small_ref[...] = own_ref[shard:, :] + a[1] + (b[1] + c[1])


def finish_kernel(
    late_ref,
    lategot_ref,
    early_ref,
    earlygot_ref,
    small_ref,
    gx_ref,
    gz_ref,
    gbc_ref,
    go_ref,
    gtaps_ref,
    gmix_ref,
    gin_ref,
    gskip_ref,
    gbias_ref,
    galog_ref,
):
    side = lax.axis_index("dir")
    half = late_ref.shape[1]
    inner = gx_ref.shape[1]
    model = go_ref.shape[1]
    shard = gx_ref.shape[0]
    mine = late_ref[...].astype(F32)
    other = lategot_ref[...].astype(F32)
    first = jnp.where(side == 0, mine, other)
    second = jnp.where(side == 0, other, mine)
    gx_ref[:, 0:half] = first
    gx_ref[:, half:inner] = second[:, 0 : inner - half]
    gbc_ref[...] = second[:, inner - half : inner - half + gbc_ref.shape[1]]
    early = early_ref[...].astype(F32) + earlygot_ref[...].astype(F32)
    go_ref[0:shard, :] = early[:, 0:model]
    go_ref[shard : 2 * shard, :] = early[:, model : 2 * model]
    gz_ref[...] = early[:, 2 * model :]
    small = jnp.concatenate([small_ref[0:8, :], small_ref[8:16, :]], axis=1)
    gtaps_ref[...] = small[0:4, 0 : gtaps_ref.shape[1]]
    gmix_ref[...] = small[4:5, 0:inner].reshape(inner)
    gin_ref[...] = small[5:6, 0:model].reshape(model)
    heads = gskip_ref.shape[0]
    gskip_ref[...] = small[6:7, 0:128].reshape(128)[0:heads]
    gbias_ref[0:1, :] = small[6:7, 128 : 128 + heads]
    gbias_ref[1:2, :] = small[6:7, 128 + heads : 128 + 2 * heads]
    galog_ref[0:1, :] = small[6:7, 256 : 256 + heads]
    galog_ref[1:2, :] = small[6:7, 256 + heads : 256 + 2 * heads]


def inputs_kernel(
    x_ref,
    c_ref,
    gain_ref,
    dproj_ref,
    dhalo_ref,
    draw_ref,
    dz_ref,
    wx_ref,
    wbc_ref,
    wz_ref,
    gin_ref,
    dproj,
):
    step = pl.program_id(0)
    inner = wx_ref.shape[1]
    steps = draw_ref.shape[0]
    narrow = wbc_ref.shape[0] - steps

    @pl.when(step == pl.num_programs(0) - 1)
    def _():
        tail = slice(dproj_ref.shape[0] - 16, dproj_ref.shape[0])
        both = dproj_ref[tail, :].astype(F32) + dhalo_ref[...].astype(F32)
        dproj[...] = dproj_ref[...]
        dproj[tail, :] = both.astype(BF16)

    @pl.when(step < pl.num_programs(0) - 1)
    def _():
        dproj[...] = dproj_ref[...]

    dn = mm_nt(dproj[:, 0:inner], wx_ref[...])
    dn = dn + mm_nt(dz_ref[...], wz_ref[...])
    dn = dn + mm(dproj[:, inner:], wbc_ref[0:narrow, :])
    dn = dn + mm_tn(draw_ref[...], wbc_ref[narrow:, :])
    x = x_ref[...].astype(F32)
    inv = lax.rsqrt(jnp.mean(x * x, axis=1, keepdims=True) + EPS)
    unit = x * inv
    f = dn * row_of(gain_ref)
    back = inv * (f - unit * jnp.mean(f * unit, axis=1, keepdims=True))
    gin_ref[...] = (c_ref[...].astype(F32) + back).astype(BF16)


def smem():
    return pl.BlockSpec(memory_space=pltpu.SMEM)


def resident():
    return pl.BlockSpec(memory_space=pltpu.VMEM)


def anywhere():
    return pl.BlockSpec(memory_space=pl.ANY)


def whole(shape):
    return pl.BlockSpec(shape, lambda i: (0,) * len(shape), pipeline_mode=pl.Buffered(1))


def rows_of(count, width):
    return pl.BlockSpec((count, width), lambda i: (i, 0))


def lanes_of(height, count):
    return pl.BlockSpec((height, count), lambda i: (0, i))


def parts_of(count, *rest):
    return pl.BlockSpec((count,) + rest, lambda i: (i,) + (0,) * len(rest))


def cost(microseconds):
    flops = int(microseconds * 1.15e9)
    return pl.CostEstimate(flops=flops, bytes_accessed=0, transcendentals=0)


def call(kernel, name, grid, in_specs, outs, scratch, cost_us, args, vmem, aliases=()):
    return pl.pallas_call(
        kernel,
        name=name,
        grid=(grid,),
        in_specs=in_specs,
        out_specs=[spec for spec, _, _ in outs],
        out_shape=[jax.ShapeDtypeStruct(shape, dtype) for _, shape, dtype in outs],
        scratch_shapes=scratch,
        input_output_aliases=dict(aliases),
        compiler_params=pltpu.CompilerParams(
            vmem_limit_bytes=vmem * MIB, dimension_semantics=("arbitrary",)
        ),
        cost_estimate=cost(cost_us),
    )(*args)


def traded(values, axis, bit, size):
    return lax.ppermute(values, axis, [(i, i ^ bit) for i in range(size)])


def ordered(first, second):
    return lax.optimization_barrier((first, second))


def sum_shards(grad, dp_count):
    index = lax.axis_index("dp")
    held = grad.reshape(dp_count, grad.shape[0] // dp_count, grad.shape[1])
    bit = 1
    while bit < dp_count:
        paired = held.reshape(held.shape[0] // 2, 2, held.shape[1], held.shape[2])
        mine = (index // bit) % 2
        kept = lax.dynamic_index_in_dim(paired, mine, 1, keepdims=False)
        sent = lax.dynamic_index_in_dim(paired, 1 - mine, 1, keepdims=False).astype(BF16)
        held = kept.astype(F32) + traded(sent, "dp", bit, dp_count).astype(F32)
        bit *= 2
    held = held[0].astype(BF16)
    return held.astype(F32) + traded(held, "dir", 1, 2).astype(F32)


def sum_all(values, dp_count):
    bit = 1
    while bit < dp_count:
        values = values + traded(values, "dp", bit, dp_count)
        bit *= 2
    return values + traded(values, "dir", 1, 2)


def local(
    dp_count,
    hidden_in,
    lengths,
    gain_in,
    w_x,
    w_z,
    w_bcdt,
    conv_w,
    dt_bias,
    a_log,
    d_skip,
    gain_mix,
    w_out,
    cotangent,
):
    x = hidden_in[0]
    cot = cotangent[0]
    count, model = x.shape
    inner = w_x.shape[1]
    channels = conv_w.shape[1]
    heads = d_skip.shape[0]
    width = inner // heads
    state = (channels - inner) // 4
    chunks = count // CHUNK
    steps = 2 * heads

    w_narrow = w_bcdt.T
    halo = lax.ppermute(x[count - 16 :], "dir", [(0, 1)])

    spread = np.repeat(np.eye(heads, dtype=np.float32), width, axis=1)
    zeros = np.zeros_like(spread)
    e0 = jnp.asarray(np.concatenate([spread, zeros, spread, zeros]), BF16)
    e1 = jnp.asarray(np.concatenate([zeros, spread, zeros, spread]), BF16)
    spans = jnp.asarray(np.repeat(np.eye(heads, dtype=np.float32), CHUNK, axis=1), BF16)
    def rows_out(size, columns, dtype):
        return (rows_of(size, columns), (count, columns), dtype)

    def full(shape, dtype):
        return (pl.BlockSpec(shape, lambda i: (0,) * len(shape)), shape, dtype)

    per = ROWS // CHUNK
    state_f32 = pltpu.VMEM((state, inner), F32)
    state_bf16 = pltpu.VMEM((state, inner), BF16)
    row_f32 = pltpu.VMEM((1, inner), F32)
    chunk_f32 = pltpu.VMEM((CHUNK, inner), F32)
    chunk_bf16 = pltpu.VMEM((CHUNK, inner), BF16)
    (
        normed,
        raw,
        dt,
        rate,
        target,
        source,
        factors,
        keeps,
        pre,
        act,
        slope,
        sl0,
        sf1,
        send,
        pre_halo,
        turn_halo,
    ) = call(
        proj_kernel,
        "proj",
        count // ROWS,
        [
            smem(),
            smem(),
            smem(),
            whole((count, model)),
            whole((16, model)),
            whole((model,)),
            whole((model, inner)),
            whole(w_narrow.shape),
            whole(conv_w.shape),
            whole(e0.shape),
            whole(e1.shape),
        ],
        [
            full((count, model), BF16),
            full((steps, count), F32),
            full((steps, count), F32),
            full((steps, 128), F32),
            full((steps, count), F32),
            full((steps, count), F32),
            full((2, count, 2 * steps), BF16),
            full((6, chunks, inner), F32),
            rows_out(ROWS, channels, BF16),
            rows_out(ROWS, channels, BF16),
            rows_out(ROWS, channels, BF16),
            (parts_of(per, state, inner), (chunks, state, inner), BF16),
            (parts_of(per, state, inner), (chunks, state, inner), BF16),
            full((state, inner), BF16),
            full((16, channels), BF16),
            full((model, 16), BF16),
        ],
        [
            pltpu.VMEM((16 + ROWS, channels), BF16),
            state_f32,
            state_f32,
            chunk_bf16,
            chunk_bf16,
        ],
        US_PROJ,
        (lengths, dt_bias, a_log, x, halo, gain_in, w_x, w_narrow, conv_w, e0, e1),
        VMEM_PROJ,
    )
    received = lax.ppermute(send, "dir", SWAP)

    gate_z, d_norm, turned = call(
        gates_kernel,
        "gates",
        count // ROWS,
        [
            rows_of(ROWS, model),
            rows_of(ROWS, model),
            whole((model, inner)),
            whole((inner, model)),
        ],
        [
            rows_out(ROWS, inner, BF16),
            rows_out(ROWS, inner, BF16),
            (lanes_of(model, ROWS), (model, count), BF16),
        ],
        [],
        US_GATES,
        (normed, cot, w_z, w_out),
        VMEM_GATES,
    )

    def down_rows(width):
        return pl.BlockSpec((CHUNK, width), lambda i: (chunks - 1 - i, 0))

    def down_lanes(height):
        return pl.BlockSpec((height, CHUNK), lambda i: (0, chunks - 1 - i))

    def down_parts(*rest):
        return pl.BlockSpec((1,) + rest, lambda i: (chunks - 1 - i,) + (0,) * len(rest))

    states = (down_parts(state, inner), (chunks, state, inner), BF16)
    out, mixed, dz, dy, r, dcc, dl0, df1, s0, s1, d_send, mix_sums = call(
        mix_kernel,
        "mix",
        chunks,
        [
            smem(),
            smem(),
            down_rows(model),
            down_rows(channels),
            down_lanes(steps),
            down_lanes(steps),
            pl.BlockSpec((1, CHUNK, 2 * steps), lambda i: (0, chunks - 1 - i, 0)),
            down_parts(state, inner),
            down_parts(state, inner),
            whole((6, chunks, inner)),
            whole((state, inner)),
            down_rows(inner),
            down_rows(inner),
            whole((inner, model)),
            whole((inner,)),
            whole(e0.shape),
            whole(e1.shape),
        ],
        [
            (down_rows(model), (count, model), BF16),
            (down_rows(inner), (count, inner), BF16),
            (down_rows(inner), (count, inner), BF16),
            (down_rows(inner), (count, inner), BF16),
            (down_lanes(steps), (steps, count), F32),
            (down_rows(2 * state), (count, 2 * state), F32),
            states,
            states,
            states,
            states,
            full((state, inner), BF16),
            full((16, inner), F32),
        ],
        [state_f32] * 3 + [chunk_f32] * 8 + [chunk_bf16] * 4 + [row_f32] * 2,
        US_MIX,
        (
            lengths,
            d_skip,
            x,
            act,
            target,
            source,
            factors,
            sl0,
            sf1,
            keeps,
            received,
            gate_z,
            d_norm,
            w_out,
            gain_mix,
            e0,
            e1,
        ),
        VMEM_MIX,
    )
    d_received = lax.ppermute(d_send, "dir", SWAP)

    def plain(kernel, name, args, outs, specs=None, out_specs=None, grid=()):
        resident = [pl.BlockSpec(memory_space=pltpu.VMEM)]
        return pl.pallas_call(
            kernel,
            name=name,
            grid=grid,
            in_specs=specs or resident * len(args),
            out_specs=out_specs or resident * len(outs),
            out_shape=[jax.ShapeDtypeStruct(shape, dtype) for shape, dtype in outs],
            compiler_params=pltpu.CompilerParams(vmem_limit_bytes=VMEM_SUMS * MIB),
            cost_estimate=cost(US_SUMS),
        )(*args)

    def halve(name, kept, got, bit):
        rows, wide = got.shape
        outs = [((rows // 2, wide), F32), ((rows // 2, wide), BF16)]
        return plain(
            functools.partial(halve_kernel, bit=bit),
            name,
            (kept, got),
            outs,
            [rows_of(2 * piece, wide)] * 2,
            [rows_of(piece, wide)] * 2,
            (rows // (2 * piece),),
        )

    blocks = 4
    shard = model // dp_count
    direct = dp_count == 16 and shard % 16 == 0
    piece = model // 16
    early_rows = (rows_of(model // 2 // blocks, 2 * inner), (model // 2, 2 * inner), BF16)
    early_mine, early_theirs, z_share = call(
        functools.partial(weights_kernel, shard=piece),
        "weights",
        blocks,
        [
            rows_of(model // blocks, count),
            whole((count, inner)),
            lanes_of(count, inner // blocks),
            whole((count, model)),
            rows_of(model // blocks, inner),
        ],
        [
            early_rows,
            early_rows,
            (pl.BlockSpec((1, 1, model // blocks), lambda i: (i, 0, 0)), (blocks, 1, model // blocks), F32),
        ],
        [],
        US_WEIGHTS,
        (turned, dz, mixed, cot, w_z),
        VMEM_WEIGHTS,
    )
    (early_mine, early_theirs), d_received = ordered((early_mine, early_theirs), d_received)

    def back(skipped, taken, start, dpre, moves):
        def rows_from(width):
            return pl.BlockSpec((CHUNK, width), lambda i: (i + skipped, 0))

        def lanes_from(height):
            return pl.BlockSpec((height, CHUNK), lambda i: (0, i + skipped))

        def parts_from(*rest):
            return pl.BlockSpec((1,) + rest, lambda i: (i + skipped,) + (0,) * len(rest))

        return call(
            functools.partial(back_kernel, skipped=skipped, chunks=chunks),
            "back" + str(skipped),
            taken,
            [
                smem(),
                smem(),
                rows_from(channels),
                rows_from(channels),
                lanes_from(steps),
                lanes_from(steps),
                pl.BlockSpec((1, CHUNK, 2 * steps), lambda i: (1, i + skipped, 0)),
                rows_from(2 * state),
                rows_from(inner),
                parts_from(state, inner),
                parts_from(state, inner),
                parts_from(state, inner),
                parts_from(state, inner),
                whole((6, chunks, inner)),
                whole((state, inner)),
                whole(start.shape),
                whole(e0.shape),
                whole(e1.shape),
                whole(spans.shape),
                anywhere(),
                anywhere(),
            ],
            [
                (rows_from(channels), (count, channels), BF16),
                (lanes_from(8 * heads), (8 * heads, count), F32),
                full((state, inner), F32),
            ],
            [
                state_f32,
                pltpu.VMEM((CHUNK, CHUNK), F32),
                pltpu.VMEM((CHUNK, heads * CHUNK), BF16),
                pltpu.VMEM((CHUNK, heads * CHUNK), BF16),
            ]
            + [chunk_bf16] * 4
            + [state_bf16] * 2,
            US_BACK * taken // chunks,
            (
                lengths,
                d_skip,
                act,
                slope,
                target,
                source,
                factors,
                dcc,
                dy,
                s0,
                s1,
                dl0,
                df1,
                keeps,
                d_received,
                start,
                e0,
                e1,
                spans,
                dpre,
                moves,
            ),
            VMEM_BACK,
            {19: 0, 20: 1} if skipped else {},
        )

    first = 1
    dpre, moves, carry = back(0, first, d_received, received, received)
    if direct:
        early_got = traded(early_theirs, "dp", 1, dp_count)
        early_keep, early_send = halve("halve_y", early_mine, early_got, 2)
        early_send, carry = ordered(early_send, carry)
        early_got = traded(early_send, "dp", 2, dp_count)
    dpre, moves, _ = back(first, chunks - first, carry, dpre, moves)
    if direct:
        early_keep, early_send = halve("halve_z", early_keep, early_got, 4)
        early_send, dpre = ordered(early_send, dpre)
        early_got = traded(early_send, "dp", 4, dp_count)

    tile = 256
    tiles = channels // tile
    def tile_of(height):
        return pl.BlockSpec((height, tile), lambda i: (0, jnp.minimum(i, tiles - 1)))

    wide = (tiles + 1) * tile
    late_out = (lanes_of(model // 2, tile), (model // 2, wide), BF16)
    dproj, dhalo, late_mine, late_theirs, draw, small = call(
        functools.partial(conv_back_kernel, shard=piece),
        "conv_back",
        tiles + 1,
        [
            smem(),
            whole((model, count)),
            whole((model, 16)),
            tile_of(count),
            tile_of(count),
            tile_of(16),
            tile_of(conv_w.shape[0]),
            whole((steps, count)),
            whole((steps, count)),
            whole((steps, 128)),
            whole((8 * heads, count)),
            whole((steps, count)),
            whole((model, inner)),
            whole(w_narrow.shape),
            whole((model,)),
            whole(z_share.shape),
            whole(mix_sums.shape),
            whole(e0.shape),
        ],
        [
            (tile_of(count), (count, channels), BF16),
            (tile_of(16), (16, channels), BF16),
            late_out,
            late_out,
            full((steps, count), BF16),
            full((16, wide), BF16),
        ],
        [
            pltpu.VMEM((3 * count + 48, CHUNK + 16), BF16),
            pltpu.VMEM((CHUNK + 16, tile), BF16),
            pltpu.VMEM((8, model), F32),
            pltpu.VMEM((8, wide), F32),
        ],
        US_CONV,
        (
            lengths,
            turned,
            turn_halo,
            dpre,
            pre,
            pre_halo,
            conv_w,
            raw,
            dt,
            rate,
            moves,
            r,
            w_x,
            w_narrow,
            gain_in,
            z_share,
            mix_sums,
            e0,
        ),
        VMEM_CONV,
    )
    d_halo = lax.ppermute(dhalo, "dir", [(1, 0)])

    (grad_in,) = call(
        inputs_kernel,
        "inputs",
        count // ROWS,
        [
            rows_of(ROWS, model),
            rows_of(ROWS, model),
            whole((model,)),
            rows_of(ROWS, channels),
            whole((16, channels)),
            lanes_of(steps, ROWS),
            rows_of(ROWS, inner),
            whole((model, inner)),
            whole(w_narrow.shape),
            whole((model, inner)),
        ],
        [rows_out(ROWS, model, BF16)],
        [pltpu.VMEM((ROWS, channels), BF16)],
        US_INPUTS,
        (x, cot, gain_in, dproj, d_halo, draw, dz, w_x, w_narrow, w_z),
        VMEM_INPUTS,
    )

    if not direct:
        def undivided(mine, theirs):
            even = lax.axis_index("dp") % 2 == 0
            both = [jnp.where(even, mine, theirs), jnp.where(even, theirs, mine)]
            both = [part.reshape(8, 1, piece, part.shape[1]) for part in both]
            return jnp.concatenate(both, axis=1).reshape(model, mine.shape[1])

        early = undivided(early_mine, early_theirs)
        g_out = early[:, :inner].reshape(16, piece, 2, model).transpose(0, 2, 1, 3)
        late = sum_shards(undivided(late_mine, late_theirs), dp_count)
        small = sum_all(small[0:8].astype(F32) + small[8:16].astype(F32), dp_count)
        return (
            out[None],
            grad_in[None],
            late[:, :inner],
            sum_shards(early[:, inner:], dp_count),
            late[:, inner : inner + 4 * state + steps],
            sum_shards(g_out.reshape(inner, model), dp_count),
            small[5, :model],
            small[0:4, :channels],
            small[6, 128 : 128 + steps].reshape(dt_bias.shape),
            small[6, 256 : 256 + steps].reshape(a_log.shape),
            small[6, :heads],
            small[4, :inner],
        )

    early_got, late_theirs = ordered(early_got, late_theirs)
    late_got = traded(late_theirs, "dp", 1, dp_count)
    small_got = traded(small, "dp", 1, dp_count)
    early_keep, early_send = halve("halve_z2", early_keep, early_got, 8)
    early_send, late_got = ordered(early_send, late_got)
    early_got = traded(early_send, "dp", 8, dp_count)
    quarter = (model // 4 + 32, wide // 2)
    kept, across, along, both = plain(
        functools.partial(quarters_kernel, shard=piece),
        "quarters",
        (late_mine, late_got, small, small_got),
        [((model // 4 + 16, wide // 2), F32), (quarter, BF16), (quarter, BF16), (quarter, BF16)],
    )
    corners = [(a, b) for a in range(2) for b in range(dp_count)]
    across = traded(across, "dir", 1, 2)
    along = traded(along, "dp", 2, dp_count)
    both = lax.ppermute(
        both,
        ("dir", "dp"),
        [(a * dp_count + b, (1 - a) * dp_count + (b ^ 2)) for a, b in corners],
    )
    (early,) = plain(sum_kernel, "early_sum", (early_keep, early_got), [((piece, 2 * inner), BF16)])
    grad_in, early, both = lax.optimization_barrier((grad_in, early, both))
    early_got = traded(early, "dir", 1, 2)
    message = (piece + 32, wide // 2)
    own, *sends = plain(
        functools.partial(levels_kernel, shard=piece),
        "levels",
        (kept, across, along, both),
        [((piece + 16, wide // 2), F32)] + [(message, BF16)] * 3,
    )
    gots = [traded(sent, "dp", 4 * bits, dp_count) for bits, sent in zip((1, 2, 3), sends)]
    late, small = plain(
        functools.partial(last_kernel, shard=piece),
        "last",
        (own, *gots),
        [((piece, wide // 2), BF16), ((16, wide // 2), F32)],
    )
    late_got = traded(late, "dir", 1, 2)
    g_x, g_zz, g_bc, g_o, g_taps, g_mix, g_in, g_skip, g_bias, g_alog = plain(
        finish_kernel,
        "finish",
        (late, late_got, early, early_got, small),
        [
            ((piece, inner), F32),
            ((piece, inner), F32),
            ((piece, w_bcdt.shape[1]), F32),
            ((2 * piece, model), F32),
            (conv_w.shape, F32),
            ((inner,), F32),
            ((model,), F32),
            ((heads,), F32),
            (dt_bias.shape, F32),
            (a_log.shape, F32),
        ],
    )
    return (
        out[None],
        grad_in[None],
        g_x,
        g_zz,
        g_bc,
        g_o,
        g_in,
        g_taps,
        g_bias,
        g_alog,
        g_skip,
        g_mix,
    )


def solution(mesh):
    return jax.shard_map(
        functools.partial(local, mesh.shape["dp"]),
        mesh=mesh,
        in_specs=(
            P("dir", "dp", None),
            P("dp", None),
            P(),
            P(),
            P(),
            P(),
            P(),
            P(),
            P(),
            P(),
            P(),
            P(),
            P("dir", "dp", None),
        ),
        out_specs=(
            P("dir", "dp", None),
            P("dir", "dp", None),
            P("dp", None),
            P("dp", None),
            P("dp", None),
            P("dp", None),
            P(),
            P(),
            P(),
            P(),
            P(),
            P(),
        ),
        check_vma=False,
    )
```

```python
import functools

import jax
import jax.numpy as jnp
import numpy as np
from jax import lax
from jax.experimental import pallas as pl
from jax.experimental.pallas import tpu as pltpu
from jax.sharding import PartitionSpec as P

F32 = jnp.float32
BF16 = jnp.bfloat16
CHUNK = 128
ROWS = 256
SUB = 64
EPS = 1e-05
LOG2E = 1.4426950408889634
SWAP = [(0, 1), (1, 0)]
MIB = 1024 * 1024
VMEM_GATES = 56
VMEM_PROJ = 56
VMEM_INTRA = 12
VMEM_MIX = 56
VMEM_WEIGHTS = 56
VMEM_BACK = 56
VMEM_CONV = 56
VMEM_INPUTS = 56
VMEM_SUMS = 8
US_GATES = 10
US_PROJ = 20
US_INTRA = 12
US_MIX = 30
US_WEIGHTS = 10
US_BACK = 30
US_CONV = 17
US_INPUTS = 16
US_SUMS = 2
NT = (((1,), (1,)), ((), ()))
TN = (((0,), (0,)), ((), ()))
EXACT = lax.Precision.HIGHEST


def mm(left, right):
    return jnp.dot(left, right, preferred_element_type=F32)


def mm_nt(left, right):
    return lax.dot_general(left, right, NT, preferred_element_type=F32)


def mm_tn(left, right):
    return lax.dot_general(left, right, TN, preferred_element_type=F32)


def exact_mm(left, right):
    return jnp.dot(left, right, precision=EXACT, preferred_element_type=F32)


def sequence_bounds(lengths_ref, half_rows):
    bounds, total = [], 0
    for position in range(lengths_ref.shape[1]):
        total = total + lengths_ref[0, position]
        bounds.append(total)
    return bounds, lax.axis_index("dir") * half_rows


def start_of(row, bounds):
    start = jnp.where(row < 0, -1, 0)
    for bound in bounds:
        start = jnp.where(row >= bound, bound, start)
    return start


def same_sequence(first, bounds):
    starts = start_of(first + lane_iota(CHUNK), bounds)
    turned = jnp.broadcast_to(starts.astype(F32), (8, CHUNK)).T[:, 0:1]
    return (turned == starts.astype(F32)) & (row_iota(CHUNK) != lane_iota(CHUNK))


def row_iota(count):
    return lax.broadcasted_iota(jnp.int32, (count, 1), 0)


def lane_iota(count):
    return lax.broadcasted_iota(jnp.int32, (1, count), 1)


def flag(condition):
    return jnp.where(condition, 1.0, 0.0)


def in_parts(values, parts):
    out = []
    for _ in range(parts):
        part = values.astype(BF16).astype(F32)
        out.append(part)
        values = values - part
    return jnp.concatenate(out, axis=0)


def fold(values):
    return jnp.sum(values.reshape(values.shape[0] // 8, 8, values.shape[1]), axis=0)


def row_of(ref):
    return ref[...].reshape(1, ref.shape[0])


def column_of(ref, steps):
    heads = steps // 2
    place = row_iota(steps)
    column = jnp.zeros((steps, 1), F32)
    for step in range(steps):
        column = jnp.where(place == step, ref[step // heads, step % heads], column)
    return column


def gates_kernel(normed_ref, c_ref, wz_ref, wo_ref, z_ref, dnorm_ref, turned_ref):
    turned_ref[...] = normed_ref[...].T
    z_ref[...] = mm(normed_ref[...], wz_ref[...]).astype(BF16)
    dnorm_ref[...] = mm_nt(c_ref[...], wo_ref[...]).astype(BF16)


def step_factors(
    lengths_ref,
    bias_ref,
    alog_ref,
    e0_ref,
    e1_ref,
    raw_ref,
    dt_ref,
    rate_ref,
    target_ref,
    source_ref,
    factors_ref,
    keeps_ref,
):
    steps, count = raw_ref.shape
    heads = steps // 2
    bounds, base = sequence_bounds(lengths_ref, count)
    rate = jnp.exp(column_of(alog_ref, steps))
    rate_ref[...] = jnp.broadcast_to(rate, (steps, 128))
    raw = raw_ref[...] + column_of(bias_ref, steps)
    raw_ref[...] = raw
    dt = jnp.maximum(raw, 0.0) + jnp.log1p(jnp.exp(-jnp.abs(raw)))
    dt_ref[...] = dt
    log_dt = jnp.log(jnp.maximum(dt, 1e-37))
    chunks = count // CHUNK
    upto = flag(row_iota(CHUNK) <= lane_iota(CHUNK))
    fall = dt * rate
    stacked = [fall[:, chunk * CHUNK : (chunk + 1) * CHUNK] for chunk in range(chunks)]
    summed = exact_mm(jnp.concatenate(stacked, axis=0), upto)
    lane = lane_iota(CHUNK)
    keeps = jnp.zeros((steps, CHUNK), F32)
    for chunk in range(chunks):
        span = slice(chunk * CHUNK, (chunk + 1) * CHUNK)
        first = base + chunk * CHUNK
        inc = summed[chunk * steps : (chunk + 1) * steps]
        dt_c, log_c = dt[:, span], log_dt[:, span]
        inc0 = inc[:heads]
        exc1 = inc[heads:] - fall[heads:, span]
        total0 = inc0[:, CHUNK - 1 :]
        total1 = inc[heads:, CHUNK - 1 :]
        target = jnp.concatenate([-inc0, exc1], axis=0) * LOG2E
        source = jnp.concatenate([inc0 + log_c[:heads], log_c[heads:] - exc1], axis=0) * LOG2E
        target_ref[:, span] = target
        source_ref[:, span] = source
        starts = start_of(first + lane, bounds)
        before = start_of(first - 1, bounds)
        left = start_of(first, bounds)
        right = start_of(first + CHUNK - 1, bounds)
        after = start_of(first + CHUNK, bounds)
        enter0 = jnp.where(starts == before, jnp.exp(-inc0), 0.0)
        enter1 = jnp.where(starts == after, jnp.exp(exc1 - total1), 0.0)
        leave0 = jnp.where(starts == right, dt_c[:heads] * jnp.exp(inc0 - total0), 0.0)
        leave1 = jnp.where(starts == left, dt_c[heads:] * jnp.exp(-exc1), 0.0)
        enter = jnp.concatenate([enter0, enter1], axis=0)
        leave = jnp.concatenate([leave0, leave1], axis=0)
        factors_ref[0, span, :] = in_parts(enter, 2).T.astype(BF16)
        factors_ref[1, span, :] = in_parts(leave, 2).T.astype(BF16)
        keep0 = jnp.where(before == right, jnp.exp(-total0), 0.0)
        keep1 = jnp.where(after == left, jnp.exp(-total1), 0.0)
        keeps = jnp.where(lane == chunk, jnp.concatenate([keep0, keep1], axis=0), keeps)
    ahead = jnp.zeros_like(keeps)
    behind = jnp.zeros_like(keeps)
    run_a = jnp.ones((steps, 1), F32)
    run_b = jnp.ones((steps, 1), F32)
    for chunk in range(chunks):
        ahead = jnp.where(lane == chunk, run_a, ahead)
        run_a = run_a * keeps[:, chunk : chunk + 1]
        last = chunks - 1 - chunk
        behind = jnp.where(lane == last, run_b, behind)
        run_b = run_b * keeps[:, last : last + 1]
    for place, values in enumerate((keeps, ahead, behind)):
        columns = in_parts(values, 2).T.astype(BF16)[0:16]
        keeps_ref[2 * place] = mm(columns, e0_ref[...])[0:chunks]
        keeps_ref[2 * place + 1] = mm(columns, e1_ref[...])[0:chunks]


def shifts(first, bounds, sign, height):
    row = lax.broadcasted_iota(jnp.int32, (height, CHUNK + 16), 0)
    col = lane_iota(CHUNK + 16)
    parts = []
    for lag in (1, 2, 3):
        later = first + col + (lag - 16 if sign < 0 else 0)
        near = later - start_of(later, bounds) < lag
        place = jnp.where(near, -CHUNK, col)
        offset = {-1: 16 - lag, 1: lag, 0: lag - height}[sign]
        parts.append(flag(place == row + offset))
    return jnp.concatenate(parts, axis=0).astype(BF16)


def proj_kernel(
    lengths_ref,
    bias_ref,
    alog_ref,
    x_ref,
    halo_ref,
    gain_ref,
    wx_ref,
    wbc_ref,
    taps_ref,
    e0_ref,
    e1_ref,
    normed_ref,
    raw_ref,
    dt_ref,
    rate_ref,
    target_ref,
    source_ref,
    factors_ref,
    keeps_ref,
    pre_ref,
    act_ref,
    slope_ref,
    s0_ref,
    sf1_ref,
    send_ref,
    prehalo_ref,
    turnhalo_ref,
    buf,
    acc0,
    acc1,
    left0,
    left1,
):
    step = pl.program_id(0)
    per = ROWS // CHUNK
    bounds, base = sequence_bounds(lengths_ref, pl.num_programs(0) * ROWS)
    inner = wx_ref.shape[1]
    channels = taps_ref.shape[1]
    state = (channels - inner) // 4

    @pl.when(step == 0)
    def _():
        count = x_ref.shape[0]
        gain = row_of(gain_ref)

        @pl.loop(0, count // CHUNK, unroll=4)
        def _(chunk):
            rows = pl.ds(pl.multiple_of(chunk * CHUNK, CHUNK), CHUNK)
            x = x_ref[rows, :].astype(F32)
            inv = lax.rsqrt(jnp.mean(x * x, axis=1, keepdims=True) + EPS)
            normed = (x * inv * gain).astype(BF16)
            normed_ref[rows, :] = normed
            raw = mm_nt(wbc_ref[channels - inner :, :], normed)
            raw_ref[:, rows] = raw.astype(BF16).astype(F32)

        step_factors(
            lengths_ref,
            bias_ref,
            alog_ref,
            e0_ref,
            e1_ref,
            raw_ref,
            dt_ref,
            rate_ref,
            target_ref,
            source_ref,
            factors_ref,
            keeps_ref,
        )
        x = halo_ref[...].astype(F32)
        inv = lax.rsqrt(jnp.mean(x * x, axis=1, keepdims=True) + EPS)
        normed = x * inv * gain
        turnhalo_ref[...] = normed.T.astype(BF16)
        normed = normed.astype(BF16)
        prehalo_ref[:, 0:inner] = mm(normed, wx_ref[...]).astype(BF16)
        prehalo_ref[:, inner:channels] = mm_nt(normed, wbc_ref[0 : channels - inner, :]).astype(BF16)
        buf[0:16, :] = prehalo_ref[...]
        acc0[...] = jnp.zeros_like(acc0)
        acc1[...] = jnp.zeros_like(acc1)

    @pl.when(step > 0)
    def _():
        buf[0:16, :] = buf[ROWS : ROWS + 16, :]

    normed = normed_ref[pl.ds(pl.multiple_of(step * ROWS, ROWS), ROWS), :]
    for tile in range(inner // 256):
        cols = slice(tile * 256, tile * 256 + 256)
        px = mm(normed, wx_ref[:, cols]).astype(BF16)
        pre_ref[:, cols] = px
        buf[16 : 16 + ROWS, cols] = px
    pb = mm_nt(normed, wbc_ref[0 : channels - inner, :]).astype(BF16)
    pre_ref[:, inner:channels] = pb
    buf[16 : 16 + ROWS, inner:channels] = pb

    first = base + step * ROWS
    for part in range(per):
        offset = part * CHUNK
        shift = shifts(first + offset, bounds, -1, CHUNK)
        here = pl.ds(pl.multiple_of(step * ROWS + offset, CHUNK), CHUNK)
        leave_cols = factors_ref[1, here, :]
        for tile in range(channels // 256):
            wide = slice(tile * 256, tile * 256 + 256)
            moved = mm(shift, buf[offset : offset + CHUNK + 16, wide])
            if tile * 256 < inner:
                leave0 = mm(leave_cols, e0_ref[:, wide])
                leave1 = mm(leave_cols, e1_ref[:, wide])
            for column in (0, 128):
                cols = slice(tile * 256 + column, tile * 256 + column + 128)
                cut = slice(column, column + 128)
                for row in range(0, CHUNK, SUB):
                    here = buf[offset + 16 + row : offset + 16 + row + SUB, cols]
                    conv = here.astype(F32) * taps_ref[3:4, cols]
                    for lag in (1, 2, 3):
                        at = (lag - 1) * CHUNK + row
                        conv = conv + moved[at : at + SUB, cut] * taps_ref[3 - lag : 4 - lag, cols]
                    sig = jax.nn.sigmoid(conv)
                    act = conv * sig
                    span = slice(offset + row, offset + row + SUB)
                    act_ref[span, cols] = act.astype(BF16)
                    slope_ref[span, cols] = (sig + act - act * sig).astype(BF16)
                    if tile * 256 < inner:
                        held = slice(row, row + SUB)
                        left0[held, cols] = (act * leave0[held, cut]).astype(BF16)
                        left1[held, cols] = (act * leave1[held, cut]).astype(BF16)
        turned = act_ref[offset : offset + CHUNK, inner:channels].astype(F32).T.astype(BF16)
        s0_ref[part] = acc0[...].astype(BF16)
        chunk = pl.ds(step * per + part, 1)
        acc0[...] = keeps_ref[0, chunk, :] * acc0[...] + mm(turned[0:state], left0[...])
        fresh1 = mm(turned[2 * state : 3 * state], left1[...])
        sf1_ref[part] = fresh1.astype(BF16)
        acc1[...] = acc1[...] + keeps_ref[3, chunk, :] * fresh1

    @pl.when(step == pl.num_programs(0) - 1)
    def _():
        send_ref[...] = jnp.where(base > 0, acc1[...], acc0[...]).astype(BF16)


def bc_columns(act_ref, inner, state):
    return [act_ref[:, inner + part * state : inner + (part + 1) * state] for part in range(4)]


def cut_pair(values, width):
    zero = jnp.zeros_like(values)
    first = lane_iota(2 * width) < width
    return jnp.concatenate([jnp.where(first, values, zero), jnp.where(first, zero, values)], axis=0)


def mix_kernel(
    lengths_ref,
    skip_ref,
    act_ref,
    target_ref,
    source_ref,
    factors_ref,
    sl0_ref,
    sf1_ref,
    keeps_ref,
    recv_ref,
    z_ref,
    dnorm_ref,
    gain_ref,
    e0_ref,
    e1_ref,
    mixed_ref,
    dz_ref,
    dy_ref,
    r_ref,
    dcc_ref,
    dl0_ref,
    df1_ref,
    s0_ref,
    s1_ref,
    send_ref,
    sums_ref,
    carry1,
    acc0,
    acc1,
    enter0,
    enter1,
    from0,
    from1,
    within,
    gated_s,
    slope_s,
    gate_s,
    in0,
    in1,
    prod0,
    prod1,
    skip_s,
    gain_s,
):
    step = pl.program_id(0)
    chunk = pl.num_programs(0) - 1 - step
    bounds, base = sequence_bounds(lengths_ref, pl.num_programs(0) * CHUNK)
    first = base + chunk * CHUNK
    inner = gain_ref.shape[0]
    heads = r_ref.shape[0] // 2
    width = inner // heads
    state = recv_ref.shape[0]
    small = 32

    @pl.when(step == 0)
    def _():
        recv = recv_ref[...].astype(F32)
        carry1[...] = jnp.where(base > 0, jnp.zeros_like(recv), recv)
        acc0[...] = jnp.zeros_like(acc0)
        acc1[...] = jnp.zeros_like(acc1)
        sums_ref[...] = jnp.zeros_like(sums_ref)
        gain_s[...] = row_of(gain_ref)
        left = lane_iota(2 * width) < width
        for pair in range(heads // 2):
            skip_s[:, pair * 2 * width : (pair + 1) * 2 * width] = jnp.where(
                left, skip_ref[2 * pair], skip_ref[2 * pair + 1]
            )

    keep0 = keeps_ref[0, pl.ds(chunk, 1), :]
    keep1 = keeps_ref[1, pl.ds(chunk, 1), :]
    ahead0 = keeps_ref[2, pl.ds(chunk, 1), :] * jnp.where(base > 0, 1.0, 0.0)
    s0 = (sl0_ref[0].astype(F32) + ahead0 * recv_ref[...].astype(F32)).astype(BF16)
    s1 = carry1[...].astype(BF16)
    carry1[...] = keep1 * carry1[...] + sf1_ref[0].astype(F32)
    s0_ref[0] = s0
    s1_ref[0] = s1
    enter_cols = factors_ref[0]
    turned = act_ref[:, inner:].astype(F32).T.astype(BF16)
    b0, c0, b1, c1 = bc_columns(act_ref, inner, state)
    enter0[...] = mm(enter_cols, e0_ref[...])
    from0[...] = mm(c0, s0)
    enter1[...] = mm(enter_cols, e1_ref[...])
    from1[...] = mm(c1, s1)
    t, s = row_iota(CHUNK), lane_iota(CHUNK)
    lower = t > s
    scores = jnp.where(lower, mm_nt(c0, b0), mm_nt(c1, b1))
    scores = jnp.where(same_sequence(first, bounds), scores, 0.0)
    columns = target_ref[...].T
    for pair in range(heads // 2):
        cols = slice(pair * 2 * width, (pair + 1) * 2 * width)
        weights = []
        for head in (2 * pair, 2 * pair + 1):
            power = jnp.where(
                lower,
                columns[:, head : head + 1] + source_ref[head : head + 1, :],
                columns[:, heads + head : heads + head + 1]
                + source_ref[heads + head : heads + head + 1, :],
            )
            weights.append((jnp.exp2(power) * scores).astype(BF16))
        x_cut = cut_pair(act_ref[:, cols], width)
        within[:, cols] = mm(jnp.concatenate(weights, axis=1), x_cut)
    tiles = [slice(tile * 128, tile * 128 + 128) for tile in range(inner // 128)]
    for row in range(0, CHUNK, small):
        rows = slice(row, row + small)
        square = jnp.zeros((small, 128), F32)
        cross = jnp.zeros((small, 128), F32)
        for cols in tiles:
            mixer = within[rows, cols] + skip_s[:, cols] * act_ref[rows, cols].astype(F32)
            mixer = mixer + enter0[rows, cols] * from0[rows, cols]
            mixer = mixer + enter1[rows, cols] * from1[rows, cols]
            z = z_ref[rows, cols].astype(F32)
            sig = jax.nn.sigmoid(z)
            gate = z * sig
            gated = mixer * gate
            square = square + gated * gated
            cross = cross + dnorm_ref[rows, cols].astype(F32) * gain_s[:, cols] * gated
            gated_s[rows, cols] = gated
            gate_s[rows, cols] = gate
            slope_s[rows, cols] = mixer * (sig + gate - gate * sig)
        live = flag(first + row + row_iota(small) < bounds[len(bounds) - 2])
        scale = lax.rsqrt(jnp.sum(square, axis=1, keepdims=True) * (1.0 / inner) + EPS)
        back = scale * scale * (jnp.sum(cross, axis=1, keepdims=True) * (1.0 / inner))
        scale = jnp.broadcast_to(scale * live, (small, 128))
        back = jnp.broadcast_to(back, (small, 128))
        for cols in tiles:
            gated = gated_s[rows, cols]
            unit = gated * scale
            gain = gain_s[:, cols]
            mixed_ref[rows, cols] = (unit * gain).astype(BF16)
            dnorm = dnorm_ref[rows, cols].astype(F32)
            sums_ref[0:8, cols] += fold(dnorm * unit)
            dgated = scale * (dnorm * gain - gated * back)
            dz_ref[rows, cols] = (dgated * slope_s[rows, cols]).astype(BF16)
            dy = dgated * gate_s[rows, cols]
            dy_ref[rows, cols] = dy.astype(BF16)
            sums_ref[8:16, cols] += fold(dy * act_ref[rows, cols].astype(F32))
            entered0 = dy * enter0[rows, cols]
            entered1 = dy * enter1[rows, cols]
            in0[rows, cols] = entered0.astype(BF16)
            in1[rows, cols] = entered1.astype(BF16)
            prod0[rows, cols] = (entered0 * from0[rows, cols]).astype(BF16)
            prod1[rows, cols] = (entered1 * from1[rows, cols]).astype(BF16)
    ones = e0_ref[0:heads, :]
    r_ref[0:heads, :] = mm_nt(ones, prod0[...])
    r_ref[heads : 2 * heads, :] = mm_nt(ones, prod1[...])
    dcc_ref[:, 0:state] = mm_nt(in0[...], s0)
    dcc_ref[:, state : 2 * state] = mm_nt(in1[...], s1)
    dl0_ref[0] = acc0[...].astype(BF16)
    acc0[...] = keep0 * acc0[...] + mm(turned[state : 2 * state], in0[...])
    df1 = mm(turned[3 * state : 4 * state], in1[...])
    df1_ref[0] = df1.astype(BF16)
    acc1[...] = acc1[...] + keeps_ref[5, pl.ds(chunk, 1), :] * df1

    @pl.when(step == pl.num_programs(0) - 1)
    def _():
        send_ref[...] = jnp.where(base > 0, acc0[...], acc1[...]).astype(BF16)


def back_kernel(
    lengths_ref,
    skip_ref,
    act_ref,
    slope_ref,
    target_ref,
    source_ref,
    factors_ref,
    dcc_ref,
    dy_ref,
    s0_ref,
    s1_ref,
    dl0_ref,
    df1_ref,
    keeps_ref,
    recv_ref,
    start_ref,
    e0_ref,
    e1_ref,
    spans_ref,
    _dpre_ref,
    _moves_ref,
    dpre_ref,
    moves_ref,
    last_ref,
    carry1,
    dscore,
    out0,
    out1,
    ds0,
    ds1,
    kept,
    *,
    skipped,
    chunks,
):
    step = pl.program_id(0)
    chunk = step + skipped
    bounds, base = sequence_bounds(lengths_ref, chunks * CHUNK)
    first = base + chunk * CHUNK
    heads = skip_ref.shape[0]
    inner = keeps_ref.shape[2]
    width = inner // heads
    state = recv_ref.shape[0]

    @pl.when(step == 0)
    def _():
        if skipped:
            carry1[...] = start_ref[...]
        else:
            recv = recv_ref[...].astype(F32)
            carry1[...] = jnp.where(base > 0, recv, jnp.zeros_like(recv))

    keep0 = keeps_ref[0, pl.ds(chunk, 1), :]
    keep1 = keeps_ref[1, pl.ds(chunk, 1), :]
    behind0 = keeps_ref[4, pl.ds(chunk, 1), :] * jnp.where(base > 0, 0.0, 1.0)
    d0 = dl0_ref[0].astype(F32) + behind0 * recv_ref[...].astype(F32)
    d1 = carry1[...]
    ds0[...] = d0.astype(BF16)
    ds1[...] = d1.astype(BF16)
    kept0 = jnp.sum(d0 * s0_ref[0].astype(F32), axis=0, keepdims=True) * keep0
    kept1 = jnp.sum(d1 * s1_ref[0].astype(F32), axis=0, keepdims=True) * keep1
    carry1[...] = keep1 * d1 + df1_ref[0].astype(F32)

    t = lane_iota(CHUNK)
    b0, c0, b1, c1 = bc_columns(act_ref, inner, state)
    same = same_sequence(first, bounds)
    both = jnp.where(row_iota(CHUNK) < t, mm_nt(b0, c0), mm_nt(b1, c1))
    both = jnp.where(same, both, 0.0)
    halves = []
    for row in range(0, CHUNK, SUB):
        early = row + row_iota(SUB) < t
        halves.append((slice(row, row + SUB), early, flag(early), both[row : row + SUB]))
    in_cols = source_ref[...].T
    leave_cols = factors_ref[0]
    dscore[...] = jnp.zeros_like(dscore)
    left = lane_iota(2 * width) < width

    def columns_of(pair):
        return slice(pair * 2 * width, (pair + 1) * 2 * width)

    def products(pair):
        cols = columns_of(pair)
        dweights = mm_nt(cut_pair(act_ref[:, cols], width), dy_ref[:, cols])
        return dweights

    def carried(pair):
        cols = columns_of(pair)
        leave0 = mm(leave_cols, e0_ref[:, cols])
        leave1 = mm(leave_cols, e1_ref[:, cols])
        return leave0, leave1, mm(b0, ds0[:, cols]), mm(b1, ds1[:, cols])

    def within(pair, dweights):
        weights, lows, alls, scored = [], [], [], [0.0] * len(halves)
        for part in (0, 1):
            head = 2 * pair + part
            parts, low_parts, all_parts = [], [], []
            sum0 = jnp.zeros((8, CHUNK), F32)
            sum1 = jnp.zeros((8, CHUNK), F32)
            for place, (rows, early, early_f, scores) in enumerate(halves):
                power = jnp.where(
                    early,
                    in_cols[rows, head : head + 1] + target_ref[head : head + 1, :],
                    in_cols[rows, heads + head : heads + head + 1]
                    + target_ref[heads + head : heads + head + 1, :],
                )
                decay = jnp.exp2(power)
                parts.append((decay * scores).astype(BF16))
                at = part * CHUNK + rows.start
                dweight = dweights[at : at + SUB] * decay
                scored[place] = scored[place] + dweight
                change = dweight * scores
                low = change * early_f
                low_parts.append(low.astype(BF16))
                all_parts.append(change.astype(BF16))
                sum0 = sum0 + fold(low)
                sum1 = sum1 + fold(change)
            weights.append(jnp.concatenate(parts, axis=0))
            lows.append(jnp.concatenate(low_parts, axis=0))
            alls.append(jnp.concatenate(all_parts, axis=0))
            moves_ref[head : head + 1, :] = jnp.sum(sum0, axis=0, keepdims=True)
            moves_ref[heads + head : heads + head + 1, :] = jnp.sum(sum1, axis=0, keepdims=True)
        for place, (rows, _, _, _) in enumerate(halves):
            dscore[rows, :] += scored[place]
        return jnp.concatenate(weights, axis=1), lows + alls

    def gathered(pair, weights, lows, states):
        cols = columns_of(pair)
        leave0, leave1, from0, from1 = states
        dx = mm(weights, cut_pair(dy_ref[:, cols], width))
        skip = jnp.where(left, skip_ref[2 * pair], skip_ref[2 * pair + 1])
        firsts, totals = [], []
        sum0 = jnp.zeros((8, 2 * width), F32)
        sum1 = jnp.zeros((8, 2 * width), F32)
        for rows, _, _, _ in halves:
            xf = act_ref[rows, cols].astype(F32)
            came0 = leave0[rows] * from0[rows]
            came1 = leave1[rows] * from1[rows]
            dconv = dx[rows] + skip * dy_ref[rows, cols].astype(F32) + came0 + came1
            dpre_ref[rows, cols] = (dconv * slope_ref[rows, cols].astype(F32)).astype(BF16)
            out0[rows, cols] = (xf * leave0[rows]).astype(BF16)
            out1[rows, cols] = (xf * leave1[rows]).astype(BF16)
            came0 = xf * came0
            came1 = xf * came1
            sum0 = sum0 + fold(came0)
            sum1 = sum1 + fold(came1)
            firsts.append(came0.astype(BF16))
            totals.append(came1.astype(BF16))
        kept[0:8, cols] = sum0
        kept[8:16, cols] = sum1
        return lows + [jnp.concatenate(firsts, axis=0), jnp.concatenate(totals, axis=0)]

    def summed(pair, lows):
        sums = mm_nt(spans_ref[...], jnp.concatenate(lows, axis=1))
        moves_ref[2 * heads + 2 * pair : 2 * heads + 2 * pair + 2, :] = sums[0:2]
        moves_ref[3 * heads + 2 * pair : 3 * heads + 2 * pair + 2, :] = sums[2:4]


    pairs = heads // 2
    ahead = {0: products(0)}
    held, done = {}, {}
    for pair in range(pairs + 2):
        if pair + 1 < pairs:
            ahead[pair + 1] = products(pair + 1)
        if 0 < pair <= pairs:
            weights, lows = held.pop(pair - 1)
            states = carried(pair - 1)
            done[pair - 1] = gathered(pair - 1, weights, lows, states)
        if pair < pairs:
            held[pair] = within(pair, ahead.pop(pair))
        if pair > 1:
            summed(pair - 2, done.pop(pair - 2))
    dscores = jnp.where(same, dscore[...], 0.0)
    dscore0 = jnp.where(row_iota(CHUNK) < t, dscores, 0.0).astype(BF16)
    dscore1 = jnp.where(row_iota(CHUNK) < t, 0.0, dscores).astype(BF16)
    kept[0:1, :] += kept0
    kept[8:9, :] += kept1
    kept_sum = mm_nt(e0_ref[0:heads, :], in_parts(kept[...], 2).astype(BF16))
    kept_sum = kept_sum[:, 0:16] + kept_sum[:, 16:32]
    for direction in (0, 1):
        column = jnp.sum(kept_sum[:, 8 * direction : 8 * direction + 8], axis=1, keepdims=True)
        moves_ref[(4 + direction) * heads : (5 + direction) * heads, :] = jnp.broadcast_to(
            column, (heads, CHUNK)
        )
    db0 = mm(dscore0, c0) + mm_nt(out0[...], ds0[...])
    db1 = mm(dscore1, c1) + mm_nt(out1[...], ds1[...])
    dc0 = mm_tn(dscore0, b0) + dcc_ref[:, 0:state]
    dc1 = mm_tn(dscore1, b1) + dcc_ref[:, state : 2 * state]
    dbc = jnp.concatenate([db0, dc0, db1, dc1], axis=1)
    dpre_ref[:, inner:] = (dbc * slope_ref[:, inner:].astype(F32)).astype(BF16)

    @pl.when(step == pl.num_programs(0) - 1)
    def _():
        last_ref[...] = carry1[...]


def steps_back(raw, dt, rate, moves, r):
    steps = raw.shape[0]
    heads = steps // 2
    chunks = raw.shape[1] // CHUNK
    s, t = row_iota(CHUNK), lane_iota(CHUNK)

    def stack(values):
        parts = [values[:, chunk * CHUNK : (chunk + 1) * CHUNK] for chunk in range(chunks)]
        return jnp.concatenate(parts, axis=0)

    def unstack(values):
        parts = [values[chunk * heads : (chunk + 1) * heads] for chunk in range(chunks)]
        return jnp.concatenate(parts, axis=1)

    got0, got, own0, own, kept0, kept1 = [
        moves[part * heads : (part + 1) * heads] for part in range(6)
    ]
    own1, got1 = own - own0, got - got0
    da0 = exact_mm(stack(got0 + r[:heads] - own0), flag(s >= t))
    da1 = exact_mm(stack(got1 + r[heads:] - own1), flag(s <= t))
    da = -jnp.concatenate([unstack(da0) + kept0, unstack(da1) + kept1], axis=0)
    dlog = jnp.concatenate([own0, own1], axis=0)
    sig = jax.nn.sigmoid(raw)
    ratio = jnp.where(raw < -20.0, 1.0, sig / jnp.maximum(dt, 1e-37))
    return dlog * ratio + da * rate * sig, jnp.sum(da * dt, axis=1, keepdims=True) * rate


def by_core(product, shard, mine_ref, theirs_ref):
    pieces = [product[place : place + shard] for place in range(0, product.shape[0], shard)]
    even = jnp.concatenate(pieces[0::2], axis=0)
    odd = jnp.concatenate(pieces[1::2], axis=0)
    core = lax.rem(lax.axis_index("dp"), 2)

    @pl.when(core == 0)
    def _():
        mine_ref[...] = even
        theirs_ref[...] = odd

    @pl.when(core == 1)
    def _():
        mine_ref[...] = odd
        theirs_ref[...] = even


def weights_kernel(
    turned_ref, dz_ref, mixed_ref, c_ref, wz_ref, mine_ref, theirs_ref, gain_ref, *, shard
):
    product = mm_tn(mixed_ref[...], c_ref[...]).astype(BF16)
    pieces = []
    for place in range(0, product.shape[0], 2 * shard):
        pieces.append(
            jnp.concatenate(
                [product[place : place + shard], product[place + shard : place + 2 * shard]], axis=1
            )
        )
    gate = mm(turned_ref[...], dz_ref[...])
    both = jnp.concatenate([jnp.concatenate(pieces, axis=0), gate.astype(BF16)], axis=1)
    by_core(both, shard, mine_ref, theirs_ref)
    share = (gate * wz_ref[...].astype(F32)).astype(BF16)
    gain_ref[0] = mm_nt(jnp.ones((8, share.shape[1]), BF16), share)[0:1]


def conv_back_kernel(
    lengths_ref,
    turned_ref,
    turnhalo_ref,
    dpre_ref,
    pre_ref,
    prehalo_ref,
    taps_ref,
    raw_ref,
    dt_ref,
    rate_ref,
    moves_ref,
    r_ref,
    w_ref,
    narrow_ref,
    gain_ref,
    share_ref,
    mix_sums_ref,
    e0_ref,
    dproj_ref,
    dhalo_ref,
    mine_ref,
    theirs_ref,
    draw_ref,
    small_ref,
    shift,
    buf,
    gains,
    sums_ref,
    *,
    shard,
):
    step = pl.program_id(0)
    count, wide = dpre_ref.shape
    chunks = count // CHUNK
    steps = raw_ref.shape[0]
    bounds, base = sequence_bounds(lengths_ref, count)

    @pl.when(step == 0)
    def _():
        for chunk in range(chunks):
            shift[chunk * 3 * CHUNK : (chunk + 1) * 3 * CHUNK, :] = shifts(
                base + chunk * CHUNK, bounds, 1, CHUNK
            )
        shift[chunks * 3 * CHUNK :, :] = shifts(base, bounds, 0, 16)
        buf[...] = jnp.zeros_like(buf)
        gains[...] = jnp.zeros_like(gains)
        sums_ref[...] = jnp.zeros_like(sums_ref)

    last = pl.num_programs(0) - 1
    inner = w_ref.shape[1]
    tile_here = pl.ds(pl.multiple_of(step * wide, wide), wide)

    def hand_over(product, weights):
        share = (product * weights.astype(F32)).astype(BF16)
        gains[...] += mm_nt(jnp.ones((8, share.shape[1]), BF16), share)
        by_core(product.astype(BF16), shard, mine_ref, theirs_ref)

    @pl.when(step < pl.num_programs(0) - 1)
    def _():
        buf[0:CHUNK, :] = dpre_ref[count - CHUNK :, :]
        moved = mm(shift[chunks * 3 * CHUNK :, :], dpre_ref[0 : CHUNK + 16, :])
        halo_sums = [None] * 4
        dproj = jnp.zeros((16, wide), F32)
        pre = prehalo_ref[...].astype(F32)
        for lag in (1, 2, 3):
            part = moved[(lag - 1) * 16 : lag * 16]
            dproj = dproj + part * taps_ref[3 - lag : 4 - lag, :]
            halo_sums[3 - lag] = jnp.sum(pre * part, axis=0, keepdims=True)
        halo_sums[3] = jnp.zeros((1, wide), F32)
        dhalo_ref[...] = dproj.astype(BF16)
        sums = [[jnp.zeros((8, 128), F32) for _ in range(4)] for _ in range(wide // 128)]
        for chunk in range(chunks):
            if chunk < chunks - 1:
                pair = dpre_ref[chunk * CHUNK : chunk * CHUNK + CHUNK + 16, :]
            else:
                pair = buf[...]
            moved = mm(shift[chunk * 3 * CHUNK : (chunk + 1) * 3 * CHUNK, :], pair)
            for place in range(wide // 128):
                cols = slice(place * 128, place * 128 + 128)
                for row in range(0, CHUNK, SUB):
                    span = slice(chunk * CHUNK + row, chunk * CHUNK + row + SUB)
                    pre = pre_ref[span, cols].astype(F32)
                    here = dpre_ref[span, cols].astype(F32)
                    dproj = here * taps_ref[3:4, cols]
                    sums[place][3] = sums[place][3] + fold(pre * here)
                    for lag in (1, 2, 3):
                        at = (lag - 1) * CHUNK + row
                        part = moved[at : at + SUB, cols]
                        dproj = dproj + part * taps_ref[3 - lag : 4 - lag, cols]
                        sums[place][3 - lag] = sums[place][3 - lag] + fold(pre * part)
                    dproj_ref[span, cols] = dproj.astype(BF16)
        for place in range(wide // 128):
            cols = slice(place * 128, place * 128 + 128)
            at = pl.ds(pl.multiple_of(step * wide + place * 128, 128), 128)
            for tap in range(4):
                sums_ref[tap : tap + 1, at] = (
                    jnp.sum(sums[place][tap], axis=0, keepdims=True) + halo_sums[tap][:, cols]
                )
        product = mm(turned_ref[...], dproj_ref[...]) + mm(turnhalo_ref[...], dhalo_ref[...])

        @pl.when(step < last - 1)
        def _():
            hand_over(product, w_ref[:, tile_here])

        @pl.when(step == last - 1)
        def _():
            hand_over(product, narrow_ref[0:wide, :].astype(F32).T)

    @pl.when(step == pl.num_programs(0) - 1)
    def _():
        rate = rate_ref[:, 0:1]
        draw, drate = steps_back(raw_ref[...], dt_ref[...], rate, moves_ref[...], r_ref[...])
        low = draw.astype(BF16)
        draw_ref[...] = low
        product = mm_nt(turned_ref[...], low)
        fill = jnp.zeros((product.shape[0], wide - steps), F32)
        steps_weights = narrow_ref[narrow_ref.shape[0] - steps :, :].astype(F32).T
        hand_over(
            jnp.concatenate([product, fill], axis=1),
            jnp.concatenate([steps_weights, fill], axis=1),
        )
        heads = steps // 2
        model = w_ref.shape[0]
        sums_ref[4:5, 0:inner] = jnp.sum(mix_sums_ref[0:8, :], axis=0, keepdims=True)
        share = jnp.concatenate([share_ref[part] for part in range(share_ref.shape[0])], axis=1)
        sums_ref[5:6, 0:model] = (gains[0:1, :] + share) / row_of(gain_ref)
        skips = in_parts(mix_sums_ref[8:16, :], 2).astype(BF16)
        skips = jnp.sum(mm_nt(e0_ref[0:heads, :], skips), axis=1, keepdims=True)
        columns = [jnp.concatenate([skips, skips], axis=0), jnp.sum(draw, axis=1, keepdims=True)]
        columns = jnp.concatenate(columns + [drate, jnp.zeros((steps, 5), F32)], axis=1).T
        for place in range(3):
            sums_ref[6:7, 128 * place : 128 * place + steps] = columns[place : place + 1]
        small_ref[...] = narrowed(two_halves(sums_ref[...]))


def halve_kernel(kept_ref, got_ref, keep_ref, send_ref, *, bit):
    shard = keep_ref.shape[0]
    mine = lax.rem(lax.axis_index("dp") // bit, 2)
    for place, out_ref in ((mine, keep_ref), (1 - mine, send_ref)):
        rows = pl.ds(pl.multiple_of(place * shard, shard), shard)
        total = kept_ref[rows, :].astype(F32) + got_ref[rows, :].astype(F32)
        out_ref[...] = total.astype(out_ref.dtype)


def sum_kernel(kept_ref, got_ref, out_ref):
    out_ref[...] = (kept_ref[...].astype(F32) + got_ref[...].astype(F32)).astype(BF16)


def narrowed(small):
    few = small[6:7] + small[7:8]
    high = few.astype(BF16).astype(F32)
    return jnp.concatenate([small[0:6], high, few - high, small[8:16]], axis=0).astype(BF16)


def two_halves(small):
    half = small.shape[1] // 2
    return jnp.concatenate([small[:, 0:half], small[:, half:]], axis=0)


def quarters_kernel(
    mine_ref,
    got_ref,
    small_ref,
    smallgot_ref,
    keep_ref,
    across_ref,
    along_ref,
    both_ref,
    *,
    shard,
):
    half = mine_ref.shape[1] // 2
    row_bit = lax.rem(lax.axis_index("dp") // 2, 2)
    side = lax.axis_index("dir")
    count = mine_ref.shape[0] // 2
    small = narrowed(small_ref[...].astype(F32) + smallgot_ref[...].astype(F32))
    keep_ref[count:, :] = small.astype(F32)
    for out_ref, row, column in (
        (keep_ref, row_bit, side),
        (across_ref, row_bit, 1 - side),
        (along_ref, 1 - row_bit, side),
        (both_ref, 1 - row_bit, 1 - side),
    ):
        if out_ref is not keep_ref:
            out_ref[count:, :] = small
        for place in range(count // shard):
            rows = slice(place * shard, (place + 1) * shard)
            here = pl.ds(pl.multiple_of((2 * place + row) * shard, shard), shard)
            cols = pl.ds(pl.multiple_of(column * half, half), half)
            total = mine_ref[here, cols].astype(F32) + got_ref[here, cols].astype(F32)
            out_ref[rows, :] = total.astype(out_ref.dtype)


def levels_kernel(keep_ref, a_ref, b_ref, c_ref, own_ref, s1_ref, s2_ref, s3_ref, *, shard):
    level = lax.axis_index("dp") // 4
    count = 4 * shard
    small = [ref[count:, :].astype(F32) for ref in (a_ref, b_ref, c_ref)]
    small = narrowed(keep_ref[count:, :] + small[0] + (small[1] + small[2]))
    own_ref[shard:, :] = small.astype(F32)
    for bits, out_ref in enumerate((own_ref, s1_ref, s2_ref, s3_ref)):
        wanted = jnp.bitwise_xor(level, bits)
        rows = pl.ds(pl.multiple_of(wanted * shard, shard), shard)
        total = keep_ref[rows, :] + a_ref[rows, :].astype(F32)
        total = total + (b_ref[rows, :].astype(F32) + c_ref[rows, :].astype(F32))
        out_ref[0:shard, :] = total.astype(out_ref.dtype)
        if bits:
            out_ref[shard:, :] = small


def last_kernel(own_ref, a_ref, b_ref, c_ref, out_ref, small_ref, *, shard):
    total = own_ref[...] + a_ref[...].astype(F32)
    total = total + (b_ref[...].astype(F32) + c_ref[...].astype(F32))
    out_ref[...] = total[0:shard].astype(BF16)
    small_ref[...] = total[shard:]


def finish_kernel(
    late_ref,
    lategot_ref,
    early_ref,
    earlygot_ref,
    small_ref,
    gx_ref,
    gz_ref,
    gbc_ref,
    go_ref,
    gtaps_ref,
    gmix_ref,
    gin_ref,
    gskip_ref,
    gbias_ref,
    galog_ref,
):
    side = lax.axis_index("dir")
    half = late_ref.shape[1]
    inner = gx_ref.shape[1]
    model = go_ref.shape[1]
    shard = gx_ref.shape[0]
    mine = late_ref[...].astype(F32)
    other = lategot_ref[...].astype(F32)
    first = jnp.where(side == 0, mine, other)
    second = jnp.where(side == 0, other, mine)
    gx_ref[:, 0:half] = first
    gx_ref[:, half:inner] = second[:, 0 : inner - half]
    gbc_ref[...] = second[:, inner - half : inner - half + gbc_ref.shape[1]]
    early = early_ref[...].astype(F32) + earlygot_ref[...].astype(F32)
    go_ref[0:shard, :] = early[:, 0:model]
    go_ref[shard : 2 * shard, :] = early[:, model : 2 * model]
    gz_ref[...] = early[:, 2 * model :]
    small = jnp.concatenate([small_ref[0:8, :], small_ref[8:16, :]], axis=1)
    gtaps_ref[...] = small[0:4, 0 : gtaps_ref.shape[1]]
    gmix_ref[...] = small[4:5, 0:inner].reshape(inner)
    gin_ref[...] = small[5:6, 0:model].reshape(model)
    few = small[6:7] + small[7:8]
    heads = gskip_ref.shape[0]
    gskip_ref[...] = few[:, 0:128].reshape(128)[0:heads]
    gbias_ref[0:1, :] = few[:, 128 : 128 + heads]
    gbias_ref[1:2, :] = few[:, 128 + heads : 128 + 2 * heads]
    galog_ref[0:1, :] = few[:, 256 : 256 + heads]
    galog_ref[1:2, :] = few[:, 256 + heads : 256 + 2 * heads]


def inputs_kernel(
    x_ref,
    c_ref,
    gain_ref,
    dproj_ref,
    dhalo_ref,
    draw_ref,
    dz_ref,
    wx_ref,
    wbc_ref,
    wz_ref,
    mixed_ref,
    wo_ref,
    gin_ref,
    out_ref,
    dproj,
):
    step = pl.program_id(0)
    inner = wx_ref.shape[1]
    steps = draw_ref.shape[0]
    narrow = wbc_ref.shape[0] - steps

    @pl.when(step == pl.num_programs(0) - 1)
    def _():
        tail = slice(dproj_ref.shape[0] - 16, dproj_ref.shape[0])
        both = dproj_ref[tail, :].astype(F32) + dhalo_ref[...].astype(F32)
        dproj[...] = dproj_ref[...]
        dproj[tail, :] = both.astype(BF16)

    @pl.when(step < pl.num_programs(0) - 1)
    def _():
        dproj[...] = dproj_ref[...]

    dn = mm_nt(dproj[:, 0:inner], wx_ref[...])
    dn = dn + mm_nt(dz_ref[...], wz_ref[...])
    dn = dn + mm(dproj[:, inner:], wbc_ref[0:narrow, :])
    dn = dn + mm_tn(draw_ref[...], wbc_ref[narrow:, :])
    x = x_ref[...].astype(F32)
    inv = lax.rsqrt(jnp.mean(x * x, axis=1, keepdims=True) + EPS)
    unit = x * inv
    out_ref[...] = (x + mm(mixed_ref[...], wo_ref[...])).astype(BF16)
    f = dn * row_of(gain_ref)
    back = inv * (f - unit * jnp.mean(f * unit, axis=1, keepdims=True))
    gin_ref[...] = (c_ref[...].astype(F32) + back).astype(BF16)


def smem():
    return pl.BlockSpec(memory_space=pltpu.SMEM)


def resident():
    return pl.BlockSpec(memory_space=pltpu.VMEM)


def anywhere():
    return pl.BlockSpec(memory_space=pl.ANY)


def whole(shape):
    return pl.BlockSpec(shape, lambda i: (0,) * len(shape), pipeline_mode=pl.Buffered(1))


def rows_of(count, width):
    return pl.BlockSpec((count, width), lambda i: (i, 0))


def lanes_of(height, count):
    return pl.BlockSpec((height, count), lambda i: (0, i))


def parts_of(count, *rest):
    return pl.BlockSpec((count,) + rest, lambda i: (i,) + (0,) * len(rest))


def cost(microseconds):
    flops = int(microseconds * 1.15e9)
    return pl.CostEstimate(flops=flops, bytes_accessed=0, transcendentals=0)


def call(kernel, name, grid, in_specs, outs, scratch, cost_us, args, vmem, aliases=()):
    return pl.pallas_call(
        kernel,
        name=name,
        grid=(grid,),
        in_specs=in_specs,
        out_specs=[spec for spec, _, _ in outs],
        out_shape=[jax.ShapeDtypeStruct(shape, dtype) for _, shape, dtype in outs],
        scratch_shapes=scratch,
        input_output_aliases=dict(aliases),
        compiler_params=pltpu.CompilerParams(
            vmem_limit_bytes=vmem * MIB, dimension_semantics=("arbitrary",)
        ),
        cost_estimate=cost(cost_us),
    )(*args)


def traded(values, axis, bit, size):
    return lax.ppermute(values, axis, [(i, i ^ bit) for i in range(size)])


def ordered(first, second):
    return lax.optimization_barrier((first, second))


def sum_shards(grad, dp_count):
    index = lax.axis_index("dp")
    held = grad.reshape(dp_count, grad.shape[0] // dp_count, grad.shape[1])
    bit = 1
    while bit < dp_count:
        paired = held.reshape(held.shape[0] // 2, 2, held.shape[1], held.shape[2])
        mine = (index // bit) % 2
        kept = lax.dynamic_index_in_dim(paired, mine, 1, keepdims=False)
        sent = lax.dynamic_index_in_dim(paired, 1 - mine, 1, keepdims=False).astype(BF16)
        held = kept.astype(F32) + traded(sent, "dp", bit, dp_count).astype(F32)
        bit *= 2
    held = held[0].astype(BF16)
    return held.astype(F32) + traded(held, "dir", 1, 2).astype(F32)


def sum_all(values, dp_count):
    bit = 1
    while bit < dp_count:
        values = values + traded(values, "dp", bit, dp_count)
        bit *= 2
    return values + traded(values, "dir", 1, 2)


def local(
    dp_count,
    hidden_in,
    lengths,
    gain_in,
    w_x,
    w_z,
    w_bcdt,
    conv_w,
    dt_bias,
    a_log,
    d_skip,
    gain_mix,
    w_out,
    cotangent,
):
    x = hidden_in[0]
    cot = cotangent[0]
    count, model = x.shape
    inner = w_x.shape[1]
    channels = conv_w.shape[1]
    heads = d_skip.shape[0]
    width = inner // heads
    state = (channels - inner) // 4
    chunks = count // CHUNK
    steps = 2 * heads

    w_narrow = w_bcdt.T
    halo = lax.ppermute(x[count - 16 :], "dir", [(0, 1)])

    spread = np.repeat(np.eye(heads, dtype=np.float32), width, axis=1)
    zeros = np.zeros_like(spread)
    e0 = jnp.asarray(np.concatenate([spread, zeros, spread, zeros]), BF16)
    e1 = jnp.asarray(np.concatenate([zeros, spread, zeros, spread]), BF16)
    spans = np.zeros((8, 6 * CHUNK), np.float32)
    for head in range(2):
        columns = slice(head * width, (head + 1) * width)
        spans[head, head * CHUNK : (head + 1) * CHUNK] = 1.0
        spans[head, 4 * CHUNK : 5 * CHUNK][columns] = 1.0
        spans[2 + head, (2 + head) * CHUNK : (3 + head) * CHUNK] = 1.0
        spans[2 + head, 4 * CHUNK : 5 * CHUNK][columns] = 1.0
        spans[2 + head, 5 * CHUNK : 6 * CHUNK][columns] = 1.0
    spans = jnp.asarray(spans, BF16)

    def rows_out(size, columns, dtype):
        return (rows_of(size, columns), (count, columns), dtype)

    def full(shape, dtype):
        return (pl.BlockSpec(shape, lambda i: (0,) * len(shape)), shape, dtype)

    per = ROWS // CHUNK
    state_f32 = pltpu.VMEM((state, inner), F32)
    state_bf16 = pltpu.VMEM((state, inner), BF16)
    row_f32 = pltpu.VMEM((1, inner), F32)
    chunk_f32 = pltpu.VMEM((CHUNK, inner), F32)
    chunk_bf16 = pltpu.VMEM((CHUNK, inner), BF16)
    (
        normed,
        raw,
        dt,
        rate,
        target,
        source,
        factors,
        keeps,
        pre,
        act,
        slope,
        sl0,
        sf1,
        send,
        pre_halo,
        turn_halo,
    ) = call(
        proj_kernel,
        "proj",
        count // ROWS,
        [
            smem(),
            smem(),
            smem(),
            whole((count, model)),
            whole((16, model)),
            whole((model,)),
            whole((model, inner)),
            whole(w_narrow.shape),
            whole(conv_w.shape),
            whole(e0.shape),
            whole(e1.shape),
        ],
        [
            full((count, model), BF16),
            full((steps, count), F32),
            full((steps, count), F32),
            full((steps, 128), F32),
            full((steps, count), F32),
            full((steps, count), F32),
            full((2, count, 2 * steps), BF16),
            full((6, chunks, inner), F32),
            rows_out(ROWS, channels, BF16),
            rows_out(ROWS, channels, BF16),
            rows_out(ROWS, channels, BF16),
            (parts_of(per, state, inner), (chunks, state, inner), BF16),
            (parts_of(per, state, inner), (chunks, state, inner), BF16),
            full((state, inner), BF16),
            full((16, channels), BF16),
            full((model, 16), BF16),
        ],
        [
            pltpu.VMEM((16 + ROWS, channels), BF16),
            state_f32,
            state_f32,
            chunk_bf16,
            chunk_bf16,
        ],
        US_PROJ,
        (lengths, dt_bias, a_log, x, halo, gain_in, w_x, w_narrow, conv_w, e0, e1),
        VMEM_PROJ,
    )
    received = lax.ppermute(send, "dir", SWAP)

    gate_z, d_norm, turned = call(
        gates_kernel,
        "gates",
        count // ROWS,
        [
            rows_of(ROWS, model),
            rows_of(ROWS, model),
            whole((model, inner)),
            whole((inner, model)),
        ],
        [
            rows_out(ROWS, inner, BF16),
            rows_out(ROWS, inner, BF16),
            (lanes_of(model, ROWS), (model, count), BF16),
        ],
        [],
        US_GATES,
        (normed, cot, w_z, w_out),
        VMEM_GATES,
    )

    def down_rows(width):
        return pl.BlockSpec((CHUNK, width), lambda i: (chunks - 1 - i, 0))

    def down_lanes(height):
        return pl.BlockSpec((height, CHUNK), lambda i: (0, chunks - 1 - i))

    def down_parts(*rest):
        return pl.BlockSpec((1,) + rest, lambda i: (chunks - 1 - i,) + (0,) * len(rest))

    states = (down_parts(state, inner), (chunks, state, inner), BF16)
    mixed, dz, dy, r, dcc, dl0, df1, s0, s1, d_send, mix_sums = call(
        mix_kernel,
        "mix",
        chunks,
        [
            smem(),
            smem(),
            down_rows(channels),
            down_lanes(steps),
            down_lanes(steps),
            pl.BlockSpec((1, CHUNK, 2 * steps), lambda i: (0, chunks - 1 - i, 0)),
            down_parts(state, inner),
            down_parts(state, inner),
            whole((6, chunks, inner)),
            whole((state, inner)),
            down_rows(inner),
            down_rows(inner),
            whole((inner,)),
            whole(e0.shape),
            whole(e1.shape),
        ],
        [
            (down_rows(inner), (count, inner), BF16),
            (down_rows(inner), (count, inner), BF16),
            (down_rows(inner), (count, inner), BF16),
            (down_lanes(steps), (steps, count), F32),
            (down_rows(2 * state), (count, 2 * state), F32),
            states,
            states,
            states,
            states,
            full((state, inner), BF16),
            full((16, inner), F32),
        ],
        [state_f32] * 3 + [chunk_f32] * 8 + [chunk_bf16] * 4 + [row_f32] * 2,
        US_MIX,
        (
            lengths,
            d_skip,
            act,
            target,
            source,
            factors,
            sl0,
            sf1,
            keeps,
            received,
            gate_z,
            d_norm,
            gain_mix,
            e0,
            e1,
        ),
        VMEM_MIX,
    )
    d_received = lax.ppermute(d_send, "dir", SWAP)

    def plain(kernel, name, args, outs, specs=None, out_specs=None, grid=()):
        resident = [pl.BlockSpec(memory_space=pltpu.VMEM)]
        return pl.pallas_call(
            kernel,
            name=name,
            grid=grid,
            in_specs=specs or resident * len(args),
            out_specs=out_specs or resident * len(outs),
            out_shape=[jax.ShapeDtypeStruct(shape, dtype) for shape, dtype in outs],
            compiler_params=pltpu.CompilerParams(vmem_limit_bytes=VMEM_SUMS * MIB),
            cost_estimate=cost(US_SUMS),
        )(*args)

    def halve(name, kept, got, bit):
        rows, wide = got.shape
        outs = [((rows // 2, wide), F32), ((rows // 2, wide), BF16)]
        return plain(
            functools.partial(halve_kernel, bit=bit),
            name,
            (kept, got),
            outs,
            [rows_of(2 * piece, wide)] * 2,
            [rows_of(piece, wide)] * 2,
            (rows // (2 * piece),),
        )

    blocks = 4
    shard = model // dp_count
    direct = dp_count == 16 and shard % 16 == 0
    piece = model // 16
    early_rows = (rows_of(model // 2 // blocks, 2 * inner), (model // 2, 2 * inner), BF16)
    early_mine, early_theirs, z_share = call(
        functools.partial(weights_kernel, shard=piece),
        "weights",
        blocks,
        [
            rows_of(model // blocks, count),
            whole((count, inner)),
            lanes_of(count, inner // blocks),
            whole((count, model)),
            rows_of(model // blocks, inner),
        ],
        [
            early_rows,
            early_rows,
            (pl.BlockSpec((1, 1, model // blocks), lambda i: (i, 0, 0)), (blocks, 1, model // blocks), F32),
        ],
        [],
        US_WEIGHTS,
        (turned, dz, mixed, cot, w_z),
        VMEM_WEIGHTS,
    )
    (early_mine, early_theirs), d_received = ordered((early_mine, early_theirs), d_received)

    def back(skipped, taken, start, dpre, moves):
        def rows_from(width):
            return pl.BlockSpec((CHUNK, width), lambda i: (i + skipped, 0))

        def lanes_from(height):
            return pl.BlockSpec((height, CHUNK), lambda i: (0, i + skipped))

        def parts_from(*rest):
            return pl.BlockSpec((1,) + rest, lambda i: (i + skipped,) + (0,) * len(rest))

        return call(
            functools.partial(back_kernel, skipped=skipped, chunks=chunks),
            "back" + str(skipped),
            taken,
            [
                smem(),
                smem(),
                rows_from(channels),
                rows_from(channels),
                lanes_from(steps),
                lanes_from(steps),
                pl.BlockSpec((1, CHUNK, 2 * steps), lambda i: (1, i + skipped, 0)),
                rows_from(2 * state),
                rows_from(inner),
                parts_from(state, inner),
                parts_from(state, inner),
                parts_from(state, inner),
                parts_from(state, inner),
                whole((6, chunks, inner)),
                whole((state, inner)),
                whole(start.shape),
                whole(e0.shape),
                whole(e1.shape),
                whole(spans.shape),
                anywhere(),
                anywhere(),
            ],
            [
                (rows_from(channels), (count, channels), BF16),
                (lanes_from(6 * heads), (6 * heads, count), F32),
                full((state, inner), F32),
            ],
            [
                state_f32,
                pltpu.VMEM((CHUNK, CHUNK), F32),
            ]
            + [chunk_bf16] * 2
            + [state_bf16] * 2
            + [pltpu.VMEM((16, inner), F32)],
            US_BACK * taken // chunks,
            (
                lengths,
                d_skip,
                act,
                slope,
                target,
                source,
                factors,
                dcc,
                dy,
                s0,
                s1,
                dl0,
                df1,
                keeps,
                d_received,
                start,
                e0,
                e1,
                spans,
                dpre,
                moves,
            ),
            VMEM_BACK,
            {19: 0, 20: 1} if skipped else {},
        )

    first = 1
    dpre, moves, carry = back(0, first, d_received, received, received)
    if direct:
        early_got = traded(early_theirs, "dp", 1, dp_count)
        early_keep, early_send = halve("halve_y", early_mine, early_got, 2)
        early_send, carry = ordered(early_send, carry)
        early_got = traded(early_send, "dp", 2, dp_count)
    dpre, moves, _ = back(first, chunks - first, carry, dpre, moves)
    if direct:
        early_keep, early_send = halve("halve_z", early_keep, early_got, 4)
        early_send, dpre = ordered(early_send, dpre)
        early_got = traded(early_send, "dp", 4, dp_count)

    tile = 256
    tiles = channels // tile
    def tile_of(height):
        return pl.BlockSpec((height, tile), lambda i: (0, jnp.minimum(i, tiles - 1)))

    wide = (tiles + 1) * tile
    late_out = (lanes_of(model // 2, tile), (model // 2, wide), BF16)
    dproj, dhalo, late_mine, late_theirs, draw, small = call(
        functools.partial(conv_back_kernel, shard=piece),
        "conv_back",
        tiles + 1,
        [
            smem(),
            whole((model, count)),
            whole((model, 16)),
            tile_of(count),
            tile_of(count),
            tile_of(16),
            tile_of(conv_w.shape[0]),
            whole((steps, count)),
            whole((steps, count)),
            whole((steps, 128)),
            whole((6 * heads, count)),
            whole((steps, count)),
            whole((model, inner)),
            whole(w_narrow.shape),
            whole((model,)),
            whole(z_share.shape),
            whole(mix_sums.shape),
            whole(e0.shape),
        ],
        [
            (tile_of(count), (count, channels), BF16),
            (tile_of(16), (16, channels), BF16),
            late_out,
            late_out,
            full((steps, count), BF16),
            full((16, wide // 2), BF16),
        ],
        [
            pltpu.VMEM((3 * count + 48, CHUNK + 16), BF16),
            pltpu.VMEM((CHUNK + 16, tile), BF16),
            pltpu.VMEM((8, model), F32),
            pltpu.VMEM((8, wide), F32),
        ],
        US_CONV,
        (
            lengths,
            turned,
            turn_halo,
            dpre,
            pre,
            pre_halo,
            conv_w,
            raw,
            dt,
            rate,
            moves,
            r,
            w_x,
            w_narrow,
            gain_in,
            z_share,
            mix_sums,
            e0,
        ),
        VMEM_CONV,
    )
    d_halo = lax.ppermute(dhalo, "dir", [(1, 0)])

    grad_in, out = call(
        inputs_kernel,
        "inputs",
        count // ROWS,
        [
            rows_of(ROWS, model),
            rows_of(ROWS, model),
            whole((model,)),
            rows_of(ROWS, channels),
            whole((16, channels)),
            lanes_of(steps, ROWS),
            rows_of(ROWS, inner),
            whole((model, inner)),
            whole(w_narrow.shape),
            whole((model, inner)),
            rows_of(ROWS, inner),
            whole((inner, model)),
        ],
        [rows_out(ROWS, model, BF16), rows_out(ROWS, model, BF16)],
        [pltpu.VMEM((ROWS, channels), BF16)],
        US_INPUTS,
        (x, cot, gain_in, dproj, d_halo, draw, dz, w_x, w_narrow, w_z, mixed, w_out),
        VMEM_INPUTS,
    )

    if not direct:
        def undivided(mine, theirs):
            even = lax.axis_index("dp") % 2 == 0
            both = [jnp.where(even, mine, theirs), jnp.where(even, theirs, mine)]
            both = [part.reshape(8, 1, piece, part.shape[1]) for part in both]
            return jnp.concatenate(both, axis=1).reshape(model, mine.shape[1])

        early = undivided(early_mine, early_theirs)
        g_out = early[:, :inner].reshape(16, piece, 2, model).transpose(0, 2, 1, 3)
        late = sum_shards(undivided(late_mine, late_theirs), dp_count)
        small = jnp.concatenate([small[0:8], small[8:16]], axis=1).astype(F32)
        small = sum_all(small, dp_count)
        return (
            out[None],
            grad_in[None],
            late[:, :inner],
            sum_shards(early[:, inner:], dp_count),
            late[:, inner : inner + 4 * state + steps],
            sum_shards(g_out.reshape(inner, model), dp_count),
            small[5, :model],
            small[0:4, :channels],
            small[6, 128 : 128 + steps].reshape(dt_bias.shape),
            small[6, 256 : 256 + steps].reshape(a_log.shape),
            small[6, :heads],
            small[4, :inner],
        )

    early_got, late_theirs = ordered(early_got, late_theirs)
    late_got = traded(late_theirs, "dp", 1, dp_count)
    small_got = traded(small, "dp", 1, dp_count)
    quarter = (model // 4 + 16, wide // 2)
    kept, across, along, both = plain(
        functools.partial(quarters_kernel, shard=piece),
        "quarters",
        (late_mine, late_got, small, small_got),
        [((model // 4 + 16, wide // 2), F32), (quarter, BF16), (quarter, BF16), (quarter, BF16)],
    )
    early_got, both = ordered(early_got, both)
    early_keep, early_send = halve("halve_z2", early_keep, early_got, 8)
    corners = [(a, b) for a in range(2) for b in range(dp_count)]
    across = traded(across, "dir", 1, 2)
    along = traded(along, "dp", 2, dp_count)
    both = lax.ppermute(
        both,
        ("dir", "dp"),
        [(a * dp_count + b, (1 - a) * dp_count + (b ^ 2)) for a, b in corners],
    )
    early_got = traded(early_send, "dp", 8, dp_count)
    (early,) = plain(sum_kernel, "early_sum", (early_keep, early_got), [((piece, 2 * inner), BF16)])
    grad_in, early, both = lax.optimization_barrier((grad_in, early, both))
    early_got = traded(early, "dir", 1, 2)
    message = (piece + 16, wide // 2)
    own, *sends = plain(
        functools.partial(levels_kernel, shard=piece),
        "levels",
        (kept, across, along, both),
        [((piece + 16, wide // 2), F32)] + [(message, BF16)] * 3,
    )
    gots = [traded(sent, "dp", 4 * bits, dp_count) for bits, sent in zip((1, 2, 3), sends)]
    late, small = plain(
        functools.partial(last_kernel, shard=piece),
        "last",
        (own, *gots),
        [((piece, wide // 2), BF16), ((16, wide // 2), F32)],
    )
    late_got = traded(late, "dir", 1, 2)
    g_x, g_zz, g_bc, g_o, g_taps, g_mix, g_in, g_skip, g_bias, g_alog = plain(
        finish_kernel,
        "finish",
        (late, late_got, early, early_got, small),
        [
            ((piece, inner), F32),
            ((piece, inner), F32),
            ((piece, w_bcdt.shape[1]), F32),
            ((2 * piece, model), F32),
            (conv_w.shape, F32),
            ((inner,), F32),
            ((model,), F32),
            ((heads,), F32),
            (dt_bias.shape, F32),
            (a_log.shape, F32),
        ],
    )
    return (
        out[None],
        grad_in[None],
        g_x,
        g_zz,
        g_bc,
        g_o,
        g_in,
        g_taps,
        g_bias,
        g_alog,
        g_skip,
        g_mix,
    )


def solution(mesh):
    return jax.shard_map(
        functools.partial(local, mesh.shape["dp"]),
        mesh=mesh,
        in_specs=(
            P("dir", "dp", None),
            P("dp", None),
            P(),
            P(),
            P(),
            P(),
            P(),
            P(),
            P(),
            P(),
            P(),
            P(),
            P("dir", "dp", None),
        ),
        out_specs=(
            P("dir", "dp", None),
            P("dir", "dp", None),
            P("dp", None),
            P("dp", None),
            P("dp", None),
            P("dp", None),
            P(),
            P(),
            P(),
            P(),
            P(),
            P(),
        ),
        check_vma=False,
    )
```

```python
import functools

import jax
import jax.numpy as jnp
import numpy as np
from jax import lax
from jax.experimental import pallas as pl
from jax.experimental.pallas import tpu as pltpu
from jax.sharding import PartitionSpec as P

F32 = jnp.float32
BF16 = jnp.bfloat16
CHUNK = 128
ROWS = 256
SUB = 64
EPS = 1e-05
LOG2E = 1.4426950408889634
SWAP = [(0, 1), (1, 0)]
MIB = 1024 * 1024
VMEM_GATES = 52
VMEM_PROJ = 56
VMEM_INTRA = 12
VMEM_MIX = 52
VMEM_WEIGHTS = 52
VMEM_BACK = 56
VMEM_CONV = 56
VMEM_INPUTS = 56
VMEM_SUMS = 8
US_GATES = 10
US_PROJ = 20
US_INTRA = 12
US_MIX = 30
US_WEIGHTS = 10
US_BACK = 30
US_CONV = 17
US_INPUTS = 16
US_SUMS = 2
NT = (((1,), (1,)), ((), ()))
TN = (((0,), (0,)), ((), ()))
EXACT = lax.Precision.HIGHEST


def mm(left, right):
    return jnp.dot(left, right, preferred_element_type=F32)


def mm_nt(left, right):
    return lax.dot_general(left, right, NT, preferred_element_type=F32)


def mm_tn(left, right):
    return lax.dot_general(left, right, TN, preferred_element_type=F32)


def exact_mm(left, right):
    return jnp.dot(left, right, precision=EXACT, preferred_element_type=F32)


def sequence_bounds(lengths_ref, half_rows):
    bounds, total = [], 0
    for position in range(lengths_ref.shape[1]):
        total = total + lengths_ref[0, position]
        bounds.append(total)
    return bounds, lax.axis_index("dir") * half_rows


def start_of(row, bounds):
    start = jnp.where(row < 0, -1, 0)
    for bound in bounds:
        start = jnp.where(row >= bound, bound, start)
    return start


def same_sequence(first, bounds):
    starts = start_of(first + lane_iota(CHUNK), bounds)
    turned = jnp.broadcast_to(starts.astype(F32), (8, CHUNK)).T[:, 0:1]
    return (turned == starts.astype(F32)) & (row_iota(CHUNK) != lane_iota(CHUNK))


def row_iota(count):
    return lax.broadcasted_iota(jnp.int32, (count, 1), 0)


def lane_iota(count):
    return lax.broadcasted_iota(jnp.int32, (1, count), 1)


def flag(condition):
    return jnp.where(condition, 1.0, 0.0)


def in_parts(values, parts):
    out = []
    for _ in range(parts):
        part = values.astype(BF16).astype(F32)
        out.append(part)
        values = values - part
    return jnp.concatenate(out, axis=0)


def fold(values):
    return jnp.sum(values.reshape(values.shape[0] // 8, 8, values.shape[1]), axis=0)


def row_of(ref):
    return ref[...].reshape(1, ref.shape[0])


def column_of(ref, steps):
    heads = steps // 2
    place = row_iota(steps)
    column = jnp.zeros((steps, 1), F32)
    for step in range(steps):
        column = jnp.where(place == step, ref[step // heads, step % heads], column)
    return column


def gates_kernel(normed_ref, c_ref, wz_ref, wo_ref, z_ref, dnorm_ref, turned_ref):
    turned_ref[...] = normed_ref[...].T
    z_ref[...] = mm(normed_ref[...], wz_ref[...]).astype(BF16)
    dnorm_ref[...] = mm_nt(c_ref[...], wo_ref[...]).astype(BF16)


def step_factors(
    lengths_ref,
    bias_ref,
    alog_ref,
    e0_ref,
    e1_ref,
    raw_ref,
    dt_ref,
    rate_ref,
    target_ref,
    source_ref,
    factors_ref,
    keeps_ref,
):
    steps, count = raw_ref.shape
    heads = steps // 2
    bounds, base = sequence_bounds(lengths_ref, count)
    rate = jnp.exp(column_of(alog_ref, steps))
    rate_ref[...] = jnp.broadcast_to(rate, (steps, 128))
    raw = raw_ref[...] + column_of(bias_ref, steps)
    raw_ref[...] = raw
    dt = jnp.maximum(raw, 0.0) + jnp.log1p(jnp.exp(-jnp.abs(raw)))
    dt_ref[...] = dt
    log_dt = jnp.log(jnp.maximum(dt, 1e-37))
    chunks = count // CHUNK
    upto = flag(row_iota(CHUNK) <= lane_iota(CHUNK))
    fall = dt * rate
    stacked = [fall[:, chunk * CHUNK : (chunk + 1) * CHUNK] for chunk in range(chunks)]
    summed = exact_mm(jnp.concatenate(stacked, axis=0), upto)
    lane = lane_iota(CHUNK)
    keeps = jnp.zeros((steps, CHUNK), F32)
    for chunk in range(chunks):
        span = slice(chunk * CHUNK, (chunk + 1) * CHUNK)
        first = base + chunk * CHUNK
        inc = summed[chunk * steps : (chunk + 1) * steps]
        dt_c, log_c = dt[:, span], log_dt[:, span]
        inc0 = inc[:heads]
        exc1 = inc[heads:] - fall[heads:, span]
        total0 = inc0[:, CHUNK - 1 :]
        total1 = inc[heads:, CHUNK - 1 :]
        target = jnp.concatenate([-inc0, exc1], axis=0) * LOG2E
        source = jnp.concatenate([inc0 + log_c[:heads], log_c[heads:] - exc1], axis=0) * LOG2E
        target_ref[:, span] = target
        source_ref[:, span] = source
        starts = start_of(first + lane, bounds)
        before = start_of(first - 1, bounds)
        left = start_of(first, bounds)
        right = start_of(first + CHUNK - 1, bounds)
        after = start_of(first + CHUNK, bounds)
        enter0 = jnp.where(starts == before, jnp.exp(-inc0), 0.0)
        enter1 = jnp.where(starts == after, jnp.exp(exc1 - total1), 0.0)
        leave0 = jnp.where(starts == right, dt_c[:heads] * jnp.exp(inc0 - total0), 0.0)
        leave1 = jnp.where(starts == left, dt_c[heads:] * jnp.exp(-exc1), 0.0)
        enter = jnp.concatenate([enter0, enter1], axis=0)
        leave = jnp.concatenate([leave0, leave1], axis=0)
        factors_ref[0, span, :] = in_parts(enter, 2).T.astype(BF16)
        factors_ref[1, span, :] = in_parts(leave, 2).T.astype(BF16)
        keep0 = jnp.where(before == right, jnp.exp(-total0), 0.0)
        keep1 = jnp.where(after == left, jnp.exp(-total1), 0.0)
        keeps = jnp.where(lane == chunk, jnp.concatenate([keep0, keep1], axis=0), keeps)
    ahead = jnp.zeros_like(keeps)
    behind = jnp.zeros_like(keeps)
    run_a = jnp.ones((steps, 1), F32)
    run_b = jnp.ones((steps, 1), F32)
    for chunk in range(chunks):
        ahead = jnp.where(lane == chunk, run_a, ahead)
        run_a = run_a * keeps[:, chunk : chunk + 1]
        last = chunks - 1 - chunk
        behind = jnp.where(lane == last, run_b, behind)
        run_b = run_b * keeps[:, last : last + 1]
    for place, values in enumerate((keeps, ahead, behind)):
        columns = in_parts(values, 2).T.astype(BF16)[0:16]
        keeps_ref[2 * place] = mm(columns, e0_ref[...])[0:chunks]
        keeps_ref[2 * place + 1] = mm(columns, e1_ref[...])[0:chunks]


def shifts(first, bounds, sign, height):
    row = lax.broadcasted_iota(jnp.int32, (height, CHUNK + 16), 0)
    col = lane_iota(CHUNK + 16)
    parts = []
    for lag in (1, 2, 3):
        later = first + col + (lag - 16 if sign < 0 else 0)
        near = later - start_of(later, bounds) < lag
        place = jnp.where(near, -CHUNK, col)
        offset = {-1: 16 - lag, 1: lag, 0: lag - height}[sign]
        parts.append(flag(place == row + offset))
    return jnp.concatenate(parts, axis=0).astype(BF16)


def proj_kernel(
    lengths_ref,
    bias_ref,
    alog_ref,
    x_ref,
    halo_ref,
    gain_ref,
    wx_ref,
    wbc_ref,
    taps_ref,
    e0_ref,
    e1_ref,
    normed_ref,
    raw_ref,
    dt_ref,
    rate_ref,
    target_ref,
    source_ref,
    factors_ref,
    keeps_ref,
    pre_ref,
    act_ref,
    slope_ref,
    s0_ref,
    sf1_ref,
    send_ref,
    prehalo_ref,
    turnhalo_ref,
    buf,
    acc0,
    acc1,
    left0,
    left1,
):
    step = pl.program_id(0)
    per = ROWS // CHUNK
    bounds, base = sequence_bounds(lengths_ref, pl.num_programs(0) * ROWS)
    inner = wx_ref.shape[1]
    channels = taps_ref.shape[1]
    state = (channels - inner) // 4

    @pl.when(step == 0)
    def _():
        count = x_ref.shape[0]
        gain = row_of(gain_ref)

        @pl.loop(0, count // CHUNK, unroll=4)
        def _(chunk):
            rows = pl.ds(pl.multiple_of(chunk * CHUNK, CHUNK), CHUNK)
            x = x_ref[rows, :].astype(F32)
            inv = lax.rsqrt(jnp.mean(x * x, axis=1, keepdims=True) + EPS)
            normed = (x * inv * gain).astype(BF16)
            normed_ref[rows, :] = normed
            raw = mm_nt(wbc_ref[channels - inner :, :], normed)
            raw_ref[:, rows] = raw.astype(BF16).astype(F32)

        step_factors(
            lengths_ref,
            bias_ref,
            alog_ref,
            e0_ref,
            e1_ref,
            raw_ref,
            dt_ref,
            rate_ref,
            target_ref,
            source_ref,
            factors_ref,
            keeps_ref,
        )
        x = halo_ref[...].astype(F32)
        inv = lax.rsqrt(jnp.mean(x * x, axis=1, keepdims=True) + EPS)
        normed = x * inv * gain
        turnhalo_ref[...] = normed.T.astype(BF16)
        normed = normed.astype(BF16)
        prehalo_ref[:, 0:inner] = mm(normed, wx_ref[...]).astype(BF16)
        prehalo_ref[:, inner:channels] = mm_nt(normed, wbc_ref[0 : channels - inner, :]).astype(BF16)
        buf[0:16, :] = prehalo_ref[...]
        acc0[...] = jnp.zeros_like(acc0)
        acc1[...] = jnp.zeros_like(acc1)

    @pl.when(step > 0)
    def _():
        buf[0:16, :] = buf[ROWS : ROWS + 16, :]

    normed = normed_ref[pl.ds(pl.multiple_of(step * ROWS, ROWS), ROWS), :]
    for tile in range(inner // 256):
        cols = slice(tile * 256, tile * 256 + 256)
        px = mm(normed, wx_ref[:, cols]).astype(BF16)
        pre_ref[:, cols] = px
        buf[16 : 16 + ROWS, cols] = px
    pb = mm_nt(normed, wbc_ref[0 : channels - inner, :]).astype(BF16)
    pre_ref[:, inner:channels] = pb
    buf[16 : 16 + ROWS, inner:channels] = pb

    first = base + step * ROWS
    for part in range(per):
        offset = part * CHUNK
        shift = shifts(first + offset, bounds, -1, CHUNK)
        here = pl.ds(pl.multiple_of(step * ROWS + offset, CHUNK), CHUNK)
        leave_cols = factors_ref[1, here, :]
        for tile in range(channels // 256):
            wide = slice(tile * 256, tile * 256 + 256)
            moved = mm(shift, buf[offset : offset + CHUNK + 16, wide])
            if tile * 256 < inner:
                leave0 = mm(leave_cols, e0_ref[:, wide])
                leave1 = mm(leave_cols, e1_ref[:, wide])
            for column in (0, 128):
                cols = slice(tile * 256 + column, tile * 256 + column + 128)
                cut = slice(column, column + 128)
                for row in range(0, CHUNK, SUB):
                    here = buf[offset + 16 + row : offset + 16 + row + SUB, cols]
                    conv = here.astype(F32) * taps_ref[3:4, cols]
                    for lag in (1, 2, 3):
                        at = (lag - 1) * CHUNK + row
                        conv = conv + moved[at : at + SUB, cut] * taps_ref[3 - lag : 4 - lag, cols]
                    sig = jax.nn.sigmoid(conv)
                    act = conv * sig
                    span = slice(offset + row, offset + row + SUB)
                    act_ref[span, cols] = act.astype(BF16)
                    slope_ref[span, cols] = (sig + act - act * sig).astype(BF16)
                    if tile * 256 < inner:
                        held = slice(row, row + SUB)
                        left0[held, cols] = (act * leave0[held, cut]).astype(BF16)
                        left1[held, cols] = (act * leave1[held, cut]).astype(BF16)
        turned = act_ref[offset : offset + CHUNK, inner:channels].astype(F32).T.astype(BF16)
        s0_ref[part] = acc0[...].astype(BF16)
        chunk = pl.ds(step * per + part, 1)
        acc0[...] = keeps_ref[0, chunk, :] * acc0[...] + mm(turned[0:state], left0[...])
        fresh1 = mm(turned[2 * state : 3 * state], left1[...])
        sf1_ref[part] = fresh1.astype(BF16)
        acc1[...] = acc1[...] + keeps_ref[3, chunk, :] * fresh1

    @pl.when(step == pl.num_programs(0) - 1)
    def _():
        send_ref[...] = jnp.where(base > 0, acc1[...], acc0[...]).astype(BF16)


def bc_columns(act_ref, inner, state):
    return [act_ref[:, inner + part * state : inner + (part + 1) * state] for part in range(4)]


def cut_pair(values, width):
    zero = jnp.zeros_like(values)
    first = lane_iota(2 * width) < width
    return jnp.concatenate([jnp.where(first, values, zero), jnp.where(first, zero, values)], axis=0)


def mix_kernel(
    lengths_ref,
    skip_ref,
    act_ref,
    target_ref,
    source_ref,
    factors_ref,
    sl0_ref,
    sf1_ref,
    keeps_ref,
    recv_ref,
    z_ref,
    dnorm_ref,
    gain_ref,
    e0_ref,
    e1_ref,
    mixed_ref,
    dz_ref,
    dy_ref,
    r_ref,
    dcc_ref,
    dl0_ref,
    df1_ref,
    s0_ref,
    s1_ref,
    send_ref,
    sums_ref,
    carry1,
    acc0,
    acc1,
    enter0,
    enter1,
    from0,
    from1,
    within,
    gated_s,
    slope_s,
    gate_s,
    in0,
    in1,
    prod0,
    prod1,
    skip_s,
    gain_s,
):
    step = pl.program_id(0)
    chunk = pl.num_programs(0) - 1 - step
    bounds, base = sequence_bounds(lengths_ref, pl.num_programs(0) * CHUNK)
    first = base + chunk * CHUNK
    inner = gain_ref.shape[0]
    heads = r_ref.shape[0] // 2
    width = inner // heads
    state = recv_ref.shape[0]
    small = 32

    @pl.when(step == 0)
    def _():
        recv = recv_ref[...].astype(F32)
        carry1[...] = jnp.where(base > 0, jnp.zeros_like(recv), recv)
        acc0[...] = jnp.zeros_like(acc0)
        acc1[...] = jnp.zeros_like(acc1)
        sums_ref[...] = jnp.zeros_like(sums_ref)
        gain_s[...] = row_of(gain_ref)
        left = lane_iota(2 * width) < width
        for pair in range(heads // 2):
            skip_s[:, pair * 2 * width : (pair + 1) * 2 * width] = jnp.where(
                left, skip_ref[2 * pair], skip_ref[2 * pair + 1]
            )

    keep0 = keeps_ref[0, pl.ds(chunk, 1), :]
    keep1 = keeps_ref[1, pl.ds(chunk, 1), :]
    ahead0 = keeps_ref[2, pl.ds(chunk, 1), :] * jnp.where(base > 0, 1.0, 0.0)
    s0 = (sl0_ref[0].astype(F32) + ahead0 * recv_ref[...].astype(F32)).astype(BF16)
    s1 = carry1[...].astype(BF16)
    carry1[...] = keep1 * carry1[...] + sf1_ref[0].astype(F32)
    s0_ref[0] = s0
    s1_ref[0] = s1
    enter_cols = factors_ref[0]
    turned = act_ref[:, inner:].astype(F32).T.astype(BF16)
    b0, c0, b1, c1 = bc_columns(act_ref, inner, state)
    enter0[...] = mm(enter_cols, e0_ref[...])
    from0[...] = mm(c0, s0)
    enter1[...] = mm(enter_cols, e1_ref[...])
    from1[...] = mm(c1, s1)
    t, s = row_iota(CHUNK), lane_iota(CHUNK)
    lower = t > s
    scores = jnp.where(lower, mm_nt(c0, b0), mm_nt(c1, b1))
    scores = jnp.where(same_sequence(first, bounds), scores, 0.0)
    columns = target_ref[...].T
    for pair in range(heads // 2):
        cols = slice(pair * 2 * width, (pair + 1) * 2 * width)
        weights = []
        for head in (2 * pair, 2 * pair + 1):
            power = jnp.where(
                lower,
                columns[:, head : head + 1] + source_ref[head : head + 1, :],
                columns[:, heads + head : heads + head + 1]
                + source_ref[heads + head : heads + head + 1, :],
            )
            weights.append((jnp.exp2(power) * scores).astype(BF16))
        x_cut = cut_pair(act_ref[:, cols], width)
        within[:, cols] = mm(jnp.concatenate(weights, axis=1), x_cut)
    tiles = [slice(tile * 128, tile * 128 + 128) for tile in range(inner // 128)]
    for row in range(0, CHUNK, small):
        rows = slice(row, row + small)
        square = jnp.zeros((small, 128), F32)
        cross = jnp.zeros((small, 128), F32)
        for cols in tiles:
            mixer = within[rows, cols] + skip_s[:, cols] * act_ref[rows, cols].astype(F32)
            mixer = mixer + enter0[rows, cols] * from0[rows, cols]
            mixer = mixer + enter1[rows, cols] * from1[rows, cols]
            z = z_ref[rows, cols].astype(F32)
            sig = jax.nn.sigmoid(z)
            gate = z * sig
            gated = mixer * gate
            square = square + gated * gated
            cross = cross + dnorm_ref[rows, cols].astype(F32) * gain_s[:, cols] * gated
            gated_s[rows, cols] = gated
            gate_s[rows, cols] = gate
            slope_s[rows, cols] = mixer * (sig + gate - gate * sig)
        live = flag(first + row + row_iota(small) < bounds[len(bounds) - 2])
        scale = lax.rsqrt(jnp.sum(square, axis=1, keepdims=True) * (1.0 / inner) + EPS)
        back = scale * scale * (jnp.sum(cross, axis=1, keepdims=True) * (1.0 / inner))
        scale = jnp.broadcast_to(scale * live, (small, 128))
        back = jnp.broadcast_to(back, (small, 128))
        for cols in tiles:
            gated = gated_s[rows, cols]
            unit = gated * scale
            gain = gain_s[:, cols]
            mixed_ref[rows, cols] = (unit * gain).astype(BF16)
            dnorm = dnorm_ref[rows, cols].astype(F32)
            sums_ref[0:8, cols] += fold(dnorm * unit)
            dgated = scale * (dnorm * gain - gated * back)
            dz_ref[rows, cols] = (dgated * slope_s[rows, cols]).astype(BF16)
            dy = dgated * gate_s[rows, cols]
            dy_ref[rows, cols] = dy.astype(BF16)
            sums_ref[8:16, cols] += fold(dy * act_ref[rows, cols].astype(F32))
            entered0 = dy * enter0[rows, cols]
            entered1 = dy * enter1[rows, cols]
            in0[rows, cols] = entered0.astype(BF16)
            in1[rows, cols] = entered1.astype(BF16)
            prod0[rows, cols] = (entered0 * from0[rows, cols]).astype(BF16)
            prod1[rows, cols] = (entered1 * from1[rows, cols]).astype(BF16)
    ones = e0_ref[0:heads, :]
    r_ref[0:heads, :] = mm_nt(ones, prod0[...])
    r_ref[heads : 2 * heads, :] = mm_nt(ones, prod1[...])
    dcc_ref[:, 0:state] = mm_nt(in0[...], s0)
    dcc_ref[:, state : 2 * state] = mm_nt(in1[...], s1)
    dl0_ref[0] = acc0[...].astype(BF16)
    acc0[...] = keep0 * acc0[...] + mm(turned[state : 2 * state], in0[...])
    df1 = mm(turned[3 * state : 4 * state], in1[...])
    df1_ref[0] = df1.astype(BF16)
    acc1[...] = acc1[...] + keeps_ref[5, pl.ds(chunk, 1), :] * df1

    @pl.when(step == pl.num_programs(0) - 1)
    def _():
        send_ref[...] = jnp.where(base > 0, acc0[...], acc1[...]).astype(BF16)


def back_kernel(
    lengths_ref,
    skip_ref,
    act_ref,
    slope_ref,
    target_ref,
    source_ref,
    factors_ref,
    dcc_ref,
    dy_ref,
    s0_ref,
    s1_ref,
    dl0_ref,
    df1_ref,
    keeps_ref,
    recv_ref,
    start_ref,
    e0_ref,
    e1_ref,
    spans_ref,
    _dpre_ref,
    _moves_ref,
    dpre_ref,
    moves_ref,
    last_ref,
    carry1,
    dscore,
    out0,
    out1,
    ds0,
    ds1,
    kept,
    *,
    skipped,
    chunks,
):
    step = pl.program_id(0)
    chunk = step + skipped
    bounds, base = sequence_bounds(lengths_ref, chunks * CHUNK)
    first = base + chunk * CHUNK
    heads = skip_ref.shape[0]
    inner = keeps_ref.shape[2]
    width = inner // heads
    state = recv_ref.shape[0]

    @pl.when(step == 0)
    def _():
        if skipped:
            carry1[...] = start_ref[...]
        else:
            recv = recv_ref[...].astype(F32)
            carry1[...] = jnp.where(base > 0, recv, jnp.zeros_like(recv))

    keep0 = keeps_ref[0, pl.ds(chunk, 1), :]
    keep1 = keeps_ref[1, pl.ds(chunk, 1), :]
    behind0 = keeps_ref[4, pl.ds(chunk, 1), :] * jnp.where(base > 0, 0.0, 1.0)
    d0 = dl0_ref[0].astype(F32) + behind0 * recv_ref[...].astype(F32)
    d1 = carry1[...]
    ds0[...] = d0.astype(BF16)
    ds1[...] = d1.astype(BF16)
    kept0 = jnp.sum(d0 * s0_ref[0].astype(F32), axis=0, keepdims=True) * keep0
    kept1 = jnp.sum(d1 * s1_ref[0].astype(F32), axis=0, keepdims=True) * keep1
    carry1[...] = keep1 * d1 + df1_ref[0].astype(F32)

    t = lane_iota(CHUNK)
    b0, c0, b1, c1 = bc_columns(act_ref, inner, state)
    same = same_sequence(first, bounds)
    both = jnp.where(row_iota(CHUNK) < t, mm_nt(b0, c0), mm_nt(b1, c1))
    both = jnp.where(same, both, 0.0)
    halves = []
    for row in range(0, CHUNK, SUB):
        early = row + row_iota(SUB) < t
        halves.append((slice(row, row + SUB), early, flag(early), both[row : row + SUB]))
    in_cols = source_ref[...].T
    leave_cols = factors_ref[0]
    dscore[...] = jnp.zeros_like(dscore)
    left = lane_iota(2 * width) < width

    def columns_of(pair):
        return slice(pair * 2 * width, (pair + 1) * 2 * width)

    def products(pair):
        cols = columns_of(pair)
        dweights = mm_nt(cut_pair(act_ref[:, cols], width), dy_ref[:, cols])
        return dweights

    def carried(pair):
        cols = columns_of(pair)
        leave0 = mm(leave_cols, e0_ref[:, cols])
        leave1 = mm(leave_cols, e1_ref[:, cols])
        return leave0, leave1, mm(b0, ds0[:, cols]), mm(b1, ds1[:, cols])

    def within(pair, dweights):
        weights, lows, alls, scored = [], [], [], [0.0] * len(halves)
        for part in (0, 1):
            head = 2 * pair + part
            parts, low_parts, all_parts = [], [], []
            sum0 = jnp.zeros((8, CHUNK), F32)
            sum1 = jnp.zeros((8, CHUNK), F32)
            for place, (rows, early, early_f, scores) in enumerate(halves):
                power = jnp.where(
                    early,
                    in_cols[rows, head : head + 1] + target_ref[head : head + 1, :],
                    in_cols[rows, heads + head : heads + head + 1]
                    + target_ref[heads + head : heads + head + 1, :],
                )
                decay = jnp.exp2(power)
                parts.append((decay * scores).astype(BF16))
                at = part * CHUNK + rows.start
                dweight = dweights[at : at + SUB] * decay
                scored[place] = scored[place] + dweight
                change = dweight * scores
                low = change * early_f
                low_parts.append(low.astype(BF16))
                all_parts.append(change.astype(BF16))
                sum0 = sum0 + fold(low)
                sum1 = sum1 + fold(change)
            weights.append(jnp.concatenate(parts, axis=0))
            lows.append(jnp.concatenate(low_parts, axis=0))
            alls.append(jnp.concatenate(all_parts, axis=0))
            moves_ref[head : head + 1, :] = jnp.sum(sum0, axis=0, keepdims=True)
            moves_ref[heads + head : heads + head + 1, :] = jnp.sum(sum1, axis=0, keepdims=True)
        for place, (rows, _, _, _) in enumerate(halves):
            dscore[rows, :] += scored[place]
        return jnp.concatenate(weights, axis=1), lows + alls

    def gathered(pair, weights, lows, states):
        cols = columns_of(pair)
        leave0, leave1, from0, from1 = states
        dx = mm(weights, cut_pair(dy_ref[:, cols], width))
        skip = jnp.where(left, skip_ref[2 * pair], skip_ref[2 * pair + 1])
        firsts, totals = [], []
        sum0 = jnp.zeros((8, 2 * width), F32)
        sum1 = jnp.zeros((8, 2 * width), F32)
        for rows, _, _, _ in halves:
            xf = act_ref[rows, cols].astype(F32)
            came0 = leave0[rows] * from0[rows]
            came1 = leave1[rows] * from1[rows]
            dconv = dx[rows] + skip * dy_ref[rows, cols].astype(F32) + came0 + came1
            dpre_ref[rows, cols] = (dconv * slope_ref[rows, cols].astype(F32)).astype(BF16)
            out0[rows, cols] = (xf * leave0[rows]).astype(BF16)
            out1[rows, cols] = (xf * leave1[rows]).astype(BF16)
            came0 = xf * came0
            came1 = xf * came1
            sum0 = sum0 + fold(came0)
            sum1 = sum1 + fold(came1)
            firsts.append(came0.astype(BF16))
            totals.append(came1.astype(BF16))
        kept[0:8, cols] = sum0
        kept[8:16, cols] = sum1
        return lows + [jnp.concatenate(firsts, axis=0), jnp.concatenate(totals, axis=0)]

    def summed(pair, lows):
        sums = mm_nt(spans_ref[...], jnp.concatenate(lows, axis=1))
        moves_ref[2 * heads + 2 * pair : 2 * heads + 2 * pair + 2, :] = sums[0:2]
        moves_ref[3 * heads + 2 * pair : 3 * heads + 2 * pair + 2, :] = sums[2:4]


    pairs = heads // 2
    ahead = {0: products(0)}
    held, done = {}, {}
    for pair in range(pairs + 2):
        if pair + 1 < pairs:
            ahead[pair + 1] = products(pair + 1)
        if 0 < pair <= pairs:
            weights, lows = held.pop(pair - 1)
            states = carried(pair - 1)
            done[pair - 1] = gathered(pair - 1, weights, lows, states)
        if pair < pairs:
            held[pair] = within(pair, ahead.pop(pair))
        if pair > 1:
            summed(pair - 2, done.pop(pair - 2))
    dscores = jnp.where(same, dscore[...], 0.0)
    dscore0 = jnp.where(row_iota(CHUNK) < t, dscores, 0.0).astype(BF16)
    dscore1 = jnp.where(row_iota(CHUNK) < t, 0.0, dscores).astype(BF16)
    kept[0:1, :] += kept0
    kept[8:9, :] += kept1
    kept_sum = mm_nt(e0_ref[0:heads, :], in_parts(kept[...], 2).astype(BF16))
    kept_sum = kept_sum[:, 0:16] + kept_sum[:, 16:32]
    for direction in (0, 1):
        column = jnp.sum(kept_sum[:, 8 * direction : 8 * direction + 8], axis=1, keepdims=True)
        moves_ref[(4 + direction) * heads : (5 + direction) * heads, :] = jnp.broadcast_to(
            column, (heads, CHUNK)
        )
    db0 = mm(dscore0, c0) + mm_nt(out0[...], ds0[...])
    db1 = mm(dscore1, c1) + mm_nt(out1[...], ds1[...])
    dc0 = mm_tn(dscore0, b0) + dcc_ref[:, 0:state]
    dc1 = mm_tn(dscore1, b1) + dcc_ref[:, state : 2 * state]
    dbc = jnp.concatenate([db0, dc0, db1, dc1], axis=1)
    dpre_ref[:, inner:] = (dbc * slope_ref[:, inner:].astype(F32)).astype(BF16)

    @pl.when(step == pl.num_programs(0) - 1)
    def _():
        last_ref[...] = carry1[...]


def steps_back(raw, dt, rate, moves, r):
    steps = raw.shape[0]
    heads = steps // 2
    chunks = raw.shape[1] // CHUNK
    s, t = row_iota(CHUNK), lane_iota(CHUNK)

    def stack(values):
        parts = [values[:, chunk * CHUNK : (chunk + 1) * CHUNK] for chunk in range(chunks)]
        return jnp.concatenate(parts, axis=0)

    def unstack(values):
        parts = [values[chunk * heads : (chunk + 1) * heads] for chunk in range(chunks)]
        return jnp.concatenate(parts, axis=1)

    got0, got, own0, own, kept0, kept1 = [
        moves[part * heads : (part + 1) * heads] for part in range(6)
    ]
    own1, got1 = own - own0, got - got0
    da0 = exact_mm(stack(got0 + r[:heads] - own0), flag(s >= t))
    da1 = exact_mm(stack(got1 + r[heads:] - own1), flag(s <= t))
    da = -jnp.concatenate([unstack(da0) + kept0, unstack(da1) + kept1], axis=0)
    dlog = jnp.concatenate([own0, own1], axis=0)
    sig = jax.nn.sigmoid(raw)
    ratio = jnp.where(raw < -20.0, 1.0, sig / jnp.maximum(dt, 1e-37))
    return dlog * ratio + da * rate * sig, jnp.sum(da * dt, axis=1, keepdims=True) * rate


def by_core(product, shard, mine_ref, theirs_ref):
    pieces = [product[place : place + shard] for place in range(0, product.shape[0], shard)]
    even = jnp.concatenate(pieces[0::2], axis=0)
    odd = jnp.concatenate(pieces[1::2], axis=0)
    core = lax.rem(lax.axis_index("dp"), 2)

    @pl.when(core == 0)
    def _():
        mine_ref[...] = even
        theirs_ref[...] = odd

    @pl.when(core == 1)
    def _():
        mine_ref[...] = odd
        theirs_ref[...] = even


def weights_kernel(
    turned_ref, dz_ref, mixed_ref, c_ref, wz_ref, mine_ref, theirs_ref, gain_ref, *, shard
):
    product = mm_tn(mixed_ref[...], c_ref[...]).astype(BF16)
    pieces = []
    for place in range(0, product.shape[0], 2 * shard):
        pieces.append(
            jnp.concatenate(
                [product[place : place + shard], product[place + shard : place + 2 * shard]], axis=1
            )
        )
    gate = mm(turned_ref[...], dz_ref[...])
    both = jnp.concatenate([jnp.concatenate(pieces, axis=0), gate.astype(BF16)], axis=1)
    by_core(both, shard, mine_ref, theirs_ref)
    share = (gate * wz_ref[...].astype(F32)).astype(BF16)
    gain_ref[0] = mm_nt(jnp.ones((8, share.shape[1]), BF16), share)[0:1]


def conv_back_kernel(
    lengths_ref,
    turned_ref,
    turnhalo_ref,
    dpre_ref,
    pre_ref,
    prehalo_ref,
    taps_ref,
    raw_ref,
    dt_ref,
    rate_ref,
    moves_ref,
    r_ref,
    w_ref,
    narrow_ref,
    gain_ref,
    share_ref,
    mix_sums_ref,
    e0_ref,
    dproj_ref,
    dhalo_ref,
    mine_ref,
    theirs_ref,
    draw_ref,
    small_ref,
    shift,
    buf,
    gains,
    sums_ref,
    *,
    shard,
):
    step = pl.program_id(0)
    count, wide = dpre_ref.shape
    chunks = count // CHUNK
    steps = raw_ref.shape[0]
    bounds, base = sequence_bounds(lengths_ref, count)

    @pl.when(step == 0)
    def _():
        for chunk in range(chunks):
            shift[chunk * 3 * CHUNK : (chunk + 1) * 3 * CHUNK, :] = shifts(
                base + chunk * CHUNK, bounds, 1, CHUNK
            )
        shift[chunks * 3 * CHUNK :, :] = shifts(base, bounds, 0, 16)
        buf[...] = jnp.zeros_like(buf)
        gains[...] = jnp.zeros_like(gains)
        sums_ref[...] = jnp.zeros_like(sums_ref)

    last = pl.num_programs(0) - 1
    inner = w_ref.shape[1]
    tile_here = pl.ds(pl.multiple_of(step * wide, wide), wide)

    def share_of(product, weights):
        share = (product * weights.astype(F32)).astype(BF16)
        gains[...] += mm_nt(jnp.ones((8, share.shape[1]), BF16), share)

    def hand_over(product, weights):
        share_of(product, weights)
        by_core(product.astype(BF16), shard, mine_ref, theirs_ref)

    @pl.when(step < pl.num_programs(0) - 1)
    def _():
        buf[0:CHUNK, :] = dpre_ref[count - CHUNK :, :]
        moved = mm(shift[chunks * 3 * CHUNK :, :], dpre_ref[0 : CHUNK + 16, :])
        halo_sums = [None] * 4
        dproj = jnp.zeros((16, wide), F32)
        pre = prehalo_ref[...].astype(F32)
        for lag in (1, 2, 3):
            part = moved[(lag - 1) * 16 : lag * 16]
            dproj = dproj + part * taps_ref[3 - lag : 4 - lag, :]
            halo_sums[3 - lag] = jnp.sum(pre * part, axis=0, keepdims=True)
        halo_sums[3] = jnp.zeros((1, wide), F32)
        dhalo_ref[...] = dproj.astype(BF16)
        sums = [[jnp.zeros((8, 128), F32) for _ in range(4)] for _ in range(wide // 128)]
        for chunk in range(chunks):
            if chunk < chunks - 1:
                pair = dpre_ref[chunk * CHUNK : chunk * CHUNK + CHUNK + 16, :]
            else:
                pair = buf[...]
            moved = mm(shift[chunk * 3 * CHUNK : (chunk + 1) * 3 * CHUNK, :], pair)
            for place in range(wide // 128):
                cols = slice(place * 128, place * 128 + 128)
                for row in range(0, CHUNK, SUB):
                    span = slice(chunk * CHUNK + row, chunk * CHUNK + row + SUB)
                    pre = pre_ref[span, cols].astype(F32)
                    here = dpre_ref[span, cols].astype(F32)
                    dproj = here * taps_ref[3:4, cols]
                    sums[place][3] = sums[place][3] + fold(pre * here)
                    for lag in (1, 2, 3):
                        at = (lag - 1) * CHUNK + row
                        part = moved[at : at + SUB, cols]
                        dproj = dproj + part * taps_ref[3 - lag : 4 - lag, cols]
                        sums[place][3 - lag] = sums[place][3 - lag] + fold(pre * part)
                    dproj_ref[span, cols] = dproj.astype(BF16)
        for place in range(wide // 128):
            cols = slice(place * 128, place * 128 + 128)
            at = pl.ds(pl.multiple_of(step * wide + place * 128, 128), 128)
            for tap in range(4):
                sums_ref[tap : tap + 1, at] = (
                    jnp.sum(sums[place][tap], axis=0, keepdims=True) + halo_sums[tap][:, cols]
                )
        product = mm(turned_ref[...], dproj_ref[...]) + mm(turnhalo_ref[...], dhalo_ref[...])
        by_core(product.astype(BF16), shard, mine_ref, theirs_ref)

        @pl.when(step < last - 1)
        def _():
            share_of(product, w_ref[:, tile_here])

        @pl.when(step == last - 1)
        def _():
            share_of(product, narrow_ref[0:wide, :].astype(F32).T)

    @pl.when(step == pl.num_programs(0) - 1)
    def _():
        rate = rate_ref[:, 0:1]
        draw, drate = steps_back(raw_ref[...], dt_ref[...], rate, moves_ref[...], r_ref[...])
        low = draw.astype(BF16)
        draw_ref[...] = low
        product = mm_nt(turned_ref[...], low)
        fill = jnp.zeros((product.shape[0], wide - steps), F32)
        steps_weights = narrow_ref[narrow_ref.shape[0] - steps :, :].astype(F32).T
        hand_over(
            jnp.concatenate([product, fill], axis=1),
            jnp.concatenate([steps_weights, fill], axis=1),
        )
        heads = steps // 2
        model = w_ref.shape[0]
        sums_ref[4:5, 0:inner] = jnp.sum(mix_sums_ref[0:8, :], axis=0, keepdims=True)
        share = jnp.concatenate([share_ref[part] for part in range(share_ref.shape[0])], axis=1)
        sums_ref[5:6, 0:model] = (gains[0:1, :] + share) / row_of(gain_ref)
        skips = in_parts(mix_sums_ref[8:16, :], 2).astype(BF16)
        skips = jnp.sum(mm_nt(e0_ref[0:heads, :], skips), axis=1, keepdims=True)
        columns = [jnp.concatenate([skips, skips], axis=0), jnp.sum(draw, axis=1, keepdims=True)]
        columns = jnp.concatenate(columns + [drate, jnp.zeros((steps, 5), F32)], axis=1).T
        for place in range(3):
            sums_ref[6:7, 128 * place : 128 * place + steps] = columns[place : place + 1]
        small_ref[...] = narrowed(two_halves(sums_ref[...]))


def halve_kernel(kept_ref, got_ref, keep_ref, send_ref, *, bit):
    shard = keep_ref.shape[0]
    mine = lax.rem(lax.axis_index("dp") // bit, 2)
    for place, out_ref in ((mine, keep_ref), (1 - mine, send_ref)):
        rows = pl.ds(pl.multiple_of(place * shard, shard), shard)
        total = kept_ref[rows, :].astype(F32) + got_ref[rows, :].astype(F32)
        out_ref[...] = total.astype(out_ref.dtype)


def sum_kernel(kept_ref, got_ref, out_ref):
    out_ref[...] = (kept_ref[...].astype(F32) + got_ref[...].astype(F32)).astype(BF16)


def narrowed(small):
    few = small[6:7] + small[7:8]
    high = few.astype(BF16).astype(F32)
    return jnp.concatenate([small[0:6], high, few - high, small[8:16]], axis=0).astype(BF16)


def two_halves(small):
    half = small.shape[1] // 2
    return jnp.concatenate([small[:, 0:half], small[:, half:]], axis=0)


def quarters_kernel(
    mine_ref,
    got_ref,
    small_ref,
    smallgot_ref,
    keep_ref,
    across_ref,
    along_ref,
    both_ref,
    *,
    shard,
):
    half = mine_ref.shape[1] // 2
    row_bit = lax.rem(lax.axis_index("dp") // 2, 2)
    side = lax.axis_index("dir")
    count = mine_ref.shape[0] // 2
    small = narrowed(small_ref[...].astype(F32) + smallgot_ref[...].astype(F32))
    keep_ref[count:, :] = small.astype(F32)
    for out_ref, row, column in (
        (keep_ref, row_bit, side),
        (across_ref, row_bit, 1 - side),
        (along_ref, 1 - row_bit, side),
        (both_ref, 1 - row_bit, 1 - side),
    ):
        if out_ref is not keep_ref:
            out_ref[count:, :] = small
        for place in range(count // shard):
            rows = slice(place * shard, (place + 1) * shard)
            here = pl.ds(pl.multiple_of((2 * place + row) * shard, shard), shard)
            cols = pl.ds(pl.multiple_of(column * half, half), half)
            total = mine_ref[here, cols].astype(F32) + got_ref[here, cols].astype(F32)
            out_ref[rows, :] = total.astype(out_ref.dtype)


def levels_kernel(keep_ref, a_ref, b_ref, c_ref, own_ref, s1_ref, s2_ref, s3_ref, *, shard):
    level = lax.axis_index("dp") // 4
    count = 4 * shard
    small = [ref[count:, :].astype(F32) for ref in (a_ref, b_ref, c_ref)]
    small = narrowed(keep_ref[count:, :] + small[0] + (small[1] + small[2]))
    own_ref[shard:, :] = small.astype(F32)
    for bits, out_ref in enumerate((own_ref, s1_ref, s2_ref, s3_ref)):
        wanted = jnp.bitwise_xor(level, bits)
        rows = pl.ds(pl.multiple_of(wanted * shard, shard), shard)
        total = keep_ref[rows, :] + a_ref[rows, :].astype(F32)
        total = total + (b_ref[rows, :].astype(F32) + c_ref[rows, :].astype(F32))
        out_ref[0:shard, :] = total.astype(out_ref.dtype)
        if bits:
            out_ref[shard:, :] = small


def last_kernel(own_ref, a_ref, b_ref, c_ref, out_ref, small_ref, *, shard):
    total = own_ref[...] + a_ref[...].astype(F32)
    total = total + (b_ref[...].astype(F32) + c_ref[...].astype(F32))
    out_ref[...] = total[0:shard].astype(BF16)
    small_ref[...] = total[shard:]


def finish_kernel(
    late_ref,
    lategot_ref,
    early_ref,
    earlygot_ref,
    small_ref,
    gx_ref,
    gz_ref,
    gbc_ref,
    go_ref,
    gtaps_ref,
    gmix_ref,
    gin_ref,
    gskip_ref,
    gbias_ref,
    galog_ref,
):
    side = lax.axis_index("dir")
    half = late_ref.shape[1]
    inner = gx_ref.shape[1]
    model = go_ref.shape[1]
    shard = gx_ref.shape[0]
    mine = late_ref[...].astype(F32)
    other = lategot_ref[...].astype(F32)
    first = jnp.where(side == 0, mine, other)
    second = jnp.where(side == 0, other, mine)
    gx_ref[:, 0:half] = first
    gx_ref[:, half:inner] = second[:, 0 : inner - half]
    gbc_ref[...] = second[:, inner - half : inner - half + gbc_ref.shape[1]]
    early = early_ref[...].astype(F32) + earlygot_ref[...].astype(F32)
    go_ref[0:shard, :] = early[:, 0:model]
    go_ref[shard : 2 * shard, :] = early[:, model : 2 * model]
    gz_ref[...] = early[:, 2 * model :]
    small = jnp.concatenate([small_ref[0:8, :], small_ref[8:16, :]], axis=1)
    gtaps_ref[...] = small[0:4, 0 : gtaps_ref.shape[1]]
    gmix_ref[...] = small[4:5, 0:inner].reshape(inner)
    gin_ref[...] = small[5:6, 0:model].reshape(model)
    few = small[6:7] + small[7:8]
    heads = gskip_ref.shape[0]
    gskip_ref[...] = few[:, 0:128].reshape(128)[0:heads]
    gbias_ref[0:1, :] = few[:, 128 : 128 + heads]
    gbias_ref[1:2, :] = few[:, 128 + heads : 128 + 2 * heads]
    galog_ref[0:1, :] = few[:, 256 : 256 + heads]
    galog_ref[1:2, :] = few[:, 256 + heads : 256 + 2 * heads]


def inputs_kernel(
    x_ref,
    c_ref,
    gain_ref,
    dproj_ref,
    dhalo_ref,
    draw_ref,
    dz_ref,
    wx_ref,
    wbc_ref,
    wz_ref,
    mixed_ref,
    wo_ref,
    gin_ref,
    out_ref,
    dproj,
):
    step = pl.program_id(0)
    inner = wx_ref.shape[1]
    steps = draw_ref.shape[0]
    narrow = wbc_ref.shape[0] - steps

    @pl.when(step == pl.num_programs(0) - 1)
    def _():
        tail = slice(dproj_ref.shape[0] - 16, dproj_ref.shape[0])
        both = dproj_ref[tail, :].astype(F32) + dhalo_ref[...].astype(F32)
        dproj[...] = dproj_ref[...]
        dproj[tail, :] = both.astype(BF16)

    @pl.when(step < pl.num_programs(0) - 1)
    def _():
        dproj[...] = dproj_ref[...]

    dn = mm_nt(dproj[:, 0:inner], wx_ref[...])
    dn = dn + mm_nt(dz_ref[...], wz_ref[...])
    dn = dn + mm(dproj[:, inner:], wbc_ref[0:narrow, :])
    dn = dn + mm_tn(draw_ref[...], wbc_ref[narrow:, :])
    x = x_ref[...].astype(F32)
    inv = lax.rsqrt(jnp.mean(x * x, axis=1, keepdims=True) + EPS)
    unit = x * inv
    out_ref[...] = (x + mm(mixed_ref[...], wo_ref[...])).astype(BF16)
    f = dn * row_of(gain_ref)
    back = inv * (f - unit * jnp.mean(f * unit, axis=1, keepdims=True))
    gin_ref[...] = (c_ref[...].astype(F32) + back).astype(BF16)


def smem():
    return pl.BlockSpec(memory_space=pltpu.SMEM)


def resident():
    return pl.BlockSpec(memory_space=pltpu.VMEM)


def anywhere():
    return pl.BlockSpec(memory_space=pl.ANY)


def whole(shape):
    return pl.BlockSpec(shape, lambda i: (0,) * len(shape), pipeline_mode=pl.Buffered(1))


def rows_of(count, width):
    return pl.BlockSpec((count, width), lambda i: (i, 0))


def lanes_of(height, count):
    return pl.BlockSpec((height, count), lambda i: (0, i))


def parts_of(count, *rest):
    return pl.BlockSpec((count,) + rest, lambda i: (i,) + (0,) * len(rest))


def cost(microseconds):
    flops = int(microseconds * 1.15e9)
    return pl.CostEstimate(flops=flops, bytes_accessed=0, transcendentals=0)


def call(kernel, name, grid, in_specs, outs, scratch, cost_us, args, vmem, aliases=()):
    return pl.pallas_call(
        kernel,
        name=name,
        grid=(grid,),
        in_specs=in_specs,
        out_specs=[spec for spec, _, _ in outs],
        out_shape=[jax.ShapeDtypeStruct(shape, dtype) for _, shape, dtype in outs],
        scratch_shapes=scratch,
        input_output_aliases=dict(aliases),
        compiler_params=pltpu.CompilerParams(
            vmem_limit_bytes=vmem * MIB, dimension_semantics=("arbitrary",)
        ),
        cost_estimate=cost(cost_us),
    )(*args)


def traded(values, axis, bit, size):
    return lax.ppermute(values, axis, [(i, i ^ bit) for i in range(size)])


def ordered(first, second):
    return lax.optimization_barrier((first, second))


def sum_shards(grad, dp_count):
    index = lax.axis_index("dp")
    held = grad.reshape(dp_count, grad.shape[0] // dp_count, grad.shape[1])
    bit = 1
    while bit < dp_count:
        paired = held.reshape(held.shape[0] // 2, 2, held.shape[1], held.shape[2])
        mine = (index // bit) % 2
        kept = lax.dynamic_index_in_dim(paired, mine, 1, keepdims=False)
        sent = lax.dynamic_index_in_dim(paired, 1 - mine, 1, keepdims=False).astype(BF16)
        held = kept.astype(F32) + traded(sent, "dp", bit, dp_count).astype(F32)
        bit *= 2
    held = held[0].astype(BF16)
    return held.astype(F32) + traded(held, "dir", 1, 2).astype(F32)


def sum_all(values, dp_count):
    bit = 1
    while bit < dp_count:
        values = values + traded(values, "dp", bit, dp_count)
        bit *= 2
    return values + traded(values, "dir", 1, 2)


def local(
    dp_count,
    hidden_in,
    lengths,
    gain_in,
    w_x,
    w_z,
    w_bcdt,
    conv_w,
    dt_bias,
    a_log,
    d_skip,
    gain_mix,
    w_out,
    cotangent,
):
    x = hidden_in[0]
    cot = cotangent[0]
    count, model = x.shape
    inner = w_x.shape[1]
    channels = conv_w.shape[1]
    heads = d_skip.shape[0]
    width = inner // heads
    state = (channels - inner) // 4
    chunks = count // CHUNK
    steps = 2 * heads

    w_narrow = w_bcdt.T
    halo = lax.ppermute(x[count - 16 :], "dir", [(0, 1)])

    spread = np.repeat(np.eye(heads, dtype=np.float32), width, axis=1)
    zeros = np.zeros_like(spread)
    e0 = jnp.asarray(np.concatenate([spread, zeros, spread, zeros]), BF16)
    e1 = jnp.asarray(np.concatenate([zeros, spread, zeros, spread]), BF16)
    spans = np.zeros((8, 6 * CHUNK), np.float32)
    for head in range(2):
        columns = slice(head * width, (head + 1) * width)
        spans[head, head * CHUNK : (head + 1) * CHUNK] = 1.0
        spans[head, 4 * CHUNK : 5 * CHUNK][columns] = 1.0
        spans[2 + head, (2 + head) * CHUNK : (3 + head) * CHUNK] = 1.0
        spans[2 + head, 4 * CHUNK : 5 * CHUNK][columns] = 1.0
        spans[2 + head, 5 * CHUNK : 6 * CHUNK][columns] = 1.0
    spans = jnp.asarray(spans, BF16)

    def rows_out(size, columns, dtype):
        return (rows_of(size, columns), (count, columns), dtype)

    def full(shape, dtype):
        return (pl.BlockSpec(shape, lambda i: (0,) * len(shape)), shape, dtype)

    per = ROWS // CHUNK
    state_f32 = pltpu.VMEM((state, inner), F32)
    state_bf16 = pltpu.VMEM((state, inner), BF16)
    row_f32 = pltpu.VMEM((1, inner), F32)
    chunk_f32 = pltpu.VMEM((CHUNK, inner), F32)
    chunk_bf16 = pltpu.VMEM((CHUNK, inner), BF16)
    (
        normed,
        raw,
        dt,
        rate,
        target,
        source,
        factors,
        keeps,
        pre,
        act,
        slope,
        sl0,
        sf1,
        send,
        pre_halo,
        turn_halo,
    ) = call(
        proj_kernel,
        "proj",
        count // ROWS,
        [
            smem(),
            smem(),
            smem(),
            whole((count, model)),
            whole((16, model)),
            whole((model,)),
            whole((model, inner)),
            whole(w_narrow.shape),
            whole(conv_w.shape),
            whole(e0.shape),
            whole(e1.shape),
        ],
        [
            full((count, model), BF16),
            full((steps, count), F32),
            full((steps, count), F32),
            full((steps, 128), F32),
            full((steps, count), F32),
            full((steps, count), F32),
            full((2, count, 2 * steps), BF16),
            full((6, chunks, inner), F32),
            rows_out(ROWS, channels, BF16),
            rows_out(ROWS, channels, BF16),
            rows_out(ROWS, channels, BF16),
            (parts_of(per, state, inner), (chunks, state, inner), BF16),
            (parts_of(per, state, inner), (chunks, state, inner), BF16),
            full((state, inner), BF16),
            full((16, channels), BF16),
            full((model, 16), BF16),
        ],
        [
            pltpu.VMEM((16 + ROWS, channels), BF16),
            state_f32,
            state_f32,
            chunk_bf16,
            chunk_bf16,
        ],
        US_PROJ,
        (lengths, dt_bias, a_log, x, halo, gain_in, w_x, w_narrow, conv_w, e0, e1),
        VMEM_PROJ,
    )
    received = lax.ppermute(send, "dir", SWAP)

    gate_z, d_norm, turned = call(
        gates_kernel,
        "gates",
        count // ROWS,
        [
            rows_of(ROWS, model),
            rows_of(ROWS, model),
            whole((model, inner)),
            whole((inner, model)),
        ],
        [
            rows_out(ROWS, inner, BF16),
            rows_out(ROWS, inner, BF16),
            (lanes_of(model, ROWS), (model, count), BF16),
        ],
        [],
        US_GATES,
        (normed, cot, w_z, w_out),
        VMEM_GATES,
    )

    def down_rows(width):
        return pl.BlockSpec((CHUNK, width), lambda i: (chunks - 1 - i, 0))

    def down_lanes(height):
        return pl.BlockSpec((height, CHUNK), lambda i: (0, chunks - 1 - i))

    def down_parts(*rest):
        return pl.BlockSpec((1,) + rest, lambda i: (chunks - 1 - i,) + (0,) * len(rest))

    states = (down_parts(state, inner), (chunks, state, inner), BF16)
    mixed, dz, dy, r, dcc, dl0, df1, s0, s1, d_send, mix_sums = call(
        mix_kernel,
        "mix",
        chunks,
        [
            smem(),
            smem(),
            down_rows(channels),
            down_lanes(steps),
            down_lanes(steps),
            pl.BlockSpec((1, CHUNK, 2 * steps), lambda i: (0, chunks - 1 - i, 0)),
            down_parts(state, inner),
            down_parts(state, inner),
            whole((6, chunks, inner)),
            whole((state, inner)),
            down_rows(inner),
            down_rows(inner),
            whole((inner,)),
            whole(e0.shape),
            whole(e1.shape),
        ],
        [
            (down_rows(inner), (count, inner), BF16),
            (down_rows(inner), (count, inner), BF16),
            (down_rows(inner), (count, inner), BF16),
            (down_lanes(steps), (steps, count), F32),
            (down_rows(2 * state), (count, 2 * state), F32),
            states,
            states,
            states,
            states,
            full((state, inner), BF16),
            full((16, inner), F32),
        ],
        [state_f32] * 3 + [chunk_f32] * 8 + [chunk_bf16] * 4 + [row_f32] * 2,
        US_MIX,
        (
            lengths,
            d_skip,
            act,
            target,
            source,
            factors,
            sl0,
            sf1,
            keeps,
            received,
            gate_z,
            d_norm,
            gain_mix,
            e0,
            e1,
        ),
        VMEM_MIX,
    )
    d_received = lax.ppermute(d_send, "dir", SWAP)

    def plain(kernel, name, args, outs, specs=None, out_specs=None, grid=()):
        resident = [pl.BlockSpec(memory_space=pltpu.VMEM)]
        return pl.pallas_call(
            kernel,
            name=name,
            grid=grid,
            in_specs=specs or resident * len(args),
            out_specs=out_specs or resident * len(outs),
            out_shape=[jax.ShapeDtypeStruct(shape, dtype) for shape, dtype in outs],
            compiler_params=pltpu.CompilerParams(vmem_limit_bytes=VMEM_SUMS * MIB),
            cost_estimate=cost(US_SUMS),
        )(*args)

    def halve(name, kept, got, bit):
        rows, wide = got.shape
        outs = [((rows // 2, wide), F32), ((rows // 2, wide), BF16)]
        return plain(
            functools.partial(halve_kernel, bit=bit),
            name,
            (kept, got),
            outs,
            [rows_of(2 * piece, wide)] * 2,
            [rows_of(piece, wide)] * 2,
            (rows // (2 * piece),),
        )

    blocks = 4
    shard = model // dp_count
    direct = dp_count == 16 and shard % 16 == 0
    piece = model // 16
    early_rows = (rows_of(model // 2 // blocks, 2 * inner), (model // 2, 2 * inner), BF16)
    early_mine, early_theirs, z_share = call(
        functools.partial(weights_kernel, shard=piece),
        "weights",
        blocks,
        [
            rows_of(model // blocks, count),
            whole((count, inner)),
            lanes_of(count, inner // blocks),
            whole((count, model)),
            rows_of(model // blocks, inner),
        ],
        [
            early_rows,
            early_rows,
            (pl.BlockSpec((1, 1, model // blocks), lambda i: (i, 0, 0)), (blocks, 1, model // blocks), F32),
        ],
        [],
        US_WEIGHTS,
        (turned, dz, mixed, cot, w_z),
        VMEM_WEIGHTS,
    )
    (early_mine, early_theirs), d_received = ordered((early_mine, early_theirs), d_received)

    def back(skipped, taken, start, dpre, moves):
        def rows_from(width):
            return pl.BlockSpec((CHUNK, width), lambda i: (i + skipped, 0))

        def lanes_from(height):
            return pl.BlockSpec((height, CHUNK), lambda i: (0, i + skipped))

        def parts_from(*rest):
            return pl.BlockSpec((1,) + rest, lambda i: (i + skipped,) + (0,) * len(rest))

        return call(
            functools.partial(back_kernel, skipped=skipped, chunks=chunks),
            "back" + str(skipped),
            taken,
            [
                smem(),
                smem(),
                rows_from(channels),
                rows_from(channels),
                lanes_from(steps),
                lanes_from(steps),
                pl.BlockSpec((1, CHUNK, 2 * steps), lambda i: (1, i + skipped, 0)),
                rows_from(2 * state),
                rows_from(inner),
                parts_from(state, inner),
                parts_from(state, inner),
                parts_from(state, inner),
                parts_from(state, inner),
                whole((6, chunks, inner)),
                whole((state, inner)),
                whole(start.shape),
                whole(e0.shape),
                whole(e1.shape),
                whole(spans.shape),
                anywhere(),
                anywhere(),
            ],
            [
                (rows_from(channels), (count, channels), BF16),
                (lanes_from(6 * heads), (6 * heads, count), F32),
                full((state, inner), F32),
            ],
            [
                state_f32,
                pltpu.VMEM((CHUNK, CHUNK), F32),
            ]
            + [chunk_bf16] * 2
            + [state_bf16] * 2
            + [pltpu.VMEM((16, inner), F32)],
            US_BACK * taken // chunks,
            (
                lengths,
                d_skip,
                act,
                slope,
                target,
                source,
                factors,
                dcc,
                dy,
                s0,
                s1,
                dl0,
                df1,
                keeps,
                d_received,
                start,
                e0,
                e1,
                spans,
                dpre,
                moves,
            ),
            VMEM_BACK,
            {19: 0, 20: 1} if skipped else {},
        )

    first = 1
    dpre, moves, carry = back(0, first, d_received, received, received)
    if direct:
        early_got = traded(early_theirs, "dp", 1, dp_count)
        early_keep, early_send = halve("halve_y", early_mine, early_got, 2)
        early_send, carry = ordered(early_send, carry)
        early_got = traded(early_send, "dp", 2, dp_count)
    dpre, moves, _ = back(first, chunks - first, carry, dpre, moves)
    if direct:
        early_keep, early_send = halve("halve_z", early_keep, early_got, 4)
        early_send, dpre = ordered(early_send, dpre)
        early_got = traded(early_send, "dp", 4, dp_count)

    tile = 256
    tiles = channels // tile
    def tile_of(height):
        return pl.BlockSpec((height, tile), lambda i: (0, jnp.minimum(i, tiles - 1)))

    wide = (tiles + 1) * tile
    late_out = (lanes_of(model // 2, tile), (model // 2, wide), BF16)
    dproj, dhalo, late_mine, late_theirs, draw, small = call(
        functools.partial(conv_back_kernel, shard=piece),
        "conv_back",
        tiles + 1,
        [
            smem(),
            whole((model, count)),
            whole((model, 16)),
            tile_of(count),
            tile_of(count),
            tile_of(16),
            tile_of(conv_w.shape[0]),
            whole((steps, count)),
            whole((steps, count)),
            whole((steps, 128)),
            whole((6 * heads, count)),
            whole((steps, count)),
            whole((model, inner)),
            whole(w_narrow.shape),
            whole((model,)),
            whole(z_share.shape),
            whole(mix_sums.shape),
            whole(e0.shape),
        ],
        [
            (tile_of(count), (count, channels), BF16),
            (tile_of(16), (16, channels), BF16),
            late_out,
            late_out,
            full((steps, count), BF16),
            full((16, wide // 2), BF16),
        ],
        [
            pltpu.VMEM((3 * count + 48, CHUNK + 16), BF16),
            pltpu.VMEM((CHUNK + 16, tile), BF16),
            pltpu.VMEM((8, model), F32),
            pltpu.VMEM((8, wide), F32),
        ],
        US_CONV,
        (
            lengths,
            turned,
            turn_halo,
            dpre,
            pre,
            pre_halo,
            conv_w,
            raw,
            dt,
            rate,
            moves,
            r,
            w_x,
            w_narrow,
            gain_in,
            z_share,
            mix_sums,
            e0,
        ),
        VMEM_CONV,
    )
    d_halo = lax.ppermute(dhalo, "dir", [(1, 0)])

    grad_in, out = call(
        inputs_kernel,
        "inputs",
        count // ROWS,
        [
            rows_of(ROWS, model),
            rows_of(ROWS, model),
            whole((model,)),
            rows_of(ROWS, channels),
            whole((16, channels)),
            lanes_of(steps, ROWS),
            rows_of(ROWS, inner),
            whole((model, inner)),
            whole(w_narrow.shape),
            whole((model, inner)),
            rows_of(ROWS, inner),
            whole((inner, model)),
        ],
        [rows_out(ROWS, model, BF16), rows_out(ROWS, model, BF16)],
        [pltpu.VMEM((ROWS, channels), BF16)],
        US_INPUTS,
        (x, cot, gain_in, dproj, d_halo, draw, dz, w_x, w_narrow, w_z, mixed, w_out),
        VMEM_INPUTS,
    )

    if not direct:
        def undivided(mine, theirs):
            even = lax.axis_index("dp") % 2 == 0
            both = [jnp.where(even, mine, theirs), jnp.where(even, theirs, mine)]
            both = [part.reshape(8, 1, piece, part.shape[1]) for part in both]
            return jnp.concatenate(both, axis=1).reshape(model, mine.shape[1])

        early = undivided(early_mine, early_theirs)
        g_out = early[:, :inner].reshape(16, piece, 2, model).transpose(0, 2, 1, 3)
        late = sum_shards(undivided(late_mine, late_theirs), dp_count)
        small = jnp.concatenate([small[0:8], small[8:16]], axis=1).astype(F32)
        small = sum_all(small, dp_count)
        return (
            out[None],
            grad_in[None],
            late[:, :inner],
            sum_shards(early[:, inner:], dp_count),
            late[:, inner : inner + 4 * state + steps],
            sum_shards(g_out.reshape(inner, model), dp_count),
            small[5, :model],
            small[0:4, :channels],
            small[6, 128 : 128 + steps].reshape(dt_bias.shape),
            small[6, 256 : 256 + steps].reshape(a_log.shape),
            small[6, :heads],
            small[4, :inner],
        )

    early_got, late_theirs = ordered(early_got, late_theirs)
    late_got = traded(late_theirs, "dp", 1, dp_count)
    small_got = traded(small, "dp", 1, dp_count)
    quarter = (model // 4 + 16, wide // 2)
    kept, across, along, both = plain(
        functools.partial(quarters_kernel, shard=piece),
        "quarters",
        (late_mine, late_got, small, small_got),
        [((model // 4 + 16, wide // 2), F32), (quarter, BF16), (quarter, BF16), (quarter, BF16)],
    )
    early_keep, early_send = halve("halve_z2", early_keep, early_got, 8)
    corners = [(a, b) for a in range(2) for b in range(dp_count)]
    across = traded(across, "dir", 1, 2)
    along = traded(along, "dp", 2, dp_count)
    both = lax.ppermute(
        both,
        ("dir", "dp"),
        [(a * dp_count + b, (1 - a) * dp_count + (b ^ 2)) for a, b in corners],
    )
    early_got = traded(early_send, "dp", 8, dp_count)
    (early,) = plain(sum_kernel, "early_sum", (early_keep, early_got), [((piece, 2 * inner), BF16)])
    grad_in, early, both = lax.optimization_barrier((grad_in, early, both))
    early_got = traded(early, "dir", 1, 2)
    message = (piece + 16, wide // 2)
    own, *sends = plain(
        functools.partial(levels_kernel, shard=piece),
        "levels",
        (kept, across, along, both),
        [((piece + 16, wide // 2), F32)] + [(message, BF16)] * 3,
    )
    gots = [traded(sent, "dp", 4 * bits, dp_count) for bits, sent in zip((1, 2, 3), sends)]
    late, small = plain(
        functools.partial(last_kernel, shard=piece),
        "last",
        (own, *gots),
        [((piece, wide // 2), BF16), ((16, wide // 2), F32)],
    )
    late_got = traded(late, "dir", 1, 2)
    g_x, g_zz, g_bc, g_o, g_taps, g_mix, g_in, g_skip, g_bias, g_alog = plain(
        finish_kernel,
        "finish",
        (late, late_got, early, early_got, small),
        [
            ((piece, inner), F32),
            ((piece, inner), F32),
            ((piece, w_bcdt.shape[1]), F32),
            ((2 * piece, model), F32),
            (conv_w.shape, F32),
            ((inner,), F32),
            ((model,), F32),
            ((heads,), F32),
            (dt_bias.shape, F32),
            (a_log.shape, F32),
        ],
    )
    return (
        out[None],
        grad_in[None],
        g_x,
        g_zz,
        g_bc,
        g_o,
        g_in,
        g_taps,
        g_bias,
        g_alog,
        g_skip,
        g_mix,
    )


def solution(mesh):
    return jax.shard_map(
        functools.partial(local, mesh.shape["dp"]),
        mesh=mesh,
        in_specs=(
            P("dir", "dp", None),
            P("dp", None),
            P(),
            P(),
            P(),
            P(),
            P(),
            P(),
            P(),
            P(),
            P(),
            P(),
            P("dir", "dp", None),
        ),
        out_specs=(
            P("dir", "dp", None),
            P("dir", "dp", None),
            P("dp", None),
            P("dp", None),
            P("dp", None),
            P("dp", None),
            P(),
            P(),
            P(),
            P(),
            P(),
            P(),
        ),
        check_vma=False,
    )
```

```python
import functools

import jax
import jax.numpy as jnp
import numpy as np
from jax import lax
from jax.experimental import pallas as pl
from jax.experimental.pallas import tpu as pltpu
from jax.sharding import PartitionSpec as P

F32 = jnp.float32
BF16 = jnp.bfloat16
CHUNK = 128
ROWS = 256
SUB = 64
EPS = 1e-05
LOG2E = 1.4426950408889634
SWAP = [(0, 1), (1, 0)]
MIB = 1024 * 1024
VMEM_GATES = 52
VMEM_PROJ = 56
VMEM_INTRA = 12
VMEM_MIX = 52
VMEM_WEIGHTS = 52
VMEM_BACK = 56
VMEM_CONV = 56
VMEM_INPUTS = 56
VMEM_SUMS = 8
US_GATES = 10
US_PROJ = 20
US_INTRA = 12
US_MIX = 30
US_WEIGHTS = 10
US_BACK = 30
US_CONV = 17
US_INPUTS = 16
US_SUMS = 2
NT = (((1,), (1,)), ((), ()))
TN = (((0,), (0,)), ((), ()))
EXACT = lax.Precision.HIGHEST


def mm(left, right):
    return jnp.dot(left, right, preferred_element_type=F32)


def mm_nt(left, right):
    return lax.dot_general(left, right, NT, preferred_element_type=F32)


def mm_tn(left, right):
    return lax.dot_general(left, right, TN, preferred_element_type=F32)


def exact_mm(left, right):
    return jnp.dot(left, right, precision=EXACT, preferred_element_type=F32)


def sequence_bounds(lengths_ref, half_rows):
    bounds, total = [], 0
    for position in range(lengths_ref.shape[1]):
        total = total + lengths_ref[0, position]
        bounds.append(total)
    return bounds, lax.axis_index("dir") * half_rows


def start_of(row, bounds):
    start = jnp.where(row < 0, -1, 0)
    for bound in bounds:
        start = jnp.where(row >= bound, bound, start)
    return start


def same_sequence(first, bounds):
    starts = start_of(first + lane_iota(CHUNK), bounds)
    turned = jnp.broadcast_to(starts.astype(F32), (8, CHUNK)).T[:, 0:1]
    return (turned == starts.astype(F32)) & (row_iota(CHUNK) != lane_iota(CHUNK))


def row_iota(count):
    return lax.broadcasted_iota(jnp.int32, (count, 1), 0)


def lane_iota(count):
    return lax.broadcasted_iota(jnp.int32, (1, count), 1)


def flag(condition):
    return jnp.where(condition, 1.0, 0.0)


def in_parts(values, parts):
    out = []
    for _ in range(parts):
        part = values.astype(BF16).astype(F32)
        out.append(part)
        values = values - part
    return jnp.concatenate(out, axis=0)


def fold(values):
    return jnp.sum(values.reshape(values.shape[0] // 8, 8, values.shape[1]), axis=0)


def row_of(ref):
    return ref[...].reshape(1, ref.shape[0])


def column_of(ref, steps):
    heads = steps // 2
    place = row_iota(steps)
    column = jnp.zeros((steps, 1), F32)
    for step in range(steps):
        column = jnp.where(place == step, ref[step // heads, step % heads], column)
    return column


def gates_kernel(normed_ref, c_ref, wz_ref, wo_ref, z_ref, dnorm_ref, turned_ref):
    turned_ref[...] = normed_ref[...].T
    z_ref[...] = mm(normed_ref[...], wz_ref[...]).astype(BF16)
    dnorm_ref[...] = mm_nt(c_ref[...], wo_ref[...]).astype(BF16)


def step_factors(
    lengths_ref,
    bias_ref,
    alog_ref,
    e0_ref,
    e1_ref,
    raw_ref,
    dt_ref,
    rate_ref,
    target_ref,
    source_ref,
    factors_ref,
    keeps_ref,
):
    steps, count = raw_ref.shape
    heads = steps // 2
    bounds, base = sequence_bounds(lengths_ref, count)
    rate = jnp.exp(column_of(alog_ref, steps))
    rate_ref[...] = jnp.broadcast_to(rate, (steps, 128))
    raw = raw_ref[...] + column_of(bias_ref, steps)
    raw_ref[...] = raw
    dt = jnp.maximum(raw, 0.0) + jnp.log1p(jnp.exp(-jnp.abs(raw)))
    dt_ref[...] = dt
    log_dt = jnp.log(jnp.maximum(dt, 1e-37))
    chunks = count // CHUNK
    upto = flag(row_iota(CHUNK) <= lane_iota(CHUNK))
    fall = dt * rate
    stacked = [fall[:, chunk * CHUNK : (chunk + 1) * CHUNK] for chunk in range(chunks)]
    summed = exact_mm(jnp.concatenate(stacked, axis=0), upto)
    lane = lane_iota(CHUNK)
    keeps = jnp.zeros((steps, CHUNK), F32)
    for chunk in range(chunks):
        span = slice(chunk * CHUNK, (chunk + 1) * CHUNK)
        first = base + chunk * CHUNK
        inc = summed[chunk * steps : (chunk + 1) * steps]
        dt_c, log_c = dt[:, span], log_dt[:, span]
        inc0 = inc[:heads]
        exc1 = inc[heads:] - fall[heads:, span]
        total0 = inc0[:, CHUNK - 1 :]
        total1 = inc[heads:, CHUNK - 1 :]
        target = jnp.concatenate([-inc0, exc1], axis=0) * LOG2E
        source = jnp.concatenate([inc0 + log_c[:heads], log_c[heads:] - exc1], axis=0) * LOG2E
        target_ref[:, span] = target
        source_ref[:, span] = source
        starts = start_of(first + lane, bounds)
        before = start_of(first - 1, bounds)
        left = start_of(first, bounds)
        right = start_of(first + CHUNK - 1, bounds)
        after = start_of(first + CHUNK, bounds)
        enter0 = jnp.where(starts == before, jnp.exp(-inc0), 0.0)
        enter1 = jnp.where(starts == after, jnp.exp(exc1 - total1), 0.0)
        leave0 = jnp.where(starts == right, dt_c[:heads] * jnp.exp(inc0 - total0), 0.0)
        leave1 = jnp.where(starts == left, dt_c[heads:] * jnp.exp(-exc1), 0.0)
        enter = jnp.concatenate([enter0, enter1], axis=0)
        leave = jnp.concatenate([leave0, leave1], axis=0)
        factors_ref[0, span, :] = in_parts(enter, 2).T.astype(BF16)
        factors_ref[1, span, :] = in_parts(leave, 2).T.astype(BF16)
        keep0 = jnp.where(before == right, jnp.exp(-total0), 0.0)
        keep1 = jnp.where(after == left, jnp.exp(-total1), 0.0)
        keeps = jnp.where(lane == chunk, jnp.concatenate([keep0, keep1], axis=0), keeps)
    ahead = jnp.zeros_like(keeps)
    behind = jnp.zeros_like(keeps)
    run_a = jnp.ones((steps, 1), F32)
    run_b = jnp.ones((steps, 1), F32)
    for chunk in range(chunks):
        ahead = jnp.where(lane == chunk, run_a, ahead)
        run_a = run_a * keeps[:, chunk : chunk + 1]
        last = chunks - 1 - chunk
        behind = jnp.where(lane == last, run_b, behind)
        run_b = run_b * keeps[:, last : last + 1]
    for place, values in enumerate((keeps, ahead, behind)):
        columns = in_parts(values, 2).T.astype(BF16)[0:16]
        keeps_ref[2 * place] = mm(columns, e0_ref[...])[0:chunks]
        keeps_ref[2 * place + 1] = mm(columns, e1_ref[...])[0:chunks]


def shifts(first, bounds, sign, height):
    row = lax.broadcasted_iota(jnp.int32, (height, CHUNK + 16), 0)
    col = lane_iota(CHUNK + 16)
    parts = []
    for lag in (1, 2, 3):
        later = first + col + (lag - 16 if sign < 0 else 0)
        near = later - start_of(later, bounds) < lag
        place = jnp.where(near, -CHUNK, col)
        offset = {-1: 16 - lag, 1: lag, 0: lag - height}[sign]
        parts.append(flag(place == row + offset))
    return jnp.concatenate(parts, axis=0).astype(BF16)


def proj_kernel(
    lengths_ref,
    bias_ref,
    alog_ref,
    x_ref,
    halo_ref,
    gain_ref,
    wx_ref,
    wbc_ref,
    taps_ref,
    e0_ref,
    e1_ref,
    normed_ref,
    raw_ref,
    dt_ref,
    rate_ref,
    target_ref,
    source_ref,
    factors_ref,
    keeps_ref,
    pre_ref,
    act_ref,
    slope_ref,
    s0_ref,
    sf1_ref,
    send_ref,
    prehalo_ref,
    turnhalo_ref,
    buf,
    acc0,
    acc1,
    left0,
    left1,
):
    step = pl.program_id(0)
    per = ROWS // CHUNK
    bounds, base = sequence_bounds(lengths_ref, pl.num_programs(0) * ROWS)
    inner = wx_ref.shape[1]
    channels = taps_ref.shape[1]
    state = (channels - inner) // 4

    @pl.when(step == 0)
    def _():
        count = x_ref.shape[0]
        gain = row_of(gain_ref)

        @pl.loop(0, count // CHUNK, unroll=4)
        def _(chunk):
            rows = pl.ds(pl.multiple_of(chunk * CHUNK, CHUNK), CHUNK)
            x = x_ref[rows, :].astype(F32)
            inv = lax.rsqrt(jnp.mean(x * x, axis=1, keepdims=True) + EPS)
            normed = (x * inv * gain).astype(BF16)
            normed_ref[rows, :] = normed
            raw = mm_nt(wbc_ref[channels - inner :, :], normed)
            raw_ref[:, rows] = raw.astype(BF16).astype(F32)

        step_factors(
            lengths_ref,
            bias_ref,
            alog_ref,
            e0_ref,
            e1_ref,
            raw_ref,
            dt_ref,
            rate_ref,
            target_ref,
            source_ref,
            factors_ref,
            keeps_ref,
        )
        x = halo_ref[...].astype(F32)
        inv = lax.rsqrt(jnp.mean(x * x, axis=1, keepdims=True) + EPS)
        normed = x * inv * gain
        turnhalo_ref[...] = normed.T.astype(BF16)
        normed = normed.astype(BF16)
        prehalo_ref[:, 0:inner] = mm(normed, wx_ref[...]).astype(BF16)
        prehalo_ref[:, inner:channels] = mm_nt(normed, wbc_ref[0 : channels - inner, :]).astype(BF16)
        buf[0:16, :] = prehalo_ref[...]
        acc0[...] = jnp.zeros_like(acc0)
        acc1[...] = jnp.zeros_like(acc1)

    @pl.when(step > 0)
    def _():
        buf[0:16, :] = buf[ROWS : ROWS + 16, :]

    normed = normed_ref[pl.ds(pl.multiple_of(step * ROWS, ROWS), ROWS), :]
    for tile in range(inner // 256):
        cols = slice(tile * 256, tile * 256 + 256)
        px = mm(normed, wx_ref[:, cols]).astype(BF16)
        pre_ref[:, cols] = px
        buf[16 : 16 + ROWS, cols] = px
    pb = mm_nt(normed, wbc_ref[0 : channels - inner, :]).astype(BF16)
    pre_ref[:, inner:channels] = pb
    buf[16 : 16 + ROWS, inner:channels] = pb

    first = base + step * ROWS
    for part in range(per):
        offset = part * CHUNK
        shift = shifts(first + offset, bounds, -1, CHUNK)
        here = pl.ds(pl.multiple_of(step * ROWS + offset, CHUNK), CHUNK)
        leave_cols = factors_ref[1, here, :]
        for tile in range(channels // 256):
            wide = slice(tile * 256, tile * 256 + 256)
            moved = mm(shift, buf[offset : offset + CHUNK + 16, wide])
            if tile * 256 < inner:
                leave0 = mm(leave_cols, e0_ref[:, wide])
                leave1 = mm(leave_cols, e1_ref[:, wide])
            for column in (0, 128):
                cols = slice(tile * 256 + column, tile * 256 + column + 128)
                cut = slice(column, column + 128)
                for row in range(0, CHUNK, SUB):
                    here = buf[offset + 16 + row : offset + 16 + row + SUB, cols]
                    conv = here.astype(F32) * taps_ref[3:4, cols]
                    for lag in (1, 2, 3):
                        at = (lag - 1) * CHUNK + row
                        conv = conv + moved[at : at + SUB, cut] * taps_ref[3 - lag : 4 - lag, cols]
                    sig = jax.nn.sigmoid(conv)
                    act = conv * sig
                    span = slice(offset + row, offset + row + SUB)
                    act_ref[span, cols] = act.astype(BF16)
                    slope_ref[span, cols] = (sig + act - act * sig).astype(BF16)
                    if tile * 256 < inner:
                        held = slice(row, row + SUB)
                        left0[held, cols] = (act * leave0[held, cut]).astype(BF16)
                        left1[held, cols] = (act * leave1[held, cut]).astype(BF16)
        turned = act_ref[offset : offset + CHUNK, inner:channels].astype(F32).T.astype(BF16)
        s0_ref[part] = acc0[...].astype(BF16)
        chunk = pl.ds(step * per + part, 1)
        acc0[...] = keeps_ref[0, chunk, :] * acc0[...] + mm(turned[0:state], left0[...])
        fresh1 = mm(turned[2 * state : 3 * state], left1[...])
        sf1_ref[part] = fresh1.astype(BF16)
        acc1[...] = acc1[...] + keeps_ref[3, chunk, :] * fresh1

    @pl.when(step == pl.num_programs(0) - 1)
    def _():
        send_ref[...] = jnp.where(base > 0, acc1[...], acc0[...]).astype(BF16)


def bc_columns(act_ref, inner, state):
    return [act_ref[:, inner + part * state : inner + (part + 1) * state] for part in range(4)]


def cut_pair(values, width):
    zero = jnp.zeros_like(values)
    first = lane_iota(2 * width) < width
    return jnp.concatenate([jnp.where(first, values, zero), jnp.where(first, zero, values)], axis=0)


def mix_kernel(
    lengths_ref,
    skip_ref,
    act_ref,
    target_ref,
    source_ref,
    factors_ref,
    sl0_ref,
    sf1_ref,
    keeps_ref,
    recv_ref,
    z_ref,
    dnorm_ref,
    gain_ref,
    e0_ref,
    e1_ref,
    mixed_ref,
    dz_ref,
    dy_ref,
    r_ref,
    dcc_ref,
    dl0_ref,
    df1_ref,
    s0_ref,
    s1_ref,
    send_ref,
    sums_ref,
    carry1,
    acc0,
    acc1,
    enter0,
    enter1,
    from0,
    from1,
    within,
    gated_s,
    slope_s,
    gate_s,
    in0,
    in1,
    prod0,
    prod1,
    skip_s,
    gain_s,
):
    step = pl.program_id(0)
    chunk = pl.num_programs(0) - 1 - step
    bounds, base = sequence_bounds(lengths_ref, pl.num_programs(0) * CHUNK)
    first = base + chunk * CHUNK
    inner = gain_ref.shape[0]
    heads = r_ref.shape[0] // 2
    width = inner // heads
    state = recv_ref.shape[0]
    small = 32

    @pl.when(step == 0)
    def _():
        recv = recv_ref[...].astype(F32)
        carry1[...] = jnp.where(base > 0, jnp.zeros_like(recv), recv)
        acc0[...] = jnp.zeros_like(acc0)
        acc1[...] = jnp.zeros_like(acc1)
        sums_ref[...] = jnp.zeros_like(sums_ref)
        gain_s[...] = row_of(gain_ref)
        left = lane_iota(2 * width) < width
        for pair in range(heads // 2):
            skip_s[:, pair * 2 * width : (pair + 1) * 2 * width] = jnp.where(
                left, skip_ref[2 * pair], skip_ref[2 * pair + 1]
            )

    keep0 = keeps_ref[0, pl.ds(chunk, 1), :]
    keep1 = keeps_ref[1, pl.ds(chunk, 1), :]
    ahead0 = keeps_ref[2, pl.ds(chunk, 1), :] * jnp.where(base > 0, 1.0, 0.0)
    s0 = (sl0_ref[0].astype(F32) + ahead0 * recv_ref[...].astype(F32)).astype(BF16)
    s1 = carry1[...].astype(BF16)
    carry1[...] = keep1 * carry1[...] + sf1_ref[0].astype(F32)
    s0_ref[0] = s0
    s1_ref[0] = s1
    enter_cols = factors_ref[0]
    turned = act_ref[:, inner:].astype(F32).T.astype(BF16)
    b0, c0, b1, c1 = bc_columns(act_ref, inner, state)
    enter0[...] = mm(enter_cols, e0_ref[...])
    from0[...] = mm(c0, s0)
    enter1[...] = mm(enter_cols, e1_ref[...])
    from1[...] = mm(c1, s1)
    t, s = row_iota(CHUNK), lane_iota(CHUNK)
    lower = t > s
    scores = jnp.where(lower, mm_nt(c0, b0), mm_nt(c1, b1))
    scores = jnp.where(same_sequence(first, bounds), scores, 0.0)
    columns = target_ref[...].T
    for pair in range(heads // 2):
        cols = slice(pair * 2 * width, (pair + 1) * 2 * width)
        weights = []
        for head in (2 * pair, 2 * pair + 1):
            power = jnp.where(
                lower,
                columns[:, head : head + 1] + source_ref[head : head + 1, :],
                columns[:, heads + head : heads + head + 1]
                + source_ref[heads + head : heads + head + 1, :],
            )
            weights.append((jnp.exp2(power) * scores).astype(BF16))
        x_cut = cut_pair(act_ref[:, cols], width)
        within[:, cols] = mm(jnp.concatenate(weights, axis=1), x_cut)
    tiles = [slice(tile * 128, tile * 128 + 128) for tile in range(inner // 128)]
    for row in range(0, CHUNK, small):
        rows = slice(row, row + small)
        square = jnp.zeros((small, 128), F32)
        cross = jnp.zeros((small, 128), F32)
        for cols in tiles:
            mixer = within[rows, cols] + skip_s[:, cols] * act_ref[rows, cols].astype(F32)
            mixer = mixer + enter0[rows, cols] * from0[rows, cols]
            mixer = mixer + enter1[rows, cols] * from1[rows, cols]
            z = z_ref[rows, cols].astype(F32)
            sig = jax.nn.sigmoid(z)
            gate = z * sig
            gated = mixer * gate
            square = square + gated * gated
            cross = cross + dnorm_ref[rows, cols].astype(F32) * gain_s[:, cols] * gated
            gated_s[rows, cols] = gated
            gate_s[rows, cols] = gate
            slope_s[rows, cols] = mixer * (sig + gate - gate * sig)
        live = flag(first + row + row_iota(small) < bounds[len(bounds) - 2])
        scale = lax.rsqrt(jnp.sum(square, axis=1, keepdims=True) * (1.0 / inner) + EPS)
        back = scale * scale * (jnp.sum(cross, axis=1, keepdims=True) * (1.0 / inner))
        scale = jnp.broadcast_to(scale * live, (small, 128))
        back = jnp.broadcast_to(back, (small, 128))
        for cols in tiles:
            gated = gated_s[rows, cols]
            unit = gated * scale
            gain = gain_s[:, cols]
            mixed_ref[rows, cols] = (unit * gain).astype(BF16)
            dnorm = dnorm_ref[rows, cols].astype(F32)
            sums_ref[0:8, cols] += fold(dnorm * unit)
            dgated = scale * (dnorm * gain - gated * back)
            dz_ref[rows, cols] = (dgated * slope_s[rows, cols]).astype(BF16)
            dy = dgated * gate_s[rows, cols]
            dy_ref[rows, cols] = dy.astype(BF16)
            sums_ref[8:16, cols] += fold(dy * act_ref[rows, cols].astype(F32))
            entered0 = dy * enter0[rows, cols]
            entered1 = dy * enter1[rows, cols]
            in0[rows, cols] = entered0.astype(BF16)
            in1[rows, cols] = entered1.astype(BF16)
            prod0[rows, cols] = (entered0 * from0[rows, cols]).astype(BF16)
            prod1[rows, cols] = (entered1 * from1[rows, cols]).astype(BF16)
    ones = e0_ref[0:heads, :]
    r_ref[0:heads, :] = mm_nt(ones, prod0[...])
    r_ref[heads : 2 * heads, :] = mm_nt(ones, prod1[...])
    dcc_ref[:, 0:state] = mm_nt(in0[...], s0)
    dcc_ref[:, state : 2 * state] = mm_nt(in1[...], s1)
    dl0_ref[0] = acc0[...].astype(BF16)
    acc0[...] = keep0 * acc0[...] + mm(turned[state : 2 * state], in0[...])
    df1 = mm(turned[3 * state : 4 * state], in1[...])
    df1_ref[0] = df1.astype(BF16)
    acc1[...] = acc1[...] + keeps_ref[5, pl.ds(chunk, 1), :] * df1

    @pl.when(step == pl.num_programs(0) - 1)
    def _():
        send_ref[...] = jnp.where(base > 0, acc0[...], acc1[...]).astype(BF16)


def back_kernel(
    lengths_ref,
    skip_ref,
    act_ref,
    slope_ref,
    target_ref,
    source_ref,
    factors_ref,
    dcc_ref,
    dy_ref,
    s0_ref,
    s1_ref,
    dl0_ref,
    df1_ref,
    keeps_ref,
    recv_ref,
    start_ref,
    e0_ref,
    e1_ref,
    spans_ref,
    _dpre_ref,
    _moves_ref,
    dpre_ref,
    moves_ref,
    last_ref,
    carry1,
    dscore,
    out0,
    out1,
    ds0,
    ds1,
    kept,
    *,
    skipped,
    chunks,
):
    step = pl.program_id(0)
    chunk = step + skipped
    bounds, base = sequence_bounds(lengths_ref, chunks * CHUNK)
    first = base + chunk * CHUNK
    heads = skip_ref.shape[0]
    inner = keeps_ref.shape[2]
    width = inner // heads
    state = recv_ref.shape[0]

    @pl.when(step == 0)
    def _():
        if skipped:
            carry1[...] = start_ref[...]
        else:
            recv = recv_ref[...].astype(F32)
            carry1[...] = jnp.where(base > 0, recv, jnp.zeros_like(recv))

    keep0 = keeps_ref[0, pl.ds(chunk, 1), :]
    keep1 = keeps_ref[1, pl.ds(chunk, 1), :]
    behind0 = keeps_ref[4, pl.ds(chunk, 1), :] * jnp.where(base > 0, 0.0, 1.0)
    d0 = dl0_ref[0].astype(F32) + behind0 * recv_ref[...].astype(F32)
    d1 = carry1[...]
    ds0[...] = d0.astype(BF16)
    ds1[...] = d1.astype(BF16)
    kept0 = jnp.sum(d0 * s0_ref[0].astype(F32), axis=0, keepdims=True) * keep0
    kept1 = jnp.sum(d1 * s1_ref[0].astype(F32), axis=0, keepdims=True) * keep1
    carry1[...] = keep1 * d1 + df1_ref[0].astype(F32)

    t = lane_iota(CHUNK)
    b0, c0, b1, c1 = bc_columns(act_ref, inner, state)
    same = same_sequence(first, bounds)
    both = jnp.where(row_iota(CHUNK) < t, mm_nt(b0, c0), mm_nt(b1, c1))
    both = jnp.where(same, both, 0.0)
    halves = []
    for row in range(0, CHUNK, SUB):
        early = row + row_iota(SUB) < t
        halves.append((slice(row, row + SUB), early, flag(early), both[row : row + SUB]))
    in_cols = source_ref[...].T
    leave_cols = factors_ref[0]
    dscore[...] = jnp.zeros_like(dscore)
    left = lane_iota(2 * width) < width

    def columns_of(pair):
        return slice(pair * 2 * width, (pair + 1) * 2 * width)

    def products(pair):
        cols = columns_of(pair)
        dweights = mm_nt(cut_pair(act_ref[:, cols], width), dy_ref[:, cols])
        return dweights

    def carried(pair):
        cols = columns_of(pair)
        leave0 = mm(leave_cols, e0_ref[:, cols])
        leave1 = mm(leave_cols, e1_ref[:, cols])
        return leave0, leave1, mm(b0, ds0[:, cols]), mm(b1, ds1[:, cols])

    def within(pair, dweights):
        weights, lows, alls, scored = [], [], [], [0.0] * len(halves)
        for part in (0, 1):
            head = 2 * pair + part
            parts, low_parts, all_parts = [], [], []
            sum0 = jnp.zeros((8, CHUNK), F32)
            sum1 = jnp.zeros((8, CHUNK), F32)
            for place, (rows, early, early_f, scores) in enumerate(halves):
                power = jnp.where(
                    early,
                    in_cols[rows, head : head + 1] + target_ref[head : head + 1, :],
                    in_cols[rows, heads + head : heads + head + 1]
                    + target_ref[heads + head : heads + head + 1, :],
                )
                decay = jnp.exp2(power)
                parts.append((decay * scores).astype(BF16))
                at = part * CHUNK + rows.start
                dweight = dweights[at : at + SUB] * decay
                scored[place] = scored[place] + dweight
                change = dweight * scores
                low = (change * early_f).astype(BF16)
                change = change.astype(BF16)
                low_parts.append(low)
                all_parts.append(change)
                sum0 = sum0 + fold(low.astype(F32))
                sum1 = sum1 + fold(change.astype(F32))
            weights.append(jnp.concatenate(parts, axis=0))
            lows.append(jnp.concatenate(low_parts, axis=0))
            alls.append(jnp.concatenate(all_parts, axis=0))
            moves_ref[head : head + 1, :] = jnp.sum(sum0, axis=0, keepdims=True)
            moves_ref[heads + head : heads + head + 1, :] = jnp.sum(sum1, axis=0, keepdims=True)
        for place, (rows, _, _, _) in enumerate(halves):
            dscore[rows, :] += scored[place]
        return jnp.concatenate(weights, axis=1), lows + alls

    def gathered(pair, weights, lows, states):
        cols = columns_of(pair)
        leave0, leave1, from0, from1 = states
        dx = mm(weights, cut_pair(dy_ref[:, cols], width))
        skip = jnp.where(left, skip_ref[2 * pair], skip_ref[2 * pair + 1])
        firsts, totals = [], []
        sum0 = jnp.zeros((8, 2 * width), F32)
        sum1 = jnp.zeros((8, 2 * width), F32)
        for rows, _, _, _ in halves:
            xf = act_ref[rows, cols].astype(F32)
            came0 = leave0[rows] * from0[rows]
            came1 = leave1[rows] * from1[rows]
            dconv = dx[rows] + skip * dy_ref[rows, cols].astype(F32) + came0 + came1
            dpre_ref[rows, cols] = (dconv * slope_ref[rows, cols].astype(F32)).astype(BF16)
            out0[rows, cols] = (xf * leave0[rows]).astype(BF16)
            out1[rows, cols] = (xf * leave1[rows]).astype(BF16)
            came0 = (xf * came0).astype(BF16)
            came1 = (xf * came1).astype(BF16)
            sum0 = sum0 + fold(came0.astype(F32))
            sum1 = sum1 + fold(came1.astype(F32))
            firsts.append(came0)
            totals.append(came1)
        kept[0:8, cols] = sum0
        kept[8:16, cols] = sum1
        return lows + [jnp.concatenate(firsts, axis=0), jnp.concatenate(totals, axis=0)]

    def summed(pair, lows):
        sums = mm_nt(spans_ref[...], jnp.concatenate(lows, axis=1))
        moves_ref[2 * heads + 2 * pair : 2 * heads + 2 * pair + 2, :] = sums[0:2]
        moves_ref[3 * heads + 2 * pair : 3 * heads + 2 * pair + 2, :] = sums[2:4]


    pairs = heads // 2
    ahead = {0: products(0)}
    held, done = {}, {}
    for pair in range(pairs + 2):
        if pair + 1 < pairs:
            ahead[pair + 1] = products(pair + 1)
        if 0 < pair <= pairs:
            weights, lows = held.pop(pair - 1)
            states = carried(pair - 1)
            done[pair - 1] = gathered(pair - 1, weights, lows, states)
        if pair < pairs:
            held[pair] = within(pair, ahead.pop(pair))
        if pair > 1:
            summed(pair - 2, done.pop(pair - 2))
    dscores = jnp.where(same, dscore[...], 0.0)
    dscore0 = jnp.where(row_iota(CHUNK) < t, dscores, 0.0).astype(BF16)
    dscore1 = jnp.where(row_iota(CHUNK) < t, 0.0, dscores).astype(BF16)
    kept[0:1, :] += kept0
    kept[8:9, :] += kept1
    kept_sum = mm_nt(e0_ref[0:heads, :], in_parts(kept[...], 2).astype(BF16))
    kept_sum = kept_sum[:, 0:16] + kept_sum[:, 16:32]
    for direction in (0, 1):
        column = jnp.sum(kept_sum[:, 8 * direction : 8 * direction + 8], axis=1, keepdims=True)
        moves_ref[(4 + direction) * heads : (5 + direction) * heads, :] = jnp.broadcast_to(
            column, (heads, CHUNK)
        )
    db0 = mm(dscore0, c0) + mm_nt(out0[...], ds0[...])
    db1 = mm(dscore1, c1) + mm_nt(out1[...], ds1[...])
    dc0 = mm_tn(dscore0, b0) + dcc_ref[:, 0:state]
    dc1 = mm_tn(dscore1, b1) + dcc_ref[:, state : 2 * state]
    dbc = jnp.concatenate([db0, dc0, db1, dc1], axis=1)
    dpre_ref[:, inner:] = (dbc * slope_ref[:, inner:].astype(F32)).astype(BF16)

    @pl.when(step == pl.num_programs(0) - 1)
    def _():
        last_ref[...] = carry1[...]


def steps_back(raw, dt, rate, moves, r):
    steps = raw.shape[0]
    heads = steps // 2
    chunks = raw.shape[1] // CHUNK
    s, t = row_iota(CHUNK), lane_iota(CHUNK)

    def stack(values):
        parts = [values[:, chunk * CHUNK : (chunk + 1) * CHUNK] for chunk in range(chunks)]
        return jnp.concatenate(parts, axis=0)

    def unstack(values):
        parts = [values[chunk * heads : (chunk + 1) * heads] for chunk in range(chunks)]
        return jnp.concatenate(parts, axis=1)

    got0, got, own0, own, kept0, kept1 = [
        moves[part * heads : (part + 1) * heads] for part in range(6)
    ]
    own1, got1 = own - own0, got - got0
    da0 = exact_mm(stack(got0 + r[:heads] - own0), flag(s >= t))
    da1 = exact_mm(stack(got1 + r[heads:] - own1), flag(s <= t))
    da = -jnp.concatenate([unstack(da0) + kept0, unstack(da1) + kept1], axis=0)
    dlog = jnp.concatenate([own0, own1], axis=0)
    sig = jax.nn.sigmoid(raw)
    ratio = jnp.where(raw < -20.0, 1.0, sig / jnp.maximum(dt, 1e-37))
    return dlog * ratio + da * rate * sig, jnp.sum(da * dt, axis=1, keepdims=True) * rate


def by_core(product, shard, mine_ref, theirs_ref):
    pieces = [product[place : place + shard] for place in range(0, product.shape[0], shard)]
    even = jnp.concatenate(pieces[0::2], axis=0)
    odd = jnp.concatenate(pieces[1::2], axis=0)
    core = lax.rem(lax.axis_index("dp"), 2)

    @pl.when(core == 0)
    def _():
        mine_ref[...] = even
        theirs_ref[...] = odd

    @pl.when(core == 1)
    def _():
        mine_ref[...] = odd
        theirs_ref[...] = even


def weights_kernel(
    turned_ref, dz_ref, mixed_ref, c_ref, wz_ref, mine_ref, theirs_ref, gain_ref, *, shard
):
    product = mm_tn(mixed_ref[...], c_ref[...]).astype(BF16)
    pieces = []
    for place in range(0, product.shape[0], 2 * shard):
        pieces.append(
            jnp.concatenate(
                [product[place : place + shard], product[place + shard : place + 2 * shard]], axis=1
            )
        )
    gate = mm(turned_ref[...], dz_ref[...])
    both = jnp.concatenate([jnp.concatenate(pieces, axis=0), gate.astype(BF16)], axis=1)
    by_core(both, shard, mine_ref, theirs_ref)
    share = (gate * wz_ref[...].astype(F32)).astype(BF16)
    gain_ref[0] = mm_nt(jnp.ones((8, share.shape[1]), BF16), share)[0:1]


def conv_back_kernel(
    lengths_ref,
    turned_ref,
    turnhalo_ref,
    dpre_ref,
    pre_ref,
    prehalo_ref,
    taps_ref,
    raw_ref,
    dt_ref,
    rate_ref,
    moves_ref,
    r_ref,
    w_ref,
    narrow_ref,
    gain_ref,
    share_ref,
    mix_sums_ref,
    e0_ref,
    dproj_ref,
    dhalo_ref,
    mine_ref,
    theirs_ref,
    draw_ref,
    small_ref,
    shift,
    buf,
    gains,
    sums_ref,
    *,
    shard,
):
    step = pl.program_id(0)
    count, wide = dpre_ref.shape
    chunks = count // CHUNK
    steps = raw_ref.shape[0]
    bounds, base = sequence_bounds(lengths_ref, count)

    @pl.when(step == 0)
    def _():
        for chunk in range(chunks):
            shift[chunk * 3 * CHUNK : (chunk + 1) * 3 * CHUNK, :] = shifts(
                base + chunk * CHUNK, bounds, 1, CHUNK
            )
        shift[chunks * 3 * CHUNK :, :] = shifts(base, bounds, 0, 16)
        buf[...] = jnp.zeros_like(buf)
        gains[...] = jnp.zeros_like(gains)
        sums_ref[...] = jnp.zeros_like(sums_ref)

    last = pl.num_programs(0) - 1
    inner = w_ref.shape[1]
    tile_here = pl.ds(pl.multiple_of(step * wide, wide), wide)

    def share_of(product, weights):
        share = (product * weights.astype(F32)).astype(BF16)
        gains[...] += mm_nt(jnp.ones((8, share.shape[1]), BF16), share)

    def hand_over(product, weights):
        share_of(product, weights)
        by_core(product.astype(BF16), shard, mine_ref, theirs_ref)

    @pl.when(step < pl.num_programs(0) - 1)
    def _():
        buf[0:CHUNK, :] = dpre_ref[count - CHUNK :, :]
        moved = mm(shift[chunks * 3 * CHUNK :, :], dpre_ref[0 : CHUNK + 16, :])
        halo_sums = [None] * 4
        dproj = jnp.zeros((16, wide), F32)
        pre = prehalo_ref[...].astype(F32)
        for lag in (1, 2, 3):
            part = moved[(lag - 1) * 16 : lag * 16]
            dproj = dproj + part * taps_ref[3 - lag : 4 - lag, :]
            halo_sums[3 - lag] = jnp.sum(pre * part, axis=0, keepdims=True)
        halo_sums[3] = jnp.zeros((1, wide), F32)
        dhalo_ref[...] = dproj.astype(BF16)
        sums = [[jnp.zeros((8, 128), F32) for _ in range(4)] for _ in range(wide // 128)]
        for chunk in range(chunks):
            if chunk < chunks - 1:
                pair = dpre_ref[chunk * CHUNK : chunk * CHUNK + CHUNK + 16, :]
            else:
                pair = buf[...]
            moved = mm(shift[chunk * 3 * CHUNK : (chunk + 1) * 3 * CHUNK, :], pair)
            for place in range(wide // 128):
                cols = slice(place * 128, place * 128 + 128)
                for row in range(0, CHUNK, SUB):
                    span = slice(chunk * CHUNK + row, chunk * CHUNK + row + SUB)
                    pre = pre_ref[span, cols].astype(F32)
                    here = dpre_ref[span, cols].astype(F32)
                    dproj = here * taps_ref[3:4, cols]
                    sums[place][3] = sums[place][3] + fold(pre * here)
                    for lag in (1, 2, 3):
                        at = (lag - 1) * CHUNK + row
                        part = moved[at : at + SUB, cols]
                        dproj = dproj + part * taps_ref[3 - lag : 4 - lag, cols]
                        sums[place][3 - lag] = sums[place][3 - lag] + fold(pre * part)
                    dproj_ref[span, cols] = dproj.astype(BF16)
        for place in range(wide // 128):
            cols = slice(place * 128, place * 128 + 128)
            at = pl.ds(pl.multiple_of(step * wide + place * 128, 128), 128)
            for tap in range(4):
                sums_ref[tap : tap + 1, at] = (
                    jnp.sum(sums[place][tap], axis=0, keepdims=True) + halo_sums[tap][:, cols]
                )
        product = mm(turned_ref[...], dproj_ref[...]) + mm(turnhalo_ref[...], dhalo_ref[...])
        by_core(product.astype(BF16), shard, mine_ref, theirs_ref)

        @pl.when(step < last - 1)
        def _():
            share_of(product, w_ref[:, tile_here])

        @pl.when(step == last - 1)
        def _():
            share_of(product, narrow_ref[0:wide, :].astype(F32).T)

    @pl.when(step == pl.num_programs(0) - 1)
    def _():
        rate = rate_ref[:, 0:1]
        draw, drate = steps_back(raw_ref[...], dt_ref[...], rate, moves_ref[...], r_ref[...])
        low = draw.astype(BF16)
        draw_ref[...] = low
        product = mm_nt(turned_ref[...], low)
        fill = jnp.zeros((product.shape[0], wide - steps), F32)
        steps_weights = narrow_ref[narrow_ref.shape[0] - steps :, :].astype(F32).T
        hand_over(
            jnp.concatenate([product, fill], axis=1),
            jnp.concatenate([steps_weights, fill], axis=1),
        )
        heads = steps // 2
        model = w_ref.shape[0]
        sums_ref[4:5, 0:inner] = jnp.sum(mix_sums_ref[0:8, :], axis=0, keepdims=True)
        share = jnp.concatenate([share_ref[part] for part in range(share_ref.shape[0])], axis=1)
        sums_ref[5:6, 0:model] = (gains[0:1, :] + share) / row_of(gain_ref)
        skips = in_parts(mix_sums_ref[8:16, :], 2).astype(BF16)
        skips = jnp.sum(mm_nt(e0_ref[0:heads, :], skips), axis=1, keepdims=True)
        columns = [jnp.concatenate([skips, skips], axis=0), jnp.sum(draw, axis=1, keepdims=True)]
        columns = jnp.concatenate(columns + [drate, jnp.zeros((steps, 5), F32)], axis=1).T
        for place in range(3):
            sums_ref[6:7, 128 * place : 128 * place + steps] = columns[place : place + 1]
        small_ref[...] = narrowed(two_halves(sums_ref[...]))


def halve_kernel(kept_ref, got_ref, keep_ref, send_ref, *, bit):
    shard = keep_ref.shape[0]
    mine = lax.rem(lax.axis_index("dp") // bit, 2)
    for place, out_ref in ((mine, keep_ref), (1 - mine, send_ref)):
        rows = pl.ds(pl.multiple_of(place * shard, shard), shard)
        total = kept_ref[rows, :].astype(F32) + got_ref[rows, :].astype(F32)
        out_ref[...] = total.astype(out_ref.dtype)


def sum_kernel(kept_ref, got_ref, out_ref):
    out_ref[...] = (kept_ref[...].astype(F32) + got_ref[...].astype(F32)).astype(BF16)


def narrowed(small):
    few = small[6:7] + small[7:8]
    high = few.astype(BF16).astype(F32)
    return jnp.concatenate([small[0:6], high, few - high, small[8:16]], axis=0).astype(BF16)


def two_halves(small):
    half = small.shape[1] // 2
    return jnp.concatenate([small[:, 0:half], small[:, half:]], axis=0)


def quarters_kernel(
    mine_ref,
    got_ref,
    small_ref,
    smallgot_ref,
    keep_ref,
    across_ref,
    along_ref,
    both_ref,
    *,
    shard,
):
    half = mine_ref.shape[1] // 2
    row_bit = lax.rem(lax.axis_index("dp") // 2, 2)
    side = lax.axis_index("dir")
    count = mine_ref.shape[0] // 2
    small = narrowed(small_ref[...].astype(F32) + smallgot_ref[...].astype(F32))
    keep_ref[count:, :] = small.astype(F32)
    for out_ref, row, column in (
        (keep_ref, row_bit, side),
        (across_ref, row_bit, 1 - side),
        (along_ref, 1 - row_bit, side),
        (both_ref, 1 - row_bit, 1 - side),
    ):
        if out_ref is not keep_ref:
            out_ref[count:, :] = small
        for place in range(count // shard):
            rows = slice(place * shard, (place + 1) * shard)
            here = pl.ds(pl.multiple_of((2 * place + row) * shard, shard), shard)
            cols = pl.ds(pl.multiple_of(column * half, half), half)
            total = mine_ref[here, cols].astype(F32) + got_ref[here, cols].astype(F32)
            out_ref[rows, :] = total.astype(out_ref.dtype)


def levels_kernel(keep_ref, a_ref, b_ref, c_ref, own_ref, s1_ref, s2_ref, s3_ref, *, shard):
    level = lax.axis_index("dp") // 4
    count = 4 * shard
    small = [ref[count:, :].astype(F32) for ref in (a_ref, b_ref, c_ref)]
    small = narrowed(keep_ref[count:, :] + small[0] + (small[1] + small[2]))
    own_ref[shard:, :] = small.astype(F32)
    for bits, out_ref in enumerate((own_ref, s1_ref, s2_ref, s3_ref)):
        wanted = jnp.bitwise_xor(level, bits)
        rows = pl.ds(pl.multiple_of(wanted * shard, shard), shard)
        total = keep_ref[rows, :] + a_ref[rows, :].astype(F32)
        total = total + (b_ref[rows, :].astype(F32) + c_ref[rows, :].astype(F32))
        out_ref[0:shard, :] = total.astype(out_ref.dtype)
        if bits:
            out_ref[shard:, :] = small


def last_kernel(own_ref, a_ref, b_ref, c_ref, out_ref, small_ref, *, shard):
    total = own_ref[...] + a_ref[...].astype(F32)
    total = total + (b_ref[...].astype(F32) + c_ref[...].astype(F32))
    out_ref[...] = total[0:shard].astype(BF16)
    small_ref[...] = total[shard:]


def finish_kernel(
    late_ref,
    lategot_ref,
    early_ref,
    earlygot_ref,
    small_ref,
    gx_ref,
    gz_ref,
    gbc_ref,
    go_ref,
    gtaps_ref,
    gmix_ref,
    gin_ref,
    gskip_ref,
    gbias_ref,
    galog_ref,
):
    side = lax.axis_index("dir")
    half = late_ref.shape[1]
    inner = gx_ref.shape[1]
    model = go_ref.shape[1]
    shard = gx_ref.shape[0]
    mine = late_ref[...].astype(F32)
    other = lategot_ref[...].astype(F32)
    first = jnp.where(side == 0, mine, other)
    second = jnp.where(side == 0, other, mine)
    gx_ref[:, 0:half] = first
    gx_ref[:, half:inner] = second[:, 0 : inner - half]
    gbc_ref[...] = second[:, inner - half : inner - half + gbc_ref.shape[1]]
    early = early_ref[...].astype(F32) + earlygot_ref[...].astype(F32)
    go_ref[0:shard, :] = early[:, 0:model]
    go_ref[shard : 2 * shard, :] = early[:, model : 2 * model]
    gz_ref[...] = early[:, 2 * model :]
    small = jnp.concatenate([small_ref[0:8, :], small_ref[8:16, :]], axis=1)
    gtaps_ref[...] = small[0:4, 0 : gtaps_ref.shape[1]]
    gmix_ref[...] = small[4:5, 0:inner].reshape(inner)
    gin_ref[...] = small[5:6, 0:model].reshape(model)
    few = small[6:7] + small[7:8]
    heads = gskip_ref.shape[0]
    gskip_ref[...] = few[:, 0:128].reshape(128)[0:heads]
    gbias_ref[0:1, :] = few[:, 128 : 128 + heads]
    gbias_ref[1:2, :] = few[:, 128 + heads : 128 + 2 * heads]
    galog_ref[0:1, :] = few[:, 256 : 256 + heads]
    galog_ref[1:2, :] = few[:, 256 + heads : 256 + 2 * heads]


def inputs_kernel(
    x_ref,
    c_ref,
    gain_ref,
    dproj_ref,
    dhalo_ref,
    draw_ref,
    dz_ref,
    wx_ref,
    wbc_ref,
    wz_ref,
    mixed_ref,
    wo_ref,
    gin_ref,
    out_ref,
    dproj,
):
    step = pl.program_id(0)
    inner = wx_ref.shape[1]
    steps = draw_ref.shape[0]
    narrow = wbc_ref.shape[0] - steps

    @pl.when(step == pl.num_programs(0) - 1)
    def _():
        tail = slice(dproj_ref.shape[0] - 16, dproj_ref.shape[0])
        both = dproj_ref[tail, :].astype(F32) + dhalo_ref[...].astype(F32)
        dproj[...] = dproj_ref[...]
        dproj[tail, :] = both.astype(BF16)

    @pl.when(step < pl.num_programs(0) - 1)
    def _():
        dproj[...] = dproj_ref[...]

    dn = mm_nt(dproj[:, 0:inner], wx_ref[...])
    dn = dn + mm_nt(dz_ref[...], wz_ref[...])
    dn = dn + mm(dproj[:, inner:], wbc_ref[0:narrow, :])
    dn = dn + mm_tn(draw_ref[...], wbc_ref[narrow:, :])
    x = x_ref[...].astype(F32)
    inv = lax.rsqrt(jnp.mean(x * x, axis=1, keepdims=True) + EPS)
    unit = x * inv
    out_ref[...] = (x + mm(mixed_ref[...], wo_ref[...])).astype(BF16)
    f = dn * row_of(gain_ref)
    back = inv * (f - unit * jnp.mean(f * unit, axis=1, keepdims=True))
    gin_ref[...] = (c_ref[...].astype(F32) + back).astype(BF16)


def smem():
    return pl.BlockSpec(memory_space=pltpu.SMEM)


def resident():
    return pl.BlockSpec(memory_space=pltpu.VMEM)


def anywhere():
    return pl.BlockSpec(memory_space=pl.ANY)


def whole(shape):
    return pl.BlockSpec(shape, lambda i: (0,) * len(shape), pipeline_mode=pl.Buffered(1))


def rows_of(count, width):
    return pl.BlockSpec((count, width), lambda i: (i, 0))


def lanes_of(height, count):
    return pl.BlockSpec((height, count), lambda i: (0, i))


def parts_of(count, *rest):
    return pl.BlockSpec((count,) + rest, lambda i: (i,) + (0,) * len(rest))


def cost(microseconds):
    flops = int(microseconds * 1.15e9)
    return pl.CostEstimate(flops=flops, bytes_accessed=0, transcendentals=0)


def call(kernel, name, grid, in_specs, outs, scratch, cost_us, args, vmem, aliases=()):
    return pl.pallas_call(
        kernel,
        name=name,
        grid=(grid,),
        in_specs=in_specs,
        out_specs=[spec for spec, _, _ in outs],
        out_shape=[jax.ShapeDtypeStruct(shape, dtype) for _, shape, dtype in outs],
        scratch_shapes=scratch,
        input_output_aliases=dict(aliases),
        compiler_params=pltpu.CompilerParams(
            vmem_limit_bytes=vmem * MIB, dimension_semantics=("arbitrary",)
        ),
        cost_estimate=cost(cost_us),
    )(*args)


def traded(values, axis, bit, size):
    return lax.ppermute(values, axis, [(i, i ^ bit) for i in range(size)])


def ordered(first, second):
    return lax.optimization_barrier((first, second))


def sum_shards(grad, dp_count):
    index = lax.axis_index("dp")
    held = grad.reshape(dp_count, grad.shape[0] // dp_count, grad.shape[1])
    bit = 1
    while bit < dp_count:
        paired = held.reshape(held.shape[0] // 2, 2, held.shape[1], held.shape[2])
        mine = (index // bit) % 2
        kept = lax.dynamic_index_in_dim(paired, mine, 1, keepdims=False)
        sent = lax.dynamic_index_in_dim(paired, 1 - mine, 1, keepdims=False).astype(BF16)
        held = kept.astype(F32) + traded(sent, "dp", bit, dp_count).astype(F32)
        bit *= 2
    held = held[0].astype(BF16)
    return held.astype(F32) + traded(held, "dir", 1, 2).astype(F32)


def sum_all(values, dp_count):
    bit = 1
    while bit < dp_count:
        values = values + traded(values, "dp", bit, dp_count)
        bit *= 2
    return values + traded(values, "dir", 1, 2)


def local(
    dp_count,
    hidden_in,
    lengths,
    gain_in,
    w_x,
    w_z,
    w_bcdt,
    conv_w,
    dt_bias,
    a_log,
    d_skip,
    gain_mix,
    w_out,
    cotangent,
):
    x = hidden_in[0]
    cot = cotangent[0]
    count, model = x.shape
    inner = w_x.shape[1]
    channels = conv_w.shape[1]
    heads = d_skip.shape[0]
    width = inner // heads
    state = (channels - inner) // 4
    chunks = count // CHUNK
    steps = 2 * heads

    w_narrow = w_bcdt.T
    halo = lax.ppermute(x[count - 16 :], "dir", [(0, 1)])

    spread = np.repeat(np.eye(heads, dtype=np.float32), width, axis=1)
    zeros = np.zeros_like(spread)
    e0 = jnp.asarray(np.concatenate([spread, zeros, spread, zeros]), BF16)
    e1 = jnp.asarray(np.concatenate([zeros, spread, zeros, spread]), BF16)
    spans = np.zeros((8, 6 * CHUNK), np.float32)
    for head in range(2):
        columns = slice(head * width, (head + 1) * width)
        spans[head, head * CHUNK : (head + 1) * CHUNK] = 1.0
        spans[head, 4 * CHUNK : 5 * CHUNK][columns] = 1.0
        spans[2 + head, (2 + head) * CHUNK : (3 + head) * CHUNK] = 1.0
        spans[2 + head, 4 * CHUNK : 5 * CHUNK][columns] = 1.0
        spans[2 + head, 5 * CHUNK : 6 * CHUNK][columns] = 1.0
    spans = jnp.asarray(spans, BF16)

    def rows_out(size, columns, dtype):
        return (rows_of(size, columns), (count, columns), dtype)

    def full(shape, dtype):
        return (pl.BlockSpec(shape, lambda i: (0,) * len(shape)), shape, dtype)

    per = ROWS // CHUNK
    state_f32 = pltpu.VMEM((state, inner), F32)
    state_bf16 = pltpu.VMEM((state, inner), BF16)
    row_f32 = pltpu.VMEM((1, inner), F32)
    chunk_f32 = pltpu.VMEM((CHUNK, inner), F32)
    chunk_bf16 = pltpu.VMEM((CHUNK, inner), BF16)
    (
        normed,
        raw,
        dt,
        rate,
        target,
        source,
        factors,
        keeps,
        pre,
        act,
        slope,
        sl0,
        sf1,
        send,
        pre_halo,
        turn_halo,
    ) = call(
        proj_kernel,
        "proj",
        count // ROWS,
        [
            smem(),
            smem(),
            smem(),
            whole((count, model)),
            whole((16, model)),
            whole((model,)),
            whole((model, inner)),
            whole(w_narrow.shape),
            whole(conv_w.shape),
            whole(e0.shape),
            whole(e1.shape),
        ],
        [
            full((count, model), BF16),
            full((steps, count), F32),
            full((steps, count), F32),
            full((steps, 128), F32),
            full((steps, count), F32),
            full((steps, count), F32),
            full((2, count, 2 * steps), BF16),
            full((6, chunks, inner), F32),
            rows_out(ROWS, channels, BF16),
            rows_out(ROWS, channels, BF16),
            rows_out(ROWS, channels, BF16),
            (parts_of(per, state, inner), (chunks, state, inner), BF16),
            (parts_of(per, state, inner), (chunks, state, inner), BF16),
            full((state, inner), BF16),
            full((16, channels), BF16),
            full((model, 16), BF16),
        ],
        [
            pltpu.VMEM((16 + ROWS, channels), BF16),
            state_f32,
            state_f32,
            chunk_bf16,
            chunk_bf16,
        ],
        US_PROJ,
        (lengths, dt_bias, a_log, x, halo, gain_in, w_x, w_narrow, conv_w, e0, e1),
        VMEM_PROJ,
    )
    received = lax.ppermute(send, "dir", SWAP)

    gate_z, d_norm, turned = call(
        gates_kernel,
        "gates",
        count // ROWS,
        [
            rows_of(ROWS, model),
            rows_of(ROWS, model),
            whole((model, inner)),
            whole((inner, model)),
        ],
        [
            rows_out(ROWS, inner, BF16),
            rows_out(ROWS, inner, BF16),
            (lanes_of(model, ROWS), (model, count), BF16),
        ],
        [],
        US_GATES,
        (normed, cot, w_z, w_out),
        VMEM_GATES,
    )

    def down_rows(width):
        return pl.BlockSpec((CHUNK, width), lambda i: (chunks - 1 - i, 0))

    def down_lanes(height):
        return pl.BlockSpec((height, CHUNK), lambda i: (0, chunks - 1 - i))

    def down_parts(*rest):
        return pl.BlockSpec((1,) + rest, lambda i: (chunks - 1 - i,) + (0,) * len(rest))

    states = (down_parts(state, inner), (chunks, state, inner), BF16)
    mixed, dz, dy, r, dcc, dl0, df1, s0, s1, d_send, mix_sums = call(
        mix_kernel,
        "mix",
        chunks,
        [
            smem(),
            smem(),
            down_rows(channels),
            down_lanes(steps),
            down_lanes(steps),
            pl.BlockSpec((1, CHUNK, 2 * steps), lambda i: (0, chunks - 1 - i, 0)),
            down_parts(state, inner),
            down_parts(state, inner),
            whole((6, chunks, inner)),
            whole((state, inner)),
            down_rows(inner),
            down_rows(inner),
            whole((inner,)),
            whole(e0.shape),
            whole(e1.shape),
        ],
        [
            (down_rows(inner), (count, inner), BF16),
            (down_rows(inner), (count, inner), BF16),
            (down_rows(inner), (count, inner), BF16),
            (down_lanes(steps), (steps, count), F32),
            (down_rows(2 * state), (count, 2 * state), F32),
            states,
            states,
            states,
            states,
            full((state, inner), BF16),
            full((16, inner), F32),
        ],
        [state_f32] * 3 + [chunk_f32] * 8 + [chunk_bf16] * 4 + [row_f32] * 2,
        US_MIX,
        (
            lengths,
            d_skip,
            act,
            target,
            source,
            factors,
            sl0,
            sf1,
            keeps,
            received,
            gate_z,
            d_norm,
            gain_mix,
            e0,
            e1,
        ),
        VMEM_MIX,
    )
    d_received = lax.ppermute(d_send, "dir", SWAP)

    def plain(kernel, name, args, outs, specs=None, out_specs=None, grid=()):
        resident = [pl.BlockSpec(memory_space=pltpu.VMEM)]
        return pl.pallas_call(
            kernel,
            name=name,
            grid=grid,
            in_specs=specs or resident * len(args),
            out_specs=out_specs or resident * len(outs),
            out_shape=[jax.ShapeDtypeStruct(shape, dtype) for shape, dtype in outs],
            compiler_params=pltpu.CompilerParams(vmem_limit_bytes=VMEM_SUMS * MIB),
            cost_estimate=cost(US_SUMS),
        )(*args)

    def halve(name, kept, got, bit):
        rows, wide = got.shape
        outs = [((rows // 2, wide), F32), ((rows // 2, wide), BF16)]
        return plain(
            functools.partial(halve_kernel, bit=bit),
            name,
            (kept, got),
            outs,
            [rows_of(2 * piece, wide)] * 2,
            [rows_of(piece, wide)] * 2,
            (rows // (2 * piece),),
        )

    blocks = 4
    shard = model // dp_count
    direct = dp_count == 16 and shard % 16 == 0
    piece = model // 16
    early_rows = (rows_of(model // 2 // blocks, 2 * inner), (model // 2, 2 * inner), BF16)
    early_mine, early_theirs, z_share = call(
        functools.partial(weights_kernel, shard=piece),
        "weights",
        blocks,
        [
            rows_of(model // blocks, count),
            whole((count, inner)),
            lanes_of(count, inner // blocks),
            whole((count, model)),
            rows_of(model // blocks, inner),
        ],
        [
            early_rows,
            early_rows,
            (pl.BlockSpec((1, 1, model // blocks), lambda i: (i, 0, 0)), (blocks, 1, model // blocks), F32),
        ],
        [],
        US_WEIGHTS,
        (turned, dz, mixed, cot, w_z),
        VMEM_WEIGHTS,
    )
    (early_mine, early_theirs), d_received = ordered((early_mine, early_theirs), d_received)

    def back(skipped, taken, start, dpre, moves):
        def rows_from(width):
            return pl.BlockSpec((CHUNK, width), lambda i: (i + skipped, 0))

        def lanes_from(height):
            return pl.BlockSpec((height, CHUNK), lambda i: (0, i + skipped))

        def parts_from(*rest):
            return pl.BlockSpec((1,) + rest, lambda i: (i + skipped,) + (0,) * len(rest))

        return call(
            functools.partial(back_kernel, skipped=skipped, chunks=chunks),
            "back" + str(skipped),
            taken,
            [
                smem(),
                smem(),
                rows_from(channels),
                rows_from(channels),
                lanes_from(steps),
                lanes_from(steps),
                pl.BlockSpec((1, CHUNK, 2 * steps), lambda i: (1, i + skipped, 0)),
                rows_from(2 * state),
                rows_from(inner),
                parts_from(state, inner),
                parts_from(state, inner),
                parts_from(state, inner),
                parts_from(state, inner),
                whole((6, chunks, inner)),
                whole((state, inner)),
                whole(start.shape),
                whole(e0.shape),
                whole(e1.shape),
                whole(spans.shape),
                anywhere(),
                anywhere(),
            ],
            [
                (rows_from(channels), (count, channels), BF16),
                (lanes_from(6 * heads), (6 * heads, count), F32),
                full((state, inner), F32),
            ],
            [
                state_f32,
                pltpu.VMEM((CHUNK, CHUNK), F32),
            ]
            + [chunk_bf16] * 2
            + [state_bf16] * 2
            + [pltpu.VMEM((16, inner), F32)],
            US_BACK * taken // chunks,
            (
                lengths,
                d_skip,
                act,
                slope,
                target,
                source,
                factors,
                dcc,
                dy,
                s0,
                s1,
                dl0,
                df1,
                keeps,
                d_received,
                start,
                e0,
                e1,
                spans,
                dpre,
                moves,
            ),
            VMEM_BACK,
            {19: 0, 20: 1} if skipped else {},
        )

    first = 1
    dpre, moves, carry = back(0, first, d_received, received, received)
    if direct:
        early_got = traded(early_theirs, "dp", 1, dp_count)
        early_keep, early_send = halve("halve_y", early_mine, early_got, 2)
        early_send, carry = ordered(early_send, carry)
        early_got = traded(early_send, "dp", 2, dp_count)
    dpre, moves, _ = back(first, chunks - first, carry, dpre, moves)
    if direct:
        early_keep, early_send = halve("halve_z", early_keep, early_got, 4)
        early_send, dpre = ordered(early_send, dpre)
        early_got = traded(early_send, "dp", 4, dp_count)

    tile = 256
    tiles = channels // tile
    def tile_of(height):
        return pl.BlockSpec((height, tile), lambda i: (0, jnp.minimum(i, tiles - 1)))

    wide = (tiles + 1) * tile
    late_out = (lanes_of(model // 2, tile), (model // 2, wide), BF16)
    dproj, dhalo, late_mine, late_theirs, draw, small = call(
        functools.partial(conv_back_kernel, shard=piece),
        "conv_back",
        tiles + 1,
        [
            smem(),
            whole((model, count)),
            whole((model, 16)),
            tile_of(count),
            tile_of(count),
            tile_of(16),
            tile_of(conv_w.shape[0]),
            whole((steps, count)),
            whole((steps, count)),
            whole((steps, 128)),
            whole((6 * heads, count)),
            whole((steps, count)),
            whole((model, inner)),
            whole(w_narrow.shape),
            whole((model,)),
            whole(z_share.shape),
            whole(mix_sums.shape),
            whole(e0.shape),
        ],
        [
            (tile_of(count), (count, channels), BF16),
            (tile_of(16), (16, channels), BF16),
            late_out,
            late_out,
            full((steps, count), BF16),
            full((16, wide // 2), BF16),
        ],
        [
            pltpu.VMEM((3 * count + 48, CHUNK + 16), BF16),
            pltpu.VMEM((CHUNK + 16, tile), BF16),
            pltpu.VMEM((8, model), F32),
            pltpu.VMEM((8, wide), F32),
        ],
        US_CONV,
        (
            lengths,
            turned,
            turn_halo,
            dpre,
            pre,
            pre_halo,
            conv_w,
            raw,
            dt,
            rate,
            moves,
            r,
            w_x,
            w_narrow,
            gain_in,
            z_share,
            mix_sums,
            e0,
        ),
        VMEM_CONV,
    )
    d_halo = lax.ppermute(dhalo, "dir", [(1, 0)])

    grad_in, out = call(
        inputs_kernel,
        "inputs",
        count // ROWS,
        [
            rows_of(ROWS, model),
            rows_of(ROWS, model),
            whole((model,)),
            rows_of(ROWS, channels),
            whole((16, channels)),
            lanes_of(steps, ROWS),
            rows_of(ROWS, inner),
            whole((model, inner)),
            whole(w_narrow.shape),
            whole((model, inner)),
            rows_of(ROWS, inner),
            whole((inner, model)),
        ],
        [rows_out(ROWS, model, BF16), rows_out(ROWS, model, BF16)],
        [pltpu.VMEM((ROWS, channels), BF16)],
        US_INPUTS,
        (x, cot, gain_in, dproj, d_halo, draw, dz, w_x, w_narrow, w_z, mixed, w_out),
        VMEM_INPUTS,
    )

    if not direct:
        def undivided(mine, theirs):
            even = lax.axis_index("dp") % 2 == 0
            both = [jnp.where(even, mine, theirs), jnp.where(even, theirs, mine)]
            both = [part.reshape(8, 1, piece, part.shape[1]) for part in both]
            return jnp.concatenate(both, axis=1).reshape(model, mine.shape[1])

        early = undivided(early_mine, early_theirs)
        g_out = early[:, :inner].reshape(16, piece, 2, model).transpose(0, 2, 1, 3)
        late = sum_shards(undivided(late_mine, late_theirs), dp_count)
        small = jnp.concatenate([small[0:8], small[8:16]], axis=1).astype(F32)
        small = sum_all(small, dp_count)
        return (
            out[None],
            grad_in[None],
            late[:, :inner],
            sum_shards(early[:, inner:], dp_count),
            late[:, inner : inner + 4 * state + steps],
            sum_shards(g_out.reshape(inner, model), dp_count),
            small[5, :model],
            small[0:4, :channels],
            small[6, 128 : 128 + steps].reshape(dt_bias.shape),
            small[6, 256 : 256 + steps].reshape(a_log.shape),
            small[6, :heads],
            small[4, :inner],
        )

    early_got, late_theirs = ordered(early_got, late_theirs)
    late_got = traded(late_theirs, "dp", 1, dp_count)
    small_got = traded(small, "dp", 1, dp_count)
    quarter = (model // 4 + 16, wide // 2)
    kept, across, along, both = plain(
        functools.partial(quarters_kernel, shard=piece),
        "quarters",
        (late_mine, late_got, small, small_got),
        [((model // 4 + 16, wide // 2), F32), (quarter, BF16), (quarter, BF16), (quarter, BF16)],
    )
    early_keep, early_send = halve("halve_z2", early_keep, early_got, 8)
    corners = [(a, b) for a in range(2) for b in range(dp_count)]
    across = traded(across, "dir", 1, 2)
    along = traded(along, "dp", 2, dp_count)
    both = lax.ppermute(
        both,
        ("dir", "dp"),
        [(a * dp_count + b, (1 - a) * dp_count + (b ^ 2)) for a, b in corners],
    )
    early_got = traded(early_send, "dp", 8, dp_count)
    (early,) = plain(sum_kernel, "early_sum", (early_keep, early_got), [((piece, 2 * inner), BF16)])
    grad_in, early, both = lax.optimization_barrier((grad_in, early, both))
    early_got = traded(early, "dir", 1, 2)
    message = (piece + 16, wide // 2)
    own, *sends = plain(
        functools.partial(levels_kernel, shard=piece),
        "levels",
        (kept, across, along, both),
        [((piece + 16, wide // 2), F32)] + [(message, BF16)] * 3,
    )
    gots = [traded(sent, "dp", 4 * bits, dp_count) for bits, sent in zip((1, 2, 3), sends)]
    late, small = plain(
        functools.partial(last_kernel, shard=piece),
        "last",
        (own, *gots),
        [((piece, wide // 2), BF16), ((16, wide // 2), F32)],
    )
    late_got = traded(late, "dir", 1, 2)
    g_x, g_zz, g_bc, g_o, g_taps, g_mix, g_in, g_skip, g_bias, g_alog = plain(
        finish_kernel,
        "finish",
        (late, late_got, early, early_got, small),
        [
            ((piece, inner), F32),
            ((piece, inner), F32),
            ((piece, w_bcdt.shape[1]), F32),
            ((2 * piece, model), F32),
            (conv_w.shape, F32),
            ((inner,), F32),
            ((model,), F32),
            ((heads,), F32),
            (dt_bias.shape, F32),
            (a_log.shape, F32),
        ],
    )
    return (
        out[None],
        grad_in[None],
        g_x,
        g_zz,
        g_bc,
        g_o,
        g_in,
        g_taps,
        g_bias,
        g_alog,
        g_skip,
        g_mix,
    )


def solution(mesh):
    return jax.shard_map(
        functools.partial(local, mesh.shape["dp"]),
        mesh=mesh,
        in_specs=(
            P("dir", "dp", None),
            P("dp", None),
            P(),
            P(),
            P(),
            P(),
            P(),
            P(),
            P(),
            P(),
            P(),
            P(),
            P("dir", "dp", None),
        ),
        out_specs=(
            P("dir", "dp", None),
            P("dir", "dp", None),
            P("dp", None),
            P("dp", None),
            P("dp", None),
            P("dp", None),
            P(),
            P(),
            P(),
            P(),
            P(),
            P(),
        ),
        check_vma=False,
    )
```
